32 devices in a mesh: pts: 32 (over z, y, x, core).
Axes of the slice: x: 2, y: 2, z: 4, core: 2. Of those that a mesh axis runs over, the one named last changes fastest.
Arguments:
- features: bfloat16 [131072, 256], P('pts'), may hold values from -6 to 6
- coords: float32 [2, 131072], P(None, 'pts'), may hold values from 0 to 1
- fourier_basis: float32 [2, 64], replicated, may hold values from -4 to 4
- block_items: int32 [1024], P('pts'), may hold values from 0 to 15, as said below
- point_mask: int32 [131072], P('pts'), may hold values from 0 to 1, as said below
- cotangent: bfloat16 [131072, 256], P('pts'), may hold values from -6 to 6
- square_weight: float32 [7, 65536], P(None, 'pts')
- square_first: float32 [7, 65536], P(None, 'pts'), may hold values from -0.00061035156 to 0.00061035156
- square_second: float32 [7, 65536], P(None, 'pts'), may hold values from 2.5518217e-08 to 4.1221733e-07
- expand_weight: float32 [2, 131072], P(None, 'pts'), may hold values from -0.375 to 0.375
- expand_first: float32 [2, 131072], P(None, 'pts'), may hold values from -0.00061035156 to 0.00061035156
- expand_second: float32 [2, 131072], P(None, 'pts'), may hold values from 2.5518217e-08 to 4.1221733e-07
- contract_weight: float32 [2, 131072], P(None, 'pts'), may hold values from -0.25 to 0.25
- contract_first: float32 [2, 131072], P(None, 'pts'), may hold values from -0.00061035156 to 0.00061035156
- contract_second: float32 [2, 131072], P(None, 'pts'), may hold values from 2.5518217e-08 to 4.1221733e-07
- fourier_weight: float32 [32768], P('pts'), may hold values from -0.5 to 0.5
- fourier_first: float32 [32768], P('pts'), may hold values from -0.00061035156 to 0.00061035156
- fourier_second: float32 [32768], P('pts'), may hold values from 2.5518217e-08 to 4.1221733e-07
- vector_weight: float32 [8, 256], replicated
- vector_first: float32 [8, 256], replicated, may hold values from -0.001953125 to 0.001953125
- vector_second: float32 [8, 256], replicated, may hold values from 2.3555276e-07 to 3.7295854e-06
- hidden_weight: float32 [2, 512], replicated, may hold values from -1.8 to 1.8
- hidden_first: float32 [2, 512], replicated, may hold values from -0.001953125 to 0.001953125
- hidden_second: float32 [2, 512], replicated, may hold values from 7.361024e-09 to 1.1777638e-07
Outputs:
- layer_output: bfloat16 [131072, 256], P('pts')
- input_grad: float32 [131072, 256], P('pts')
- grad_norm: float32 [], replicated
- new_square_first: float32 [7, 65536], P(None, 'pts')
- new_square_second: float32 [7, 65536], P(None, 'pts')
- new_square_weight: float32 [7, 65536], P(None, 'pts')
- new_expand_first: float32 [2, 131072], P(None, 'pts')
- new_expand_second: float32 [2, 131072], P(None, 'pts')
- new_expand_weight: float32 [2, 131072], P(None, 'pts')
- new_contract_first: float32 [2, 131072], P(None, 'pts')
- new_contract_second: float32 [2, 131072], P(None, 'pts')
- new_contract_weight: float32 [2, 131072], P(None, 'pts')
- new_fourier_first: float32 [32768], P('pts')
- new_fourier_second: float32 [32768], P('pts')
- new_fourier_weight: float32 [32768], P('pts')
- new_vector_first: float32 [8, 256], replicated
- new_vector_second: float32 [8, 256], replicated
- new_vector_weight: float32 [8, 256], replicated
- new_hidden_first: float32 [2, 512], replicated
- new_hidden_second: float32 [2, 512], replicated
- new_hidden_weight: float32 [2, 512], replicated
The draws below stay inside these ranges and needn't reach their ends.
Inputs may be any that keep to these rules, and one draw needn't show every extreme that they name: `block_items`: each of the 16 items owns two or more blocks of 128 points; the item of the first block also owns the last block. `point_mask`: the first point of every block of 128 points is 1.
All inputs are finite; a program needn't handle non-finite values.
Results may differ from the reference program's by a relative error of at most 0.02.
Values may be sent and summed in bfloat16 or wider, within the bound.
A program may use at most 192 MiB of HBM per device.

```python
import math
import jax
import jax.numpy as jnp
from jax import lax

D = 256
H = 8
E = 32
F = 512
FOUR = 128
BLOCK = 128
STEP = 10
TOKENS = 131072
ITEMS = 16
PARAMS = 1018880


def draw_block_items(key, part):
    key = jax.random.fold_in(key, 11)
    blocks = TOKENS // BLOCK
    heft_key, shuffle_key = jax.random.split(key)
    item_heft = jax.random.randint(heft_key, (ITEMS,), 1, 9)
    total_heft = jnp.sum(item_heft)
    spare_blocks = blocks - 2 * ITEMS
    counts = 2 + item_heft * spare_blocks // total_heft
    counts = counts.at[0].add(blocks - jnp.sum(counts))
    run_ends = jnp.cumsum(counts)
    positions = jnp.arange(blocks, dtype=jnp.int32)
    sorted_ids = jnp.sum((positions[:, None] >= run_ends[None, :]).astype(jnp.int32), axis=1)
    shuffled = sorted_ids[jax.random.permutation(shuffle_key, blocks)]
    first_item = shuffled[0]
    others = jnp.where((shuffled == first_item) & (positions > 0), positions, 0)
    swap_at = jnp.max(others)
    last_value = shuffled[blocks - 1]
    swapped = shuffled.at[swap_at].set(last_value)
    swapped = swapped.at[blocks - 1].set(first_item)
    return swapped.astype(jnp.int32)


def draw_point_mask(key, part):
    key = jax.random.fold_in(key, 23)
    blocks = TOKENS // BLOCK
    threshold = 300 + 600 * jnp.arange(blocks, dtype=jnp.int32) // max(blocks - 1, 1)
    tickets = jax.random.randint(key, (blocks, BLOCK), 0, 1000)
    live_points = (tickets < threshold[:, None]).astype(jnp.int32)
    leading_point = (jnp.arange(BLOCK) == 0).astype(jnp.int32)
    return jnp.maximum(live_points, leading_point[None, :]).reshape(TOKENS).astype(jnp.int32)


def draw_square_weight(key, part):
    key = jax.random.fold_in(key, 37)
    scales = jnp.array([1.0, 1.0, 1.0, math.sqrt(8.0), 1.0, 1.0, math.sqrt(8.0)], jnp.float32) * D ** (-0.5)
    noise = jax.random.normal(key, (7, D * D), jnp.float32)
    return noise * scales[:, None]


def draw_vector_weight(key, part):
    key = jax.random.fold_in(key, 41)
    ramp = jnp.arange(D, dtype=jnp.float32) / D
    rising = 0.6 + 1.2 * ramp
    noise = jax.random.normal(key, (8, D), jnp.float32) * 0.3
    gain_rows = rising[None, :] * (1.0 + 0.2 * noise)
    row_index = jnp.arange(8)[:, None]
    is_gain = (row_index == 0) | (row_index == 2) | (row_index == 4)
    return jnp.where(is_gain, gain_rows, noise)


def level_of(rng, dims, pieces, low, top_value):
    def one(axis_at, parts):
        heights = jax.random.uniform(jax.random.fold_in(jax.random.fold_in(rng, 6), axis_at), (parts,), jnp.float32, low / len(pieces), top_value / len(pieces))
        return jnp.repeat(jnp.exp(heights), dims[axis_at] // parts).reshape((-1,) + (1,) * (len(dims) - axis_at - 1))

    level = one(*pieces[0])
    for cut in pieces[1:]:
        level = level * one(*cut)
    return level


def scatter_about(own_key, shape, deviation, bound, cuts=(), held_as=jnp.bfloat16):
    values = deviation * jax.random.normal(own_key, shape, jnp.float32)
    if cuts:
        values = values * level_of(own_key, shape, cuts, -0.22, 0.18)
    return jnp.clip(values, -bound, bound).astype(held_as)


def setup_inputs(seed: int = 0) -> dict:
    key_list = jax.random.split(jax.random.key(seed), 25)
    features = scatter_about(key_list[0], (TOKENS, D), 1.0, 6.0, ((0, 32),))
    coords = jnp.clip(1.0 * jax.random.uniform(key_list[1], (2, TOKENS), jnp.float32) ** level_of(key_list[1], (2, TOKENS), ((1, 32),), -0.2, 0.2), 0.0, 1.0)
    fourier_basis = scatter_about(key_list[2], (2, FOUR // 2), 1.0, 4.0, (), jnp.float32)
    block_items = draw_block_items(jax.random.fold_in(key_list[24], 71), 0)
    point_mask = draw_point_mask(jax.random.fold_in(key_list[24], 71), 0)
    cotangent = scatter_about(key_list[5], (TOKENS, D), 1.0, 6.0, ((0, 32),))
    square_weight = draw_square_weight(jax.random.fold_in(key_list[24], 71), 0)
    square_first = scatter_about(key_list[7], (7, D * D), (0.111 * PARAMS ** -0.5), 0.00061035156, ((1, 32),), jnp.float32)
    square_second = jnp.clip(jnp.exp(math.log(4.12217332268483e-07) - 2.7821581 * jax.random.uniform(key_list[8], (7, D * D), jnp.float32) ** level_of(key_list[8], (7, D * D), ((1, 32),), -0.2, 0.2)), 2.551821687291067e-08, 4.12217332268483e-07)
    expand_weight = scatter_about(key_list[9], (2, D * F), D ** -0.5, 0.375, ((1, 32),), jnp.float32)
    expand_first = scatter_about(key_list[10], (2, D * F), (0.111 * PARAMS ** -0.5), 0.00061035156, ((1, 32),), jnp.float32)
    expand_second = jnp.clip(jnp.exp(math.log(4.12217332268483e-07) - 2.7821581 * jax.random.uniform(key_list[11], (2, D * F), jnp.float32) ** level_of(key_list[11], (2, D * F), ((1, 32),), -0.2, 0.2)), 2.551821687291067e-08, 4.12217332268483e-07)
    contract_weight = scatter_about(key_list[12], (2, F * D), F ** -0.5, 0.25, ((1, 32),), jnp.float32)
    contract_first = scatter_about(key_list[13], (2, F * D), (0.111 * PARAMS ** -0.5), 0.00061035156, ((1, 32),), jnp.float32)
    contract_second = jnp.clip(jnp.exp(math.log(4.12217332268483e-07) - 2.7821581 * jax.random.uniform(key_list[14], (2, F * D), jnp.float32) ** level_of(key_list[14], (2, F * D), ((1, 32),), -0.2, 0.2)), 2.551821687291067e-08, 4.12217332268483e-07)
    fourier_weight = scatter_about(key_list[15], (FOUR * D,), FOUR ** -0.5, 0.5, ((0, 32),), jnp.float32)
    fourier_first = scatter_about(key_list[16], (FOUR * D,), (0.111 * PARAMS ** -0.5), 0.00061035156, ((0, 32),), jnp.float32)
    fourier_second = jnp.clip(jnp.exp(math.log(4.12217332268483e-07) - 2.7821581 * jax.random.uniform(key_list[17], (FOUR * D,), jnp.float32) ** level_of(key_list[17], (FOUR * D,), ((0, 32),), -0.2, 0.2)), 2.551821687291067e-08, 4.12217332268483e-07)
    vector_weight = draw_vector_weight(jax.random.fold_in(key_list[24], 71), 0)
    vector_first = scatter_about(key_list[19], (8, D), (0.333 * PARAMS ** -0.5), 0.001953125, (), jnp.float32)
    vector_second = jnp.clip(jnp.exp(jax.random.uniform(key_list[20], (8, D), jnp.float32, math.log(2.35552761296276e-07), math.log(3.7295853871910367e-06))), 2.35552761296276e-07, 3.7295853871910367e-06)
    hidden_weight = scatter_about(key_list[21], (2, F), 0.3, 1.8, (), jnp.float32)
    hidden_first = scatter_about(key_list[22], (2, F), (0.333 * PARAMS ** -0.5), 0.001953125, (), jnp.float32)
    hidden_second = jnp.clip(jnp.exp(jax.random.uniform(key_list[23], (2, F), jnp.float32, math.log(7.361023790508625e-09), math.log(1.17776380648138e-07))), 7.361023790508625e-09, 1.17776380648138e-07)
    return {"features": features, "coords": coords, "fourier_basis": fourier_basis, "block_items": block_items, "point_mask": point_mask, "cotangent": cotangent, "square_weight": square_weight, "square_first": square_first, "square_second": square_second, "expand_weight": expand_weight, "expand_first": expand_first, "expand_second": expand_second, "contract_weight": contract_weight, "contract_first": contract_first, "contract_second": contract_second, "fourier_weight": fourier_weight, "fourier_first": fourier_first, "fourier_second": fourier_second, "vector_weight": vector_weight, "vector_first": vector_first, "vector_second": vector_second, "hidden_weight": hidden_weight, "hidden_first": hidden_first, "hidden_second": hidden_second}


@jax.custom_vjp
def low(v):
    return lax.optimization_barrier(v.astype(jnp.bfloat16)).astype(jnp.float32)

@jax.custom_vjp
def low_back(v):
    return v

def low_keep(v):
    return (low(v), None)

def low_pass(kept, grad):
    return (grad,)

def back_keep(v):
    return (v, None)

def back_low(kept, grad):
    return (low(grad),)
low.defvjp(low_keep, low_pass)
low_back.defvjp(back_keep, back_low)
NORM_EPS = 1e-05
GELU_C = math.sqrt(2.0 / math.pi)
GELU_A = 0.044715
BETA_ONE = 0.9
BETA_TWO = 0.95
ADAM_EPS = 1e-08
WEIGHT_DECAY = 0.1
RATE_MATRIX = 0.05
RATE_VECTOR = 0.25
CLIP_NORM = 1.0
HIGHEST_PRECISION = lax.Precision.HIGHEST

def matmul(left, right):
    return jnp.dot(left, right, precision=HIGHEST_PRECISION, preferred_element_type=jnp.float32)

def layer_norm(values, norm_gain, norm_bias):
    centred = values - lax.optimization_barrier(jnp.mean(values, axis=-1, keepdims=True))
    variance = lax.optimization_barrier(jnp.mean(centred * centred, axis=-1, keepdims=True))
    return centred * lax.rsqrt(variance + NORM_EPS) * norm_gain + norm_bias

def gelu(values):
    return 0.5 * values * (1.0 + jnp.tanh(GELU_C * (values + GELU_A * values * values * values)))

def rotary_tables(coords):
    quarter = E // 4
    frequency = math.pi * (jnp.arange(quarter, dtype=jnp.float32) + 1.0) / quarter
    first_angle = coords[0][:, None] * frequency[None, :]
    second_angle = coords[1][:, None] * frequency[None, :]
    angles = jnp.concatenate([first_angle, first_angle, second_angle, second_angle], axis=1)
    return (jnp.cos(angles), jnp.sin(angles))

def rotate(values, cosine, sine):
    quarter = E // 4
    swapped = jnp.concatenate([-values[..., quarter:2 * quarter], values[..., :quarter], -values[..., 3 * quarter:], values[..., 2 * quarter:3 * quarter]], axis=-1)
    return values * cosine[:, None, :] + swapped * sine[:, None, :]

def fourier_features(coords, fourier_basis):
    phases = 2.0 * math.pi * (coords[0][:, None] * fourier_basis[0][None, :] + coords[1][:, None] * fourier_basis[1][None, :])
    return jnp.concatenate([jnp.cos(phases), jnp.sin(phases)], axis=1)

def galerkin(queries, keys_in, values_in, mask_rows, onehot, inverse_count):
    blocks = onehot.shape[0]
    masked = keys_in * mask_rows[:, None, None]
    key_blocks = masked.reshape(blocks, BLOCK, H, E)
    value_blocks = values_in.reshape(blocks, BLOCK, H, E)
    per_block = jnp.einsum('bphe,bphf->bhef', key_blocks, value_blocks, precision=HIGHEST_PRECISION)
    table = jnp.einsum('ba,bhef->ahef', onehot, per_block, precision=HIGHEST_PRECISION)
    summary = low(low_back(table) * inverse_count[:, None, None, None])
    block_summary = jnp.einsum('ba,ahef->bhef', onehot, summary, precision=HIGHEST_PRECISION)
    mixed = jnp.einsum('bphe,bhef->bphf', queries.reshape(blocks, BLOCK, H, E), block_summary, precision=HIGHEST_PRECISION)
    return mixed.reshape(-1, H, E) * mask_rows[:, None, None]

def adam_update(weight, first, second, grad, factor, rate):
    clipped = grad * factor
    new_first = BETA_ONE * first + (1.0 - BETA_ONE) * clipped
    new_second = BETA_TWO * second + (1.0 - BETA_TWO) * clipped * clipped
    first_hat = new_first / (1.0 - BETA_ONE ** STEP)
    second_hat = new_second / (1.0 - BETA_TWO ** STEP)
    new_weight = weight - rate * (first_hat / (jnp.sqrt(second_hat) + ADAM_EPS) + WEIGHT_DECAY * weight)
    return (new_first, new_second, new_weight)

def reference(features, coords, fourier_basis, block_items, point_mask, cotangent, square_weight, square_first, square_second, expand_weight, expand_first, expand_second, contract_weight, contract_first, contract_second, fourier_weight, fourier_first, fourier_second, vector_weight, vector_first, vector_second, hidden_weight, hidden_first, hidden_second):
    mask_rows = point_mask.astype(jnp.float32)
    blocks = block_items.shape[0]
    onehot = (block_items[:, None] == jnp.arange(ITEMS, dtype=jnp.int32)[None, :]).astype(jnp.float32)
    block_count = lax.optimization_barrier(jnp.sum(mask_rows.reshape(blocks, BLOCK), axis=1))
    item_count = jnp.einsum('ba,b->a', onehot, block_count, precision=HIGHEST_PRECISION)
    inverse_count = 1.0 / item_count
    cosine, sine = rotary_tables(coords)
    phase_rows = low(fourier_features(coords, fourier_basis))

    def forward(inputs, square, expand, contract, fourier, vector, hidden):
        square_low = low(square).reshape(7, D, D)
        expand_low = low(expand).reshape(2, D, F)
        contract_low = low(contract).reshape(2, F, D)
        fourier_low = low(fourier).reshape(FOUR, D)
        normed = low(layer_norm(inputs, vector[0], vector[1]))
        queries = low_back(matmul(normed, square_low[0]))
        keys_raw = low_back(matmul(normed, square_low[1]))
        values_raw = low_back(matmul(normed, square_low[2]))
        queries_rot = low(rotate(queries.reshape(-1, H, E), cosine, sine))
        keys_rot = low(rotate(keys_raw.reshape(-1, H, E), cosine, sine))
        values_low = low(values_raw.reshape(-1, H, E))
        attended = low(low_back(galerkin(queries_rot, keys_rot, values_low, mask_rows, onehot, inverse_count))).reshape(-1, D)
        first_sum = inputs + low_back(matmul(attended, square_low[3]))
        normed_mid = low(layer_norm(first_sum, vector[2], vector[3]))
        hidden_pre = low_back(matmul(normed_mid, expand_low[0])) + hidden[0]
        encoded = first_sum + low_back(matmul(low(gelu(hidden_pre)), contract_low[0])) + vector[6]
        normed_out = low(layer_norm(encoded, vector[4], vector[5]))
        keys_cross = low(low_back(matmul(normed_out, square_low[4])))
        values_cross = low(low_back(matmul(normed_out, square_low[5])))
        queries_cross = low(low_back(matmul(phase_rows, fourier_low)))
        decoded = low(low_back(galerkin(queries_cross.reshape(-1, H, E), keys_cross.reshape(-1, H, E), values_cross.reshape(-1, H, E), mask_rows, onehot, inverse_count))).reshape(-1, D)
        latent = low_back(matmul(decoded, square_low[6]))
        spread_pre = low_back(matmul(low(latent), expand_low[1])) + hidden[1]
        return latent + low_back(matmul(low(gelu(spread_pre)), contract_low[1])) + vector[7]
    output, pullback = jax.vjp(forward, features.astype(jnp.float32), square_weight, expand_weight, contract_weight, fourier_weight, vector_weight, hidden_weight)
    grads = pullback(cotangent.astype(jnp.float32))
    squares = sum((jnp.sum(grad_part * grad_part) for grad_part in grads[1:]))
    grad_norm = jnp.sqrt(squares)
    factor = jnp.minimum(1.0, CLIP_NORM / (grad_norm + 1e-06))
    new_square = adam_update(square_weight, square_first, square_second, grads[1], factor, RATE_MATRIX)
    new_expand = adam_update(expand_weight, expand_first, expand_second, grads[2], factor, RATE_MATRIX)
    new_contract = adam_update(contract_weight, contract_first, contract_second, grads[3], factor, RATE_MATRIX)
    new_fourier = adam_update(fourier_weight, fourier_first, fourier_second, grads[4], factor, RATE_MATRIX)
    new_vector = adam_update(vector_weight, vector_first, vector_second, grads[5], factor, RATE_VECTOR)
    new_hidden = adam_update(hidden_weight, hidden_first, hidden_second, grads[6], factor, RATE_VECTOR)
    return (output.astype(jnp.bfloat16), grads[0], grad_norm, new_square[0], new_square[1], new_square[2], new_expand[0], new_expand[1], new_expand[2], new_contract[0], new_contract[1], new_contract[2], new_fourier[0], new_fourier[1], new_fourier[2], new_vector[0], new_vector[1], new_vector[2], new_hidden[0], new_hidden[1], new_hidden[2])
```

```python
import functools
import math
import types

import jax
import jax.numpy as jnp
from jax import lax
from jax.experimental import pallas as pl
from jax.experimental.pallas import tpu as pltpu
from jax.sharding import PartitionSpec as P

H = 8
E = 32
F = 512
FOUR = 128
BLOCK = 128
ITEM_PTS = 8192
STEP = 10


NORM_EPS = 1e-05
GELU_C = math.sqrt(2.0 / math.pi)
GELU_A = 0.044715
BETA_ONE = 0.9
BETA_TWO = 0.95
ADAM_EPS = 1e-08
WEIGHT_DECAY = 0.1
RATE_MATRIX = 0.05
RATE_VECTOR = 0.25
CLIP_NORM = 1.0
HIGHEST_PRECISION = lax.Precision.HIGHEST


def matmul(left, right):
    return jnp.dot(left, right, preferred_element_type=jnp.float32)


def matmul_left(left, right):
    return lax.dot_general(
        left, right, (((0,), (0,)), ((), ())), preferred_element_type=jnp.float32
    )


def matmul_right(left, right):
    return lax.dot_general(
        left, right, (((1,), (1,)), ((), ())), preferred_element_type=jnp.float32
    )


def gelu(values):
    return 0.5 * values * (1.0 + jnp.tanh(GELU_C * (values + GELU_A * values * values * values)))


def gelu_slope(values):
    tangent = jnp.tanh(GELU_C * (values + GELU_A * values * values * values))
    return 0.5 * (1.0 + tangent) + 0.5 * values * (1.0 - tangent * tangent) * GELU_C * (
        1.0 + 3.0 * GELU_A * values * values
    )


def norm_parts(values, norm_gain, norm_bias):
    centred = values - jnp.mean(values, axis=-1, keepdims=True)
    variance = jnp.mean(centred * centred, axis=-1, keepdims=True)
    root_inv = lax.rsqrt(variance + NORM_EPS)
    scaled = centred * root_inv
    return (scaled * norm_gain + norm_bias, scaled, root_inv)


def norm_back(upstream, scaled, root_inv, norm_gain):
    through = upstream * norm_gain
    centre = jnp.mean(through, axis=-1, keepdims=True)
    along = jnp.mean(through * scaled, axis=-1, keepdims=True)
    return root_inv * (through - centre - scaled * along)


def rotary_tables(coords):
    quarter = E // 4
    frequency = math.pi * (jnp.arange(quarter, dtype=jnp.float32) + 1.0) / quarter
    first_angle = coords[0][:, None] * frequency[None, :]
    second_angle = coords[1][:, None] * frequency[None, :]
    angles = jnp.concatenate([first_angle, first_angle, second_angle, second_angle], axis=1)
    return (jnp.cos(angles), jnp.sin(angles))


def rotate(values, cosine, sine):
    quarter = E // 4
    swapped = jnp.concatenate(
        [
            -values[..., quarter : 2 * quarter],
            values[..., :quarter],
            -values[..., 3 * quarter :],
            values[..., 2 * quarter : 3 * quarter],
        ],
        axis=-1,
    )
    return values * cosine[:, None, :] + swapped * sine[:, None, :]


def rotate_back(grads, cosine, sine):
    quarter = E // 4
    scaled = grads * sine[:, None, :]
    swapped = jnp.concatenate(
        [
            scaled[..., quarter : 2 * quarter],
            -scaled[..., :quarter],
            scaled[..., 3 * quarter :],
            -scaled[..., 2 * quarter : 3 * quarter],
        ],
        axis=-1,
    )
    return grads * cosine[:, None, :] + swapped


def fourier_features(coords, fourier_basis):
    phases = (
        2.0
        * math.pi
        * (
            coords[0][:, None] * fourier_basis[0][None, :]
            + coords[1][:, None] * fourier_basis[1][None, :]
        )
    )
    return jnp.concatenate([jnp.cos(phases), jnp.sin(phases)], axis=1)


def block_table(left, right, onehot):
    blocks = onehot.shape[0]
    per_block = jnp.einsum(
        "bphe,bphf->bhef",
        left.reshape(blocks, BLOCK, H, E),
        right.reshape(blocks, BLOCK, H, E),
        preferred_element_type=jnp.float32,
    )
    return jnp.einsum("ba,bhef->ahef", onehot, per_block, precision=HIGHEST_PRECISION)


def scale_round(table, inverse_count):
    return (table * inverse_count[:, None, None, None]).astype(jnp.bfloat16)


def spread(summary, onehot):
    selected = jnp.einsum(
        "ba,ahef->bhef", onehot.astype(jnp.bfloat16), summary, preferred_element_type=jnp.float32
    )
    return selected.astype(jnp.bfloat16)


def apply_summary(rows_low, block_summary, transposed):
    blocks = block_summary.shape[0]
    pattern = "bphf,bhef->bphe" if transposed else "bphe,bhef->bphf"
    mixed = jnp.einsum(
        pattern,
        rows_low.reshape(blocks, BLOCK, H, E),
        block_summary,
        preferred_element_type=jnp.float32,
    )
    return mixed.reshape(-1, H * E)


def galerkin_backward(
    grad_low, queries_low, keys_masked, values_low, block_summary, onehot, mask_float, reducer
):
    grad_masked = grad_low * mask_float.astype(jnp.bfloat16)
    grad_queries = apply_summary(grad_masked, block_summary, True)
    summary_grad = reducer(block_table(queries_low, grad_masked, onehot))
    block_grad = spread(summary_grad, onehot)
    grad_keys = apply_summary(values_low, block_grad, True) * mask_float
    grad_values = apply_summary(keys_masked, block_grad, False)
    return (grad_queries, grad_keys, grad_values)


def adam_update(weight, first, second, grad, factor, rate):
    clipped = grad * factor
    new_first = BETA_ONE * first + (1.0 - BETA_ONE) * clipped
    new_second = BETA_TWO * second + (1.0 - BETA_TWO) * clipped * clipped
    first_hat = new_first / (1.0 - BETA_ONE**STEP)
    second_hat = new_second / (1.0 - BETA_TWO**STEP)
    new_weight = weight - rate * (
        first_hat / (jnp.sqrt(second_hat) + ADAM_EPS) + WEIGHT_DECAY * weight
    )
    return (new_first, new_second, new_weight)


def own_share(full, width, along, start_index):
    return lax.dynamic_slice_in_dim(full, start_index * width, width, along)


def plain(
    features,
    coords,
    fourier_basis,
    block_items,
    point_mask,
    cotangent,
    square_weight,
    square_first,
    square_second,
    expand_weight,
    expand_first,
    expand_second,
    contract_weight,
    contract_first,
    contract_second,
    fourier_weight,
    fourier_first,
    fourier_second,
    vector_weight,
    vector_first,
    vector_second,
    hidden_weight,
    hidden_first,
    hidden_second,
):
    rows = features.shape[0]
    width = features.shape[1]
    blocks = rows // BLOCK
    devices = lax.axis_size("pts")
    items_total = rows * devices // ITEM_PTS
    gathered = (
        lax.all_gather(square_weight.astype(jnp.bfloat16), "pts", axis=1, tiled=True),
        lax.all_gather(expand_weight.astype(jnp.bfloat16), "pts", axis=1, tiled=True),
        lax.all_gather(contract_weight.astype(jnp.bfloat16), "pts", axis=1, tiled=True),
        lax.all_gather(fourier_weight.astype(jnp.bfloat16), "pts", axis=0, tiled=True),
    )
    square_full = gathered[0].reshape(7, width, width)
    expand_full = gathered[1].reshape(2, width, F)
    contract_full = gathered[2].reshape(2, F, width)
    fourier_full = gathered[3].reshape(FOUR, width)
    onehot = (block_items[:, None] == jnp.arange(items_total, dtype=jnp.int32)[None, :]).astype(
        jnp.float32
    )
    mask_float = point_mask.astype(jnp.float32)[:, None]
    mask_low = mask_float.astype(jnp.bfloat16)
    block_count = jnp.sum(mask_float.reshape(blocks, BLOCK), axis=1)
    local_count = jnp.dot(block_count, onehot, precision=HIGHEST_PRECISION)
    cosine, sine = rotary_tables(coords)
    phase_low = fourier_features(coords, fourier_basis).astype(jnp.bfloat16)
    inputs = features.astype(jnp.float32)
    normed, scaled_one, root_one = norm_parts(inputs, vector_weight[0], vector_weight[1])
    normed_low = normed.astype(jnp.bfloat16)
    joint_weight = jnp.concatenate([square_full[0], square_full[1], square_full[2]], axis=1)
    projected = matmul(normed_low, joint_weight)
    queries_low = (
        rotate(projected[:, :width].reshape(rows, H, E), cosine, sine)
        .reshape(rows, width)
        .astype(jnp.bfloat16)
    )
    keys_low = (
        rotate(projected[:, width : 2 * width].reshape(rows, H, E), cosine, sine)
        .reshape(rows, width)
        .astype(jnp.bfloat16)
    )
    keys_masked = keys_low * mask_low
    values_low = projected[:, 2 * width :].astype(jnp.bfloat16)
    self_local = block_table(keys_masked, values_low, onehot)
    self_table, item_count = lax.psum((self_local, local_count), "pts")
    inverse_count = 1.0 / item_count
    self_items = scale_round(self_table, inverse_count)
    self_summary = spread(self_items, onehot)
    attended_low = (apply_summary(queries_low, self_summary, False) * mask_float).astype(
        jnp.bfloat16
    )
    first_sum = inputs + matmul(attended_low, square_full[3])
    normed_mid, scaled_two, root_two = norm_parts(first_sum, vector_weight[2], vector_weight[3])
    middle_low = normed_mid.astype(jnp.bfloat16)
    hidden_pre = matmul(middle_low, expand_full[0]) + hidden_weight[0]
    hidden_low = gelu(hidden_pre).astype(jnp.bfloat16)
    encoded = first_sum + matmul(hidden_low, contract_full[0]) + vector_weight[6]
    normed_out, scaled_three, root_three = norm_parts(encoded, vector_weight[4], vector_weight[5])
    outer_low = normed_out.astype(jnp.bfloat16)
    pair_weight = jnp.concatenate([square_full[4], square_full[5]], axis=1)
    cross_projected = matmul(outer_low, pair_weight)
    cross_keys = cross_projected[:, :width].astype(jnp.bfloat16) * mask_low
    cross_values = cross_projected[:, width:].astype(jnp.bfloat16)
    cross_queries = matmul(phase_low, fourier_full).astype(jnp.bfloat16)
    cross_local = block_table(cross_keys, cross_values, onehot)
    cross_items = scale_round(lax.psum(cross_local, "pts"), inverse_count)
    cross_summary = spread(cross_items, onehot)
    decoded_low = (apply_summary(cross_queries, cross_summary, False) * mask_float).astype(
        jnp.bfloat16
    )
    latent = matmul(decoded_low, square_full[6])
    latent_low = latent.astype(jnp.bfloat16)
    spread_pre = matmul(latent_low, expand_full[1]) + hidden_weight[1]
    spread_low = gelu(spread_pre).astype(jnp.bfloat16)
    output = latent + matmul(spread_low, contract_full[1]) + vector_weight[7]
    cross_reducer = lambda table_part: scale_round(lax.psum(table_part, "pts"), inverse_count)
    self_reducer = lambda table_part: scale_round(lax.psum(table_part, "pts"), inverse_count)
    grad_output = cotangent.astype(jnp.float32)
    grad_bias_end = jnp.sum(grad_output, axis=0)
    grad_contract_spread = matmul_left(spread_low, cotangent)
    grad_spread = matmul_right(cotangent, contract_full[1]) * gelu_slope(spread_pre)
    grad_hidden_spread = jnp.sum(grad_spread, axis=0)
    grad_spread_low = grad_spread.astype(jnp.bfloat16)
    grad_expand_spread = matmul_left(latent_low, grad_spread_low)
    grad_latent = (grad_output + matmul_right(grad_spread_low, expand_full[1])).astype(jnp.bfloat16)
    grad_out_cross = matmul_left(decoded_low, grad_latent)
    grad_decoded = matmul_right(grad_latent, square_full[6]).astype(jnp.bfloat16)
    cross_back = galerkin_backward(
        grad_decoded,
        cross_queries,
        cross_keys,
        cross_values,
        cross_summary,
        onehot,
        mask_float,
        cross_reducer,
    )
    grad_fourier_full = matmul_left(phase_low, cross_back[0].astype(jnp.bfloat16))
    grad_pair_low = jnp.concatenate([cross_back[1], cross_back[2]], axis=1).astype(jnp.bfloat16)
    grad_pair_full = matmul_left(outer_low, grad_pair_low)
    grad_normed_out = matmul_right(grad_pair_low, pair_weight)
    grad_gain_three = jnp.sum(grad_normed_out * scaled_three, axis=0)
    grad_bias_three = jnp.sum(grad_normed_out, axis=0)
    grad_encoded = norm_back(grad_normed_out, scaled_three, root_three, vector_weight[4])
    grad_bias_middle = jnp.sum(grad_encoded, axis=0)
    grad_encoded_low = grad_encoded.astype(jnp.bfloat16)
    grad_contract_enc = matmul_left(hidden_low, grad_encoded_low)
    grad_hidden = matmul_right(grad_encoded_low, contract_full[0]) * gelu_slope(hidden_pre)
    grad_hidden_enc = jnp.sum(grad_hidden, axis=0)
    grad_hidden_low = grad_hidden.astype(jnp.bfloat16)
    grad_expand_enc = matmul_left(middle_low, grad_hidden_low)
    grad_middle = matmul_right(grad_hidden_low, expand_full[0])
    grad_gain_two = jnp.sum(grad_middle * scaled_two, axis=0)
    grad_bias_two = jnp.sum(grad_middle, axis=0)
    grad_first = grad_encoded + norm_back(grad_middle, scaled_two, root_two, vector_weight[2])
    grad_first_low = grad_first.astype(jnp.bfloat16)
    grad_out_self = matmul_left(attended_low, grad_first_low)
    grad_attended = matmul_right(grad_first_low, square_full[3]).astype(jnp.bfloat16)
    self_back = galerkin_backward(
        grad_attended,
        queries_low,
        keys_masked,
        values_low,
        self_summary,
        onehot,
        mask_float,
        self_reducer,
    )
    grad_queries = rotate_back(self_back[0].reshape(rows, H, E), cosine, sine).reshape(rows, width)
    grad_keys = rotate_back(self_back[1].reshape(rows, H, E), cosine, sine).reshape(rows, width)
    grad_joint_low = jnp.concatenate([grad_queries, grad_keys, self_back[2]], axis=1).astype(
        jnp.bfloat16
    )
    grad_joint_full = matmul_left(normed_low, grad_joint_low)
    grad_normed = matmul_right(grad_joint_low, joint_weight)
    grad_gain_one = jnp.sum(grad_normed * scaled_one, axis=0)
    grad_bias_one = jnp.sum(grad_normed, axis=0)
    grad_inputs = grad_first + norm_back(grad_normed, scaled_one, root_one, vector_weight[0])
    grad_square = jnp.stack(
        [
            grad_joint_full[:, :width],
            grad_joint_full[:, width : 2 * width],
            grad_joint_full[:, 2 * width :],
            grad_out_self,
            grad_pair_full[:, :width],
            grad_pair_full[:, width:],
            grad_out_cross,
        ]
    ).reshape(7, width * width)
    grad_expand = jnp.stack([grad_expand_enc, grad_expand_spread]).reshape(2, width * F)
    grad_contract = jnp.stack([grad_contract_enc, grad_contract_spread]).reshape(2, F * width)
    grad_fourier = grad_fourier_full.reshape(FOUR * width)
    grad_vector = jnp.stack(
        [
            grad_gain_one,
            grad_bias_one,
            grad_gain_two,
            grad_bias_two,
            grad_gain_three,
            grad_bias_three,
            grad_bias_middle,
            grad_bias_end,
        ]
    )
    grad_hidden_rows = jnp.stack([grad_hidden_enc, grad_hidden_spread])
    totals = lax.psum(
        (grad_square, grad_expand, grad_contract, grad_fourier, grad_vector, grad_hidden_rows),
        "pts",
    )
    squares = sum((jnp.sum(total_part * total_part) for total_part in totals))
    start_index = lax.axis_index("pts")
    share_square = own_share(totals[0], square_weight.shape[1], 1, start_index)
    share_expand = own_share(totals[1], expand_weight.shape[1], 1, start_index)
    share_contract = own_share(totals[2], contract_weight.shape[1], 1, start_index)
    share_fourier = own_share(totals[3], fourier_weight.shape[0], 0, start_index)
    vector_total = totals[4]
    hidden_total = totals[5]
    grad_norm = jnp.sqrt(squares)
    factor = jnp.minimum(1.0, CLIP_NORM / (grad_norm + 1e-06))
    new_square = adam_update(
        square_weight, square_first, square_second, share_square, factor, RATE_MATRIX
    )
    new_expand = adam_update(
        expand_weight, expand_first, expand_second, share_expand, factor, RATE_MATRIX
    )
    new_contract = adam_update(
        contract_weight, contract_first, contract_second, share_contract, factor, RATE_MATRIX
    )
    new_fourier = adam_update(
        fourier_weight, fourier_first, fourier_second, share_fourier, factor, RATE_MATRIX
    )
    new_vector = adam_update(
        vector_weight, vector_first, vector_second, vector_total, factor, RATE_VECTOR
    )
    new_hidden = adam_update(
        hidden_weight, hidden_first, hidden_second, hidden_total, factor, RATE_VECTOR
    )
    return (
        output.astype(jnp.bfloat16),
        grad_inputs,
        grad_norm,
        new_square[0],
        new_square[1],
        new_square[2],
        new_expand[0],
        new_expand[1],
        new_expand[2],
        new_contract[0],
        new_contract[1],
        new_contract[2],
        new_fourier[0],
        new_fourier[1],
        new_fourier[2],
        new_vector[0],
        new_vector[1],
        new_vector[2],
        new_hidden[0],
        new_hidden[1],
        new_hidden[2],
    )


GROUP = 8
TILE = 256
LANES = 128
VMEM_BYTES = 64 * 1024 * 1024


def dot(left, right):
    return jnp.dot(left, right, preferred_element_type=jnp.float32)


def dot_bt(left, right):
    return lax.dot_general(
        left, right, (((1,), (1,)), ((), ())), preferred_element_type=jnp.float32
    )


def dot_at(left, right):
    return lax.dot_general(
        left, right, (((0,), (0,)), ((), ())), preferred_element_type=jnp.float32
    )


def low(values):
    return values.astype(jnp.bfloat16)


def column_norm(values):
    inverse = 1.0 / values.shape[0]
    centred = values - jnp.sum(values, axis=0, keepdims=True) * inverse
    variance = jnp.sum(centred * centred, axis=0, keepdims=True) * inverse
    root_inv = lax.rsqrt(variance + NORM_EPS)
    return (centred * root_inv, root_inv)


def column_norm_back(upstream, scaled, root_inv, gain):
    inverse = 1.0 / upstream.shape[0]
    through = upstream * gain
    centre = jnp.sum(through, axis=0, keepdims=True) * inverse
    along = jnp.sum(through * scaled, axis=0, keepdims=True) * inverse
    return root_inv * (through - centre - scaled * along)


def gelu_both(values):
    square = values * values
    half = 0.5 + 0.5 * jnp.tanh(values * (GELU_C + (GELU_C * GELU_A) * square))
    slope = half + values * (half * (1.0 - half)) * (
        2.0 * GELU_C + (6.0 * GELU_C * GELU_A) * square
    )
    return (values * half, slope)


def turn(values, cosine, sine, sign):
    quarter = E // 4
    first_cos, second_cos = cosine[:quarter], cosine[quarter:]
    first_sin, second_sin = sine[:quarter] * sign, sine[quarter:] * sign
    parts = []
    for base in range(0, values.shape[0], E):
        one, two, three, four = (
            values[base + quarter * step : base + quarter * (step + 1)] for step in range(4)
        )
        parts += [
            one * first_cos - two * first_sin,
            two * first_cos + one * first_sin,
            three * second_cos - four * second_sin,
            four * second_cos + three * second_sin,
        ]
    return jnp.concatenate(parts, axis=0)


def compress(full):
    width = full.shape[1]
    head = lax.broadcasted_iota(jnp.int32, (E, width), 1) // E
    result = full[:E]
    for index in range(1, H):
        result = jnp.where(head == index, full[E * index : E * (index + 1)], result)
    return result


def lane_sum(values):
    result = values[:, :LANES]
    for start in range(LANES, values.shape[1], LANES):
        result = result + values[:, start : start + LANES]
    return result


def remote(source, target, send_sem, recv_sem, device):
    return pltpu.make_async_remote_copy(
        src_ref=source,
        dst_ref=target,
        send_sem=send_sem,
        recv_sem=recv_sem,
        device_id=(device,),
        device_id_type=pl.DeviceIdType.MESH,
    )


class Place:
    def __init__(self, devices):
        self.devices = devices
        self.outers = devices // GROUP
        self.me = lax.axis_index("pts")
        self.inner = lax.rem(self.me, GROUP)
        self.outer = lax.div(self.me, GROUP)
        self.core = lax.rem(self.me, 2)
        self.pair = lax.div(self.inner, 2)

    def inner_at(self, step):
        return lax.rem(self.inner + step, GROUP)

    def outer_at(self, step):
        return lax.rem(self.outer + step, self.outers)

    def pair_at(self, step):
        return lax.rem(self.pair + step, 4)

    def device(self, outer, inner):
        return outer * GROUP + inner


class Gather:
    def __init__(self, place, buffer, sems):
        self.place, self.buffer = place, buffer
        self.send, self.recv = sems

    def first(self, step, start):
        at = self.place
        slot = self.buffer.at[at.core, at.pair, at.outer if start else at.outer_at(step)]
        mine = self.buffer.at[at.core, at.pair, at.outer]
        source = at.outer if start else at.outer_at(step)
        return remote(
            mine, slot, self.send.at[0, step], self.recv.at[0, source],
            at.device(at.outer_at(step), at.inner),
        )

    def second(self, step, start):
        at = self.place
        source = at.pair if start else at.pair_at(step)
        return remote(
            self.buffer.at[at.core, at.pair], self.buffer.at[at.core, source],
            self.send.at[1, step], self.recv.at[1, source],
            at.device(at.outer, at.pair_at(step) * 2 + at.core),
        )

    def third(self, start):
        at = self.place
        source = at.core if start else 1 - at.core
        return remote(
            self.buffer.at[at.core], self.buffer.at[source], self.send.at[2, 0],
            self.recv.at[2, 0], at.device(at.outer, at.pair * 2 + 1 - at.core),
        )

    def start_first(self):
        for step in range(1, self.place.outers):
            self.first(step, True).start()

    def start_second(self):
        for step in range(1, self.place.outers):
            self.first(step, False).wait()
        for step in range(1, 4):
            self.second(step, True).start()

    def start_third(self):
        for step in range(1, 4):
            self.second(step, False).wait()
        self.third(True).start()

    def finish(self):
        self.third(False).wait()


class TableSum:
    def __init__(self, place, scratch):
        self.place, self.s, self.turn = place, scratch, 0

    def swap(self, step, start):
        at, s = self.place, self.s
        source = at.inner if start else at.inner_at(step)
        return remote(
            s.table_send.at[at.inner_at(step)], s.table_recv.at[source], s.sem_ts.at[0, step],
            s.sem_tr.at[0, source], at.device(at.outer, at.inner_at(step)),
        )

    def cross(self, step, start):
        at, s = self.place, self.s
        source = at.outer if start else at.outer_at(step)
        return remote(
            s.table_part, s.table_cross.at[self.turn, source], s.sem_ts.at[1 + self.turn, step],
            s.sem_tr.at[1 + self.turn, source],
            at.device(at.outer_at(step), at.inner),
        )

    def share(self, step, start, result):
        at, s = self.place, self.s
        source = at.inner if start else at.inner_at(step)
        return remote(
            result.at[at.inner], result.at[source], s.sem_ts.at[3, step], s.sem_tr.at[3, source],
            at.device(at.outer, at.inner_at(step)),
        )

    def start(self):
        at, s = self.place, self.s
        high = low(s.per_block[...])
        rest = low(s.per_block[...] - high.astype(jnp.float32))
        table = low(dot(s.spread[...], high) + dot(s.spread[...], rest))
        for chunk in range(at.devices):
            s.table_send[chunk % GROUP, chunk // GROUP] = table[chunk * 16 : (chunk + 1) * 16]
        for step in range(1, GROUP):
            self.swap(step, True).start()

    def middle(self):
        at, s = self.place, self.s
        total = s.table_send[at.inner].astype(jnp.float32)
        for step in range(1, GROUP):
            self.swap(step, False).wait()
            total = total + s.table_recv[at.inner_at(step)].astype(jnp.float32)
        s.table_part[...] = low(total)
        for step in range(1, at.outers):
            self.cross(step, True).start()

    def late(self, result):
        at, s = self.place, self.s
        total = s.table_part[...].astype(jnp.float32)
        for step in range(1, at.outers):
            self.cross(step, False).wait()
            total = total + s.table_cross[self.turn, at.outer_at(step)].astype(jnp.float32)
        for outer in range(at.outers):
            result[at.inner, outer] = low(total[outer] * s.inverse[outer : outer + 1, :])
        for step in range(1, GROUP):
            self.share(step, True, result).start()

    def finish(self, result):
        for step in range(1, GROUP):
            self.share(step, False, result).wait()
        self.turn = 1 - self.turn


class GradSum:
    def __init__(self, place, scratch, key):
        self.place = place
        self.full, self.half, self.quarter, self.last = (
            getattr(scratch, name + key) for name in ("full_", "half_", "quarter_", "last_")
        )
        self.send, self.recv = getattr(scratch, f"sem_{key}s"), getattr(scratch, f"sem_{key}r")

    def swap(self):
        at = self.place
        return remote(
            self.full.at[1 - at.core], self.half, self.send.at[0, 0], self.recv.at[0, 0],
            at.device(at.outer, at.pair * 2 + 1 - at.core),
        )

    def across(self, step, start):
        at = self.place
        source = at.pair if start else at.pair_at(step)
        return remote(
            self.half.at[at.pair_at(step)], self.quarter.at[source], self.send.at[1, step],
            self.recv.at[1, source], at.device(at.outer, at.pair_at(step) * 2 + at.core),
        )

    def along(self, step, start):
        at = self.place
        source = at.outer if start else at.outer_at(step)
        return remote(
            self.quarter.at[at.pair, at.outer_at(step)], self.last.at[source], self.send.at[2, step],
            self.recv.at[2, source], at.device(at.outer_at(step), at.inner),
        )

    def start(self, chunk_of):
        at = self.place

        @pl.loop(0, at.devices)
        def _(chunk):
            inner = lax.rem(chunk, GROUP)
            self.full[lax.rem(inner, 2), lax.div(inner, 2), lax.div(chunk, GROUP)] = low(
                chunk_of(chunk)
            )

        self.swap().start()

    def second(self):
        at = self.place
        self.swap().wait()

        @pl.loop(0, 4)
        def _(pair):
            self.half[pair] = low(
                self.full[at.core, pair].astype(jnp.float32) + self.half[pair].astype(jnp.float32)
            )

        for step in range(1, 4):
            self.across(step, True).start()

    def third(self):
        at = self.place
        total = self.half[at.pair].astype(jnp.float32)
        for step in range(1, 4):
            self.across(step, False).wait()
            total = total + self.quarter[at.pair_at(step)].astype(jnp.float32)
        self.quarter[at.pair] = low(total)
        for step in range(1, at.outers):
            self.along(step, True).start()

    def finish(self):
        at = self.place
        total = self.quarter[at.pair, at.outer].astype(jnp.float32)
        for step in range(1, at.outers):
            self.along(step, False).wait()
            total = total + self.last[at.outer_at(step)].astype(jnp.float32)
        return total


def layer_kernel(names, devices, *refs):
    s = types.SimpleNamespace(**dict(zip(names, refs)))
    at = Place(devices)
    points, width = s.features.shape
    tiles = points // TILE
    blocks = points // BLOCK
    share = width // devices
    tile_blocks = TILE // BLOCK
    f32 = jnp.float32

    barrier = pltpu.get_barrier_semaphore()
    for step in range(1, GROUP):
        pl.semaphore_signal(
            barrier, inc=1, device_id=(at.device(at.outer, at.inner_at(step)),),
            device_id_type=pl.DeviceIdType.MESH,
        )
    for step in range(1, at.outers):
        pl.semaphore_signal(
            barrier, inc=1, device_id=(at.device(at.outer_at(step), at.inner),),
            device_id_type=pl.DeviceIdType.MESH,
        )

    def columns(tile):
        return pl.ds(pl.multiple_of(tile * TILE, TILE), TILE)

    def block_columns(block):
        return pl.ds(pl.multiple_of(block * BLOCK, BLOCK), BLOCK)

    def column(index):
        return s.cols[:, index : index + 1]

    def hidden_column(index):
        return jnp.concatenate([column(8 + 2 * index), column(9 + 2 * index)], axis=0)

    def out_copy(tile, target, slots, sems, index):
        slot = lax.rem(tile, 2)
        where = pl.ds(pl.multiple_of(tile * TILE, TILE), TILE)
        return pltpu.make_async_copy(slots.at[slot], target.at[where, :], sems.at[index, slot])

    def put_out(tile, target, slots, sems, index, values):
        @pl.when(tile >= 2)
        def _():
            out_copy(tile - 2, target, slots, sems, index).wait()

        slots[lax.rem(tile, 2)] = values
        out_copy(tile, target, slots, sems, index).start()

    def end_out(target, slots, sems, index):
        for tile in range(tiles - 2, tiles):
            out_copy(tile, target, slots, sems, index).wait()

    for matrix in range(7):
        for row in range(share):
            s.pack[matrix * share + row : matrix * share + row + 1, :] = s.square_weight[
                matrix : matrix + 1, row * width : (row + 1) * width
            ]
    for matrix in range(2):
        for half in range(2):
            for row in range(share):
                place = (7 + 2 * matrix + half) * share + row
                start = row * F + half * width
                s.pack[place : place + 1, :] = s.expand_weight[
                    matrix : matrix + 1, start : start + width
                ]
        for row in range(2 * share):
            place = (11 + 2 * matrix) * share + row
            s.pack[place : place + 1, :] = s.contract_weight[
                matrix : matrix + 1, row * width : (row + 1) * width
            ]
    s.pack[15 * share : 16 * share, :LANES] = s.fourier_weight[...]
    s.pack[15 * share : 16 * share, LANES:] = jnp.zeros((share, LANES), f32)
    live = s.point_mask[...].astype(f32)
    counts = dot_bt(jnp.ones((8, LANES), jnp.bfloat16), low(live))
    s.pack[15 * share : 15 * share + 1, LANES : LANES + blocks] = counts[:1]
    lane = lax.broadcasted_iota(jnp.int32, (1, LANES), 1)
    wide_block = lax.broadcasted_iota(jnp.int32, (1, E * blocks), 1) // E
    item_row = jnp.zeros((1, LANES), f32)
    item_wide = jnp.zeros((1, E * blocks), jnp.int32)
    for block in range(blocks):
        item_row = jnp.where(lane == block, s.items[block].astype(f32), item_row)
        item_wide = jnp.where(wide_block == block, s.items[block], item_wide)
    s.pack[15 * share + 1 : 15 * share + 2, LANES:] = item_row
    packed = low(s.pack[...])
    split = s.gather_one.shape[3]
    s.gather_one[at.core, at.pair, at.outer] = packed[:split]
    s.gather_two[at.core, at.pair, at.outer] = packed[split:]

    pl.semaphore_wait(barrier, GROUP - 1 + at.outers - 1)
    one = Gather(at, s.gather_one, (s.sem_g1s, s.sem_g1r))
    two = Gather(at, s.gather_two, (s.sem_g2s, s.sem_g2r))
    one.start_first()
    two.start_first()

    row_at = lax.broadcasted_iota(jnp.int32, (width, width), 0)
    lane_at = lax.broadcasted_iota(jnp.int32, (width, width), 1)
    s.eye[...] = jnp.where(row_at == lane_at, 1.0, 0.0).astype(jnp.bfloat16)
    s.heads[...] = jnp.where(row_at // E == lane_at // E, 1.0, 0.0).astype(jnp.bfloat16)
    s.small[...] = jnp.zeros(s.small.shape, f32)
    s.small[0:8, :] = s.vector_weight[...]
    for row in range(2):
        for half in range(2):
            s.small[8 + 2 * row + half : 9 + 2 * row + half, :] = s.hidden_weight[
                row : row + 1, half * width : (half + 1) * width
            ]
    s.small[12:14, : FOUR // 2] = s.fourier_basis[...]
    s.cols[...] = s.small[...].T
    rows_wide = lax.broadcasted_iota(jnp.int32, s.spread.shape, 0)
    lanes_wide = lax.broadcasted_iota(jnp.int32, s.spread.shape, 1)
    s.spread[...] = jnp.where(
        (item_wide == rows_wide // E) & (rows_wide % E == lanes_wide % E), 1.0, 0.0
    ).astype(jnp.bfloat16)
    s.vector_sum[...] = jnp.zeros(s.vector_sum.shape, f32)
    for grad in (s.grad_qkv, s.grad_o, s.grad_kv, s.grad_do, s.grad_w1, s.grad_p1, s.grad_w2, s.grad_p2, s.grad_dq):
        grad[...] = jnp.zeros(grad.shape, f32)
    speed = (lax.broadcasted_iota(jnp.int32, (E // 4, 1), 0).astype(f32) + 1.0) * (
        math.pi / (E // 4)
    )

    def add_sum(index, values):
        for part in range(values.shape[0] // width):
            s.vector_sum[index + part] += lane_sum(values[part * width : (part + 1) * width])

    def features_turned(tile):
        return dot_bt(s.eye[...], s.features[columns(tile), :])

    def before(tile, _):
        where = columns(tile)
        scaled, root = column_norm(features_turned(tile))
        s.root_one[0:1, where] = root
        s.u1[:, where] = low(scaled * column(0) + column(1))
        x_row, y_row = s.coords[0:1, where], s.coords[1:2, where]
        angles = jnp.concatenate([speed * x_row, speed * y_row], axis=0)
        s.cosine[:, where] = jnp.cos(angles)
        s.sine[:, where] = jnp.sin(angles)
        basis = s.cols[: FOUR // 2, :]
        phases = 2.0 * math.pi * (basis[:, 12:13] * x_row + basis[:, 13:14] * y_row)
        s.phi[:, where] = low(jnp.concatenate([jnp.cos(phases), jnp.sin(phases)], axis=0))
        for block in range(tile_blocks):
            s.mask[0:1, pl.ds(pl.multiple_of(tile * TILE + block * BLOCK, BLOCK), BLOCK)] = (
                s.point_mask[pl.ds(tile * tile_blocks + block, 1), :].astype(f32)
            )

    lax.fori_loop(0, tiles // 4, before, None)
    one.start_second()
    lax.fori_loop(tiles // 4, tiles // 2, before, None)
    one.start_third()
    two.start_second()
    lax.fori_loop(tiles // 2, tiles, before, None)
    one.finish()

    group = 16 // share

    def chunk_pair(buffer, index):
        parts = []
        for step in range(group):
            chunk = index * group + step
            inner = lax.rem(chunk, GROUP)
            parts.append(
                buffer[lax.rem(inner, 2), lax.div(inner, 2), lax.div(chunk, GROUP)].astype(f32)
            )
        return parts

    def join(parts, piece):
        return low(
            jnp.concatenate([part[piece * share : (piece + 1) * share] for part in parts], axis=0)
        )

    @pl.loop(0, devices // group)
    def _(index):
        parts = chunk_pair(s.gather_one, index)
        where = pl.ds(pl.multiple_of(index * 16, 16), 16)
        for piece in range(3):
            s.w_qkv[where, piece * width : (piece + 1) * width] = join(parts, piece)
        s.w_o[where, :] = join(parts, 3)

    def flip(matrix):
        return low(dot_bt(s.eye[...], matrix))

    for piece in range(3):
        s.t_qkv[piece * width : (piece + 1) * width, :] = flip(
            s.w_qkv[:, piece * width : (piece + 1) * width]
        )
    s.t_o[...] = flip(s.w_o[...])

    def block_product(left, right):
        return compress(dot_bt(left, right))

    def put_products(tile, left, right):
        for block in range(tile_blocks):
            lanes = slice(block * BLOCK, (block + 1) * BLOCK)
            where = pl.ds(pl.multiple_of((tile * tile_blocks + block) * E, E), E)
            s.per_block[where, :] = block_product(left[:, lanes], right[:, lanes])

    def summary(table, tile, block):
        item = s.items[tile * tile_blocks + block]
        first = item * 2
        inner, outer = lax.rem(first, GROUP), lax.div(first, GROUP)
        rows = jnp.concatenate([table[inner, outer], table[inner + 1, outer]], axis=0)
        return jnp.concatenate([rows] * H, axis=0) * s.heads[...]

    def per_block(tile, function):
        return jnp.concatenate([function(block) for block in range(tile_blocks)], axis=1)

    def lanes_of(block):
        return slice(block * BLOCK, (block + 1) * BLOCK)

    def phase_a(tile, _):
        where = columns(tile)
        projected = dot(s.t_qkv[...], s.u1[:, where])
        cosine, sine = s.cosine[:, where], s.sine[:, where]
        s.q[:, where] = low(turn(projected[:width], cosine, sine, 1.0))
        keys = low(turn(projected[width : 2 * width], cosine, sine, 1.0) * s.mask[0:1, where])
        values = low(projected[2 * width :])
        s.k[:, where] = keys
        s.v[:, where] = values
        put_products(tile, values, keys)

    lax.fori_loop(0, tiles // 2, phase_a, None)
    two.start_third()
    lax.fori_loop(tiles // 2, tiles, phase_a, None)
    two.finish()

    def take_two(index, carried):
        parts = chunk_pair(s.gather_two, index)
        where = pl.ds(pl.multiple_of(index * 16, 16), 16)
        for piece in range(2):
            s.w_kv[where, piece * width : (piece + 1) * width] = join(parts, piece)
            s.w_w1[where, piece * width : (piece + 1) * width] = join(parts, 3 + piece)
            s.w_p1[where, piece * width : (piece + 1) * width] = join(parts, 5 + piece)
        s.w_do[where, :] = join(parts, 2)
        both = pl.ds(pl.multiple_of(index * 32, 32), 32)
        for piece, target in ((7, s.w_w2), (9, s.w_p2)):
            target[both, :] = low(
                jnp.concatenate([part[piece * share : (piece + 2) * share] for part in parts], axis=0)
            )
        found = []
        for outer in range(at.outers):
            mine = lax.div(outer * GROUP + at.inner, 2).astype(f32)
            total = carried[outer]
            for part in parts:
                count_row = part[11 * share : 11 * share + 1, LANES:]
                item_at = part[11 * share + 1 : 11 * share + 2, LANES:]
                total = total + jnp.where(item_at == mine, count_row, 0.0)
            found.append(total)
        s.fourier[where, :] = jnp.concatenate(
            [part[11 * share : 12 * share, :LANES] for part in parts], axis=0
        )
        return tuple(found)

    table_sum = TableSum(at, s)
    table_sum.start()
    found = lax.fori_loop(
        0, devices // group, take_two, tuple(jnp.zeros((1, LANES), f32) for _ in range(at.outers))
    )
    for outer in range(at.outers):
        s.inverse[outer : outer + 1, :] = jnp.broadcast_to(
            1.0 / jnp.sum(found[outer], axis=1, keepdims=True), (1, width)
        )
    w_dq = jnp.concatenate(
        [s.fourier[pl.ds(0, FOUR, stride=2), :], s.fourier[pl.ds(1, FOUR, stride=2), :]], axis=1
    )
    table_sum.middle()
    s.t_dq[...] = low(w_dq.T)
    for piece in range(2):
        cols = slice(piece * width, (piece + 1) * width)
        s.t_kv[cols, :] = flip(s.w_kv[:, cols])
        s.t_w1[cols, :] = flip(s.w_w1[:, cols])
        s.t_p1[cols, :] = flip(s.w_p1[:, cols])
        s.t_w2[:, cols] = flip(s.w_w2[cols, :])
        s.t_p2[:, cols] = flip(s.w_p2[cols, :])
    s.t_do[...] = flip(s.w_do[...])
    table_sum.late(s.table_self)

    def cross_queries(tile, _):
        where = columns(tile)
        s.qd[:, where] = low(dot(s.t_dq[...], s.phi[:, where]))

    lax.fori_loop(0, tiles, cross_queries, None)
    table_sum.finish(s.table_self)

    def phase_b(tile, _):
        where = columns(tile)
        mask = s.mask[0:1, where]
        queries = s.q[:, where]
        mixed = per_block(
            tile, lambda b: dot(summary(s.table_self, tile, b), queries[:, lanes_of(b)])
        )
        attended = low(mixed * mask)
        s.o[:, where] = attended
        first_sum = features_turned(tile) + dot(s.t_o[...], attended)
        scaled_two, root_two = column_norm(first_sum)
        s.root_two[0:1, where] = root_two
        s.xh2[:, where] = low(scaled_two)
        middle = low(scaled_two * column(2) + column(3))
        s.u2[:, where] = middle
        hidden, slope = gelu_both(dot(s.t_w1[...], middle) + hidden_column(0))
        hidden = low(hidden)
        s.e1[:, where] = hidden
        s.slope[:, where] = low(slope)
        encoded = first_sum + dot(s.t_w2[...], hidden) + column(6)
        scaled_three, root_three = column_norm(encoded)
        s.root_three[0:1, where] = root_three
        s.xh3[:, where] = low(scaled_three)
        outer = low(scaled_three * column(4) + column(5))
        s.u3[:, where] = outer
        pair = dot(s.t_kv[...], outer)
        keys = low(pair[:width] * mask)
        values = low(pair[width:])
        s.kd[:, where] = keys
        s.vd[:, where] = values
        put_products(tile, values, keys)

    lax.fori_loop(0, tiles, phase_b, None)
    table_sum.start()
    table_sum.middle()
    table_sum.late(s.table_other)
    table_sum.finish(s.table_other)

    def phase_c(tile, _):
        where = columns(tile)
        mask = s.mask[0:1, where]
        queries = s.qd[:, where]
        tables = [summary(s.table_other, tile, block) for block in range(tile_blocks)]
        decoded = low(
            per_block(tile, lambda b: dot(tables[b], queries[:, lanes_of(b)])) * mask
        )
        latent = dot(s.t_do[...], decoded)
        latent_low = low(latent)
        hidden, slope = gelu_both(dot(s.t_p1[...], latent_low) + hidden_column(1))
        hidden = low(hidden)
        output = latent + dot(s.t_p2[...], hidden) + column(7)
        put_out(tile, s.layer_output, s.output_slots, s.sem_out, 0, low(dot_bt(s.eye[...], low(output))))
        upstream = s.cotangent[where, :]
        turned = dot_bt(s.eye[...], upstream)
        add_sum(7, turned)
        grad_spread = dot_bt(s.w_p2[...], upstream) * slope
        add_sum(10, grad_spread)
        grad_spread = low(grad_spread)
        grad_latent = low(turned + dot(s.w_p1[...], grad_spread))
        grad_decoded = low(dot(s.w_do[...], grad_latent) * mask)
        grad_queries = low(
            per_block(tile, lambda b: dot_at(tables[b], grad_decoded[:, lanes_of(b)]))
        )
        put_products(tile, grad_decoded, queries)
        s.grad_p2[...] += dot(hidden, upstream)
        s.grad_p1[...] += dot_bt(latent_low, grad_spread)
        s.grad_do[...] += dot_bt(decoded, grad_latent)
        s.grad_dq[...] += dot_bt(s.phi[:, where], grad_queries)

    lax.fori_loop(0, tiles, phase_c, None)
    table_sum.start()
    end_out(s.layer_output, s.output_slots, s.sem_out, 0)
    s.fourier[pl.ds(0, FOUR, stride=2), :] = s.grad_dq[:, :LANES]
    s.fourier[pl.ds(1, FOUR, stride=2), :] = s.grad_dq[:, LANES:]
    zeros = jnp.zeros((share, LANES), f32)

    def rows_of(chunk, count=1):
        size = share * count
        return pl.ds(pl.multiple_of(chunk * size, size), size)

    def chunk_c(chunk):
        where = rows_of(chunk)
        return jnp.concatenate(
            [
                s.grad_do[where, :],
                s.grad_p1[where, :width],
                s.grad_p1[where, width:],
                s.grad_p2[rows_of(chunk, 2), :],
                jnp.concatenate([s.fourier[where, :], zeros], axis=1),
            ],
            axis=0,
        )

    sum_c = GradSum(at, s, "c")
    sum_c.start(chunk_c)
    table_sum.middle()
    sum_c.second()
    table_sum.late(s.table_other)
    table_sum.finish(s.table_other)

    def phase_d(tile, _):
        where = columns(tile)
        mask = s.mask[0:1, where]
        keys, values = s.kd[:, where], s.vd[:, where]
        tables = [summary(s.table_other, tile, block) for block in range(tile_blocks)]
        grad_keys = per_block(tile, lambda b: dot_at(tables[b], values[:, lanes_of(b)])) * mask
        grad_values = per_block(tile, lambda b: dot(tables[b], keys[:, lanes_of(b)]))
        grad_pair = low(jnp.concatenate([grad_keys, grad_values], axis=0))
        s.grad_kv[...] += dot_bt(s.u3[:, where], grad_pair)
        grad_outer = dot(s.w_kv[...], grad_pair)
        scaled = s.xh3[:, where].astype(f32)
        add_sum(4, grad_outer * scaled)
        add_sum(5, grad_outer)
        grad_encoded = column_norm_back(
            grad_outer, scaled, s.root_three[0:1, where], column(4)
        )
        add_sum(6, grad_encoded)
        grad_encoded_low = low(grad_encoded)
        s.grad_w2[...] += dot_bt(s.e1[:, where], grad_encoded_low)
        grad_hidden = dot(s.w_w2[...], grad_encoded_low) * s.slope[:, where].astype(f32)
        add_sum(8, grad_hidden)
        grad_hidden = low(grad_hidden)
        s.grad_w1[...] += dot_bt(s.u2[:, where], grad_hidden)
        grad_middle = dot(s.w_w1[...], grad_hidden)
        scaled = s.xh2[:, where].astype(f32)
        add_sum(2, grad_middle * scaled)
        add_sum(3, grad_middle)
        grad_first = grad_encoded + column_norm_back(
            grad_middle, scaled, s.root_two[0:1, where], column(2)
        )
        grad_first = low(grad_first)
        s.xh2[:, where] = grad_first
        s.grad_o[...] += dot_bt(s.o[:, where], grad_first)
        grad_attended = low(dot(s.w_o[...], grad_first) * mask)
        s.kd[:, where] = grad_attended
        put_products(tile, grad_attended, s.q[:, where])

    lax.fori_loop(0, tiles // 2, phase_d, None)
    sum_c.third()
    lax.fori_loop(tiles // 2, tiles, phase_d, None)
    table_sum.start()
    s.grads_c[...] = sum_c.finish()

    def chunk_d(chunk):
        where = rows_of(chunk)
        return jnp.concatenate(
            [
                s.grad_kv[where, :width],
                s.grad_kv[where, width:],
                s.grad_o[where, :],
                s.grad_w1[where, :width],
                s.grad_w1[where, width:],
                s.grad_w2[rows_of(chunk, 2), :],
                jnp.zeros((share, width), f32),
            ],
            axis=0,
        )

    sum_d = GradSum(at, s, "d")
    sum_d.start(chunk_d)
    table_sum.middle()

    def query_grads(tile, _):
        where = columns(tile)
        upstream = s.kd[:, where]
        grad = per_block(
            tile, lambda b: dot_at(summary(s.table_self, tile, b), upstream[:, lanes_of(b)])
        )
        grad = low(turn(grad, s.cosine[:, where], s.sine[:, where], -1.0))
        s.q[:, where] = grad
        s.grad_qkv[:, :width] += dot_bt(s.u1[:, where], grad)

    lax.fori_loop(0, tiles // 2, query_grads, None)
    sum_d.second()
    table_sum.late(s.table_other)
    lax.fori_loop(tiles // 2, tiles, query_grads, None)
    table_sum.finish(s.table_other)

    def phase_e(tile, _):
        where = columns(tile)
        mask = s.mask[0:1, where]
        keys, values = s.k[:, where], s.v[:, where]
        tables = [summary(s.table_other, tile, block) for block in range(tile_blocks)]
        grad_keys = per_block(tile, lambda b: dot_at(tables[b], values[:, lanes_of(b)])) * mask
        grad_values = low(per_block(tile, lambda b: dot(tables[b], keys[:, lanes_of(b)])))
        grad_keys = low(turn(grad_keys, s.cosine[:, where], s.sine[:, where], -1.0))
        pair = jnp.concatenate([grad_keys, grad_values], axis=0)
        s.grad_qkv[:, width:] += dot_bt(s.u1[:, where], pair)
        grad_normed = dot(s.w_qkv[...], jnp.concatenate([s.q[:, where], pair], axis=0))
        turned = features_turned(tile)
        root = s.root_one[0:1, where]
        scaled = (turned - jnp.sum(turned, axis=0, keepdims=True) * (1.0 / width)) * root
        add_sum(0, grad_normed * scaled)
        add_sum(1, grad_normed)
        grad_input = s.xh2[:, where].astype(f32) + column_norm_back(
            grad_normed, scaled, root, column(0)
        )
        put_out(tile, s.input_grad, s.input_slots, s.sem_out, 1, grad_input.T)

    lax.fori_loop(0, tiles // 2, phase_e, None)
    sum_d.third()
    lax.fori_loop(tiles // 2, tiles, phase_e, None)

    lane_wide = lax.broadcasted_iota(jnp.int32, (width, LANES), 1)
    sums = jnp.zeros((width, LANES), f32)
    for index in range(12):
        sums = jnp.where(
            lane_wide == index, jnp.sum(s.vector_sum[index], axis=1, keepdims=True), sums
        )
    s.vector_cols[...] = sums

    def chunk_e(chunk):
        where = rows_of(chunk)
        return jnp.concatenate(
            [
                s.grad_qkv[where, :width],
                s.grad_qkv[where, width : 2 * width],
                s.grad_qkv[where, 2 * width :],
                jnp.concatenate([s.vector_cols[where, :], zeros], axis=1),
            ],
            axis=0,
        )

    sum_e = GradSum(at, s, "e")
    sum_e.start(chunk_e)
    s.grads_d[...] = sum_d.finish()
    end_out(s.input_grad, s.input_slots, s.sem_out, 1)
    sum_e.second()
    early = jnp.sum(s.grads_c[...] * s.grads_c[...], axis=0, keepdims=True) + jnp.sum(
        s.grads_d[...] * s.grads_d[...], axis=0, keepdims=True
    )
    sum_e.third()
    grads_e = sum_e.finish()
    s.grads_e[...] = grads_e
    squares = jnp.sum(early + jnp.sum(grads_e * grads_e, axis=0, keepdims=True), axis=1, keepdims=True)
    vector_rows = grads_e[3 * share : 4 * share, :LANES]
    row_small = lax.broadcasted_iota(jnp.int32, (share, LANES), 0)
    lane_small = lax.broadcasted_iota(jnp.int32, (share, LANES), 1)
    s.final[at.inner, at.outer] = jnp.where(
        (row_small == 0) & (lane_small == 12), squares, vector_rows
    )

    def final_along(step, start):
        source = at.outer if start else at.outer_at(step)
        return remote(
            s.final.at[at.inner, at.outer], s.final.at[at.inner, source], s.sem_fs.at[0, step],
            s.sem_fr.at[0, source], at.device(at.outer_at(step), at.inner),
        )

    def final_inner(step, start):
        source = at.inner if start else at.inner_at(step)
        return remote(
            s.final.at[at.inner], s.final.at[source], s.sem_fs.at[1, step],
            s.sem_fr.at[1, source], at.device(at.outer, at.inner_at(step)),
        )

    for step in range(1, at.outers):
        final_along(step, True).start()
    for step in range(1, at.outers):
        final_along(step, False).wait()
    for step in range(1, GROUP):
        final_inner(step, True).start()
    for step in range(1, GROUP):
        final_inner(step, False).wait()

    @pl.loop(0, devices)
    def _(chunk):
        s.vector_all[rows_of(chunk), :] = s.final[lax.rem(chunk, GROUP), lax.div(chunk, GROUP)]


def update_kernel(share, *refs):
    grads_c, grads_d, grads_e, vector_all = refs[:4]
    weights = refs[4:22]
    norm_out = refs[22]
    results = refs[23:41]
    flat_square, flat_expand, flat_contract = refs[41:]
    width = grads_c.shape[1]
    places = [(grads_e, 0), (grads_e, 1), (grads_e, 2), (grads_d, 2), (grads_d, 0), (grads_d, 1), (grads_c, 0)]
    for matrix, (source, piece) in enumerate(places):
        for row in range(share):
            start = piece * share + row
            flat_square[matrix : matrix + 1, row * width : (row + 1) * width] = source[
                start : start + 1, :
            ]
    for matrix, (source, piece) in enumerate(((grads_d, 3), (grads_c, 1))):
        for half in range(2):
            for row in range(share):
                start = (piece + half) * share + row
                target = row * F + half * width
                flat_expand[matrix : matrix + 1, target : target + width] = source[
                    start : start + 1, :
                ]
    for matrix, (source, piece) in enumerate(((grads_d, 5), (grads_c, 3))):
        for row in range(2 * share):
            start = piece * share + row
            flat_contract[matrix : matrix + 1, row * width : (row + 1) * width] = source[
                start : start + 1, :
            ]
    fourier = grads_c[5 * share : 6 * share, :LANES]
    turned = vector_all[...].T
    norm = jnp.sqrt(jnp.sum(turned[12:13, :], axis=1, keepdims=True))
    norm_out[...] = norm
    factor = jnp.minimum(1.0, CLIP_NORM / (norm + 1e-06))
    hidden = jnp.concatenate(
        [
            jnp.concatenate([turned[8:9], turned[9:10]], axis=1),
            jnp.concatenate([turned[10:11], turned[11:12]], axis=1),
        ],
        axis=0,
    )
    grads = (flat_square[...], flat_expand[...], flat_contract[...], fourier, turned[:8], hidden)
    rates = (RATE_MATRIX,) * 4 + (RATE_VECTOR,) * 2
    for index, (grad, rate) in enumerate(zip(grads, rates)):
        weight, first, second = (weights[3 * index + part][...] for part in range(3))
        values = adam_update(weight, first, second, grad, factor, rate)
        for part in range(3):
            results[3 * index + part][...] = values[part]


def fused(devices, features, coords, fourier_basis, block_items, point_mask, cotangent, *weights):
    points, width = features.shape
    blocks = points // BLOCK
    outers = devices // GROUP
    share = width // devices
    items = points * devices // ITEM_PTS
    bf16, f32 = jnp.bfloat16, jnp.float32
    square, expand, contract, fourier, vector, hidden = (weights[3 * i] for i in range(6))
    vmem = lambda shape, dtype: pltpu.VMEM(shape, dtype)
    inputs = {
        "items": block_items,
        "features": features,
        "coords": coords,
        "fourier_basis": fourier_basis,
        "point_mask": point_mask.reshape(blocks, BLOCK),
        "cotangent": cotangent,
        "square_weight": square,
        "expand_weight": expand,
        "contract_weight": contract,
        "fourier_weight": fourier.reshape(share, LANES),
        "vector_weight": vector,
        "hidden_weight": hidden,
    }
    rows_c, rows_d, rows_e = 6 * share, 8 * share, 4 * share
    outputs = {
        "layer_output": ((points, width), bf16),
        "input_grad": ((points, width), f32),
        "grads_c": ((rows_c, width), f32),
        "grads_d": ((rows_d, width), f32),
        "grads_e": ((rows_e, width), f32),
        "vector_all": ((width, LANES), f32),
    }
    tall = lambda rows: vmem((rows, points), bf16)
    scratch = {
        "pack": vmem((16 * share, width), f32),
        "gather_one": vmem((2, 4, outers, 4 * share, width), bf16),
        "gather_two": vmem((2, 4, outers, 12 * share, width), bf16),
        "eye": vmem((width, width), bf16),
        "heads": vmem((width, width), bf16),
        "small": vmem((LANES, width), f32),
        "cols": vmem((width, LANES), f32),
        "spread": vmem((items * E, blocks * E), bf16),
        "vector_sum": vmem((12, width, LANES), f32),
        "vector_cols": vmem((width, LANES), f32),
        "grad_qkv": vmem((width, 3 * width), f32),
        "grad_o": vmem((width, width), f32),
        "grad_kv": vmem((width, 2 * width), f32),
        "grad_do": vmem((width, width), f32),
        "grad_w1": vmem((width, F), f32),
        "grad_p1": vmem((width, F), f32),
        "grad_w2": vmem((F, width), f32),
        "grad_p2": vmem((F, width), f32),
        "grad_dq": vmem((FOUR, width), f32),
        "fourier": vmem((2 * FOUR, LANES), f32),
        "w_qkv": vmem((width, 3 * width), bf16),
        "t_qkv": vmem((3 * width, width), bf16),
        "w_o": vmem((width, width), bf16),
        "t_o": vmem((width, width), bf16),
        "w_kv": vmem((width, 2 * width), bf16),
        "t_kv": vmem((2 * width, width), bf16),
        "w_do": vmem((width, width), bf16),
        "t_do": vmem((width, width), bf16),
        "w_w1": vmem((width, F), bf16),
        "t_w1": vmem((F, width), bf16),
        "w_p1": vmem((width, F), bf16),
        "t_p1": vmem((F, width), bf16),
        "w_w2": vmem((F, width), bf16),
        "t_w2": vmem((width, F), bf16),
        "w_p2": vmem((F, width), bf16),
        "t_p2": vmem((width, F), bf16),
        "t_dq": vmem((width, FOUR), bf16),
        "mask": vmem((1, points), f32),
        "root_one": vmem((1, points), f32),
        "root_two": vmem((1, points), f32),
        "root_three": vmem((1, points), f32),
        "cosine": vmem((E // 2, points), f32),
        "sine": vmem((E // 2, points), f32),
        "phi": tall(FOUR),
        "u1": tall(width),
        "q": tall(width),
        "k": tall(width),
        "v": tall(width),
        "qd": tall(width),
        "o": tall(width),
        "xh2": tall(width),
        "u2": tall(width),
        "e1": tall(F),
        "slope": tall(F),
        "xh3": tall(width),
        "u3": tall(width),
        "kd": tall(width),
        "vd": tall(width),
        "per_block": vmem((blocks * E, width), f32),
        "inverse": vmem((max(8, outers), width), f32),
        "table_send": vmem((GROUP, outers, 16, width), bf16),
        "table_recv": vmem((GROUP, outers, 16, width), bf16),
        "table_part": vmem((outers, 16, width), bf16),
        "table_cross": vmem((2, outers, outers, 16, width), bf16),
        "table_self": vmem((GROUP, outers, 16, width), bf16),
        "table_other": vmem((GROUP, outers, 16, width), bf16),
        "final": vmem((GROUP, outers, share, LANES), f32),
        "output_slots": vmem((2, TILE, width), bf16),
        "input_slots": vmem((2, TILE, width), f32),
        "sem_out": pltpu.SemaphoreType.DMA((2, 2)),
    }
    for key, rows in (("c", rows_c), ("d", rows_d), ("e", rows_e)):
        scratch["full_" + key] = vmem((2, 4, outers, rows, width), bf16)
        for part in ("half_", "quarter_"):
            scratch[part + key] = vmem((4, outers, rows, width), bf16)
        scratch["last_" + key] = vmem((outers, rows, width), bf16)
    many = max(GROUP, outers)
    for key in ("ts", "tr", "g1s", "g1r", "g2s", "g2r", "cs", "cr", "ds", "dr", "es", "er"):
        scratch["sem_" + key] = pltpu.SemaphoreType.DMA((4, many))
    for key in ("fs", "fr"):
        scratch["sem_" + key] = pltpu.SemaphoreType.DMA((2, many))
    names = list(inputs) + list(outputs) + list(scratch)
    in_specs = [pl.BlockSpec(memory_space=pltpu.SMEM)] + [
        pl.BlockSpec(memory_space=pltpu.VMEM) for _ in range(len(inputs) - 1)
    ]
    whole = pl.BlockSpec(memory_space=pltpu.VMEM)
    made = pl.pallas_call(
        functools.partial(layer_kernel, names, devices),
        out_shape=[jax.ShapeDtypeStruct(*shape) for shape in outputs.values()],
        in_specs=in_specs,
        out_specs=[pl.BlockSpec(memory_space=pl.ANY)] * 2 + [whole] * (len(outputs) - 2),
        scratch_shapes=list(scratch.values()),
        compiler_params=pltpu.CompilerParams(
            collective_id=0, has_side_effects=True, vmem_limit_bytes=VMEM_BYTES
        ),
    )(*inputs.values())
    layer_output, input_grad, *sums = made
    flat = list(weights)
    for part in range(9, 12):
        flat[part] = flat[part].reshape(share, LANES)
    shapes = [jax.ShapeDtypeStruct((1, 1), f32)] + [
        jax.ShapeDtypeStruct(flat[index].shape, f32) for index in range(18)
    ]
    order = []
    for index in range(6):
        order += [shapes[1 + 3 * index]] * 3
    updated = pl.pallas_call(
        functools.partial(update_kernel, share),
        out_shape=[shapes[0]] + order,
        in_specs=[whole] * 22,
        out_specs=[whole] * 19,
        scratch_shapes=[
            vmem(square.shape, f32),
            vmem(expand.shape, f32),
            vmem(contract.shape, f32),
        ],
        compiler_params=pltpu.CompilerParams(vmem_limit_bytes=16 * 1024 * 1024),
    )(*sums, *flat)
    norm, *rest = updated
    for part in range(9, 12):
        rest[part] = rest[part].reshape(fourier.shape)
    return (layer_output, input_grad, norm.reshape(()), *rest)


def shards(features, *others):
    devices = lax.axis_size("pts")
    width = features.shape[1]
    if devices % GROUP == 0 and width % (8 * devices) == 0:
        return fused(devices, features, *others)
    return plain(features, *others)


def solution(mesh):
    in_specs = (
        P("pts", None),
        P(None, "pts"),
        P(),
        P("pts"),
        P("pts"),
        P("pts", None),
        P(None, "pts"),
        P(None, "pts"),
        P(None, "pts"),
        P(None, "pts"),
        P(None, "pts"),
        P(None, "pts"),
        P(None, "pts"),
        P(None, "pts"),
        P(None, "pts"),
        P("pts"),
        P("pts"),
        P("pts"),
        P(),
        P(),
        P(),
        P(),
        P(),
        P(),
    )
    out_specs = (
        P("pts", None),
        P("pts", None),
        P(),
        P(None, "pts"),
        P(None, "pts"),
        P(None, "pts"),
        P(None, "pts"),
        P(None, "pts"),
        P(None, "pts"),
        P(None, "pts"),
        P(None, "pts"),
        P(None, "pts"),
        P("pts"),
        P("pts"),
        P("pts"),
        P(),
        P(),
        P(),
        P(),
        P(),
        P(),
    )
    return jax.shard_map(shards, mesh=mesh, in_specs=in_specs, out_specs=out_specs, check_vma=False)
```

```python
import functools
import math
import types

import jax
import jax.numpy as jnp
from jax import lax
from jax.experimental import pallas as pl
from jax.experimental.pallas import tpu as pltpu
from jax.sharding import PartitionSpec as P

H = 8
E = 32
F = 512
FOUR = 128
BLOCK = 128
ITEM_PTS = 8192
STEP = 10


NORM_EPS = 1e-05
GELU_C = math.sqrt(2.0 / math.pi)
GELU_A = 0.044715
BETA_ONE = 0.9
BETA_TWO = 0.95
ADAM_EPS = 1e-08
WEIGHT_DECAY = 0.1
RATE_MATRIX = 0.05
RATE_VECTOR = 0.25
CLIP_NORM = 1.0
HIGHEST_PRECISION = lax.Precision.HIGHEST


def matmul(left, right):
    return jnp.dot(left, right, preferred_element_type=jnp.float32)


def matmul_left(left, right):
    return lax.dot_general(
        left, right, (((0,), (0,)), ((), ())), preferred_element_type=jnp.float32
    )


def matmul_right(left, right):
    return lax.dot_general(
        left, right, (((1,), (1,)), ((), ())), preferred_element_type=jnp.float32
    )


def gelu(values):
    return 0.5 * values * (1.0 + jnp.tanh(GELU_C * (values + GELU_A * values * values * values)))


def gelu_slope(values):
    tangent = jnp.tanh(GELU_C * (values + GELU_A * values * values * values))
    return 0.5 * (1.0 + tangent) + 0.5 * values * (1.0 - tangent * tangent) * GELU_C * (
        1.0 + 3.0 * GELU_A * values * values
    )


def norm_parts(values, norm_gain, norm_bias):
    centred = values - jnp.mean(values, axis=-1, keepdims=True)
    variance = jnp.mean(centred * centred, axis=-1, keepdims=True)
    root_inv = lax.rsqrt(variance + NORM_EPS)
    scaled = centred * root_inv
    return (scaled * norm_gain + norm_bias, scaled, root_inv)


def norm_back(upstream, scaled, root_inv, norm_gain):
    through = upstream * norm_gain
    centre = jnp.mean(through, axis=-1, keepdims=True)
    along = jnp.mean(through * scaled, axis=-1, keepdims=True)
    return root_inv * (through - centre - scaled * along)


def rotary_tables(coords):
    quarter = E // 4
    frequency = math.pi * (jnp.arange(quarter, dtype=jnp.float32) + 1.0) / quarter
    first_angle = coords[0][:, None] * frequency[None, :]
    second_angle = coords[1][:, None] * frequency[None, :]
    angles = jnp.concatenate([first_angle, first_angle, second_angle, second_angle], axis=1)
    return (jnp.cos(angles), jnp.sin(angles))


def rotate(values, cosine, sine):
    quarter = E // 4
    swapped = jnp.concatenate(
        [
            -values[..., quarter : 2 * quarter],
            values[..., :quarter],
            -values[..., 3 * quarter :],
            values[..., 2 * quarter : 3 * quarter],
        ],
        axis=-1,
    )
    return values * cosine[:, None, :] + swapped * sine[:, None, :]


def rotate_back(grads, cosine, sine):
    quarter = E // 4
    scaled = grads * sine[:, None, :]
    swapped = jnp.concatenate(
        [
            scaled[..., quarter : 2 * quarter],
            -scaled[..., :quarter],
            scaled[..., 3 * quarter :],
            -scaled[..., 2 * quarter : 3 * quarter],
        ],
        axis=-1,
    )
    return grads * cosine[:, None, :] + swapped


def fourier_features(coords, fourier_basis):
    phases = (
        2.0
        * math.pi
        * (
            coords[0][:, None] * fourier_basis[0][None, :]
            + coords[1][:, None] * fourier_basis[1][None, :]
        )
    )
    return jnp.concatenate([jnp.cos(phases), jnp.sin(phases)], axis=1)


def block_table(left, right, onehot):
    blocks = onehot.shape[0]
    per_block = jnp.einsum(
        "bphe,bphf->bhef",
        left.reshape(blocks, BLOCK, H, E),
        right.reshape(blocks, BLOCK, H, E),
        preferred_element_type=jnp.float32,
    )
    return jnp.einsum("ba,bhef->ahef", onehot, per_block, precision=HIGHEST_PRECISION)


def scale_round(table, inverse_count):
    return (table * inverse_count[:, None, None, None]).astype(jnp.bfloat16)


def spread(summary, onehot):
    selected = jnp.einsum(
        "ba,ahef->bhef", onehot.astype(jnp.bfloat16), summary, preferred_element_type=jnp.float32
    )
    return selected.astype(jnp.bfloat16)


def apply_summary(rows_low, block_summary, transposed):
    blocks = block_summary.shape[0]
    pattern = "bphf,bhef->bphe" if transposed else "bphe,bhef->bphf"
    mixed = jnp.einsum(
        pattern,
        rows_low.reshape(blocks, BLOCK, H, E),
        block_summary,
        preferred_element_type=jnp.float32,
    )
    return mixed.reshape(-1, H * E)


def galerkin_backward(
    grad_low, queries_low, keys_masked, values_low, block_summary, onehot, mask_float, reducer
):
    grad_masked = grad_low * mask_float.astype(jnp.bfloat16)
    grad_queries = apply_summary(grad_masked, block_summary, True)
    summary_grad = reducer(block_table(queries_low, grad_masked, onehot))
    block_grad = spread(summary_grad, onehot)
    grad_keys = apply_summary(values_low, block_grad, True) * mask_float
    grad_values = apply_summary(keys_masked, block_grad, False)
    return (grad_queries, grad_keys, grad_values)


def adam_update(weight, first, second, grad, factor, rate):
    clipped = grad * factor
    new_first = BETA_ONE * first + (1.0 - BETA_ONE) * clipped
    new_second = BETA_TWO * second + (1.0 - BETA_TWO) * clipped * clipped
    first_hat = new_first / (1.0 - BETA_ONE**STEP)
    second_hat = new_second / (1.0 - BETA_TWO**STEP)
    new_weight = weight - rate * (
        first_hat / (jnp.sqrt(second_hat) + ADAM_EPS) + WEIGHT_DECAY * weight
    )
    return (new_first, new_second, new_weight)


def own_share(full, width, along, start_index):
    return lax.dynamic_slice_in_dim(full, start_index * width, width, along)


def plain(
    features,
    coords,
    fourier_basis,
    block_items,
    point_mask,
    cotangent,
    square_weight,
    square_first,
    square_second,
    expand_weight,
    expand_first,
    expand_second,
    contract_weight,
    contract_first,
    contract_second,
    fourier_weight,
    fourier_first,
    fourier_second,
    vector_weight,
    vector_first,
    vector_second,
    hidden_weight,
    hidden_first,
    hidden_second,
):
    rows = features.shape[0]
    width = features.shape[1]
    blocks = rows // BLOCK
    devices = lax.axis_size("pts")
    items_total = rows * devices // ITEM_PTS
    gathered = (
        lax.all_gather(square_weight.astype(jnp.bfloat16), "pts", axis=1, tiled=True),
        lax.all_gather(expand_weight.astype(jnp.bfloat16), "pts", axis=1, tiled=True),
        lax.all_gather(contract_weight.astype(jnp.bfloat16), "pts", axis=1, tiled=True),
        lax.all_gather(fourier_weight.astype(jnp.bfloat16), "pts", axis=0, tiled=True),
    )
    square_full = gathered[0].reshape(7, width, width)
    expand_full = gathered[1].reshape(2, width, F)
    contract_full = gathered[2].reshape(2, F, width)
    fourier_full = gathered[3].reshape(FOUR, width)
    onehot = (block_items[:, None] == jnp.arange(items_total, dtype=jnp.int32)[None, :]).astype(
        jnp.float32
    )
    mask_float = point_mask.astype(jnp.float32)[:, None]
    mask_low = mask_float.astype(jnp.bfloat16)
    block_count = jnp.sum(mask_float.reshape(blocks, BLOCK), axis=1)
    local_count = jnp.dot(block_count, onehot, precision=HIGHEST_PRECISION)
    cosine, sine = rotary_tables(coords)
    phase_low = fourier_features(coords, fourier_basis).astype(jnp.bfloat16)
    inputs = features.astype(jnp.float32)
    normed, scaled_one, root_one = norm_parts(inputs, vector_weight[0], vector_weight[1])
    normed_low = normed.astype(jnp.bfloat16)
    joint_weight = jnp.concatenate([square_full[0], square_full[1], square_full[2]], axis=1)
    projected = matmul(normed_low, joint_weight)
    queries_low = (
        rotate(projected[:, :width].reshape(rows, H, E), cosine, sine)
        .reshape(rows, width)
        .astype(jnp.bfloat16)
    )
    keys_low = (
        rotate(projected[:, width : 2 * width].reshape(rows, H, E), cosine, sine)
        .reshape(rows, width)
        .astype(jnp.bfloat16)
    )
    keys_masked = keys_low * mask_low
    values_low = projected[:, 2 * width :].astype(jnp.bfloat16)
    self_local = block_table(keys_masked, values_low, onehot)
    self_table, item_count = lax.psum((self_local, local_count), "pts")
    inverse_count = 1.0 / item_count
    self_items = scale_round(self_table, inverse_count)
    self_summary = spread(self_items, onehot)
    attended_low = (apply_summary(queries_low, self_summary, False) * mask_float).astype(
        jnp.bfloat16
    )
    first_sum = inputs + matmul(attended_low, square_full[3])
    normed_mid, scaled_two, root_two = norm_parts(first_sum, vector_weight[2], vector_weight[3])
    middle_low = normed_mid.astype(jnp.bfloat16)
    hidden_pre = matmul(middle_low, expand_full[0]) + hidden_weight[0]
    hidden_low = gelu(hidden_pre).astype(jnp.bfloat16)
    encoded = first_sum + matmul(hidden_low, contract_full[0]) + vector_weight[6]
    normed_out, scaled_three, root_three = norm_parts(encoded, vector_weight[4], vector_weight[5])
    outer_low = normed_out.astype(jnp.bfloat16)
    pair_weight = jnp.concatenate([square_full[4], square_full[5]], axis=1)
    cross_projected = matmul(outer_low, pair_weight)
    cross_keys = cross_projected[:, :width].astype(jnp.bfloat16) * mask_low
    cross_values = cross_projected[:, width:].astype(jnp.bfloat16)
    cross_queries = matmul(phase_low, fourier_full).astype(jnp.bfloat16)
    cross_local = block_table(cross_keys, cross_values, onehot)
    cross_items = scale_round(lax.psum(cross_local, "pts"), inverse_count)
    cross_summary = spread(cross_items, onehot)
    decoded_low = (apply_summary(cross_queries, cross_summary, False) * mask_float).astype(
        jnp.bfloat16
    )
    latent = matmul(decoded_low, square_full[6])
    latent_low = latent.astype(jnp.bfloat16)
    spread_pre = matmul(latent_low, expand_full[1]) + hidden_weight[1]
    spread_low = gelu(spread_pre).astype(jnp.bfloat16)
    output = latent + matmul(spread_low, contract_full[1]) + vector_weight[7]
    cross_reducer = lambda table_part: scale_round(lax.psum(table_part, "pts"), inverse_count)
    self_reducer = lambda table_part: scale_round(lax.psum(table_part, "pts"), inverse_count)
    grad_output = cotangent.astype(jnp.float32)
    grad_bias_end = jnp.sum(grad_output, axis=0)
    grad_contract_spread = matmul_left(spread_low, cotangent)
    grad_spread = matmul_right(cotangent, contract_full[1]) * gelu_slope(spread_pre)
    grad_hidden_spread = jnp.sum(grad_spread, axis=0)
    grad_spread_low = grad_spread.astype(jnp.bfloat16)
    grad_expand_spread = matmul_left(latent_low, grad_spread_low)
    grad_latent = (grad_output + matmul_right(grad_spread_low, expand_full[1])).astype(jnp.bfloat16)
    grad_out_cross = matmul_left(decoded_low, grad_latent)
    grad_decoded = matmul_right(grad_latent, square_full[6]).astype(jnp.bfloat16)
    cross_back = galerkin_backward(
        grad_decoded,
        cross_queries,
        cross_keys,
        cross_values,
        cross_summary,
        onehot,
        mask_float,
        cross_reducer,
    )
    grad_fourier_full = matmul_left(phase_low, cross_back[0].astype(jnp.bfloat16))
    grad_pair_low = jnp.concatenate([cross_back[1], cross_back[2]], axis=1).astype(jnp.bfloat16)
    grad_pair_full = matmul_left(outer_low, grad_pair_low)
    grad_normed_out = matmul_right(grad_pair_low, pair_weight)
    grad_gain_three = jnp.sum(grad_normed_out * scaled_three, axis=0)
    grad_bias_three = jnp.sum(grad_normed_out, axis=0)
    grad_encoded = norm_back(grad_normed_out, scaled_three, root_three, vector_weight[4])
    grad_bias_middle = jnp.sum(grad_encoded, axis=0)
    grad_encoded_low = grad_encoded.astype(jnp.bfloat16)
    grad_contract_enc = matmul_left(hidden_low, grad_encoded_low)
    grad_hidden = matmul_right(grad_encoded_low, contract_full[0]) * gelu_slope(hidden_pre)
    grad_hidden_enc = jnp.sum(grad_hidden, axis=0)
    grad_hidden_low = grad_hidden.astype(jnp.bfloat16)
    grad_expand_enc = matmul_left(middle_low, grad_hidden_low)
    grad_middle = matmul_right(grad_hidden_low, expand_full[0])
    grad_gain_two = jnp.sum(grad_middle * scaled_two, axis=0)
    grad_bias_two = jnp.sum(grad_middle, axis=0)
    grad_first = grad_encoded + norm_back(grad_middle, scaled_two, root_two, vector_weight[2])
    grad_first_low = grad_first.astype(jnp.bfloat16)
    grad_out_self = matmul_left(attended_low, grad_first_low)
    grad_attended = matmul_right(grad_first_low, square_full[3]).astype(jnp.bfloat16)
    self_back = galerkin_backward(
        grad_attended,
        queries_low,
        keys_masked,
        values_low,
        self_summary,
        onehot,
        mask_float,
        self_reducer,
    )
    grad_queries = rotate_back(self_back[0].reshape(rows, H, E), cosine, sine).reshape(rows, width)
    grad_keys = rotate_back(self_back[1].reshape(rows, H, E), cosine, sine).reshape(rows, width)
    grad_joint_low = jnp.concatenate([grad_queries, grad_keys, self_back[2]], axis=1).astype(
        jnp.bfloat16
    )
    grad_joint_full = matmul_left(normed_low, grad_joint_low)
    grad_normed = matmul_right(grad_joint_low, joint_weight)
    grad_gain_one = jnp.sum(grad_normed * scaled_one, axis=0)
    grad_bias_one = jnp.sum(grad_normed, axis=0)
    grad_inputs = grad_first + norm_back(grad_normed, scaled_one, root_one, vector_weight[0])
    grad_square = jnp.stack(
        [
            grad_joint_full[:, :width],
            grad_joint_full[:, width : 2 * width],
            grad_joint_full[:, 2 * width :],
            grad_out_self,
            grad_pair_full[:, :width],
            grad_pair_full[:, width:],
            grad_out_cross,
        ]
    ).reshape(7, width * width)
    grad_expand = jnp.stack([grad_expand_enc, grad_expand_spread]).reshape(2, width * F)
    grad_contract = jnp.stack([grad_contract_enc, grad_contract_spread]).reshape(2, F * width)
    grad_fourier = grad_fourier_full.reshape(FOUR * width)
    grad_vector = jnp.stack(
        [
            grad_gain_one,
            grad_bias_one,
            grad_gain_two,
            grad_bias_two,
            grad_gain_three,
            grad_bias_three,
            grad_bias_middle,
            grad_bias_end,
        ]
    )
    grad_hidden_rows = jnp.stack([grad_hidden_enc, grad_hidden_spread])
    totals = lax.psum(
        (grad_square, grad_expand, grad_contract, grad_fourier, grad_vector, grad_hidden_rows),
        "pts",
    )
    squares = sum((jnp.sum(total_part * total_part) for total_part in totals))
    start_index = lax.axis_index("pts")
    share_square = own_share(totals[0], square_weight.shape[1], 1, start_index)
    share_expand = own_share(totals[1], expand_weight.shape[1], 1, start_index)
    share_contract = own_share(totals[2], contract_weight.shape[1], 1, start_index)
    share_fourier = own_share(totals[3], fourier_weight.shape[0], 0, start_index)
    vector_total = totals[4]
    hidden_total = totals[5]
    grad_norm = jnp.sqrt(squares)
    factor = jnp.minimum(1.0, CLIP_NORM / (grad_norm + 1e-06))
    new_square = adam_update(
        square_weight, square_first, square_second, share_square, factor, RATE_MATRIX
    )
    new_expand = adam_update(
        expand_weight, expand_first, expand_second, share_expand, factor, RATE_MATRIX
    )
    new_contract = adam_update(
        contract_weight, contract_first, contract_second, share_contract, factor, RATE_MATRIX
    )
    new_fourier = adam_update(
        fourier_weight, fourier_first, fourier_second, share_fourier, factor, RATE_MATRIX
    )
    new_vector = adam_update(
        vector_weight, vector_first, vector_second, vector_total, factor, RATE_VECTOR
    )
    new_hidden = adam_update(
        hidden_weight, hidden_first, hidden_second, hidden_total, factor, RATE_VECTOR
    )
    return (
        output.astype(jnp.bfloat16),
        grad_inputs,
        grad_norm,
        new_square[0],
        new_square[1],
        new_square[2],
        new_expand[0],
        new_expand[1],
        new_expand[2],
        new_contract[0],
        new_contract[1],
        new_contract[2],
        new_fourier[0],
        new_fourier[1],
        new_fourier[2],
        new_vector[0],
        new_vector[1],
        new_vector[2],
        new_hidden[0],
        new_hidden[1],
        new_hidden[2],
    )


GROUP = 8
TILE = 512
LANES = 128
PIECES = 8
VMEM_BYTES = 64 * 1024 * 1024


def dot(left, right):
    return jnp.dot(left, right, preferred_element_type=jnp.float32)


def dot_bt(left, right):
    return lax.dot_general(
        left, right, (((1,), (1,)), ((), ())), preferred_element_type=jnp.float32
    )


def dot_at(left, right):
    return lax.dot_general(
        left, right, (((0,), (0,)), ((), ())), preferred_element_type=jnp.float32
    )


def low(values):
    return values.astype(jnp.bfloat16)


def column_norm(values):
    inverse = 1.0 / values.shape[0]
    centred = values - jnp.sum(values, axis=0, keepdims=True) * inverse
    variance = jnp.sum(centred * centred, axis=0, keepdims=True) * inverse
    root_inv = lax.rsqrt(variance + NORM_EPS)
    return (centred * root_inv, root_inv)


def column_norm_back(upstream, scaled, root_inv, gain):
    inverse = 1.0 / upstream.shape[0]
    through = upstream * gain
    centre = jnp.sum(through, axis=0, keepdims=True) * inverse
    along = jnp.sum(through * scaled, axis=0, keepdims=True) * inverse
    return root_inv * (through - centre - scaled * along)


def gelu_both(values):
    square = values * values
    half = 0.5 + 0.5 * jnp.tanh(values * (GELU_C + (GELU_C * GELU_A) * square))
    slope = half + values * (half * (1.0 - half)) * (
        2.0 * GELU_C + (6.0 * GELU_C * GELU_A) * square
    )
    return (values * half, slope)


def turn(values, cosine, sine, sign):
    quarter = E // 4
    first_cos, second_cos = cosine[:quarter], cosine[quarter:]
    first_sin, second_sin = sine[:quarter] * sign, sine[quarter:] * sign
    parts = []
    for base in range(0, values.shape[0], E):
        one, two, three, four = (
            values[base + quarter * step : base + quarter * (step + 1)] for step in range(4)
        )
        parts += [
            one * first_cos - two * first_sin,
            two * first_cos + one * first_sin,
            three * second_cos - four * second_sin,
            four * second_cos + three * second_sin,
        ]
    return jnp.concatenate(parts, axis=0)


def compress(full):
    width = full.shape[1]
    head = lax.broadcasted_iota(jnp.int32, (E, width), 1) // E
    result = full[:E]
    for index in range(1, H):
        result = jnp.where(head == index, full[E * index : E * (index + 1)], result)
    return result


def lane_sum(values):
    result = values[:, :LANES]
    for start in range(LANES, values.shape[1], LANES):
        result = result + values[:, start : start + LANES]
    return result


def remote(source, target, send_sem, recv_sem, device):
    return pltpu.make_async_remote_copy(
        src_ref=source,
        dst_ref=target,
        send_sem=send_sem,
        recv_sem=recv_sem,
        device_id=(device,),
        device_id_type=pl.DeviceIdType.MESH,
    )


class Place:
    def __init__(self, devices):
        self.devices = devices
        self.outers = devices // GROUP
        self.me = lax.axis_index("pts")
        self.inner = lax.rem(self.me, GROUP)
        self.outer = lax.div(self.me, GROUP)
        self.core = lax.rem(self.me, 2)
        self.pair = lax.div(self.inner, 2)

    def inner_at(self, step):
        return lax.rem(self.inner + step, GROUP)

    def outer_at(self, step):
        return lax.rem(self.outer + step, self.outers)

    def pair_at(self, step):
        return lax.rem(self.pair + step, 4)

    def device(self, outer, inner):
        return outer * GROUP + inner


class Gather:
    def __init__(self, place, buffer, sems):
        self.place, self.buffer = place, buffer
        self.send, self.recv = sems

    def first(self, step, start):
        at = self.place
        slot = self.buffer.at[at.core, at.pair, at.outer if start else at.outer_at(step)]
        mine = self.buffer.at[at.core, at.pair, at.outer]
        source = at.outer if start else at.outer_at(step)
        return remote(
            mine, slot, self.send.at[0, step], self.recv.at[0, source],
            at.device(at.outer_at(step), at.inner),
        )

    def second(self, step, start):
        at = self.place
        source = at.pair if start else at.pair_at(step)
        return remote(
            self.buffer.at[at.core, at.pair], self.buffer.at[at.core, source],
            self.send.at[1, step], self.recv.at[1, source],
            at.device(at.outer, at.pair_at(step) * 2 + at.core),
        )

    def third(self, start):
        at = self.place
        source = at.core if start else 1 - at.core
        return remote(
            self.buffer.at[at.core], self.buffer.at[source], self.send.at[2, 0],
            self.recv.at[2, 0], at.device(at.outer, at.pair * 2 + 1 - at.core),
        )

    def start_first(self):
        for step in range(1, self.place.outers):
            self.first(step, True).start()

    def start_second(self):
        for step in range(1, self.place.outers):
            self.first(step, False).wait()
        for step in range(1, 4):
            self.second(step, True).start()

    def start_third(self):
        for step in range(1, 4):
            self.second(step, False).wait()
        self.third(True).start()

    def finish(self):
        self.third(False).wait()


class TableSum:
    def __init__(self, place, scratch):
        self.place, self.s, self.turn = place, scratch, 0

    def swap(self, step, start):
        at, s = self.place, self.s
        source = at.inner if start else at.inner_at(step)
        return remote(
            s.table_send.at[at.inner_at(step)], s.table_recv.at[source], s.sem_ts.at[0, step],
            s.sem_tr.at[0, source], at.device(at.outer, at.inner_at(step)),
        )

    def cross(self, step, start):
        at, s = self.place, self.s
        source = at.outer if start else at.outer_at(step)
        return remote(
            s.table_part, s.table_cross.at[self.turn, source], s.sem_ts.at[1 + self.turn, step],
            s.sem_tr.at[1 + self.turn, source],
            at.device(at.outer_at(step), at.inner),
        )

    def share(self, step, start, result):
        at, s = self.place, self.s
        source = at.inner if start else at.inner_at(step)
        return remote(
            result.at[at.inner], result.at[source], s.sem_ts.at[3, step], s.sem_tr.at[3, source],
            at.device(at.outer, at.inner_at(step)),
        )

    def start(self):
        at, s = self.place, self.s
        high = low(s.per_block[...])
        rest = low(s.per_block[...] - high.astype(jnp.float32))
        table = low(dot(s.spread[...], high) + dot(s.spread[...], rest))
        for chunk in range(at.devices):
            s.table_send[chunk % GROUP, chunk // GROUP] = table[chunk * 16 : (chunk + 1) * 16]
        for step in range(1, GROUP):
            self.swap(step, True).start()

    def middle(self):
        at, s = self.place, self.s
        total = s.table_send[at.inner].astype(jnp.float32)
        for step in range(1, GROUP):
            self.swap(step, False).wait()
            total = total + s.table_recv[at.inner_at(step)].astype(jnp.float32)
        s.table_part[...] = low(total)
        for step in range(1, at.outers):
            self.cross(step, True).start()

    def late(self, result):
        at, s = self.place, self.s
        total = s.table_part[...].astype(jnp.float32)
        for step in range(1, at.outers):
            self.cross(step, False).wait()
            total = total + s.table_cross[self.turn, at.outer_at(step)].astype(jnp.float32)
        for outer in range(at.outers):
            result[at.inner, outer] = low(total[outer] * s.inverse[outer : outer + 1, :])
        for step in range(1, GROUP):
            self.share(step, True, result).start()

    def finish(self, result):
        for step in range(1, GROUP):
            self.share(step, False, result).wait()
        self.turn = 1 - self.turn


class GradSum:
    def __init__(self, place, scratch, key, first):
        self.place = place
        self.half, self.quarter, self.last = (
            getattr(scratch, name + key) for name in ("half_", "quarter_", "last_")
        )
        self.full = scratch.gather_two.at[:, :, :, first : first + self.last.shape[1]]
        self.send, self.recv = getattr(scratch, f"sem_{key}s"), getattr(scratch, f"sem_{key}r")

    def swap(self):
        at = self.place
        return remote(
            self.full.at[1 - at.core], self.half, self.send.at[0, 0], self.recv.at[0, 0],
            at.device(at.outer, at.pair * 2 + 1 - at.core),
        )

    def across(self, step, start):
        at = self.place
        source = at.pair if start else at.pair_at(step)
        return remote(
            self.half.at[at.pair_at(step)], self.quarter.at[source], self.send.at[1, step],
            self.recv.at[1, source], at.device(at.outer, at.pair_at(step) * 2 + at.core),
        )

    def along(self, step, start):
        at = self.place
        source = at.outer if start else at.outer_at(step)
        return remote(
            self.quarter.at[at.pair, at.outer_at(step)], self.last.at[source], self.send.at[2, step],
            self.recv.at[2, source], at.device(at.outer_at(step), at.inner),
        )

    def start(self, chunk_of):
        at = self.place

        @pl.loop(0, at.devices)
        def _(chunk):
            inner = lax.rem(chunk, GROUP)
            self.full[lax.rem(inner, 2), lax.div(inner, 2), lax.div(chunk, GROUP)] = low(
                chunk_of(chunk)
            )

        self.swap().start()

    def second(self):
        at = self.place
        self.swap().wait()

        @pl.loop(0, 4)
        def _(pair):
            self.half[pair] = low(
                self.full[at.core, pair].astype(jnp.float32) + self.half[pair].astype(jnp.float32)
            )

        for step in range(1, 4):
            self.across(step, True).start()

    def third(self):
        at = self.place
        total = self.half[at.pair].astype(jnp.float32)
        for step in range(1, 4):
            self.across(step, False).wait()
            total = total + self.quarter[at.pair_at(step)].astype(jnp.float32)
        self.quarter[at.pair] = low(total)
        for step in range(1, at.outers):
            self.along(step, True).start()

    def finish(self):
        at = self.place
        total = self.quarter[at.pair, at.outer].astype(jnp.float32)
        for step in range(1, at.outers):
            self.along(step, False).wait()
            total = total + self.last[at.outer_at(step)].astype(jnp.float32)
        return total


def layer_kernel(names, devices, *refs):
    s = types.SimpleNamespace(**dict(zip(names, refs)))
    at = Place(devices)
    points, width = s.features.shape
    tiles = points // TILE
    blocks = points // BLOCK
    share = width // devices
    tile_blocks = TILE // BLOCK
    f32 = jnp.float32

    barrier = pltpu.get_barrier_semaphore()
    for step in range(1, GROUP):
        pl.semaphore_signal(
            barrier, inc=1, device_id=(at.device(at.outer, at.inner_at(step)),),
            device_id_type=pl.DeviceIdType.MESH,
        )
    for step in range(1, at.outers):
        pl.semaphore_signal(
            barrier, inc=1, device_id=(at.device(at.outer_at(step), at.inner),),
            device_id_type=pl.DeviceIdType.MESH,
        )

    def columns(tile):
        return pl.ds(pl.multiple_of(tile * TILE, TILE), TILE)

    def block_columns(block):
        return pl.ds(pl.multiple_of(block * BLOCK, BLOCK), BLOCK)

    def column(index):
        return s.cols[:, index : index + 1]

    def hidden_column(index):
        return jnp.concatenate([column(8 + 2 * index), column(9 + 2 * index)], axis=0)

    def out_copy(tile, target, slots, sems, index):
        slot = lax.rem(tile, 2)
        where = pl.ds(pl.multiple_of(tile * TILE, TILE), TILE)
        return pltpu.make_async_copy(slots.at[slot], target.at[where, :], sems.at[index, slot])

    def put_out(tile, target, slots, sems, index, values):
        @pl.when(tile >= 2)
        def _():
            out_copy(tile - 2, target, slots, sems, index).wait()

        slots[lax.rem(tile, 2)] = values
        out_copy(tile, target, slots, sems, index).start()

    def end_out(target, slots, sems, index):
        for tile in range(tiles - 2, tiles):
            out_copy(tile, target, slots, sems, index).wait()

    for matrix in range(7):
        for row in range(share):
            s.pack[matrix * share + row : matrix * share + row + 1, :] = s.square_weight[
                matrix : matrix + 1, row * width : (row + 1) * width
            ]
    for matrix in range(2):
        for half in range(2):
            for row in range(share):
                place = (7 + 2 * matrix + half) * share + row
                start = row * F + half * width
                s.pack[place : place + 1, :] = s.expand_weight[
                    matrix : matrix + 1, start : start + width
                ]
        for row in range(2 * share):
            place = (11 + 2 * matrix) * share + row
            s.pack[place : place + 1, :] = s.contract_weight[
                matrix : matrix + 1, row * width : (row + 1) * width
            ]
    s.pack[15 * share : 16 * share, :LANES] = s.fourier_weight[...]
    s.pack[15 * share : 16 * share, LANES:] = jnp.zeros((share, LANES), f32)
    live = s.point_mask[...].astype(f32)
    counts = dot_bt(jnp.ones((8, LANES), jnp.bfloat16), low(live))
    s.pack[15 * share : 15 * share + 1, LANES : LANES + blocks] = counts[:1]
    lane = lax.broadcasted_iota(jnp.int32, (1, LANES), 1)
    wide_block = lax.broadcasted_iota(jnp.int32, (1, E * blocks), 1) // E
    item_row = jnp.zeros((1, LANES), f32)
    item_wide = jnp.zeros((1, E * blocks), jnp.int32)
    for block in range(blocks):
        item_row = jnp.where(lane == block, s.items[block].astype(f32), item_row)
        item_wide = jnp.where(wide_block == block, s.items[block], item_wide)
    s.pack[15 * share + 1 : 15 * share + 2, LANES:] = item_row
    packed = low(s.pack[...])
    split = s.gather_one.shape[3]
    s.gather_one[at.core, at.pair, at.outer] = packed[:split]
    s.gather_two[at.core, at.pair, at.outer] = packed[split:]

    pl.semaphore_wait(barrier, GROUP - 1 + at.outers - 1)
    one = Gather(at, s.gather_one, (s.sem_g1s, s.sem_g1r))
    two = Gather(at, s.gather_two, (s.sem_g2s, s.sem_g2r))
    one.start_first()
    two.start_first()

    row_at = lax.broadcasted_iota(jnp.int32, (width, width), 0)
    lane_at = lax.broadcasted_iota(jnp.int32, (width, width), 1)
    s.eye[...] = jnp.where(row_at == lane_at, 1.0, 0.0).astype(jnp.bfloat16)
    s.heads[...] = jnp.where(row_at // E == lane_at // E, 1.0, 0.0).astype(jnp.bfloat16)
    s.small[...] = jnp.zeros(s.small.shape, f32)
    s.small[0:8, :] = s.vector_weight[...]
    for row in range(2):
        for half in range(2):
            s.small[8 + 2 * row + half : 9 + 2 * row + half, :] = s.hidden_weight[
                row : row + 1, half * width : (half + 1) * width
            ]
    s.small[12:14, : FOUR // 2] = s.fourier_basis[...]
    s.cols[...] = s.small[...].T
    rows_wide = lax.broadcasted_iota(jnp.int32, s.spread.shape, 0)
    lanes_wide = lax.broadcasted_iota(jnp.int32, s.spread.shape, 1)
    s.spread[...] = jnp.where(
        (item_wide == rows_wide // E) & (rows_wide % E == lanes_wide % E), 1.0, 0.0
    ).astype(jnp.bfloat16)
    s.vector_sum[...] = jnp.zeros(s.vector_sum.shape, f32)
    for grad in (s.grad_qkv, s.grad_o, s.grad_kv, s.grad_do, s.grad_w1, s.grad_p1, s.grad_w2, s.grad_p2, s.grad_dq):
        grad[...] = jnp.zeros(grad.shape, f32)
    speed = (lax.broadcasted_iota(jnp.int32, (E // 4, 1), 0).astype(f32) + 1.0) * (
        math.pi / (E // 4)
    )

    def add_sum(index, values):
        for part in range(values.shape[0] // width):
            s.vector_sum[index + part] += lane_sum(values[part * width : (part + 1) * width])

    def features_turned(tile):
        return dot_bt(s.eye[...], s.features[columns(tile), :])

    def before(tile, _):
        where = columns(tile)
        scaled, root = column_norm(features_turned(tile))
        s.root_one[0:1, where] = root
        s.u1[:, where] = low(scaled * column(0) + column(1))
        x_row, y_row = s.coords[0:1, where], s.coords[1:2, where]
        angles = jnp.concatenate([speed * x_row, speed * y_row], axis=0)
        s.cosine[:, where] = jnp.cos(angles)
        s.sine[:, where] = jnp.sin(angles)
        basis = s.cols[: FOUR // 2, :]
        phases = 2.0 * math.pi * (basis[:, 12:13] * x_row + basis[:, 13:14] * y_row)
        s.phi[:, where] = low(jnp.concatenate([jnp.cos(phases), jnp.sin(phases)], axis=0))
        for block in range(tile_blocks):
            s.mask[0:1, pl.ds(pl.multiple_of(tile * TILE + block * BLOCK, BLOCK), BLOCK)] = (
                s.point_mask[pl.ds(tile * tile_blocks + block, 1), :].astype(f32)
            )

    lax.fori_loop(0, tiles // 4, before, None)
    one.start_second()
    lax.fori_loop(tiles // 4, tiles // 2, before, None)
    one.start_third()
    two.start_second()
    lax.fori_loop(tiles // 2, tiles, before, None)
    one.finish()

    group = 16 // share

    def chunk_pair(buffer, index):
        parts = []
        for step in range(group):
            chunk = index * group + step
            inner = lax.rem(chunk, GROUP)
            parts.append(
                buffer[lax.rem(inner, 2), lax.div(inner, 2), lax.div(chunk, GROUP)].astype(f32)
            )
        return parts

    def join(parts, piece):
        return low(
            jnp.concatenate([part[piece * share : (piece + 1) * share] for part in parts], axis=0)
        )

    @pl.loop(0, devices // group)
    def _(index):
        parts = chunk_pair(s.gather_one, index)
        where = pl.ds(pl.multiple_of(index * 16, 16), 16)
        for piece in range(3):
            s.w_qkv[where, piece * width : (piece + 1) * width] = join(parts, piece)
        s.w_o[where, :] = join(parts, 3)

    def flip(matrix):
        return low(dot_bt(s.eye[...], matrix))

    for piece in range(3):
        s.t_qkv[piece * width : (piece + 1) * width, :] = flip(
            s.w_qkv[:, piece * width : (piece + 1) * width]
        )
    s.t_o[...] = flip(s.w_o[...])

    def block_product(left, right):
        return compress(dot_bt(left, right))

    def put_products(tile, left, right):
        for block in range(tile_blocks):
            lanes = slice(block * BLOCK, (block + 1) * BLOCK)
            where = pl.ds(pl.multiple_of((tile * tile_blocks + block) * E, E), E)
            s.per_block[where, :] = block_product(left[:, lanes], right[:, lanes])

    def summary(table, tile, block):
        item = s.items[tile * tile_blocks + block]
        first = item * 2
        inner, outer = lax.rem(first, GROUP), lax.div(first, GROUP)
        rows = jnp.concatenate([table[inner, outer], table[inner + 1, outer]], axis=0)
        return jnp.concatenate([rows] * H, axis=0) * s.heads[...]

    def per_block(tile, function):
        return jnp.concatenate([function(block) for block in range(tile_blocks)], axis=1)

    def lanes_of(block):
        return slice(block * BLOCK, (block + 1) * BLOCK)

    def phase_a(tile, _):
        where = columns(tile)
        projected = dot(s.t_qkv[...], s.u1[:, where])
        cosine, sine = s.cosine[:, where], s.sine[:, where]
        s.q[:, where] = low(turn(projected[:width], cosine, sine, 1.0))
        keys = low(turn(projected[width : 2 * width], cosine, sine, 1.0) * s.mask[0:1, where])
        values = low(projected[2 * width :])
        s.k[:, where] = keys
        s.v[:, where] = values
        put_products(tile, values, keys)

    lax.fori_loop(0, tiles // 2, phase_a, None)
    two.start_third()
    lax.fori_loop(tiles // 2, tiles, phase_a, None)
    two.finish()

    def take_two(index, carried):
        parts = chunk_pair(s.gather_two, index)
        where = pl.ds(pl.multiple_of(index * 16, 16), 16)
        for piece in range(2):
            s.w_kv[where, piece * width : (piece + 1) * width] = join(parts, piece)
            s.w_w1[where, piece * width : (piece + 1) * width] = join(parts, 3 + piece)
            s.w_p1[where, piece * width : (piece + 1) * width] = join(parts, 5 + piece)
        s.w_do[where, :] = join(parts, 2)
        both = pl.ds(pl.multiple_of(index * 32, 32), 32)
        for piece, target in ((7, s.w_w2), (9, s.w_p2)):
            target[both, :] = low(
                jnp.concatenate([part[piece * share : (piece + 2) * share] for part in parts], axis=0)
            )
        found = []
        for outer in range(at.outers):
            mine = lax.div(outer * GROUP + at.inner, 2).astype(f32)
            total = carried[outer]
            for part in parts:
                count_row = part[11 * share : 11 * share + 1, LANES:]
                item_at = part[11 * share + 1 : 11 * share + 2, LANES:]
                total = total + jnp.where(item_at == mine, count_row, 0.0)
            found.append(total)
        s.fourier[where, :] = jnp.concatenate(
            [part[11 * share : 12 * share, :LANES] for part in parts], axis=0
        )
        return tuple(found)

    table_sum = TableSum(at, s)
    table_sum.start()
    found = lax.fori_loop(
        0, devices // group, take_two, tuple(jnp.zeros((1, LANES), f32) for _ in range(at.outers))
    )
    for outer in range(at.outers):
        s.inverse[outer : outer + 1, :] = jnp.broadcast_to(
            1.0 / jnp.sum(found[outer], axis=1, keepdims=True), (1, width)
        )
    w_dq = jnp.concatenate(
        [s.fourier[pl.ds(0, FOUR, stride=2), :], s.fourier[pl.ds(1, FOUR, stride=2), :]], axis=1
    )
    table_sum.middle()
    s.t_dq[...] = low(w_dq.T)
    for piece in range(2):
        cols = slice(piece * width, (piece + 1) * width)
        s.t_kv[cols, :] = flip(s.w_kv[:, cols])
        s.t_w1[cols, :] = flip(s.w_w1[:, cols])
        s.t_p1[cols, :] = flip(s.w_p1[:, cols])
        s.t_w2[:, cols] = flip(s.w_w2[cols, :])
        s.t_p2[:, cols] = flip(s.w_p2[cols, :])
    s.t_do[...] = flip(s.w_do[...])
    table_sum.late(s.table_self)

    def cross_queries(tile, _):
        where = columns(tile)
        s.qd[:, where] = low(dot(s.t_dq[...], s.phi[:, where]))

    lax.fori_loop(0, tiles, cross_queries, None)
    table_sum.finish(s.table_self)

    def phase_b(tile, _):
        where = columns(tile)
        mask = s.mask[0:1, where]
        queries = s.q[:, where]
        mixed = per_block(
            tile, lambda b: dot(summary(s.table_self, tile, b), queries[:, lanes_of(b)])
        )
        attended = low(mixed * mask)
        s.o[:, where] = attended
        first_sum = features_turned(tile) + dot(s.t_o[...], attended)
        scaled_two, root_two = column_norm(first_sum)
        s.root_two[0:1, where] = root_two
        s.xh2[:, where] = low(scaled_two)
        middle = low(scaled_two * column(2) + column(3))
        s.u2[:, where] = middle
        hidden, slope = gelu_both(dot(s.t_w1[...], middle) + hidden_column(0))
        hidden = low(hidden)
        s.e1[:, where] = hidden
        s.slope[:, where] = low(slope)
        encoded = first_sum + dot(s.t_w2[...], hidden) + column(6)
        scaled_three, root_three = column_norm(encoded)
        s.root_three[0:1, where] = root_three
        s.xh3[:, where] = low(scaled_three)
        outer = low(scaled_three * column(4) + column(5))
        s.u3[:, where] = outer
        pair = dot(s.t_kv[...], outer)
        keys = low(pair[:width] * mask)
        values = low(pair[width:])
        s.kd[:, where] = keys
        s.vd[:, where] = values
        put_products(tile, values, keys)

    lax.fori_loop(0, tiles, phase_b, None)
    table_sum.start()
    table_sum.middle()
    table_sum.late(s.table_other)
    table_sum.finish(s.table_other)

    def phase_c(tile, _):
        where = columns(tile)
        mask = s.mask[0:1, where]
        queries = s.qd[:, where]
        tables = [summary(s.table_other, tile, block) for block in range(tile_blocks)]
        decoded = low(
            per_block(tile, lambda b: dot(tables[b], queries[:, lanes_of(b)])) * mask
        )
        latent = dot(s.t_do[...], decoded)
        latent_low = low(latent)
        hidden, slope = gelu_both(dot(s.t_p1[...], latent_low) + hidden_column(1))
        hidden = low(hidden)
        output = latent + dot(s.t_p2[...], hidden) + column(7)
        put_out(tile, s.layer_output, s.output_slots, s.sem_out, 0, low(output).T)
        upstream = s.cotangent[where, :]
        turned = dot_bt(s.eye[...], upstream)
        add_sum(7, turned)
        grad_spread = dot_bt(s.w_p2[...], upstream) * slope
        add_sum(10, grad_spread)
        grad_spread = low(grad_spread)
        grad_latent = low(turned + dot(s.w_p1[...], grad_spread))
        grad_decoded = low(dot(s.w_do[...], grad_latent) * mask)
        grad_queries = low(
            per_block(tile, lambda b: dot_at(tables[b], grad_decoded[:, lanes_of(b)]))
        )
        put_products(tile, grad_decoded, queries)
        s.grad_p2[...] += dot(hidden, upstream)
        s.grad_p1[...] += dot_bt(latent_low, grad_spread)
        s.grad_do[...] += dot_bt(decoded, grad_latent)
        s.grad_dq[...] += dot_bt(s.phi[:, where], grad_queries)

    lax.fori_loop(0, tiles, phase_c, None)
    table_sum.start()
    end_out(s.layer_output, s.output_slots, s.sem_out, 0)
    s.fourier[pl.ds(0, FOUR, stride=2), :] = s.grad_dq[:, :LANES]
    s.fourier[pl.ds(1, FOUR, stride=2), :] = s.grad_dq[:, LANES:]
    zeros = jnp.zeros((share, LANES), f32)

    def rows_of(chunk, count=1):
        size = share * count
        return pl.ds(pl.multiple_of(chunk * size, size), size)

    def chunk_c(chunk):
        where = rows_of(chunk)
        return jnp.concatenate(
            [
                s.grad_do[where, :],
                s.grad_p1[where, :width],
                s.grad_p1[where, width:],
                s.grad_p2[rows_of(chunk, 2), :],
                jnp.concatenate([s.fourier[where, :], zeros], axis=1),
            ],
            axis=0,
        )

    sum_c = GradSum(at, s, "c", 0)
    sum_c.start(chunk_c)
    table_sum.middle()
    sum_c.second()
    table_sum.late(s.table_other)
    table_sum.finish(s.table_other)

    def phase_d(tile, _):
        where = columns(tile)
        mask = s.mask[0:1, where]
        keys, values = s.kd[:, where], s.vd[:, where]
        tables = [summary(s.table_other, tile, block) for block in range(tile_blocks)]
        grad_keys = per_block(tile, lambda b: dot_at(tables[b], values[:, lanes_of(b)])) * mask
        grad_values = per_block(tile, lambda b: dot(tables[b], keys[:, lanes_of(b)]))
        grad_pair = low(jnp.concatenate([grad_keys, grad_values], axis=0))
        s.grad_kv[...] += dot_bt(s.u3[:, where], grad_pair)
        grad_outer = dot(s.w_kv[...], grad_pair)
        scaled = s.xh3[:, where].astype(f32)
        add_sum(4, grad_outer * scaled)
        add_sum(5, grad_outer)
        grad_encoded = column_norm_back(
            grad_outer, scaled, s.root_three[0:1, where], column(4)
        )
        add_sum(6, grad_encoded)
        grad_encoded_low = low(grad_encoded)
        s.grad_w2[...] += dot_bt(s.e1[:, where], grad_encoded_low)
        grad_hidden = dot(s.w_w2[...], grad_encoded_low) * s.slope[:, where].astype(f32)
        add_sum(8, grad_hidden)
        grad_hidden = low(grad_hidden)
        s.grad_w1[...] += dot_bt(s.u2[:, where], grad_hidden)
        grad_middle = dot(s.w_w1[...], grad_hidden)
        scaled = s.xh2[:, where].astype(f32)
        add_sum(2, grad_middle * scaled)
        add_sum(3, grad_middle)
        grad_first = grad_encoded + column_norm_back(
            grad_middle, scaled, s.root_two[0:1, where], column(2)
        )
        grad_first = low(grad_first)
        s.xh2[:, where] = grad_first
        s.grad_o[...] += dot_bt(s.o[:, where], grad_first)
        grad_attended = low(dot(s.w_o[...], grad_first) * mask)
        s.kd[:, where] = grad_attended
        put_products(tile, grad_attended, s.q[:, where])

    lax.fori_loop(0, tiles // 2, phase_d, None)
    sum_c.third()
    lax.fori_loop(tiles // 2, tiles, phase_d, None)
    table_sum.start()
    s.grads_c[...] = sum_c.finish()

    def chunk_d(chunk):
        where = rows_of(chunk)
        return jnp.concatenate(
            [
                s.grad_kv[where, :width],
                s.grad_kv[where, width:],
                s.grad_o[where, :],
                s.grad_w1[where, :width],
                s.grad_w1[where, width:],
                s.grad_w2[rows_of(chunk, 2), :],
                jnp.zeros((share, width), f32),
            ],
            axis=0,
        )

    sum_d = GradSum(at, s, "d", 0)
    sum_d.start(chunk_d)
    table_sum.middle()

    def query_grads(tile, _):
        where = columns(tile)
        upstream = s.kd[:, where]
        grad = per_block(
            tile, lambda b: dot_at(summary(s.table_self, tile, b), upstream[:, lanes_of(b)])
        )
        grad = low(turn(grad, s.cosine[:, where], s.sine[:, where], -1.0))
        s.q[:, where] = grad
        s.grad_qkv[:, :width] += dot_bt(s.u1[:, where], grad)

    lax.fori_loop(0, tiles // 2, query_grads, None)
    sum_d.second()
    table_sum.late(s.table_other)
    lax.fori_loop(tiles // 2, tiles, query_grads, None)
    table_sum.finish(s.table_other)

    def phase_e(tile, _):
        where = columns(tile)
        mask = s.mask[0:1, where]
        keys, values = s.k[:, where], s.v[:, where]
        tables = [summary(s.table_other, tile, block) for block in range(tile_blocks)]
        grad_keys = per_block(tile, lambda b: dot_at(tables[b], values[:, lanes_of(b)])) * mask
        grad_values = low(per_block(tile, lambda b: dot(tables[b], keys[:, lanes_of(b)])))
        grad_keys = low(turn(grad_keys, s.cosine[:, where], s.sine[:, where], -1.0))
        pair = jnp.concatenate([grad_keys, grad_values], axis=0)
        s.grad_qkv[:, width:] += dot_bt(s.u1[:, where], pair)
        grad_normed = dot(s.w_qkv[...], jnp.concatenate([s.q[:, where], pair], axis=0))
        turned = features_turned(tile)
        root = s.root_one[0:1, where]
        scaled = (turned - jnp.sum(turned, axis=0, keepdims=True) * (1.0 / width)) * root
        add_sum(0, grad_normed * scaled)
        add_sum(1, grad_normed)
        grad_input = s.xh2[:, where].astype(f32) + column_norm_back(
            grad_normed, scaled, root, column(0)
        )
        put_out(tile, s.input_grad, s.input_slots, s.sem_out, 1, grad_input.T)

    lax.fori_loop(0, tiles // 2, phase_e, None)
    sum_d.third()
    lax.fori_loop(tiles // 2, tiles, phase_e, None)

    lane_wide = lax.broadcasted_iota(jnp.int32, (width, LANES), 1)
    sums = jnp.zeros((width, LANES), f32)
    for index in range(12):
        sums = jnp.where(
            lane_wide == index, jnp.sum(s.vector_sum[index], axis=1, keepdims=True), sums
        )
    s.vector_cols[...] = sums

    def chunk_e(chunk):
        where = rows_of(chunk)
        return jnp.concatenate(
            [
                s.grad_qkv[where, :width],
                s.grad_qkv[where, width : 2 * width],
                s.grad_qkv[where, 2 * width :],
                jnp.concatenate([s.vector_cols[where, :], zeros], axis=1),
            ],
            axis=0,
        )

    sum_e = GradSum(at, s, "e", 8 * share)
    sum_e.start(chunk_e)
    s.grads_d[...] = sum_d.finish()
    end_out(s.input_grad, s.input_slots, s.sem_out, 1)
    sum_e.second()
    early = jnp.sum(s.grads_c[...] * s.grads_c[...], axis=0, keepdims=True) + jnp.sum(
        s.grads_d[...] * s.grads_d[...], axis=0, keepdims=True
    )
    sum_e.third()
    grads_e = sum_e.finish()
    s.grads_e[...] = grads_e
    squares = jnp.sum(early + jnp.sum(grads_e * grads_e, axis=0, keepdims=True), axis=1, keepdims=True)
    vector_rows = grads_e[3 * share : 4 * share, :LANES]
    row_small = lax.broadcasted_iota(jnp.int32, (share, LANES), 0)
    lane_small = lax.broadcasted_iota(jnp.int32, (share, LANES), 1)
    s.final[at.inner, at.outer] = jnp.where(
        (row_small == 0) & (lane_small == 12), squares, vector_rows
    )

    def final_along(step, start):
        source = at.outer if start else at.outer_at(step)
        return remote(
            s.final.at[at.inner, at.outer], s.final.at[at.inner, source], s.sem_fs.at[0, step],
            s.sem_fr.at[0, source], at.device(at.outer_at(step), at.inner),
        )

    def final_inner(step, start):
        source = at.inner if start else at.inner_at(step)
        return remote(
            s.final.at[at.inner], s.final.at[source], s.sem_fs.at[1, step],
            s.sem_fr.at[1, source], at.device(at.outer, at.inner_at(step)),
        )

    for step in range(1, at.outers):
        final_along(step, True).start()
    for step in range(1, at.outers):
        final_along(step, False).wait()
    for step in range(1, GROUP):
        final_inner(step, True).start()
    for step in range(1, GROUP):
        final_inner(step, False).wait()

    @pl.loop(0, devices)
    def _(chunk):
        s.vector_all[rows_of(chunk), :] = s.final[lax.rem(chunk, GROUP), lax.div(chunk, GROUP)]


def update_kernel(share, *refs):
    sources, refs = refs[:2], refs[2:]
    grads_c, grads_d, grads_e, vector_all = refs[:4]
    weights = refs[4:22]
    targets = refs[22:24]
    norm_out = refs[24]
    results = refs[25:43]
    flat_square, flat_expand, flat_contract, *held, sems = refs[43:]
    loads, stores = [], []
    for index, (source, target) in enumerate(zip(sources, targets)):
        size = source.shape[0] // PIECES
        for piece in range(PIECES):
            where = slice(piece * size, (piece + 1) * size)
            own = held[index].at[where]
            loads.append(pltpu.make_async_copy(source.at[where], own, sems.at[0, index, piece]))
            stores.append(pltpu.make_async_copy(own, target.at[where], sems.at[1, index, piece]))
    for load in loads:
        load.start()
    width = grads_c.shape[1]
    places = [(grads_e, 0), (grads_e, 1), (grads_e, 2), (grads_d, 2), (grads_d, 0), (grads_d, 1), (grads_c, 0)]
    for matrix, (source, piece) in enumerate(places):
        for row in range(share):
            start = piece * share + row
            flat_square[matrix : matrix + 1, row * width : (row + 1) * width] = source[
                start : start + 1, :
            ]
    for matrix, (source, piece) in enumerate(((grads_d, 3), (grads_c, 1))):
        for half in range(2):
            for row in range(share):
                start = (piece + half) * share + row
                target = row * F + half * width
                flat_expand[matrix : matrix + 1, target : target + width] = source[
                    start : start + 1, :
                ]
    for matrix, (source, piece) in enumerate(((grads_d, 5), (grads_c, 3))):
        for row in range(2 * share):
            start = piece * share + row
            flat_contract[matrix : matrix + 1, row * width : (row + 1) * width] = source[
                start : start + 1, :
            ]
    for load, store in zip(loads, stores):
        load.wait()
        store.start()
    fourier = grads_c[5 * share : 6 * share, :LANES]
    turned = vector_all[...].T
    norm = jnp.sqrt(jnp.sum(turned[12:13, :], axis=1, keepdims=True))
    norm_out[...] = norm
    factor = jnp.minimum(1.0, CLIP_NORM / (norm + 1e-06))
    hidden = jnp.concatenate(
        [
            jnp.concatenate([turned[8:9], turned[9:10]], axis=1),
            jnp.concatenate([turned[10:11], turned[11:12]], axis=1),
        ],
        axis=0,
    )
    grads = (flat_square[...], flat_expand[...], flat_contract[...], fourier, turned[:8], hidden)
    rates = (RATE_MATRIX,) * 4 + (RATE_VECTOR,) * 2
    for index, (grad, rate) in enumerate(zip(grads, rates)):
        weight, first, second = (weights[3 * index + part][...] for part in range(3))
        values = adam_update(weight, first, second, grad, factor, rate)
        for part in range(3):
            results[3 * index + part][...] = values[part]
    for store in stores:
        store.wait()


def fused(devices, features, coords, fourier_basis, block_items, point_mask, cotangent, *weights):
    points, width = features.shape
    blocks = points // BLOCK
    outers = devices // GROUP
    share = width // devices
    items = points * devices // ITEM_PTS
    bf16, f32 = jnp.bfloat16, jnp.float32
    square, expand, contract, fourier, vector, hidden = (weights[3 * i] for i in range(6))
    vmem = lambda shape, dtype: pltpu.VMEM(shape, dtype)
    inputs = {
        "items": block_items,
        "features": features,
        "coords": coords,
        "fourier_basis": fourier_basis,
        "point_mask": point_mask.reshape(blocks, BLOCK),
        "cotangent": cotangent,
        "square_weight": square,
        "expand_weight": expand,
        "contract_weight": contract,
        "fourier_weight": fourier.reshape(share, LANES),
        "vector_weight": vector,
        "hidden_weight": hidden,
    }
    rows_c, rows_d, rows_e = 6 * share, 8 * share, 4 * share
    outputs = {
        "layer_output": ((points, width), bf16),
        "input_grad": ((points, width), f32),
        "grads_c": ((rows_c, width), f32),
        "grads_d": ((rows_d, width), f32),
        "grads_e": ((rows_e, width), f32),
        "vector_all": ((width, LANES), f32),
    }
    tall = lambda rows: vmem((rows, points), bf16)
    scratch = {
        "pack": vmem((16 * share, width), f32),
        "gather_one": vmem((2, 4, outers, 4 * share, width), bf16),
        "gather_two": vmem((2, 4, outers, 12 * share, width), bf16),
        "eye": vmem((width, width), bf16),
        "heads": vmem((width, width), bf16),
        "small": vmem((LANES, width), f32),
        "cols": vmem((width, LANES), f32),
        "spread": vmem((items * E, blocks * E), bf16),
        "vector_sum": vmem((12, width, LANES), f32),
        "vector_cols": vmem((width, LANES), f32),
        "grad_qkv": vmem((width, 3 * width), f32),
        "grad_o": vmem((width, width), f32),
        "grad_kv": vmem((width, 2 * width), f32),
        "grad_do": vmem((width, width), f32),
        "grad_w1": vmem((width, F), f32),
        "grad_p1": vmem((width, F), f32),
        "grad_w2": vmem((F, width), f32),
        "grad_p2": vmem((F, width), f32),
        "grad_dq": vmem((FOUR, width), f32),
        "fourier": vmem((2 * FOUR, LANES), f32),
        "w_qkv": vmem((width, 3 * width), bf16),
        "t_qkv": vmem((3 * width, width), bf16),
        "w_o": vmem((width, width), bf16),
        "t_o": vmem((width, width), bf16),
        "w_kv": vmem((width, 2 * width), bf16),
        "t_kv": vmem((2 * width, width), bf16),
        "w_do": vmem((width, width), bf16),
        "t_do": vmem((width, width), bf16),
        "w_w1": vmem((width, F), bf16),
        "t_w1": vmem((F, width), bf16),
        "w_p1": vmem((width, F), bf16),
        "t_p1": vmem((F, width), bf16),
        "w_w2": vmem((F, width), bf16),
        "t_w2": vmem((width, F), bf16),
        "w_p2": vmem((F, width), bf16),
        "t_p2": vmem((width, F), bf16),
        "t_dq": vmem((width, FOUR), bf16),
        "mask": vmem((1, points), f32),
        "root_one": vmem((1, points), f32),
        "root_two": vmem((1, points), f32),
        "root_three": vmem((1, points), f32),
        "cosine": vmem((E // 2, points), f32),
        "sine": vmem((E // 2, points), f32),
        "phi": tall(FOUR),
        "u1": tall(width),
        "q": tall(width),
        "k": tall(width),
        "v": tall(width),
        "qd": tall(width),
        "o": tall(width),
        "xh2": tall(width),
        "u2": tall(width),
        "e1": tall(F),
        "slope": tall(F),
        "xh3": tall(width),
        "u3": tall(width),
        "kd": tall(width),
        "vd": tall(width),
        "per_block": vmem((blocks * E, width), f32),
        "inverse": vmem((max(8, outers), width), f32),
        "table_send": vmem((GROUP, outers, 16, width), bf16),
        "table_recv": vmem((GROUP, outers, 16, width), bf16),
        "table_part": vmem((outers, 16, width), bf16),
        "table_cross": vmem((2, outers, outers, 16, width), bf16),
        "table_self": vmem((GROUP, outers, 16, width), bf16),
        "table_other": vmem((GROUP, outers, 16, width), bf16),
        "final": vmem((GROUP, outers, share, LANES), f32),
        "output_slots": vmem((2, TILE, width), bf16),
        "input_slots": vmem((2, TILE, width), f32),
        "sem_out": pltpu.SemaphoreType.DMA((2, 2)),
    }
    for key, rows in (("c", rows_c), ("d", rows_d), ("e", rows_e)):
        for part in ("half_", "quarter_"):
            scratch[part + key] = vmem((4, outers, rows, width), bf16)
        scratch["last_" + key] = vmem((outers, rows, width), bf16)
    many = max(GROUP, outers)
    for key in ("ts", "tr", "g1s", "g1r", "g2s", "g2r", "cs", "cr", "ds", "dr", "es", "er"):
        scratch["sem_" + key] = pltpu.SemaphoreType.DMA((4, many))
    for key in ("fs", "fr"):
        scratch["sem_" + key] = pltpu.SemaphoreType.DMA((2, many))
    names = list(inputs) + list(outputs) + list(scratch)
    in_specs = [pl.BlockSpec(memory_space=pltpu.SMEM)] + [
        pl.BlockSpec(memory_space=pltpu.VMEM) for _ in range(len(inputs) - 1)
    ]
    whole = pl.BlockSpec(memory_space=pltpu.VMEM)
    made = pl.pallas_call(
        functools.partial(layer_kernel, names, devices),
        out_shape=[jax.ShapeDtypeStruct(*shape) for shape in outputs.values()],
        in_specs=in_specs,
        out_specs=[pl.BlockSpec(memory_space=pl.ANY)] * 2 + [whole] * (len(outputs) - 2),
        scratch_shapes=list(scratch.values()),
        compiler_params=pltpu.CompilerParams(
            collective_id=0, has_side_effects=True, vmem_limit_bytes=VMEM_BYTES
        ),
    )(*inputs.values())
    flat = list(weights)
    for part in range(9, 12):
        flat[part] = flat[part].reshape(share, LANES)
    shapes = [jax.ShapeDtypeStruct((1, 1), f32)] + [
        jax.ShapeDtypeStruct(flat[index].shape, f32) for index in range(18)
    ]
    order = []
    for index in range(6):
        order += [shapes[1 + 3 * index]] * 3
    updated = pl.pallas_call(
        functools.partial(update_kernel, share),
        out_shape=[jax.ShapeDtypeStruct(*shape) for shape in list(outputs.values())[:2]]
        + [shapes[0]]
        + order,
        in_specs=[pl.BlockSpec(memory_space=pl.ANY)] * 2 + [whole] * 22,
        out_specs=[pl.BlockSpec(memory_space=pl.ANY)] * 2 + [whole] * 19,
        scratch_shapes=[
            vmem(square.shape, f32),
            vmem(expand.shape, f32),
            vmem(contract.shape, f32),
            vmem((points, width), bf16),
            vmem((points, width), f32),
            pltpu.SemaphoreType.DMA((2, 2, PIECES)),
        ],
        compiler_params=pltpu.CompilerParams(vmem_limit_bytes=VMEM_BYTES),
    )(*made, *flat)
    layer_output, input_grad, norm, *rest = updated
    for part in range(9, 12):
        rest[part] = rest[part].reshape(fourier.shape)
    return (layer_output, input_grad, norm.reshape(()), *rest)


def shards(features, *others):
    devices = lax.axis_size("pts")
    width = features.shape[1]
    if devices % GROUP == 0 and width % (8 * devices) == 0:
        return fused(devices, features, *others)
    return plain(features, *others)


def solution(mesh):
    in_specs = (
        P("pts", None),
        P(None, "pts"),
        P(),
        P("pts"),
        P("pts"),
        P("pts", None),
        P(None, "pts"),
        P(None, "pts"),
        P(None, "pts"),
        P(None, "pts"),
        P(None, "pts"),
        P(None, "pts"),
        P(None, "pts"),
        P(None, "pts"),
        P(None, "pts"),
        P("pts"),
        P("pts"),
        P("pts"),
        P(),
        P(),
        P(),
        P(),
        P(),
        P(),
    )
    out_specs = (
        P("pts", None),
        P("pts", None),
        P(),
        P(None, "pts"),
        P(None, "pts"),
        P(None, "pts"),
        P(None, "pts"),
        P(None, "pts"),
        P(None, "pts"),
        P(None, "pts"),
        P(None, "pts"),
        P(None, "pts"),
        P("pts"),
        P("pts"),
        P("pts"),
        P(),
        P(),
        P(),
        P(),
        P(),
        P(),
    )
    return jax.shard_map(shards, mesh=mesh, in_specs=in_specs, out_specs=out_specs, check_vma=False)
```

```python
import functools
import math
import types

import jax
import jax.numpy as jnp
from jax import lax
from jax.experimental import pallas as pl
from jax.experimental.pallas import tpu as pltpu
from jax.sharding import PartitionSpec as P

H = 8
E = 32
F = 512
FOUR = 128
BLOCK = 128
ITEM_PTS = 8192
STEP = 10


NORM_EPS = 1e-05
GELU_C = math.sqrt(2.0 / math.pi)
GELU_A = 0.044715
BETA_ONE = 0.9
BETA_TWO = 0.95
ADAM_EPS = 1e-08
WEIGHT_DECAY = 0.1
RATE_MATRIX = 0.05
RATE_VECTOR = 0.25
CLIP_NORM = 1.0
HIGHEST_PRECISION = lax.Precision.HIGHEST


def matmul(left, right):
    return jnp.dot(left, right, preferred_element_type=jnp.float32)


def matmul_left(left, right):
    return lax.dot_general(
        left, right, (((0,), (0,)), ((), ())), preferred_element_type=jnp.float32
    )


def matmul_right(left, right):
    return lax.dot_general(
        left, right, (((1,), (1,)), ((), ())), preferred_element_type=jnp.float32
    )


def gelu(values):
    return 0.5 * values * (1.0 + jnp.tanh(GELU_C * (values + GELU_A * values * values * values)))


def gelu_slope(values):
    tangent = jnp.tanh(GELU_C * (values + GELU_A * values * values * values))
    return 0.5 * (1.0 + tangent) + 0.5 * values * (1.0 - tangent * tangent) * GELU_C * (
        1.0 + 3.0 * GELU_A * values * values
    )


def norm_parts(values, norm_gain, norm_bias):
    centred = values - jnp.mean(values, axis=-1, keepdims=True)
    variance = jnp.mean(centred * centred, axis=-1, keepdims=True)
    root_inv = lax.rsqrt(variance + NORM_EPS)
    scaled = centred * root_inv
    return (scaled * norm_gain + norm_bias, scaled, root_inv)


def norm_back(upstream, scaled, root_inv, norm_gain):
    through = upstream * norm_gain
    centre = jnp.mean(through, axis=-1, keepdims=True)
    along = jnp.mean(through * scaled, axis=-1, keepdims=True)
    return root_inv * (through - centre - scaled * along)


def rotary_tables(coords):
    quarter = E // 4
    frequency = math.pi * (jnp.arange(quarter, dtype=jnp.float32) + 1.0) / quarter
    first_angle = coords[0][:, None] * frequency[None, :]
    second_angle = coords[1][:, None] * frequency[None, :]
    angles = jnp.concatenate([first_angle, first_angle, second_angle, second_angle], axis=1)
    return (jnp.cos(angles), jnp.sin(angles))


def rotate(values, cosine, sine):
    quarter = E // 4
    swapped = jnp.concatenate(
        [
            -values[..., quarter : 2 * quarter],
            values[..., :quarter],
            -values[..., 3 * quarter :],
            values[..., 2 * quarter : 3 * quarter],
        ],
        axis=-1,
    )
    return values * cosine[:, None, :] + swapped * sine[:, None, :]


def rotate_back(grads, cosine, sine):
    quarter = E // 4
    scaled = grads * sine[:, None, :]
    swapped = jnp.concatenate(
        [
            scaled[..., quarter : 2 * quarter],
            -scaled[..., :quarter],
            scaled[..., 3 * quarter :],
            -scaled[..., 2 * quarter : 3 * quarter],
        ],
        axis=-1,
    )
    return grads * cosine[:, None, :] + swapped


def fourier_features(coords, fourier_basis):
    phases = (
        2.0
        * math.pi
        * (
            coords[0][:, None] * fourier_basis[0][None, :]
            + coords[1][:, None] * fourier_basis[1][None, :]
        )
    )
    return jnp.concatenate([jnp.cos(phases), jnp.sin(phases)], axis=1)


def block_table(left, right, onehot):
    blocks = onehot.shape[0]
    per_block = jnp.einsum(
        "bphe,bphf->bhef",
        left.reshape(blocks, BLOCK, H, E),
        right.reshape(blocks, BLOCK, H, E),
        preferred_element_type=jnp.float32,
    )
    return jnp.einsum("ba,bhef->ahef", onehot, per_block, precision=HIGHEST_PRECISION)


def scale_round(table, inverse_count):
    return (table * inverse_count[:, None, None, None]).astype(jnp.bfloat16)


def spread(summary, onehot):
    selected = jnp.einsum(
        "ba,ahef->bhef", onehot.astype(jnp.bfloat16), summary, preferred_element_type=jnp.float32
    )
    return selected.astype(jnp.bfloat16)


def apply_summary(rows_low, block_summary, transposed):
    blocks = block_summary.shape[0]
    pattern = "bphf,bhef->bphe" if transposed else "bphe,bhef->bphf"
    mixed = jnp.einsum(
        pattern,
        rows_low.reshape(blocks, BLOCK, H, E),
        block_summary,
        preferred_element_type=jnp.float32,
    )
    return mixed.reshape(-1, H * E)


def galerkin_backward(
    grad_low, queries_low, keys_masked, values_low, block_summary, onehot, mask_float, reducer
):
    grad_masked = grad_low * mask_float.astype(jnp.bfloat16)
    grad_queries = apply_summary(grad_masked, block_summary, True)
    summary_grad = reducer(block_table(queries_low, grad_masked, onehot))
    block_grad = spread(summary_grad, onehot)
    grad_keys = apply_summary(values_low, block_grad, True) * mask_float
    grad_values = apply_summary(keys_masked, block_grad, False)
    return (grad_queries, grad_keys, grad_values)


def adam_update(weight, first, second, grad, factor, rate):
    clipped = grad * factor
    new_first = BETA_ONE * first + (1.0 - BETA_ONE) * clipped
    new_second = BETA_TWO * second + (1.0 - BETA_TWO) * clipped * clipped
    first_hat = new_first / (1.0 - BETA_ONE**STEP)
    second_hat = new_second / (1.0 - BETA_TWO**STEP)
    new_weight = weight - rate * (
        first_hat / (jnp.sqrt(second_hat) + ADAM_EPS) + WEIGHT_DECAY * weight
    )
    return (new_first, new_second, new_weight)


def own_share(full, width, along, start_index):
    return lax.dynamic_slice_in_dim(full, start_index * width, width, along)


def plain(
    features,
    coords,
    fourier_basis,
    block_items,
    point_mask,
    cotangent,
    square_weight,
    square_first,
    square_second,
    expand_weight,
    expand_first,
    expand_second,
    contract_weight,
    contract_first,
    contract_second,
    fourier_weight,
    fourier_first,
    fourier_second,
    vector_weight,
    vector_first,
    vector_second,
    hidden_weight,
    hidden_first,
    hidden_second,
):
    rows = features.shape[0]
    width = features.shape[1]
    blocks = rows // BLOCK
    devices = lax.axis_size("pts")
    items_total = rows * devices // ITEM_PTS
    gathered = (
        lax.all_gather(square_weight.astype(jnp.bfloat16), "pts", axis=1, tiled=True),
        lax.all_gather(expand_weight.astype(jnp.bfloat16), "pts", axis=1, tiled=True),
        lax.all_gather(contract_weight.astype(jnp.bfloat16), "pts", axis=1, tiled=True),
        lax.all_gather(fourier_weight.astype(jnp.bfloat16), "pts", axis=0, tiled=True),
    )
    square_full = gathered[0].reshape(7, width, width)
    expand_full = gathered[1].reshape(2, width, F)
    contract_full = gathered[2].reshape(2, F, width)
    fourier_full = gathered[3].reshape(FOUR, width)
    onehot = (block_items[:, None] == jnp.arange(items_total, dtype=jnp.int32)[None, :]).astype(
        jnp.float32
    )
    mask_float = point_mask.astype(jnp.float32)[:, None]
    mask_low = mask_float.astype(jnp.bfloat16)
    block_count = jnp.sum(mask_float.reshape(blocks, BLOCK), axis=1)
    local_count = jnp.dot(block_count, onehot, precision=HIGHEST_PRECISION)
    cosine, sine = rotary_tables(coords)
    phase_low = fourier_features(coords, fourier_basis).astype(jnp.bfloat16)
    inputs = features.astype(jnp.float32)
    normed, scaled_one, root_one = norm_parts(inputs, vector_weight[0], vector_weight[1])
    normed_low = normed.astype(jnp.bfloat16)
    joint_weight = jnp.concatenate([square_full[0], square_full[1], square_full[2]], axis=1)
    projected = matmul(normed_low, joint_weight)
    queries_low = (
        rotate(projected[:, :width].reshape(rows, H, E), cosine, sine)
        .reshape(rows, width)
        .astype(jnp.bfloat16)
    )
    keys_low = (
        rotate(projected[:, width : 2 * width].reshape(rows, H, E), cosine, sine)
        .reshape(rows, width)
        .astype(jnp.bfloat16)
    )
    keys_masked = keys_low * mask_low
    values_low = projected[:, 2 * width :].astype(jnp.bfloat16)
    self_local = block_table(keys_masked, values_low, onehot)
    self_table, item_count = lax.psum((self_local, local_count), "pts")
    inverse_count = 1.0 / item_count
    self_items = scale_round(self_table, inverse_count)
    self_summary = spread(self_items, onehot)
    attended_low = (apply_summary(queries_low, self_summary, False) * mask_float).astype(
        jnp.bfloat16
    )
    first_sum = inputs + matmul(attended_low, square_full[3])
    normed_mid, scaled_two, root_two = norm_parts(first_sum, vector_weight[2], vector_weight[3])
    middle_low = normed_mid.astype(jnp.bfloat16)
    hidden_pre = matmul(middle_low, expand_full[0]) + hidden_weight[0]
    hidden_low = gelu(hidden_pre).astype(jnp.bfloat16)
    encoded = first_sum + matmul(hidden_low, contract_full[0]) + vector_weight[6]
    normed_out, scaled_three, root_three = norm_parts(encoded, vector_weight[4], vector_weight[5])
    outer_low = normed_out.astype(jnp.bfloat16)
    pair_weight = jnp.concatenate([square_full[4], square_full[5]], axis=1)
    cross_projected = matmul(outer_low, pair_weight)
    cross_keys = cross_projected[:, :width].astype(jnp.bfloat16) * mask_low
    cross_values = cross_projected[:, width:].astype(jnp.bfloat16)
    cross_queries = matmul(phase_low, fourier_full).astype(jnp.bfloat16)
    cross_local = block_table(cross_keys, cross_values, onehot)
    cross_items = scale_round(lax.psum(cross_local, "pts"), inverse_count)
    cross_summary = spread(cross_items, onehot)
    decoded_low = (apply_summary(cross_queries, cross_summary, False) * mask_float).astype(
        jnp.bfloat16
    )
    latent = matmul(decoded_low, square_full[6])
    latent_low = latent.astype(jnp.bfloat16)
    spread_pre = matmul(latent_low, expand_full[1]) + hidden_weight[1]
    spread_low = gelu(spread_pre).astype(jnp.bfloat16)
    output = latent + matmul(spread_low, contract_full[1]) + vector_weight[7]
    cross_reducer = lambda table_part: scale_round(lax.psum(table_part, "pts"), inverse_count)
    self_reducer = lambda table_part: scale_round(lax.psum(table_part, "pts"), inverse_count)
    grad_output = cotangent.astype(jnp.float32)
    grad_bias_end = jnp.sum(grad_output, axis=0)
    grad_contract_spread = matmul_left(spread_low, cotangent)
    grad_spread = matmul_right(cotangent, contract_full[1]) * gelu_slope(spread_pre)
    grad_hidden_spread = jnp.sum(grad_spread, axis=0)
    grad_spread_low = grad_spread.astype(jnp.bfloat16)
    grad_expand_spread = matmul_left(latent_low, grad_spread_low)
    grad_latent = (grad_output + matmul_right(grad_spread_low, expand_full[1])).astype(jnp.bfloat16)
    grad_out_cross = matmul_left(decoded_low, grad_latent)
    grad_decoded = matmul_right(grad_latent, square_full[6]).astype(jnp.bfloat16)
    cross_back = galerkin_backward(
        grad_decoded,
        cross_queries,
        cross_keys,
        cross_values,
        cross_summary,
        onehot,
        mask_float,
        cross_reducer,
    )
    grad_fourier_full = matmul_left(phase_low, cross_back[0].astype(jnp.bfloat16))
    grad_pair_low = jnp.concatenate([cross_back[1], cross_back[2]], axis=1).astype(jnp.bfloat16)
    grad_pair_full = matmul_left(outer_low, grad_pair_low)
    grad_normed_out = matmul_right(grad_pair_low, pair_weight)
    grad_gain_three = jnp.sum(grad_normed_out * scaled_three, axis=0)
    grad_bias_three = jnp.sum(grad_normed_out, axis=0)
    grad_encoded = norm_back(grad_normed_out, scaled_three, root_three, vector_weight[4])
    grad_bias_middle = jnp.sum(grad_encoded, axis=0)
    grad_encoded_low = grad_encoded.astype(jnp.bfloat16)
    grad_contract_enc = matmul_left(hidden_low, grad_encoded_low)
    grad_hidden = matmul_right(grad_encoded_low, contract_full[0]) * gelu_slope(hidden_pre)
    grad_hidden_enc = jnp.sum(grad_hidden, axis=0)
    grad_hidden_low = grad_hidden.astype(jnp.bfloat16)
    grad_expand_enc = matmul_left(middle_low, grad_hidden_low)
    grad_middle = matmul_right(grad_hidden_low, expand_full[0])
    grad_gain_two = jnp.sum(grad_middle * scaled_two, axis=0)
    grad_bias_two = jnp.sum(grad_middle, axis=0)
    grad_first = grad_encoded + norm_back(grad_middle, scaled_two, root_two, vector_weight[2])
    grad_first_low = grad_first.astype(jnp.bfloat16)
    grad_out_self = matmul_left(attended_low, grad_first_low)
    grad_attended = matmul_right(grad_first_low, square_full[3]).astype(jnp.bfloat16)
    self_back = galerkin_backward(
        grad_attended,
        queries_low,
        keys_masked,
        values_low,
        self_summary,
        onehot,
        mask_float,
        self_reducer,
    )
    grad_queries = rotate_back(self_back[0].reshape(rows, H, E), cosine, sine).reshape(rows, width)
    grad_keys = rotate_back(self_back[1].reshape(rows, H, E), cosine, sine).reshape(rows, width)
    grad_joint_low = jnp.concatenate([grad_queries, grad_keys, self_back[2]], axis=1).astype(
        jnp.bfloat16
    )
    grad_joint_full = matmul_left(normed_low, grad_joint_low)
    grad_normed = matmul_right(grad_joint_low, joint_weight)
    grad_gain_one = jnp.sum(grad_normed * scaled_one, axis=0)
    grad_bias_one = jnp.sum(grad_normed, axis=0)
    grad_inputs = grad_first + norm_back(grad_normed, scaled_one, root_one, vector_weight[0])
    grad_square = jnp.stack(
        [
            grad_joint_full[:, :width],
            grad_joint_full[:, width : 2 * width],
            grad_joint_full[:, 2 * width :],
            grad_out_self,
            grad_pair_full[:, :width],
            grad_pair_full[:, width:],
            grad_out_cross,
        ]
    ).reshape(7, width * width)
    grad_expand = jnp.stack([grad_expand_enc, grad_expand_spread]).reshape(2, width * F)
    grad_contract = jnp.stack([grad_contract_enc, grad_contract_spread]).reshape(2, F * width)
    grad_fourier = grad_fourier_full.reshape(FOUR * width)
    grad_vector = jnp.stack(
        [
            grad_gain_one,
            grad_bias_one,
            grad_gain_two,
            grad_bias_two,
            grad_gain_three,
            grad_bias_three,
            grad_bias_middle,
            grad_bias_end,
        ]
    )
    grad_hidden_rows = jnp.stack([grad_hidden_enc, grad_hidden_spread])
    totals = lax.psum(
        (grad_square, grad_expand, grad_contract, grad_fourier, grad_vector, grad_hidden_rows),
        "pts",
    )
    squares = sum((jnp.sum(total_part * total_part) for total_part in totals))
    start_index = lax.axis_index("pts")
    share_square = own_share(totals[0], square_weight.shape[1], 1, start_index)
    share_expand = own_share(totals[1], expand_weight.shape[1], 1, start_index)
    share_contract = own_share(totals[2], contract_weight.shape[1], 1, start_index)
    share_fourier = own_share(totals[3], fourier_weight.shape[0], 0, start_index)
    vector_total = totals[4]
    hidden_total = totals[5]
    grad_norm = jnp.sqrt(squares)
    factor = jnp.minimum(1.0, CLIP_NORM / (grad_norm + 1e-06))
    new_square = adam_update(
        square_weight, square_first, square_second, share_square, factor, RATE_MATRIX
    )
    new_expand = adam_update(
        expand_weight, expand_first, expand_second, share_expand, factor, RATE_MATRIX
    )
    new_contract = adam_update(
        contract_weight, contract_first, contract_second, share_contract, factor, RATE_MATRIX
    )
    new_fourier = adam_update(
        fourier_weight, fourier_first, fourier_second, share_fourier, factor, RATE_MATRIX
    )
    new_vector = adam_update(
        vector_weight, vector_first, vector_second, vector_total, factor, RATE_VECTOR
    )
    new_hidden = adam_update(
        hidden_weight, hidden_first, hidden_second, hidden_total, factor, RATE_VECTOR
    )
    return (
        output.astype(jnp.bfloat16),
        grad_inputs,
        grad_norm,
        new_square[0],
        new_square[1],
        new_square[2],
        new_expand[0],
        new_expand[1],
        new_expand[2],
        new_contract[0],
        new_contract[1],
        new_contract[2],
        new_fourier[0],
        new_fourier[1],
        new_fourier[2],
        new_vector[0],
        new_vector[1],
        new_vector[2],
        new_hidden[0],
        new_hidden[1],
        new_hidden[2],
    )


GROUP = 8
TILE = 512
LANES = 128
PIECES = 8
VMEM_BYTES = 64 * 1024 * 1024


def dot(left, right):
    return jnp.dot(left, right, preferred_element_type=jnp.float32)


def dot_bt(left, right):
    return lax.dot_general(
        left, right, (((1,), (1,)), ((), ())), preferred_element_type=jnp.float32
    )


def dot_at(left, right):
    return lax.dot_general(
        left, right, (((0,), (0,)), ((), ())), preferred_element_type=jnp.float32
    )


def low(values):
    return values.astype(jnp.bfloat16)


def column_norm(values):
    inverse = 1.0 / values.shape[0]
    centred = values - jnp.sum(values, axis=0, keepdims=True) * inverse
    variance = jnp.sum(centred * centred, axis=0, keepdims=True) * inverse
    root_inv = lax.rsqrt(variance + NORM_EPS)
    return (centred * root_inv, root_inv)


def column_norm_back(upstream, scaled, root_inv, gain):
    inverse = 1.0 / upstream.shape[0]
    through = upstream * gain
    centre = jnp.sum(through, axis=0, keepdims=True) * inverse
    along = jnp.sum(through * scaled, axis=0, keepdims=True) * inverse
    return root_inv * (through - centre - scaled * along)


def gelu_both(values):
    square = values * values
    half = 0.5 + 0.5 * jnp.tanh(values * (GELU_C + (GELU_C * GELU_A) * square))
    slope = half + values * (half * (1.0 - half)) * (
        2.0 * GELU_C + (6.0 * GELU_C * GELU_A) * square
    )
    return (values * half, slope)


def turn(values, cosine, sine, sign):
    quarter = E // 4
    first_cos, second_cos = cosine[:quarter], cosine[quarter:]
    first_sin, second_sin = sine[:quarter] * sign, sine[quarter:] * sign
    parts = []
    for base in range(0, values.shape[0], E):
        one, two, three, four = (
            values[base + quarter * step : base + quarter * (step + 1)] for step in range(4)
        )
        parts += [
            one * first_cos - two * first_sin,
            two * first_cos + one * first_sin,
            three * second_cos - four * second_sin,
            four * second_cos + three * second_sin,
        ]
    return jnp.concatenate(parts, axis=0)


def compress(full):
    width = full.shape[1]
    head = lax.broadcasted_iota(jnp.int32, (E, width), 1) // E
    result = full[:E]
    for index in range(1, H):
        result = jnp.where(head == index, full[E * index : E * (index + 1)], result)
    return result


def lane_sum(values):
    result = values[:, :LANES]
    for start in range(LANES, values.shape[1], LANES):
        result = result + values[:, start : start + LANES]
    return result


def remote(source, target, send_sem, recv_sem, device):
    return pltpu.make_async_remote_copy(
        src_ref=source,
        dst_ref=target,
        send_sem=send_sem,
        recv_sem=recv_sem,
        device_id=(device,),
        device_id_type=pl.DeviceIdType.MESH,
    )


class Place:
    def __init__(self, devices):
        self.devices = devices
        self.outers = devices // GROUP
        self.me = lax.axis_index("pts")
        self.inner = lax.rem(self.me, GROUP)
        self.outer = lax.div(self.me, GROUP)
        self.core = lax.rem(self.me, 2)
        self.pair = lax.div(self.inner, 2)

    def inner_at(self, step):
        return lax.rem(self.inner + step, GROUP)

    def outer_at(self, step):
        return lax.rem(self.outer + step, self.outers)

    def pair_at(self, step):
        return lax.rem(self.pair + step, 4)

    def device(self, outer, inner):
        return outer * GROUP + inner


class Gather:
    def __init__(self, place, buffer, sems):
        self.place, self.buffer = place, buffer
        self.send, self.recv = sems

    def first(self, step, start):
        at = self.place
        slot = self.buffer.at[at.core, at.pair, at.outer if start else at.outer_at(step)]
        mine = self.buffer.at[at.core, at.pair, at.outer]
        source = at.outer if start else at.outer_at(step)
        return remote(
            mine, slot, self.send.at[0, step], self.recv.at[0, source],
            at.device(at.outer_at(step), at.inner),
        )

    def second(self, step, start):
        at = self.place
        source = at.pair if start else at.pair_at(step)
        return remote(
            self.buffer.at[at.core, at.pair], self.buffer.at[at.core, source],
            self.send.at[1, step], self.recv.at[1, source],
            at.device(at.outer, at.pair_at(step) * 2 + at.core),
        )

    def third(self, start):
        at = self.place
        source = at.core if start else 1 - at.core
        return remote(
            self.buffer.at[at.core], self.buffer.at[source], self.send.at[2, 0],
            self.recv.at[2, 0], at.device(at.outer, at.pair * 2 + 1 - at.core),
        )

    def start_first(self):
        for step in range(1, self.place.outers):
            self.first(step, True).start()

    def start_second(self):
        for step in range(1, self.place.outers):
            self.first(step, False).wait()
        for step in range(1, 4):
            self.second(step, True).start()

    def start_third(self):
        for step in range(1, 4):
            self.second(step, False).wait()
        self.third(True).start()

    def finish(self):
        self.third(False).wait()


class TableSum:
    def __init__(self, place, scratch):
        self.place, self.s, self.turn = place, scratch, 0

    def swap(self, step, start):
        at, s = self.place, self.s
        source = at.inner if start else at.inner_at(step)
        return remote(
            s.table_send.at[at.inner_at(step)], s.table_recv.at[source], s.sem_ts.at[0, step],
            s.sem_tr.at[0, source], at.device(at.outer, at.inner_at(step)),
        )

    def cross(self, step, start):
        at, s = self.place, self.s
        source = at.outer if start else at.outer_at(step)
        return remote(
            s.table_part, s.table_cross.at[self.turn, source], s.sem_ts.at[1 + self.turn, step],
            s.sem_tr.at[1 + self.turn, source],
            at.device(at.outer_at(step), at.inner),
        )

    def share(self, step, start, result):
        at, s = self.place, self.s
        source = at.inner if start else at.inner_at(step)
        return remote(
            result.at[at.inner], result.at[source], s.sem_ts.at[3, step], s.sem_tr.at[3, source],
            at.device(at.outer, at.inner_at(step)),
        )

    def start(self):
        at, s = self.place, self.s
        high = low(s.per_block[...])
        rest = low(s.per_block[...] - high.astype(jnp.float32))
        table = low(dot(s.spread[...], high) + dot(s.spread[...], rest))
        for chunk in range(at.devices):
            s.table_send[chunk % GROUP, chunk // GROUP] = table[chunk * 16 : (chunk + 1) * 16]
        for step in range(1, GROUP):
            self.swap(step, True).start()

    def middle(self):
        at, s = self.place, self.s
        total = s.table_send[at.inner].astype(jnp.float32)
        for step in range(1, GROUP):
            self.swap(step, False).wait()
            total = total + s.table_recv[at.inner_at(step)].astype(jnp.float32)
        s.table_part[...] = low(total)
        for step in range(1, at.outers):
            self.cross(step, True).start()

    def late(self, result):
        at, s = self.place, self.s
        total = s.table_part[...].astype(jnp.float32)
        for step in range(1, at.outers):
            self.cross(step, False).wait()
            total = total + s.table_cross[self.turn, at.outer_at(step)].astype(jnp.float32)
        for outer in range(at.outers):
            result[at.inner, outer] = low(total[outer] * s.inverse[outer : outer + 1, :])
        for step in range(1, GROUP):
            self.share(step, True, result).start()

    def finish(self, result):
        for step in range(1, GROUP):
            self.share(step, False, result).wait()
        self.turn = 1 - self.turn


class GradSum:
    def __init__(self, place, scratch, key, first):
        self.place = place
        self.half, self.quarter, self.last = (
            getattr(scratch, name + key) for name in ("half_", "quarter_", "last_")
        )
        self.full = scratch.gather_two.at[:, :, :, first : first + self.last.shape[1]]
        self.send, self.recv = getattr(scratch, f"sem_{key}s"), getattr(scratch, f"sem_{key}r")

    def swap(self):
        at = self.place
        return remote(
            self.full.at[1 - at.core], self.half, self.send.at[0, 0], self.recv.at[0, 0],
            at.device(at.outer, at.pair * 2 + 1 - at.core),
        )

    def across(self, step, start):
        at = self.place
        source = at.pair if start else at.pair_at(step)
        return remote(
            self.half.at[at.pair_at(step)], self.quarter.at[source], self.send.at[1, step],
            self.recv.at[1, source], at.device(at.outer, at.pair_at(step) * 2 + at.core),
        )

    def along(self, step, start):
        at = self.place
        source = at.outer if start else at.outer_at(step)
        return remote(
            self.quarter.at[at.pair, at.outer_at(step)], self.last.at[source], self.send.at[2, step],
            self.recv.at[2, source], at.device(at.outer_at(step), at.inner),
        )

    def start(self, chunk_of):
        at = self.place

        @pl.loop(0, at.devices)
        def _(chunk):
            inner = lax.rem(chunk, GROUP)
            self.full[lax.rem(inner, 2), lax.div(inner, 2), lax.div(chunk, GROUP)] = low(
                chunk_of(chunk)
            )

        self.swap().start()

    def second(self):
        at = self.place
        self.swap().wait()

        @pl.loop(0, 4)
        def _(pair):
            self.half[pair] = low(
                self.full[at.core, pair].astype(jnp.float32) + self.half[pair].astype(jnp.float32)
            )

        for step in range(1, 4):
            self.across(step, True).start()

    def third(self):
        at = self.place
        total = self.half[at.pair].astype(jnp.float32)
        for step in range(1, 4):
            self.across(step, False).wait()
            total = total + self.quarter[at.pair_at(step)].astype(jnp.float32)
        self.quarter[at.pair] = low(total)
        for step in range(1, at.outers):
            self.along(step, True).start()

    def finish(self):
        at = self.place
        total = self.quarter[at.pair, at.outer].astype(jnp.float32)
        for step in range(1, at.outers):
            self.along(step, False).wait()
            total = total + self.last[at.outer_at(step)].astype(jnp.float32)
        return total


def layer_kernel(names, devices, *refs):
    s = types.SimpleNamespace(**dict(zip(names, refs)))
    at = Place(devices)
    points, width = s.features_far.shape
    tiles = points // TILE
    blocks = points // BLOCK
    share = width // devices
    tile_blocks = TILE // BLOCK
    f32 = jnp.float32

    barrier = pltpu.get_barrier_semaphore()
    for step in range(1, GROUP):
        pl.semaphore_signal(
            barrier, inc=1, device_id=(at.device(at.outer, at.inner_at(step)),),
            device_id_type=pl.DeviceIdType.MESH,
        )
    for step in range(1, at.outers):
        pl.semaphore_signal(
            barrier, inc=1, device_id=(at.device(at.outer_at(step), at.inner),),
            device_id_type=pl.DeviceIdType.MESH,
        )

    quarter = points // 4
    feature_loads = [
        pltpu.make_async_copy(
            s.features_far.at[part * quarter : (part + 1) * quarter],
            s.features.at[part * quarter : (part + 1) * quarter],
            s.sem_in.at[part],
        )
        for part in range(4)
    ]
    for load in feature_loads:
        load.start()

    class Aside:
        def __init__(self, first, *buffers):
            self.pairs = []
            row = first
            for buffer in buffers:
                for start in range(0, buffer.shape[0], LANES):
                    near = buffer.at[start : start + LANES]
                    far = s.aside.at[row : row + LANES]
                    self.pairs.append((near, far, s.sem_aside.at[row // LANES]))
                    row += LANES

        def store(self):
            for near, far, sem in self.pairs:
                pltpu.make_async_copy(near, far, sem).start()

        def stored(self):
            for near, far, sem in self.pairs:
                pltpu.make_async_copy(near, far, sem).wait()

        def load(self):
            for near, far, sem in self.pairs:
                pltpu.make_async_copy(far, near, sem).start()

        def loaded(self):
            for near, far, sem in self.pairs:
                pltpu.make_async_copy(far, near, sem).wait()

    aside_a = Aside(0, s.u1, s.kv)
    aside_b = Aside(3 * width, s.e1, s.o, s.u2, s.u3)

    def columns(tile):
        return pl.ds(pl.multiple_of(tile * TILE, TILE), TILE)

    def block_columns(block):
        return pl.ds(pl.multiple_of(block * BLOCK, BLOCK), BLOCK)

    def column(index):
        return s.cols[:, index : index + 1]

    def hidden_column(index):
        return jnp.concatenate([column(8 + 2 * index), column(9 + 2 * index)], axis=0)

    def out_copy(tile, target, slots, sems, index):
        slot = lax.rem(tile, 2)
        where = pl.ds(pl.multiple_of(tile * TILE, TILE), TILE)
        return pltpu.make_async_copy(slots.at[slot], target.at[where, :], sems.at[index, slot])

    def put_out(tile, target, slots, sems, index, values):
        @pl.when(tile >= 2)
        def _():
            out_copy(tile - 2, target, slots, sems, index).wait()

        slots[lax.rem(tile, 2)] = values
        out_copy(tile, target, slots, sems, index).start()

    def end_out(target, slots, sems, index):
        for tile in range(tiles - 2, tiles):
            out_copy(tile, target, slots, sems, index).wait()

    for matrix in range(7):
        for row in range(share):
            s.pack[matrix * share + row : matrix * share + row + 1, :] = s.square_weight[
                matrix : matrix + 1, row * width : (row + 1) * width
            ]
    for matrix in range(2):
        for half in range(2):
            for row in range(share):
                place = (7 + 2 * matrix + half) * share + row
                start = row * F + half * width
                s.pack[place : place + 1, :] = s.expand_weight[
                    matrix : matrix + 1, start : start + width
                ]
        for row in range(2 * share):
            place = (11 + 2 * matrix) * share + row
            s.pack[place : place + 1, :] = s.contract_weight[
                matrix : matrix + 1, row * width : (row + 1) * width
            ]
    s.pack[15 * share : 16 * share, :LANES] = s.fourier_weight[...]
    s.pack[15 * share : 16 * share, LANES:] = jnp.zeros((share, LANES), f32)
    live = s.point_mask[...].astype(f32)
    counts = dot_bt(jnp.ones((8, LANES), jnp.bfloat16), low(live))
    s.pack[15 * share : 15 * share + 1, LANES : LANES + blocks] = counts[:1]
    lane = lax.broadcasted_iota(jnp.int32, (1, LANES), 1)
    wide_block = lax.broadcasted_iota(jnp.int32, (1, E * blocks), 1) // E
    item_row = jnp.zeros((1, LANES), f32)
    item_wide = jnp.zeros((1, E * blocks), jnp.int32)
    for block in range(blocks):
        item_row = jnp.where(lane == block, s.items[block].astype(f32), item_row)
        item_wide = jnp.where(wide_block == block, s.items[block], item_wide)
    s.pack[15 * share + 1 : 15 * share + 2, LANES:] = item_row
    packed = low(s.pack[...])
    split = s.gather_one.shape[3]
    s.gather_one[at.core, at.pair, at.outer] = packed[:split]
    s.gather_two[at.core, at.pair, at.outer] = packed[split:]

    pl.semaphore_wait(barrier, GROUP - 1 + at.outers - 1)
    one = Gather(at, s.gather_one, (s.sem_g1s, s.sem_g1r))
    two = Gather(at, s.gather_two, (s.sem_g2s, s.sem_g2r))
    one.start_first()

    row_at = lax.broadcasted_iota(jnp.int32, (width, width), 0)
    lane_at = lax.broadcasted_iota(jnp.int32, (width, width), 1)
    s.eye[...] = jnp.where(row_at == lane_at, 1.0, 0.0).astype(jnp.bfloat16)
    s.heads[...] = jnp.where(row_at // E == lane_at // E, 1.0, 0.0).astype(jnp.bfloat16)
    s.small[...] = jnp.zeros(s.small.shape, f32)
    s.small[0:8, :] = s.vector_weight[...]
    for row in range(2):
        for half in range(2):
            s.small[8 + 2 * row + half : 9 + 2 * row + half, :] = s.hidden_weight[
                row : row + 1, half * width : (half + 1) * width
            ]
    s.small[12:14, : FOUR // 2] = s.fourier_basis[...]
    s.cols[...] = s.small[...].T
    rows_wide = lax.broadcasted_iota(jnp.int32, s.spread.shape, 0)
    lanes_wide = lax.broadcasted_iota(jnp.int32, s.spread.shape, 1)
    s.spread[...] = jnp.where(
        (item_wide == rows_wide // E) & (rows_wide % E == lanes_wide % E), 1.0, 0.0
    ).astype(jnp.bfloat16)
    s.vector_sum[...] = jnp.zeros(s.vector_sum.shape, f32)
    speed = (lax.broadcasted_iota(jnp.int32, (E // 4, 1), 0).astype(f32) + 1.0) * (
        math.pi / (E // 4)
    )

    def add_sum(index, values):
        for part in range(values.shape[0] // width):
            s.vector_sum[index + part] += lane_sum(values[part * width : (part + 1) * width])

    def features_turned(tile):
        return dot_bt(s.eye[...], s.features[columns(tile), :])

    def before(tile, _):
        where = columns(tile)
        scaled, root = column_norm(features_turned(tile))
        s.root_one[0:1, where] = root
        s.u1[:, where] = low(scaled * column(0) + column(1))
        x_row, y_row = s.coords[0:1, where], s.coords[1:2, where]
        angles = jnp.concatenate([speed * x_row, speed * y_row], axis=0)
        s.cosine[:, where] = jnp.cos(angles)
        s.sine[:, where] = jnp.sin(angles)
        basis = s.cols[: FOUR // 2, :]
        phases = 2.0 * math.pi * (basis[:, 12:13] * x_row + basis[:, 13:14] * y_row)
        s.phi[:, where] = low(jnp.concatenate([jnp.cos(phases), jnp.sin(phases)], axis=0))
        for block in range(tile_blocks):
            s.mask[0:1, pl.ds(pl.multiple_of(tile * TILE + block * BLOCK, BLOCK), BLOCK)] = (
                s.point_mask[pl.ds(tile * tile_blocks + block, 1), :].astype(f32)
            )

    for load in feature_loads:
        load.wait()
    lax.fori_loop(0, tiles // 4, before, None)
    one.start_second()
    two.start_first()
    lax.fori_loop(tiles // 4, tiles // 2, before, None)
    one.start_third()
    two.start_second()
    lax.fori_loop(tiles // 2, tiles, before, None)
    one.finish()

    group = 16 // share

    def chunk_pair(buffer, index):
        parts = []
        for step in range(group):
            chunk = index * group + step
            inner = lax.rem(chunk, GROUP)
            parts.append(
                buffer[lax.rem(inner, 2), lax.div(inner, 2), lax.div(chunk, GROUP)].astype(f32)
            )
        return parts

    def join(parts, piece):
        return low(
            jnp.concatenate([part[piece * share : (piece + 1) * share] for part in parts], axis=0)
        )

    @pl.loop(0, devices // group)
    def _(index):
        parts = chunk_pair(s.gather_one, index)
        where = pl.ds(pl.multiple_of(index * 16, 16), 16)
        for piece in range(3):
            s.w_qkv[where, piece * width : (piece + 1) * width] = join(parts, piece)
        s.w_o[where, :] = join(parts, 3)

    def flip(matrix):
        return low(dot_bt(s.eye[...], matrix))

    for piece in range(3):
        s.t_qkv[piece * width : (piece + 1) * width, :] = flip(
            s.w_qkv[:, piece * width : (piece + 1) * width]
        )
    s.t_o[...] = flip(s.w_o[...])

    def block_product(left, right):
        return compress(dot_bt(left, right))

    def put_products(tile, left, right):
        for block in range(tile_blocks):
            lanes = slice(block * BLOCK, (block + 1) * BLOCK)
            where = pl.ds(pl.multiple_of((tile * tile_blocks + block) * E, E), E)
            s.per_block[where, :] = block_product(left[:, lanes], right[:, lanes])

    def summary(table, tile, block):
        item = s.items[tile * tile_blocks + block]
        first = item * 2
        inner, outer = lax.rem(first, GROUP), lax.div(first, GROUP)
        rows = jnp.concatenate([table[inner, outer], table[inner + 1, outer]], axis=0)
        return jnp.concatenate([rows] * H, axis=0) * s.heads[...]

    def per_block(tile, function):
        return jnp.concatenate([function(block) for block in range(tile_blocks)], axis=1)

    def lanes_of(block):
        return slice(block * BLOCK, (block + 1) * BLOCK)

    def phase_a(tile, _):
        where = columns(tile)
        projected = dot(s.t_qkv[...], s.u1[:, where])
        cosine, sine = s.cosine[:, where], s.sine[:, where]
        s.q[:, where] = low(turn(projected[:width], cosine, sine, 1.0))
        keys = low(turn(projected[width : 2 * width], cosine, sine, 1.0) * s.mask[0:1, where])
        values = low(projected[2 * width :])
        s.kv[:width, where] = keys
        s.kv[width:, where] = values
        put_products(tile, values, keys)

    lax.fori_loop(0, tiles, phase_a, None)
    table_sum = TableSum(at, s)
    table_sum.start()
    aside_a.store()
    two.start_third()

    def take_two(index, carried):
        parts = chunk_pair(s.gather_two, index)
        where = pl.ds(pl.multiple_of(index * 16, 16), 16)
        for piece in range(2):
            s.w_kv[where, piece * width : (piece + 1) * width] = join(parts, piece)
            s.w_w1[where, piece * width : (piece + 1) * width] = join(parts, 3 + piece)
            s.w_p1[where, piece * width : (piece + 1) * width] = join(parts, 5 + piece)
        s.w_do[where, :] = join(parts, 2)
        both = pl.ds(pl.multiple_of(index * 32, 32), 32)
        for piece, target in ((7, s.w_w2), (9, s.w_p2)):
            target[both, :] = low(
                jnp.concatenate([part[piece * share : (piece + 2) * share] for part in parts], axis=0)
            )
        found = []
        for outer in range(at.outers):
            mine = lax.div(outer * GROUP + at.inner, 2).astype(f32)
            total = carried[outer]
            for part in parts:
                count_row = part[11 * share : 11 * share + 1, LANES:]
                item_at = part[11 * share + 1 : 11 * share + 2, LANES:]
                total = total + jnp.where(item_at == mine, count_row, 0.0)
            found.append(total)
        s.fourier[where, :] = jnp.concatenate(
            [part[11 * share : 12 * share, :LANES] for part in parts], axis=0
        )
        return tuple(found)

    table_sum.middle()
    two.finish()
    found = lax.fori_loop(
        0, devices // group, take_two, tuple(jnp.zeros((1, LANES), f32) for _ in range(at.outers))
    )
    for outer in range(at.outers):
        s.inverse[outer : outer + 1, :] = jnp.broadcast_to(
            1.0 / jnp.sum(found[outer], axis=1, keepdims=True), (1, width)
        )
    w_dq = jnp.concatenate(
        [s.fourier[pl.ds(0, FOUR, stride=2), :], s.fourier[pl.ds(1, FOUR, stride=2), :]], axis=1
    )
    s.t_dq[...] = low(w_dq.T)
    table_sum.late(s.table_self)
    for piece in range(2):
        cols = slice(piece * width, (piece + 1) * width)
        s.t_kv[cols, :] = flip(s.w_kv[:, cols])
        s.t_w1[cols, :] = flip(s.w_w1[:, cols])
        s.t_p1[cols, :] = flip(s.w_p1[:, cols])
        s.t_w2[:, cols] = flip(s.w_w2[cols, :])
        s.t_p2[:, cols] = flip(s.w_p2[cols, :])
    s.t_do[...] = flip(s.w_do[...])
    table_sum.finish(s.table_self)

    def phase_b(tile, _):
        where = columns(tile)
        mask = s.mask[0:1, where]
        queries = s.q[:, where]
        mixed = per_block(
            tile, lambda b: dot(summary(s.table_self, tile, b), queries[:, lanes_of(b)])
        )
        attended = low(mixed * mask)
        s.o[:, where] = attended
        first_sum = features_turned(tile) + dot(s.t_o[...], attended)
        scaled_two, root_two = column_norm(first_sum)
        s.root_two[0:1, where] = root_two
        s.xh2[:, where] = low(scaled_two)
        middle = low(scaled_two * column(2) + column(3))
        s.u2[:, where] = middle
        hidden_pre = dot(s.t_w1[...], middle) + hidden_column(0)
        hidden = low(gelu(hidden_pre))
        s.e1[:, where] = hidden
        s.slope[:, where] = low(hidden_pre)
        encoded = first_sum + dot(s.t_w2[...], hidden) + column(6)
        scaled_three, root_three = column_norm(encoded)
        s.root_three[0:1, where] = root_three
        s.xh3[:, where] = low(scaled_three)
        outer = low(scaled_three * column(4) + column(5))
        s.u3[:, where] = outer
        pair = dot(s.t_kv[...], outer)
        keys = low(pair[:width] * mask)
        values = low(pair[width:])
        s.kvd[:width, where] = keys
        s.kvd[width:, where] = values
        put_products(tile, values, keys)

    lax.fori_loop(0, tiles, phase_b, None)
    table_sum.start()
    aside_b.store()

    def cotangent_load(tile):
        slot = lax.rem(tile, 2)
        where = pl.ds(pl.multiple_of(tile * TILE, TILE), TILE)
        return pltpu.make_async_copy(
            s.cotangent_far.at[where, :], s.output_slots.at[slot], s.sem_in.at[4 + slot]
        )

    cotangent_load(0).start()
    cotangent_load(1).start()
    aside_a.stored()

    def cross_inputs(tile, _):
        where = columns(tile)
        s.qd[:, where] = low(dot(s.t_dq[...], s.phi[:, where]))
        cotangent_load(tile).wait()
        upstream = s.output_slots[lax.rem(tile, 2)]
        turned = upstream.T
        s.u1[:, where] = turned
        add_sum(7, turned.astype(f32))
        s.kv[:, where] = low(dot(s.w_p2[...], turned))

        @pl.when(tile + 2 < tiles)
        def _():
            cotangent_load(tile + 2).start()

    def slopes(tile, _):
        where = columns(tile)
        s.slope[:, where] = low(gelu_slope(s.slope[:, where].astype(f32)))

    lax.fori_loop(0, tiles, cross_inputs, None)
    table_sum.middle()
    lax.fori_loop(0, tiles, slopes, None)
    table_sum.late(s.table_other)
    aside_b.stored()
    table_sum.finish(s.table_other)

    def phase_c(tile, _):
        where = columns(tile)
        mask = s.mask[0:1, where]
        queries = s.qd[:, where]
        tables = [summary(s.table_other, tile, block) for block in range(tile_blocks)]
        decoded = low(
            per_block(tile, lambda b: dot(tables[b], queries[:, lanes_of(b)])) * mask
        )
        s.u2[:, where] = decoded
        latent_low = low(dot(s.t_do[...], decoded))
        s.o[:, where] = latent_low
        hidden, slope = gelu_both(dot(s.t_p1[...], latent_low) + hidden_column(1))
        s.e1[:, where] = low(hidden)
        grad_spread = s.kv[:, where].astype(f32) * slope
        add_sum(10, grad_spread)
        grad_spread = low(grad_spread)
        s.kv[:, where] = grad_spread
        grad_latent = low(s.u1[:, where].astype(f32) + dot(s.w_p1[...], grad_spread))
        s.u3[:, where] = grad_latent
        grad_decoded = low(dot(s.w_do[...], grad_latent) * mask)
        put_products(tile, grad_decoded, queries)
        s.qd[:, where] = grad_decoded

    lax.fori_loop(0, tiles, phase_c, None)
    table_sum.start()

    def cross_query_grads(tile, _):
        where = columns(tile)
        upstream = s.qd[:, where]
        grad = per_block(
            tile, lambda b: dot_at(summary(s.table_other, tile, b), upstream[:, lanes_of(b)])
        )
        s.qd[:, where] = low(grad)

    def outputs(tile, _):
        where = columns(tile)
        output = dot(s.t_do[...], s.u2[:, where]) + dot(s.t_p2[...], s.e1[:, where]) + column(7)
        put_out(tile, s.layer_output, s.output_slots, s.sem_out, 0, low(output).T)

    lax.fori_loop(0, tiles, cross_query_grads, None)
    s.grad_dq[...] = dot_bt(s.phi[...], s.qd[...])
    s.fourier[pl.ds(0, FOUR, stride=2), :] = s.grad_dq[:, :LANES]
    s.fourier[pl.ds(1, FOUR, stride=2), :] = s.grad_dq[:, LANES:]
    s.grad_do[...] = dot_bt(s.u2[...], s.u3[...])
    table_sum.middle()
    s.grad_p1[...] = dot_bt(s.o[...], s.kv[...])
    s.grad_p2[...] = dot_bt(s.e1[...], s.u1[...])
    zeros = jnp.zeros((share, LANES), f32)

    def rows_of(chunk, count=1):
        size = share * count
        return pl.ds(pl.multiple_of(chunk * size, size), size)

    def chunk_c(chunk):
        where = rows_of(chunk)
        return jnp.concatenate(
            [
                s.grad_do[where, :],
                s.grad_p1[where, :width],
                s.grad_p1[where, width:],
                s.grad_p2[rows_of(chunk, 2), :],
                jnp.concatenate([s.fourier[where, :], zeros], axis=1),
            ],
            axis=0,
        )

    sum_c = GradSum(at, s, "c", 0)
    sum_c.start(chunk_c)
    table_sum.late(s.table_third)
    lax.fori_loop(0, tiles, outputs, None)
    end_out(s.layer_output, s.output_slots, s.sem_out, 0)
    aside_a.load()
    aside_b.load()
    sum_c.second()
    table_sum.finish(s.table_third)

    def phase_d(tile, _):
        where = columns(tile)
        mask = s.mask[0:1, where]
        keys, values = s.kvd[:width, where], s.kvd[width:, where]
        tables = [summary(s.table_third, tile, block) for block in range(tile_blocks)]
        grad_keys = per_block(tile, lambda b: dot_at(tables[b], values[:, lanes_of(b)])) * mask
        grad_values = per_block(tile, lambda b: dot(tables[b], keys[:, lanes_of(b)]))
        grad_pair = low(jnp.concatenate([grad_keys, grad_values], axis=0))
        s.kvd[:, where] = grad_pair
        grad_outer = dot(s.w_kv[...], grad_pair)
        scaled = s.xh3[:, where].astype(f32)
        add_sum(4, grad_outer * scaled)
        add_sum(5, grad_outer)
        grad_encoded = column_norm_back(
            grad_outer, scaled, s.root_three[0:1, where], column(4)
        )
        add_sum(6, grad_encoded)
        grad_encoded_low = low(grad_encoded)
        s.xh3[:, where] = grad_encoded_low
        grad_hidden = dot(s.w_w2[...], grad_encoded_low) * s.slope[:, where].astype(f32)
        add_sum(8, grad_hidden)
        grad_hidden = low(grad_hidden)
        s.slope[:, where] = grad_hidden
        grad_middle = dot(s.w_w1[...], grad_hidden)
        scaled = s.xh2[:, where].astype(f32)
        add_sum(2, grad_middle * scaled)
        add_sum(3, grad_middle)
        grad_first = grad_encoded + column_norm_back(
            grad_middle, scaled, s.root_two[0:1, where], column(2)
        )
        grad_first = low(grad_first)
        s.xh2[:, where] = grad_first
        grad_attended = low(dot(s.w_o[...], grad_first) * mask)
        s.qd[:, where] = grad_attended
        put_products(tile, grad_attended, s.q[:, where])

    lax.fori_loop(0, tiles // 2, phase_d, None)
    sum_c.third()
    lax.fori_loop(tiles // 2, tiles, phase_d, None)
    table_sum.start()
    s.grads_c[...] = sum_c.finish()
    aside_a.loaded()
    aside_b.loaded()

    def query_grads(tile, _):
        where = columns(tile)
        upstream = s.qd[:, where]
        grad = per_block(
            tile, lambda b: dot_at(summary(s.table_self, tile, b), upstream[:, lanes_of(b)])
        )
        s.q[:, where] = low(turn(grad, s.cosine[:, where], s.sine[:, where], -1.0))

    lax.fori_loop(0, tiles, query_grads, None)
    s.grad_o[...] = dot_bt(s.o[...], s.xh2[...])
    table_sum.middle()
    s.grad_kv[...] = dot_bt(s.u3[...], s.kvd[...])
    s.grad_w2[...] = dot_bt(s.e1[...], s.xh3[...])
    s.grad_w1[...] = dot_bt(s.u2[...], s.slope[...])
    table_sum.late(s.table_other)

    def chunk_d(chunk):
        where = rows_of(chunk)
        return jnp.concatenate(
            [
                s.grad_kv[where, :width],
                s.grad_kv[where, width:],
                s.grad_o[where, :],
                s.grad_w1[where, :width],
                s.grad_w1[where, width:],
                s.grad_w2[rows_of(chunk, 2), :],
                jnp.zeros((share, width), f32),
            ],
            axis=0,
        )

    sum_d = GradSum(at, s, "d", 0)
    sum_d.start(chunk_d)
    s.grad_qkv[:, :width] = dot_bt(s.u1[...], s.q[...])
    table_sum.finish(s.table_other)

    def phase_e(tile, _):
        where = columns(tile)
        mask = s.mask[0:1, where]
        keys, values = s.kv[:width, where], s.kv[width:, where]
        tables = [summary(s.table_other, tile, block) for block in range(tile_blocks)]
        grad_keys = per_block(tile, lambda b: dot_at(tables[b], values[:, lanes_of(b)])) * mask
        grad_values = low(per_block(tile, lambda b: dot(tables[b], keys[:, lanes_of(b)])))
        s.kv[:width, where] = low(turn(grad_keys, s.cosine[:, where], s.sine[:, where], -1.0))
        s.kv[width:, where] = grad_values

    lax.fori_loop(0, tiles, phase_e, None)
    sum_d.second()
    s.grad_qkv[:, width:] = dot_bt(s.u1[...], s.kv[...])

    def chunk_e(chunk):
        where = rows_of(chunk)
        return jnp.concatenate(
            [
                s.grad_qkv[where, :width],
                s.grad_qkv[where, width : 2 * width],
                s.grad_qkv[where, 2 * width :],
                jnp.zeros((share, width), f32),
            ],
            axis=0,
        )

    sum_e = GradSum(at, s, "e", 8 * share)
    sum_e.start(chunk_e)

    def phase_f(tile, _):
        where = columns(tile)
        grad_normed = dot(
            s.w_qkv[...], jnp.concatenate([s.q[:, where], s.kv[:, where]], axis=0)
        )
        turned = features_turned(tile)
        root = s.root_one[0:1, where]
        scaled = (turned - jnp.sum(turned, axis=0, keepdims=True) * (1.0 / width)) * root
        add_sum(0, grad_normed * scaled)
        add_sum(1, grad_normed)
        grad_input = s.xh2[:, where].astype(f32) + column_norm_back(
            grad_normed, scaled, root, column(0)
        )
        put_out(tile, s.input_grad, s.input_slots, s.sem_out, 1, grad_input.T)

    lax.fori_loop(0, tiles // 4, phase_f, None)
    sum_e.second()
    lax.fori_loop(tiles // 4, tiles // 2, phase_f, None)
    sum_d.third()
    lax.fori_loop(tiles // 2, 3 * tiles // 4, phase_f, None)
    sum_e.third()
    lax.fori_loop(3 * tiles // 4, tiles, phase_f, None)
    end_out(s.input_grad, s.input_slots, s.sem_out, 1)
    s.grads_d[...] = sum_d.finish()
    s.grads_e[...] = sum_e.finish()
    squares = sum(
        jnp.sum(grads[...] * grads[...], axis=0, keepdims=True)
        for grads in (s.grads_c, s.grads_d, s.grads_e)
    )

    lane_wide = lax.broadcasted_iota(jnp.int32, (width, LANES), 1)
    sums = jnp.zeros((width, LANES), f32)
    for index in range(12):
        sums = jnp.where(
            lane_wide == index, jnp.sum(s.vector_sum[index], axis=1, keepdims=True), sums
        )
    s.vector_cols[...] = sums
    turned_sums = s.vector_cols[...].T
    s.final_inner[at.inner] = jnp.concatenate(
        [turned_sums[:12], squares, jnp.zeros((3, width), f32)], axis=0
    )

    def final_near(step, start):
        source = at.inner if start else at.inner_at(step)
        return remote(
            s.final_inner.at[at.inner], s.final_inner.at[source], s.sem_fs.at[0, step],
            s.sem_fr.at[0, source], at.device(at.outer, at.inner_at(step)),
        )

    def final_far(step, start):
        source = at.outer if start else at.outer_at(step)
        return remote(
            s.final_outer.at[at.outer], s.final_outer.at[source], s.sem_fs.at[1, step],
            s.sem_fr.at[1, source], at.device(at.outer_at(step), at.inner),
        )

    for step in range(1, GROUP):
        final_near(step, True).start()
    for step in range(1, GROUP):
        final_near(step, False).wait()
    total = s.final_inner[0]
    for index in range(1, GROUP):
        total = total + s.final_inner[index]
    s.final_outer[at.outer] = total
    for step in range(1, at.outers):
        final_far(step, True).start()
    for step in range(1, at.outers):
        final_far(step, False).wait()
    total = s.final_outer[0]
    for index in range(1, at.outers):
        total = total + s.final_outer[index]
    s.vector_all[...] = total


def update_kernel(share, *refs):
    sources, refs = refs[:2], refs[2:]
    grads_c, grads_d, grads_e, vector_all = refs[:4]
    weights = refs[4:22]
    targets = refs[22:24]
    norm_out = refs[24]
    results = refs[25:43]
    flat_square, flat_expand, flat_contract, *held, sems = refs[43:]
    loads, stores = [], []
    for index, (source, target) in enumerate(zip(sources, targets)):
        size = source.shape[0] // PIECES
        for piece in range(PIECES):
            where = slice(piece * size, (piece + 1) * size)
            own = held[index].at[where]
            loads.append(pltpu.make_async_copy(source.at[where], own, sems.at[0, index, piece]))
            stores.append(pltpu.make_async_copy(own, target.at[where], sems.at[1, index, piece]))
    for load in loads:
        load.start()
    width = grads_c.shape[1]
    places = [(grads_e, 0), (grads_e, 1), (grads_e, 2), (grads_d, 2), (grads_d, 0), (grads_d, 1), (grads_c, 0)]
    for matrix, (source, piece) in enumerate(places):
        for row in range(share):
            start = piece * share + row
            flat_square[matrix : matrix + 1, row * width : (row + 1) * width] = source[
                start : start + 1, :
            ]
    for matrix, (source, piece) in enumerate(((grads_d, 3), (grads_c, 1))):
        for half in range(2):
            for row in range(share):
                start = (piece + half) * share + row
                target = row * F + half * width
                flat_expand[matrix : matrix + 1, target : target + width] = source[
                    start : start + 1, :
                ]
    for matrix, (source, piece) in enumerate(((grads_d, 5), (grads_c, 3))):
        for row in range(2 * share):
            start = piece * share + row
            flat_contract[matrix : matrix + 1, row * width : (row + 1) * width] = source[
                start : start + 1, :
            ]
    for load, store in zip(loads, stores):
        load.wait()
        store.start()
    fourier = grads_c[5 * share : 6 * share, :LANES]
    turned = vector_all[...]
    rows = jnp.sum(turned[:12] * turned[:12], axis=0, keepdims=True) + turned[12:13]
    norm = jnp.sqrt(jnp.sum(rows, axis=1, keepdims=True))
    norm_out[...] = norm
    factor = jnp.minimum(1.0, CLIP_NORM / (norm + 1e-06))
    hidden = jnp.concatenate(
        [
            jnp.concatenate([turned[8:9], turned[9:10]], axis=1),
            jnp.concatenate([turned[10:11], turned[11:12]], axis=1),
        ],
        axis=0,
    )
    grads = (flat_square[...], flat_expand[...], flat_contract[...], fourier, turned[:8], hidden)
    rates = (RATE_MATRIX,) * 4 + (RATE_VECTOR,) * 2
    for index, (grad, rate) in enumerate(zip(grads, rates)):
        weight, first, second = (weights[3 * index + part][...] for part in range(3))
        values = adam_update(weight, first, second, grad, factor, rate)
        for part in range(3):
            results[3 * index + part][...] = values[part]
    for store in stores:
        store.wait()


def fused(devices, features, coords, fourier_basis, block_items, point_mask, cotangent, *weights):
    points, width = features.shape
    blocks = points // BLOCK
    outers = devices // GROUP
    share = width // devices
    items = points * devices // ITEM_PTS
    bf16, f32 = jnp.bfloat16, jnp.float32
    square, expand, contract, fourier, vector, hidden = (weights[3 * i] for i in range(6))
    vmem = lambda shape, dtype: pltpu.VMEM(shape, dtype)
    inputs = {
        "items": block_items,
        "features_far": features,
        "coords": coords,
        "fourier_basis": fourier_basis,
        "point_mask": point_mask.reshape(blocks, BLOCK),
        "cotangent_far": cotangent,
        "square_weight": square,
        "expand_weight": expand,
        "contract_weight": contract,
        "fourier_weight": fourier.reshape(share, LANES),
        "vector_weight": vector,
        "hidden_weight": hidden,
    }
    rows_c, rows_d, rows_e = 6 * share, 8 * share, 4 * share
    outputs = {
        "layer_output": ((points, width), bf16),
        "input_grad": ((points, width), f32),
        "grads_c": ((rows_c, width), f32),
        "grads_d": ((rows_d, width), f32),
        "grads_e": ((rows_e, width), f32),
        "vector_all": ((16, width), f32),
        "aside": ((8 * width, points), bf16),
    }
    tall = lambda rows: vmem((rows, points), bf16)
    scratch = {
        "pack": vmem((16 * share, width), f32),
        "gather_one": vmem((2, 4, outers, 4 * share, width), bf16),
        "gather_two": vmem((2, 4, outers, 12 * share, width), bf16),
        "eye": vmem((width, width), bf16),
        "heads": vmem((width, width), bf16),
        "small": vmem((LANES, width), f32),
        "cols": vmem((width, LANES), f32),
        "spread": vmem((items * E, blocks * E), bf16),
        "vector_sum": vmem((12, width, LANES), f32),
        "vector_cols": vmem((width, LANES), f32),
        "grad_qkv": vmem((width, 3 * width), f32),
        "grad_o": vmem((width, width), f32),
        "grad_kv": vmem((width, 2 * width), f32),
        "grad_do": vmem((width, width), f32),
        "grad_w1": vmem((width, F), f32),
        "grad_p1": vmem((width, F), f32),
        "grad_w2": vmem((F, width), f32),
        "grad_p2": vmem((F, width), f32),
        "grad_dq": vmem((FOUR, width), f32),
        "fourier": vmem((2 * FOUR, LANES), f32),
        "w_qkv": vmem((width, 3 * width), bf16),
        "t_qkv": vmem((3 * width, width), bf16),
        "w_o": vmem((width, width), bf16),
        "t_o": vmem((width, width), bf16),
        "w_kv": vmem((width, 2 * width), bf16),
        "t_kv": vmem((2 * width, width), bf16),
        "w_do": vmem((width, width), bf16),
        "t_do": vmem((width, width), bf16),
        "w_w1": vmem((width, F), bf16),
        "t_w1": vmem((F, width), bf16),
        "w_p1": vmem((width, F), bf16),
        "t_p1": vmem((F, width), bf16),
        "w_w2": vmem((F, width), bf16),
        "t_w2": vmem((width, F), bf16),
        "w_p2": vmem((F, width), bf16),
        "t_p2": vmem((width, F), bf16),
        "t_dq": vmem((width, FOUR), bf16),
        "mask": vmem((1, points), f32),
        "root_one": vmem((1, points), f32),
        "root_two": vmem((1, points), f32),
        "root_three": vmem((1, points), f32),
        "cosine": vmem((E // 2, points), f32),
        "sine": vmem((E // 2, points), f32),
        "phi": tall(FOUR),
        "u1": tall(width),
        "q": tall(width),
        "kv": tall(2 * width),
        "qd": tall(width),
        "o": tall(width),
        "xh2": tall(width),
        "u2": tall(width),
        "e1": tall(F),
        "slope": tall(F),
        "xh3": tall(width),
        "u3": tall(width),
        "kvd": tall(2 * width),
        "per_block": vmem((blocks * E, width), f32),
        "inverse": vmem((max(8, outers), width), f32),
        "table_send": vmem((GROUP, outers, 16, width), bf16),
        "table_recv": vmem((GROUP, outers, 16, width), bf16),
        "table_part": vmem((outers, 16, width), bf16),
        "table_cross": vmem((2, outers, outers, 16, width), bf16),
        "table_self": vmem((GROUP, outers, 16, width), bf16),
        "table_other": vmem((GROUP, outers, 16, width), bf16),
        "final_inner": vmem((GROUP, 16, width), f32),
        "final_outer": vmem((outers, 16, width), f32),
        "features": vmem((points, width), bf16),
        "sem_in": pltpu.SemaphoreType.DMA((6,)),
        "sem_aside": pltpu.SemaphoreType.DMA((8 * width // LANES,)),
        "table_third": vmem((GROUP, outers, 16, width), bf16),
        "output_slots": vmem((2, TILE, width), bf16),
        "input_slots": vmem((2, TILE, width), f32),
        "sem_out": pltpu.SemaphoreType.DMA((2, 2)),
    }
    for key, rows in (("c", rows_c), ("d", rows_d), ("e", rows_e)):
        for part in ("half_", "quarter_"):
            scratch[part + key] = vmem((4, outers, rows, width), bf16)
        scratch["last_" + key] = vmem((outers, rows, width), bf16)
    many = max(GROUP, outers)
    for key in ("ts", "tr", "g1s", "g1r", "g2s", "g2r", "cs", "cr", "ds", "dr", "es", "er"):
        scratch["sem_" + key] = pltpu.SemaphoreType.DMA((4, many))
    for key in ("fs", "fr"):
        scratch["sem_" + key] = pltpu.SemaphoreType.DMA((2, many))
    names = list(inputs) + list(outputs) + list(scratch)
    spaces = {"items": pltpu.SMEM, "features_far": pl.ANY, "cotangent_far": pl.ANY}
    in_specs = [pl.BlockSpec(memory_space=spaces.get(name, pltpu.VMEM)) for name in inputs]
    whole = pl.BlockSpec(memory_space=pltpu.VMEM)
    made = pl.pallas_call(
        functools.partial(layer_kernel, names, devices),
        out_shape=[jax.ShapeDtypeStruct(*shape) for shape in outputs.values()],
        in_specs=in_specs,
        out_specs=[pl.BlockSpec(memory_space=pl.ANY)] * 2
        + [whole] * 4
        + [pl.BlockSpec(memory_space=pl.ANY)],
        scratch_shapes=list(scratch.values()),
        compiler_params=pltpu.CompilerParams(
            collective_id=0, has_side_effects=True, vmem_limit_bytes=VMEM_BYTES
        ),
    )(*inputs.values())
    flat = list(weights)
    for part in range(9, 12):
        flat[part] = flat[part].reshape(share, LANES)
    shapes = [jax.ShapeDtypeStruct((1, 1), f32)] + [
        jax.ShapeDtypeStruct(flat[index].shape, f32) for index in range(18)
    ]
    order = []
    for index in range(6):
        order += [shapes[1 + 3 * index]] * 3
    updated = pl.pallas_call(
        functools.partial(update_kernel, share),
        out_shape=[jax.ShapeDtypeStruct(*shape) for shape in list(outputs.values())[:2]]
        + [shapes[0]]
        + order,
        in_specs=[pl.BlockSpec(memory_space=pl.ANY)] * 2 + [whole] * 22,
        out_specs=[pl.BlockSpec(memory_space=pl.ANY)] * 2 + [whole] * 19,
        scratch_shapes=[
            vmem(square.shape, f32),
            vmem(expand.shape, f32),
            vmem(contract.shape, f32),
            vmem((points, width), bf16),
            vmem((points, width), f32),
            pltpu.SemaphoreType.DMA((2, 2, PIECES)),
        ],
        compiler_params=pltpu.CompilerParams(vmem_limit_bytes=VMEM_BYTES),
    )(*made[:6], *flat)
    layer_output, input_grad, norm, *rest = updated
    for part in range(9, 12):
        rest[part] = rest[part].reshape(fourier.shape)
    return (layer_output, input_grad, norm.reshape(()), *rest)


def shards(features, *others):
    devices = lax.axis_size("pts")
    width = features.shape[1]
    if devices % GROUP == 0 and width % (8 * devices) == 0:
        return fused(devices, features, *others)
    return plain(features, *others)


def solution(mesh):
    in_specs = (
        P("pts", None),
        P(None, "pts"),
        P(),
        P("pts"),
        P("pts"),
        P("pts", None),
        P(None, "pts"),
        P(None, "pts"),
        P(None, "pts"),
        P(None, "pts"),
        P(None, "pts"),
        P(None, "pts"),
        P(None, "pts"),
        P(None, "pts"),
        P(None, "pts"),
        P("pts"),
        P("pts"),
        P("pts"),
        P(),
        P(),
        P(),
        P(),
        P(),
        P(),
    )
    out_specs = (
        P("pts", None),
        P("pts", None),
        P(),
        P(None, "pts"),
        P(None, "pts"),
        P(None, "pts"),
        P(None, "pts"),
        P(None, "pts"),
        P(None, "pts"),
        P(None, "pts"),
        P(None, "pts"),
        P(None, "pts"),
        P("pts"),
        P("pts"),
        P("pts"),
        P(),
        P(),
        P(),
        P(),
        P(),
        P(),
    )
    return jax.shard_map(shards, mesh=mesh, in_specs=in_specs, out_specs=out_specs, check_vma=False)
```

```python
import functools
import math
import types

import jax
import jax.numpy as jnp
from jax import lax
from jax.experimental import pallas as pl
from jax.experimental.pallas import tpu as pltpu
from jax.sharding import PartitionSpec as P

H = 8
E = 32
F = 512
FOUR = 128
BLOCK = 128
ITEM_PTS = 8192
STEP = 10


NORM_EPS = 1e-05
GELU_C = math.sqrt(2.0 / math.pi)
GELU_A = 0.044715
BETA_ONE = 0.9
BETA_TWO = 0.95
ADAM_EPS = 1e-08
WEIGHT_DECAY = 0.1
RATE_MATRIX = 0.05
RATE_VECTOR = 0.25
CLIP_NORM = 1.0
HIGHEST_PRECISION = lax.Precision.HIGHEST


def matmul(left, right):
    return jnp.dot(left, right, preferred_element_type=jnp.float32)


def matmul_left(left, right):
    return lax.dot_general(
        left, right, (((0,), (0,)), ((), ())), preferred_element_type=jnp.float32
    )


def matmul_right(left, right):
    return lax.dot_general(
        left, right, (((1,), (1,)), ((), ())), preferred_element_type=jnp.float32
    )


def gelu(values):
    return 0.5 * values * (1.0 + jnp.tanh(GELU_C * (values + GELU_A * values * values * values)))


def gelu_slope(values):
    tangent = jnp.tanh(GELU_C * (values + GELU_A * values * values * values))
    return 0.5 * (1.0 + tangent) + 0.5 * values * (1.0 - tangent * tangent) * GELU_C * (
        1.0 + 3.0 * GELU_A * values * values
    )


def norm_parts(values, norm_gain, norm_bias):
    centred = values - jnp.mean(values, axis=-1, keepdims=True)
    variance = jnp.mean(centred * centred, axis=-1, keepdims=True)
    root_inv = lax.rsqrt(variance + NORM_EPS)
    scaled = centred * root_inv
    return (scaled * norm_gain + norm_bias, scaled, root_inv)


def norm_back(upstream, scaled, root_inv, norm_gain):
    through = upstream * norm_gain
    centre = jnp.mean(through, axis=-1, keepdims=True)
    along = jnp.mean(through * scaled, axis=-1, keepdims=True)
    return root_inv * (through - centre - scaled * along)


def rotary_tables(coords):
    quarter = E // 4
    frequency = math.pi * (jnp.arange(quarter, dtype=jnp.float32) + 1.0) / quarter
    first_angle = coords[0][:, None] * frequency[None, :]
    second_angle = coords[1][:, None] * frequency[None, :]
    angles = jnp.concatenate([first_angle, first_angle, second_angle, second_angle], axis=1)
    return (jnp.cos(angles), jnp.sin(angles))


def rotate(values, cosine, sine):
    quarter = E // 4
    swapped = jnp.concatenate(
        [
            -values[..., quarter : 2 * quarter],
            values[..., :quarter],
            -values[..., 3 * quarter :],
            values[..., 2 * quarter : 3 * quarter],
        ],
        axis=-1,
    )
    return values * cosine[:, None, :] + swapped * sine[:, None, :]


def rotate_back(grads, cosine, sine):
    quarter = E // 4
    scaled = grads * sine[:, None, :]
    swapped = jnp.concatenate(
        [
            scaled[..., quarter : 2 * quarter],
            -scaled[..., :quarter],
            scaled[..., 3 * quarter :],
            -scaled[..., 2 * quarter : 3 * quarter],
        ],
        axis=-1,
    )
    return grads * cosine[:, None, :] + swapped


def fourier_features(coords, fourier_basis):
    phases = (
        2.0
        * math.pi
        * (
            coords[0][:, None] * fourier_basis[0][None, :]
            + coords[1][:, None] * fourier_basis[1][None, :]
        )
    )
    return jnp.concatenate([jnp.cos(phases), jnp.sin(phases)], axis=1)


def block_table(left, right, onehot):
    blocks = onehot.shape[0]
    per_block = jnp.einsum(
        "bphe,bphf->bhef",
        left.reshape(blocks, BLOCK, H, E),
        right.reshape(blocks, BLOCK, H, E),
        preferred_element_type=jnp.float32,
    )
    return jnp.einsum("ba,bhef->ahef", onehot, per_block, precision=HIGHEST_PRECISION)


def scale_round(table, inverse_count):
    return (table * inverse_count[:, None, None, None]).astype(jnp.bfloat16)


def spread(summary, onehot):
    selected = jnp.einsum(
        "ba,ahef->bhef", onehot.astype(jnp.bfloat16), summary, preferred_element_type=jnp.float32
    )
    return selected.astype(jnp.bfloat16)


def apply_summary(rows_low, block_summary, transposed):
    blocks = block_summary.shape[0]
    pattern = "bphf,bhef->bphe" if transposed else "bphe,bhef->bphf"
    mixed = jnp.einsum(
        pattern,
        rows_low.reshape(blocks, BLOCK, H, E),
        block_summary,
        preferred_element_type=jnp.float32,
    )
    return mixed.reshape(-1, H * E)


def galerkin_backward(
    grad_low, queries_low, keys_masked, values_low, block_summary, onehot, mask_float, reducer
):
    grad_masked = grad_low * mask_float.astype(jnp.bfloat16)
    grad_queries = apply_summary(grad_masked, block_summary, True)
    summary_grad = reducer(block_table(queries_low, grad_masked, onehot))
    block_grad = spread(summary_grad, onehot)
    grad_keys = apply_summary(values_low, block_grad, True) * mask_float
    grad_values = apply_summary(keys_masked, block_grad, False)
    return (grad_queries, grad_keys, grad_values)


def adam_update(weight, first, second, grad, factor, rate):
    clipped = grad * factor
    new_first = BETA_ONE * first + (1.0 - BETA_ONE) * clipped
    new_second = BETA_TWO * second + (1.0 - BETA_TWO) * clipped * clipped
    first_hat = new_first / (1.0 - BETA_ONE**STEP)
    second_hat = new_second / (1.0 - BETA_TWO**STEP)
    new_weight = weight - rate * (
        first_hat / (jnp.sqrt(second_hat) + ADAM_EPS) + WEIGHT_DECAY * weight
    )
    return (new_first, new_second, new_weight)


def own_share(full, width, along, start_index):
    return lax.dynamic_slice_in_dim(full, start_index * width, width, along)


def plain(
    features,
    coords,
    fourier_basis,
    block_items,
    point_mask,
    cotangent,
    square_weight,
    square_first,
    square_second,
    expand_weight,
    expand_first,
    expand_second,
    contract_weight,
    contract_first,
    contract_second,
    fourier_weight,
    fourier_first,
    fourier_second,
    vector_weight,
    vector_first,
    vector_second,
    hidden_weight,
    hidden_first,
    hidden_second,
):
    rows = features.shape[0]
    width = features.shape[1]
    blocks = rows // BLOCK
    devices = lax.axis_size("pts")
    items_total = rows * devices // ITEM_PTS
    gathered = (
        lax.all_gather(square_weight.astype(jnp.bfloat16), "pts", axis=1, tiled=True),
        lax.all_gather(expand_weight.astype(jnp.bfloat16), "pts", axis=1, tiled=True),
        lax.all_gather(contract_weight.astype(jnp.bfloat16), "pts", axis=1, tiled=True),
        lax.all_gather(fourier_weight.astype(jnp.bfloat16), "pts", axis=0, tiled=True),
    )
    square_full = gathered[0].reshape(7, width, width)
    expand_full = gathered[1].reshape(2, width, F)
    contract_full = gathered[2].reshape(2, F, width)
    fourier_full = gathered[3].reshape(FOUR, width)
    onehot = (block_items[:, None] == jnp.arange(items_total, dtype=jnp.int32)[None, :]).astype(
        jnp.float32
    )
    mask_float = point_mask.astype(jnp.float32)[:, None]
    mask_low = mask_float.astype(jnp.bfloat16)
    block_count = jnp.sum(mask_float.reshape(blocks, BLOCK), axis=1)
    local_count = jnp.dot(block_count, onehot, precision=HIGHEST_PRECISION)
    cosine, sine = rotary_tables(coords)
    phase_low = fourier_features(coords, fourier_basis).astype(jnp.bfloat16)
    inputs = features.astype(jnp.float32)
    normed, scaled_one, root_one = norm_parts(inputs, vector_weight[0], vector_weight[1])
    normed_low = normed.astype(jnp.bfloat16)
    joint_weight = jnp.concatenate([square_full[0], square_full[1], square_full[2]], axis=1)
    projected = matmul(normed_low, joint_weight)
    queries_low = (
        rotate(projected[:, :width].reshape(rows, H, E), cosine, sine)
        .reshape(rows, width)
        .astype(jnp.bfloat16)
    )
    keys_low = (
        rotate(projected[:, width : 2 * width].reshape(rows, H, E), cosine, sine)
        .reshape(rows, width)
        .astype(jnp.bfloat16)
    )
    keys_masked = keys_low * mask_low
    values_low = projected[:, 2 * width :].astype(jnp.bfloat16)
    self_local = block_table(keys_masked, values_low, onehot)
    self_table, item_count = lax.psum((self_local, local_count), "pts")
    inverse_count = 1.0 / item_count
    self_items = scale_round(self_table, inverse_count)
    self_summary = spread(self_items, onehot)
    attended_low = (apply_summary(queries_low, self_summary, False) * mask_float).astype(
        jnp.bfloat16
    )
    first_sum = inputs + matmul(attended_low, square_full[3])
    normed_mid, scaled_two, root_two = norm_parts(first_sum, vector_weight[2], vector_weight[3])
    middle_low = normed_mid.astype(jnp.bfloat16)
    hidden_pre = matmul(middle_low, expand_full[0]) + hidden_weight[0]
    hidden_low = gelu(hidden_pre).astype(jnp.bfloat16)
    encoded = first_sum + matmul(hidden_low, contract_full[0]) + vector_weight[6]
    normed_out, scaled_three, root_three = norm_parts(encoded, vector_weight[4], vector_weight[5])
    outer_low = normed_out.astype(jnp.bfloat16)
    pair_weight = jnp.concatenate([square_full[4], square_full[5]], axis=1)
    cross_projected = matmul(outer_low, pair_weight)
    cross_keys = cross_projected[:, :width].astype(jnp.bfloat16) * mask_low
    cross_values = cross_projected[:, width:].astype(jnp.bfloat16)
    cross_queries = matmul(phase_low, fourier_full).astype(jnp.bfloat16)
    cross_local = block_table(cross_keys, cross_values, onehot)
    cross_items = scale_round(lax.psum(cross_local, "pts"), inverse_count)
    cross_summary = spread(cross_items, onehot)
    decoded_low = (apply_summary(cross_queries, cross_summary, False) * mask_float).astype(
        jnp.bfloat16
    )
    latent = matmul(decoded_low, square_full[6])
    latent_low = latent.astype(jnp.bfloat16)
    spread_pre = matmul(latent_low, expand_full[1]) + hidden_weight[1]
    spread_low = gelu(spread_pre).astype(jnp.bfloat16)
    output = latent + matmul(spread_low, contract_full[1]) + vector_weight[7]
    cross_reducer = lambda table_part: scale_round(lax.psum(table_part, "pts"), inverse_count)
    self_reducer = lambda table_part: scale_round(lax.psum(table_part, "pts"), inverse_count)
    grad_output = cotangent.astype(jnp.float32)
    grad_bias_end = jnp.sum(grad_output, axis=0)
    grad_contract_spread = matmul_left(spread_low, cotangent)
    grad_spread = matmul_right(cotangent, contract_full[1]) * gelu_slope(spread_pre)
    grad_hidden_spread = jnp.sum(grad_spread, axis=0)
    grad_spread_low = grad_spread.astype(jnp.bfloat16)
    grad_expand_spread = matmul_left(latent_low, grad_spread_low)
    grad_latent = (grad_output + matmul_right(grad_spread_low, expand_full[1])).astype(jnp.bfloat16)
    grad_out_cross = matmul_left(decoded_low, grad_latent)
    grad_decoded = matmul_right(grad_latent, square_full[6]).astype(jnp.bfloat16)
    cross_back = galerkin_backward(
        grad_decoded,
        cross_queries,
        cross_keys,
        cross_values,
        cross_summary,
        onehot,
        mask_float,
        cross_reducer,
    )
    grad_fourier_full = matmul_left(phase_low, cross_back[0].astype(jnp.bfloat16))
    grad_pair_low = jnp.concatenate([cross_back[1], cross_back[2]], axis=1).astype(jnp.bfloat16)
    grad_pair_full = matmul_left(outer_low, grad_pair_low)
    grad_normed_out = matmul_right(grad_pair_low, pair_weight)
    grad_gain_three = jnp.sum(grad_normed_out * scaled_three, axis=0)
    grad_bias_three = jnp.sum(grad_normed_out, axis=0)
    grad_encoded = norm_back(grad_normed_out, scaled_three, root_three, vector_weight[4])
    grad_bias_middle = jnp.sum(grad_encoded, axis=0)
    grad_encoded_low = grad_encoded.astype(jnp.bfloat16)
    grad_contract_enc = matmul_left(hidden_low, grad_encoded_low)
    grad_hidden = matmul_right(grad_encoded_low, contract_full[0]) * gelu_slope(hidden_pre)
    grad_hidden_enc = jnp.sum(grad_hidden, axis=0)
    grad_hidden_low = grad_hidden.astype(jnp.bfloat16)
    grad_expand_enc = matmul_left(middle_low, grad_hidden_low)
    grad_middle = matmul_right(grad_hidden_low, expand_full[0])
    grad_gain_two = jnp.sum(grad_middle * scaled_two, axis=0)
    grad_bias_two = jnp.sum(grad_middle, axis=0)
    grad_first = grad_encoded + norm_back(grad_middle, scaled_two, root_two, vector_weight[2])
    grad_first_low = grad_first.astype(jnp.bfloat16)
    grad_out_self = matmul_left(attended_low, grad_first_low)
    grad_attended = matmul_right(grad_first_low, square_full[3]).astype(jnp.bfloat16)
    self_back = galerkin_backward(
        grad_attended,
        queries_low,
        keys_masked,
        values_low,
        self_summary,
        onehot,
        mask_float,
        self_reducer,
    )
    grad_queries = rotate_back(self_back[0].reshape(rows, H, E), cosine, sine).reshape(rows, width)
    grad_keys = rotate_back(self_back[1].reshape(rows, H, E), cosine, sine).reshape(rows, width)
    grad_joint_low = jnp.concatenate([grad_queries, grad_keys, self_back[2]], axis=1).astype(
        jnp.bfloat16
    )
    grad_joint_full = matmul_left(normed_low, grad_joint_low)
    grad_normed = matmul_right(grad_joint_low, joint_weight)
    grad_gain_one = jnp.sum(grad_normed * scaled_one, axis=0)
    grad_bias_one = jnp.sum(grad_normed, axis=0)
    grad_inputs = grad_first + norm_back(grad_normed, scaled_one, root_one, vector_weight[0])
    grad_square = jnp.stack(
        [
            grad_joint_full[:, :width],
            grad_joint_full[:, width : 2 * width],
            grad_joint_full[:, 2 * width :],
            grad_out_self,
            grad_pair_full[:, :width],
            grad_pair_full[:, width:],
            grad_out_cross,
        ]
    ).reshape(7, width * width)
    grad_expand = jnp.stack([grad_expand_enc, grad_expand_spread]).reshape(2, width * F)
    grad_contract = jnp.stack([grad_contract_enc, grad_contract_spread]).reshape(2, F * width)
    grad_fourier = grad_fourier_full.reshape(FOUR * width)
    grad_vector = jnp.stack(
        [
            grad_gain_one,
            grad_bias_one,
            grad_gain_two,
            grad_bias_two,
            grad_gain_three,
            grad_bias_three,
            grad_bias_middle,
            grad_bias_end,
        ]
    )
    grad_hidden_rows = jnp.stack([grad_hidden_enc, grad_hidden_spread])
    totals = lax.psum(
        (grad_square, grad_expand, grad_contract, grad_fourier, grad_vector, grad_hidden_rows),
        "pts",
    )
    squares = sum((jnp.sum(total_part * total_part) for total_part in totals))
    start_index = lax.axis_index("pts")
    share_square = own_share(totals[0], square_weight.shape[1], 1, start_index)
    share_expand = own_share(totals[1], expand_weight.shape[1], 1, start_index)
    share_contract = own_share(totals[2], contract_weight.shape[1], 1, start_index)
    share_fourier = own_share(totals[3], fourier_weight.shape[0], 0, start_index)
    vector_total = totals[4]
    hidden_total = totals[5]
    grad_norm = jnp.sqrt(squares)
    factor = jnp.minimum(1.0, CLIP_NORM / (grad_norm + 1e-06))
    new_square = adam_update(
        square_weight, square_first, square_second, share_square, factor, RATE_MATRIX
    )
    new_expand = adam_update(
        expand_weight, expand_first, expand_second, share_expand, factor, RATE_MATRIX
    )
    new_contract = adam_update(
        contract_weight, contract_first, contract_second, share_contract, factor, RATE_MATRIX
    )
    new_fourier = adam_update(
        fourier_weight, fourier_first, fourier_second, share_fourier, factor, RATE_MATRIX
    )
    new_vector = adam_update(
        vector_weight, vector_first, vector_second, vector_total, factor, RATE_VECTOR
    )
    new_hidden = adam_update(
        hidden_weight, hidden_first, hidden_second, hidden_total, factor, RATE_VECTOR
    )
    return (
        output.astype(jnp.bfloat16),
        grad_inputs,
        grad_norm,
        new_square[0],
        new_square[1],
        new_square[2],
        new_expand[0],
        new_expand[1],
        new_expand[2],
        new_contract[0],
        new_contract[1],
        new_contract[2],
        new_fourier[0],
        new_fourier[1],
        new_fourier[2],
        new_vector[0],
        new_vector[1],
        new_vector[2],
        new_hidden[0],
        new_hidden[1],
        new_hidden[2],
    )


GROUP = 8
TILE = 1024
PUT = 512
LANES = 128
PIECES = 8
VMEM_BYTES = 64 * 1024 * 1024


def dot(left, right):
    return jnp.dot(left, right, preferred_element_type=jnp.float32)


def dot_bt(left, right):
    return lax.dot_general(
        left, right, (((1,), (1,)), ((), ())), preferred_element_type=jnp.float32
    )


def dot_at(left, right):
    return lax.dot_general(
        left, right, (((0,), (0,)), ((), ())), preferred_element_type=jnp.float32
    )


def low(values):
    return values.astype(jnp.bfloat16)


def column_norm(values):
    inverse = 1.0 / values.shape[0]
    centred = values - jnp.sum(values, axis=0, keepdims=True) * inverse
    variance = jnp.sum(centred * centred, axis=0, keepdims=True) * inverse
    root_inv = lax.rsqrt(variance + NORM_EPS)
    return (centred * root_inv, root_inv)


def column_norm_back(upstream, scaled, root_inv, gain):
    inverse = 1.0 / upstream.shape[0]
    through = upstream * gain
    centre = jnp.sum(through, axis=0, keepdims=True) * inverse
    along = jnp.sum(through * scaled, axis=0, keepdims=True) * inverse
    return root_inv * (through - centre - scaled * along)


def gelu_both(values):
    square = values * values
    half = 0.5 + 0.5 * jnp.tanh(values * (GELU_C + (GELU_C * GELU_A) * square))
    slope = half + values * (half * (1.0 - half)) * (
        2.0 * GELU_C + (6.0 * GELU_C * GELU_A) * square
    )
    return (values * half, slope)


def turn(values, cosine, sine, sign):
    quarter = E // 4
    first_cos, second_cos = cosine[:quarter], cosine[quarter:]
    first_sin, second_sin = sine[:quarter] * sign, sine[quarter:] * sign
    parts = []
    for base in range(0, values.shape[0], E):
        one, two, three, four = (
            values[base + quarter * step : base + quarter * (step + 1)] for step in range(4)
        )
        parts += [
            one * first_cos - two * first_sin,
            two * first_cos + one * first_sin,
            three * second_cos - four * second_sin,
            four * second_cos + three * second_sin,
        ]
    return jnp.concatenate(parts, axis=0)


def compress(full):
    width = full.shape[1]
    head = lax.broadcasted_iota(jnp.int32, (E, width), 1) // E
    result = full[:E]
    for index in range(1, H):
        result = jnp.where(head == index, full[E * index : E * (index + 1)], result)
    return result


def lane_sum(values):
    result = values[:, :LANES]
    for start in range(LANES, values.shape[1], LANES):
        result = result + values[:, start : start + LANES]
    return result


def remote(source, target, send_sem, recv_sem, device):
    return pltpu.make_async_remote_copy(
        src_ref=source,
        dst_ref=target,
        send_sem=send_sem,
        recv_sem=recv_sem,
        device_id=(device,),
        device_id_type=pl.DeviceIdType.MESH,
    )


class Place:
    def __init__(self, devices):
        self.devices = devices
        self.outers = devices // GROUP
        self.me = lax.axis_index("pts")
        self.inner = lax.rem(self.me, GROUP)
        self.outer = lax.div(self.me, GROUP)
        self.core = lax.rem(self.me, 2)
        self.pair = lax.div(self.inner, 2)
        self.chips = devices // 2
        self.chip = lax.div(self.me, 2)

    def chip_at(self, step):
        return lax.rem(self.chip + step, self.chips)

    def inner_at(self, step):
        return lax.rem(self.inner + step, GROUP)

    def outer_at(self, step):
        return lax.rem(self.outer + step, self.outers)

    def pair_at(self, step):
        return lax.rem(self.pair + step, 4)

    def device(self, outer, inner):
        return outer * GROUP + inner


class Gather:
    def __init__(self, place, buffer, sems):
        self.place, self.buffer = place, buffer
        self.send, self.recv = sems

    def first(self, step, start):
        at = self.place
        slot = self.buffer.at[at.core, at.pair, at.outer if start else at.outer_at(step)]
        mine = self.buffer.at[at.core, at.pair, at.outer]
        source = at.outer if start else at.outer_at(step)
        return remote(
            mine, slot, self.send.at[0, step], self.recv.at[0, source],
            at.device(at.outer_at(step), at.inner),
        )

    def second(self, step, start):
        at = self.place
        source = at.pair if start else at.pair_at(step)
        return remote(
            self.buffer.at[at.core, at.pair], self.buffer.at[at.core, source],
            self.send.at[1, step], self.recv.at[1, source],
            at.device(at.outer, at.pair_at(step) * 2 + at.core),
        )

    def third(self, start):
        at = self.place
        source = at.core if start else 1 - at.core
        return remote(
            self.buffer.at[at.core], self.buffer.at[source], self.send.at[2, 0],
            self.recv.at[2, 0], at.device(at.outer, at.pair * 2 + 1 - at.core),
        )

    def start_first(self):
        for step in range(1, self.place.outers):
            self.first(step, True).start()

    def start_second(self):
        for step in range(1, self.place.outers):
            self.first(step, False).wait()
        for step in range(1, 4):
            self.second(step, True).start()

    def start_third(self):
        for step in range(1, 4):
            self.second(step, False).wait()
        self.third(True).start()

    def finish(self):
        self.third(False).wait()


class ChipSum:
    def __init__(self, place, scratch, key):
        self.place = place
        self.full, self.half, self.others = (
            getattr(scratch, name + key) for name in ("chip_full_", "chip_half_", "chip_others_")
        )
        self.send, self.recv = getattr(scratch, f"sem_{key}s"), getattr(scratch, f"sem_{key}r")

    def swap(self):
        at = self.place
        return remote(
            self.full.at[1 - at.core], self.half, self.send.at[0, 0], self.recv.at[0, 0],
            at.chip * 2 + 1 - at.core,
        )

    def cross(self, step, start):
        at = self.place
        source = at.chip if start else at.chip_at(step)
        return remote(
            self.half.at[at.chip_at(step)], self.others.at[source], self.send.at[1, step],
            self.recv.at[1, source], at.chip_at(step) * 2 + at.core,
        )

    def start(self):
        self.swap().start()

    def middle(self):
        at = self.place
        self.swap().wait()
        self.half[...] = low(
            self.full[at.core].astype(jnp.float32) + self.half[...].astype(jnp.float32)
        )
        for step in range(1, at.chips):
            self.cross(step, True).start()

    def total(self):
        at = self.place
        total = self.half[at.chip].astype(jnp.float32)
        for step in range(1, at.chips):
            self.cross(step, False).wait()
            total = total + self.others[at.chip_at(step)].astype(jnp.float32)
        return total


class TableSum(ChipSum):
    def __init__(self, place, scratch):
        super().__init__(place, scratch, "t")
        self.s = scratch

    def share(self, step, start, result):
        at = self.place
        source = at.chip if start else at.chip_at(step)
        return remote(
            result.at[at.core, at.chip], result.at[at.core, source], self.send.at[2, step],
            self.recv.at[2, source], at.chip_at(step) * 2 + at.core,
        )

    def swap_back(self, start, result):
        at = self.place
        source = at.core if start else 1 - at.core
        return remote(
            result.at[at.core], result.at[source], self.send.at[3, 0], self.recv.at[3, 0],
            at.chip * 2 + 1 - at.core,
        )

    def start(self):
        s = self.s
        table = low(dot(s.spread[...], s.per_block[...]))
        for chunk in range(self.place.devices):
            self.full[chunk % 2, chunk // 2] = table[chunk * 16 : (chunk + 1) * 16]
        super().start()

    def late(self, result):
        at, s = self.place, self.s
        result[at.core, at.chip] = low(self.total() * s.inverse[0:1, :])
        for step in range(1, at.chips):
            self.share(step, True, result).start()

    def last(self, result):
        for step in range(1, self.place.chips):
            self.share(step, False, result).wait()
        self.swap_back(True, result).start()

    def finish(self, result):
        self.swap_back(False, result).wait()


class GradSum:
    def __init__(self, place, scratch, key, first):
        self.place = place
        self.half, self.quarter, self.last = (
            getattr(scratch, name + key) for name in ("half_", "quarter_", "last_")
        )
        self.full = scratch.gather_two.at[:, :, :, first : first + self.last.shape[1]]
        self.send, self.recv = getattr(scratch, f"sem_{key}s"), getattr(scratch, f"sem_{key}r")

    def swap(self):
        at = self.place
        return remote(
            self.full.at[1 - at.core], self.half, self.send.at[0, 0], self.recv.at[0, 0],
            at.device(at.outer, at.pair * 2 + 1 - at.core),
        )

    def across(self, step, start):
        at = self.place
        source = at.pair if start else at.pair_at(step)
        return remote(
            self.half.at[at.pair_at(step)], self.quarter.at[source], self.send.at[1, step],
            self.recv.at[1, source], at.device(at.outer, at.pair_at(step) * 2 + at.core),
        )

    def along(self, step, start):
        at = self.place
        source = at.outer if start else at.outer_at(step)
        return remote(
            self.quarter.at[at.pair, at.outer_at(step)], self.last.at[source], self.send.at[2, step],
            self.recv.at[2, source], at.device(at.outer_at(step), at.inner),
        )

    def start(self, chunk_of):
        at = self.place

        @pl.loop(0, at.devices)
        def _(chunk):
            inner = lax.rem(chunk, GROUP)
            self.full[lax.rem(inner, 2), lax.div(inner, 2), lax.div(chunk, GROUP)] = low(
                chunk_of(chunk)
            )

        self.swap().start()

    def second(self):
        at = self.place
        self.swap().wait()

        @pl.loop(0, 4)
        def _(pair):
            self.half[pair] = low(
                self.full[at.core, pair].astype(jnp.float32) + self.half[pair].astype(jnp.float32)
            )

        for step in range(1, 4):
            self.across(step, True).start()

    def third(self):
        at = self.place
        total = self.half[at.pair].astype(jnp.float32)
        for step in range(1, 4):
            self.across(step, False).wait()
            total = total + self.quarter[at.pair_at(step)].astype(jnp.float32)
        self.quarter[at.pair] = low(total)
        for step in range(1, at.outers):
            self.along(step, True).start()

    def finish(self):
        at = self.place
        total = self.quarter[at.pair, at.outer].astype(jnp.float32)
        for step in range(1, at.outers):
            self.along(step, False).wait()
            total = total + self.last[at.outer_at(step)].astype(jnp.float32)
        return total


def layer_kernel(names, devices, *refs):
    s = types.SimpleNamespace(**dict(zip(names, refs)))
    at = Place(devices)
    points, width = s.features_far.shape
    tiles = points // TILE
    blocks = points // BLOCK
    share = width // devices
    tile_blocks = TILE // BLOCK
    f32 = jnp.float32

    barrier = pltpu.get_barrier_semaphore()
    pl.semaphore_signal(
        barrier, inc=1, device_id=(at.chip * 2 + 1 - at.core,),
        device_id_type=pl.DeviceIdType.MESH,
    )
    for step in range(1, at.chips):
        pl.semaphore_signal(
            barrier, inc=1, device_id=(at.chip_at(step) * 2 + at.core,),
            device_id_type=pl.DeviceIdType.MESH,
        )

    def tile_load(source, tile, first):
        slot = lax.rem(tile, 2)
        where = pl.ds(pl.multiple_of(tile * TILE, TILE), TILE)
        return pltpu.make_async_copy(
            source.at[where, :], s.load_slots.at[slot], s.sem_in.at[first + slot]
        )

    for tile in range(2):
        tile_load(s.features_far, tile, 0).start()

    class Aside:
        def __init__(self, first, *buffers):
            self.pairs = []
            row = first
            for buffer in buffers:
                for start in range(0, buffer.shape[0], LANES):
                    near = buffer.at[start : start + LANES]
                    far = s.aside.at[row : row + LANES]
                    self.pairs.append((near, far, s.sem_aside.at[row // LANES]))
                    row += LANES

        def store(self):
            for near, far, sem in self.pairs:
                pltpu.make_async_copy(near, far, sem).start()

        def stored(self):
            for near, far, sem in self.pairs:
                pltpu.make_async_copy(near, far, sem).wait()

        def load(self):
            for near, far, sem in self.pairs:
                pltpu.make_async_copy(far, near, sem).start()

        def loaded(self):
            for near, far, sem in self.pairs:
                pltpu.make_async_copy(far, near, sem).wait()

    aside_a = Aside(0, s.u1, s.kv)
    aside_b = Aside(3 * width, s.e1, s.o, s.u2, s.u3)

    def columns(tile):
        return pl.ds(pl.multiple_of(tile * TILE, TILE), TILE)

    def block_columns(block):
        return pl.ds(pl.multiple_of(block * BLOCK, BLOCK), BLOCK)

    def column(index):
        return s.cols[:, index : index + 1]

    def hidden_column(index):
        return jnp.concatenate([column(8 + 2 * index), column(9 + 2 * index)], axis=0)

    def out_copy(piece, target, slots, index):
        slot = lax.rem(piece, 2)
        where = pl.ds(pl.multiple_of(piece * PUT, PUT), PUT)
        return pltpu.make_async_copy(slots.at[slot], target.at[where, :], s.sem_out.at[index, slot])

    def put_out(tile, target, slots, index, values):
        for step in range(TILE // PUT):
            piece = tile * (TILE // PUT) + step

            @pl.when(piece >= 2)
            def _():
                out_copy(piece - 2, target, slots, index).wait()

            slots[lax.rem(piece, 2)] = values[:, step * PUT : (step + 1) * PUT].T
            out_copy(piece, target, slots, index).start()

    def end_out(target, slots, index):
        for piece in range(points // PUT - 2, points // PUT):
            out_copy(piece, target, slots, index).wait()

    for matrix in range(7):
        for row in range(share):
            s.pack[matrix * share + row : matrix * share + row + 1, :] = s.square_weight[
                matrix : matrix + 1, row * width : (row + 1) * width
            ]
    for matrix in range(2):
        for half in range(2):
            for row in range(share):
                place = (7 + 2 * matrix + half) * share + row
                start = row * F + half * width
                s.pack[place : place + 1, :] = s.expand_weight[
                    matrix : matrix + 1, start : start + width
                ]
        for row in range(2 * share):
            place = (11 + 2 * matrix) * share + row
            s.pack[place : place + 1, :] = s.contract_weight[
                matrix : matrix + 1, row * width : (row + 1) * width
            ]
    s.pack[15 * share : 16 * share, :LANES] = s.fourier_weight[...]
    s.pack[15 * share : 16 * share, LANES:] = jnp.zeros((share, LANES), f32)
    live = s.point_mask[...].astype(f32)
    counts = dot_bt(jnp.ones((8, LANES), jnp.bfloat16), low(live))
    s.pack[15 * share : 15 * share + 1, LANES : LANES + blocks] = counts[:1]
    lane = lax.broadcasted_iota(jnp.int32, (1, LANES), 1)
    wide_block = lax.broadcasted_iota(jnp.int32, (1, E * blocks), 1) // E
    item_row = jnp.zeros((1, LANES), f32)
    item_wide = jnp.zeros((1, E * blocks), jnp.int32)
    for block in range(blocks):
        item_row = jnp.where(lane == block, s.items[block].astype(f32), item_row)
        item_wide = jnp.where(wide_block == block, s.items[block], item_wide)
    s.pack[15 * share + 1 : 15 * share + 2, LANES:] = item_row
    packed = low(s.pack[...])
    split = s.gather_one.shape[3]
    s.gather_one[at.core, at.pair, at.outer] = packed[:split]
    s.gather_two[at.core, at.pair, at.outer] = packed[split:]

    pl.semaphore_wait(barrier, at.chips)
    one = Gather(at, s.gather_one, (s.sem_g1s, s.sem_g1r))
    two = Gather(at, s.gather_two, (s.sem_g2s, s.sem_g2r))
    one.start_first()

    row_at = lax.broadcasted_iota(jnp.int32, (width, width), 0)
    lane_at = lax.broadcasted_iota(jnp.int32, (width, width), 1)
    s.eye[...] = jnp.where(row_at == lane_at, 1.0, 0.0).astype(jnp.bfloat16)
    s.heads[...] = jnp.where(row_at // E == lane_at // E, 1.0, 0.0).astype(jnp.bfloat16)
    s.small[...] = jnp.zeros(s.small.shape, f32)
    s.small[0:8, :] = s.vector_weight[...]
    for row in range(2):
        for half in range(2):
            s.small[8 + 2 * row + half : 9 + 2 * row + half, :] = s.hidden_weight[
                row : row + 1, half * width : (half + 1) * width
            ]
    s.small[12:14, : FOUR // 2] = s.fourier_basis[...]
    s.cols[...] = s.small[...].T
    rows_wide = lax.broadcasted_iota(jnp.int32, s.spread.shape, 0)
    lanes_wide = lax.broadcasted_iota(jnp.int32, s.spread.shape, 1)
    s.spread[...] = jnp.where(
        (item_wide == rows_wide // E) & (rows_wide % E == lanes_wide % E), 1.0, 0.0
    ).astype(jnp.bfloat16)
    s.vector_sum[...] = jnp.zeros(s.vector_sum.shape, f32)
    speed = (lax.broadcasted_iota(jnp.int32, (E // 4, 1), 0).astype(f32) + 1.0) * (
        math.pi / (E // 4)
    )

    def add_sum(index, values):
        for part in range(values.shape[0] // width):
            s.vector_sum[index + part] += lane_sum(values[part * width : (part + 1) * width])

    def turned_load(source, tile, first):
        tile_load(source, tile, first).wait()
        turned = dot_bt(s.eye[...], s.load_slots[lax.rem(tile, 2)])

        @pl.when(tile + 2 < tiles)
        def _():
            tile_load(source, tile + 2, first).start()

        return turned

    def before(tile, _):
        where = columns(tile)
        turned = turned_load(s.features_far, tile, 0)
        s.turned[:, where] = low(turned)
        scaled, root = column_norm(turned)
        s.root_one[0:1, where] = root
        s.u1[:, where] = low(scaled * column(0) + column(1))
        x_row, y_row = s.coords[0:1, where], s.coords[1:2, where]
        angles = jnp.concatenate([speed * x_row, speed * y_row], axis=0)
        s.cosine[:, where] = jnp.cos(angles)
        s.sine[:, where] = jnp.sin(angles)
        basis = s.cols[: FOUR // 2, :]
        phases = 2.0 * math.pi * (basis[:, 12:13] * x_row + basis[:, 13:14] * y_row)
        s.phi[:, where] = low(jnp.concatenate([jnp.cos(phases), jnp.sin(phases)], axis=0))
        for block in range(tile_blocks):
            s.mask[0:1, pl.ds(pl.multiple_of(tile * TILE + block * BLOCK, BLOCK), BLOCK)] = (
                s.point_mask[pl.ds(tile * tile_blocks + block, 1), :].astype(f32)
            )

    lax.fori_loop(0, tiles // 4, before, None)
    one.start_second()
    two.start_first()
    lax.fori_loop(tiles // 4, tiles // 2, before, None)
    one.start_third()
    two.start_second()
    lax.fori_loop(tiles // 2, tiles, before, None)
    one.finish()

    group = 16 // share

    def chunk_pair(buffer, index):
        parts = []
        for step in range(group):
            chunk = index * group + step
            inner = lax.rem(chunk, GROUP)
            parts.append(
                buffer[lax.rem(inner, 2), lax.div(inner, 2), lax.div(chunk, GROUP)].astype(f32)
            )
        return parts

    def join(parts, piece):
        return low(
            jnp.concatenate([part[piece * share : (piece + 1) * share] for part in parts], axis=0)
        )

    @pl.loop(0, devices // group)
    def _(index):
        parts = chunk_pair(s.gather_one, index)
        where = pl.ds(pl.multiple_of(index * 16, 16), 16)
        for piece in range(3):
            s.w_qkv[where, piece * width : (piece + 1) * width] = join(parts, piece)
        s.w_o[where, :] = join(parts, 3)

    def flip(matrix):
        return low(dot_bt(s.eye[...], matrix))

    for piece in range(3):
        s.t_qkv[piece * width : (piece + 1) * width, :] = flip(
            s.w_qkv[:, piece * width : (piece + 1) * width]
        )
    s.t_o[...] = flip(s.w_o[...])

    def block_product(left, right):
        return compress(dot_bt(left, right))

    def put_products(tile, left, right):
        for block in range(tile_blocks):
            lanes = slice(block * BLOCK, (block + 1) * BLOCK)
            where = pl.ds(pl.multiple_of((tile * tile_blocks + block) * E, E), E)
            s.per_block[where, :] = low(block_product(left[:, lanes], right[:, lanes]))

    def summary(table, tile, block):
        item = s.items[tile * tile_blocks + block]
        rows = jnp.concatenate([table[0, item], table[1, item]], axis=0)
        return jnp.concatenate([rows] * H, axis=0) * s.heads[...]

    def per_block(tile, function):
        return jnp.concatenate([function(block) for block in range(tile_blocks)], axis=1)

    def lanes_of(block):
        return slice(block * BLOCK, (block + 1) * BLOCK)

    def phase_a(tile, _):
        where = columns(tile)
        projected = dot(s.t_qkv[...], s.u1[:, where])
        cosine, sine = s.cosine[:, where], s.sine[:, where]
        s.q[:, where] = low(turn(projected[:width], cosine, sine, 1.0))
        keys = low(turn(projected[width : 2 * width], cosine, sine, 1.0) * s.mask[0:1, where])
        values = low(projected[2 * width :])
        s.kv[:width, where] = keys
        s.kv[width:, where] = values
        put_products(tile, values, keys)

    lax.fori_loop(0, tiles, phase_a, None)
    table_sum = TableSum(at, s)
    table_sum.start()
    aside_a.store()
    table_sum.middle()
    two.start_third()

    def take_two(index, carried):
        parts = chunk_pair(s.gather_two, index)
        where = pl.ds(pl.multiple_of(index * 16, 16), 16)
        for piece in range(2):
            s.w_kv[where, piece * width : (piece + 1) * width] = join(parts, piece)
            s.w_w1[where, piece * width : (piece + 1) * width] = join(parts, 3 + piece)
            s.w_p1[where, piece * width : (piece + 1) * width] = join(parts, 5 + piece)
        s.w_do[where, :] = join(parts, 2)
        both = pl.ds(pl.multiple_of(index * 32, 32), 32)
        for piece, target in ((7, s.w_w2), (9, s.w_p2)):
            target[both, :] = low(
                jnp.concatenate([part[piece * share : (piece + 2) * share] for part in parts], axis=0)
            )
        for part in parts:
            count_row = part[11 * share : 11 * share + 1, LANES:]
            item_at = part[11 * share + 1 : 11 * share + 2, LANES:]
            carried = carried + jnp.where(item_at == own_item, count_row, 0.0)
        s.fourier[where, :] = jnp.concatenate(
            [part[11 * share : 12 * share, :LANES] for part in parts], axis=0
        )
        return carried

    two.finish()
    own_item = at.chip.astype(f32)
    found = lax.fori_loop(0, devices // group, take_two, jnp.zeros((1, LANES), f32))
    s.inverse[0:1, :] = jnp.broadcast_to(1.0 / jnp.sum(found, axis=1, keepdims=True), (1, width))
    w_dq = jnp.concatenate(
        [s.fourier[pl.ds(0, FOUR, stride=2), :], s.fourier[pl.ds(1, FOUR, stride=2), :]], axis=1
    )
    s.t_dq[...] = low(w_dq.T)
    table_sum.late(s.table_self)
    for piece in range(2):
        cols = slice(piece * width, (piece + 1) * width)
        s.t_kv[cols, :] = flip(s.w_kv[:, cols])
        s.t_w1[cols, :] = flip(s.w_w1[:, cols])
        s.t_p1[cols, :] = flip(s.w_p1[:, cols])
        s.t_w2[:, cols] = flip(s.w_w2[cols, :])
        s.t_p2[:, cols] = flip(s.w_p2[cols, :])
    s.t_do[...] = flip(s.w_do[...])
    table_sum.last(s.table_self)
    table_sum.finish(s.table_self)

    def phase_b(tile, _):
        where = columns(tile)
        mask = s.mask[0:1, where]
        queries = s.q[:, where]
        mixed = per_block(
            tile, lambda b: dot(summary(s.table_self, tile, b), queries[:, lanes_of(b)])
        )
        attended = low(mixed * mask)
        s.o[:, where] = attended
        first_sum = s.turned[:, where].astype(f32) + dot(s.t_o[...], attended)
        scaled_two, root_two = column_norm(first_sum)
        s.root_two[0:1, where] = root_two
        s.xh2[:, where] = low(scaled_two)
        middle = low(scaled_two * column(2) + column(3))
        s.u2[:, where] = middle
        hidden_pre = dot(s.t_w1[...], middle) + hidden_column(0)
        hidden = low(gelu(hidden_pre))
        s.e1[:, where] = hidden
        s.slope[:, where] = low(hidden_pre)
        encoded = first_sum + dot(s.t_w2[...], hidden) + column(6)
        scaled_three, root_three = column_norm(encoded)
        s.root_three[0:1, where] = root_three
        s.xh3[:, where] = low(scaled_three)
        outer = low(scaled_three * column(4) + column(5))
        s.u3[:, where] = outer
        pair = dot(s.t_kv[...], outer)
        keys = low(pair[:width] * mask)
        values = low(pair[width:])
        s.kvd[:width, where] = keys
        s.kvd[width:, where] = values
        put_products(tile, values, keys)

    lax.fori_loop(0, tiles, phase_b, None)
    table_sum.start()
    aside_b.store()
    table_sum.middle()

    for tile in range(2):
        tile_load(s.cotangent_far, tile, 2).start()
    aside_a.stored()

    def cross_inputs(tile, _):
        where = columns(tile)
        s.qd[:, where] = low(dot(s.t_dq[...], s.phi[:, where]))
        turned = turned_load(s.cotangent_far, tile, 2)
        add_sum(7, turned)
        turned = low(turned)
        s.u1[:, where] = turned
        s.kv[:, where] = low(dot(s.w_p2[...], turned))

    def slopes(tile, _):
        where = columns(tile)
        s.slope[:, where] = low(gelu_slope(s.slope[:, where].astype(f32)))

    lax.fori_loop(0, tiles, cross_inputs, None)
    table_sum.late(s.table_other)
    lax.fori_loop(0, tiles, slopes, None)
    aside_b.stored()
    table_sum.last(s.table_other)
    table_sum.finish(s.table_other)

    def phase_c(tile, _):
        where = columns(tile)
        mask = s.mask[0:1, where]
        queries = s.qd[:, where]
        tables = [summary(s.table_other, tile, block) for block in range(tile_blocks)]
        decoded = low(
            per_block(tile, lambda b: dot(tables[b], queries[:, lanes_of(b)])) * mask
        )
        s.u2[:, where] = decoded
        latent_low = low(dot(s.t_do[...], decoded))
        s.o[:, where] = latent_low
        hidden, slope = gelu_both(dot(s.t_p1[...], latent_low) + hidden_column(1))
        s.e1[:, where] = low(hidden)
        grad_spread = s.kv[:, where].astype(f32) * slope
        add_sum(10, grad_spread)
        grad_spread = low(grad_spread)
        s.kv[:, where] = grad_spread
        grad_latent = low(s.u1[:, where].astype(f32) + dot(s.w_p1[...], grad_spread))
        s.u3[:, where] = grad_latent
        grad_decoded = low(dot(s.w_do[...], grad_latent) * mask)
        put_products(tile, grad_decoded, queries)
        s.qd[:, where] = grad_decoded

    lax.fori_loop(0, tiles, phase_c, None)
    table_sum.start()
    table_sum.middle()

    def cross_query_grads(tile, _):
        where = columns(tile)
        upstream = s.qd[:, where]
        grad = per_block(
            tile, lambda b: dot_at(summary(s.table_other, tile, b), upstream[:, lanes_of(b)])
        )
        s.qd[:, where] = low(grad)

    def outputs(tile, _):
        where = columns(tile)
        output = dot(s.t_do[...], s.u2[:, where]) + dot(s.t_p2[...], s.e1[:, where]) + column(7)
        put_out(tile, s.layer_output, s.output_slots, 0, low(output))

    lax.fori_loop(0, tiles, cross_query_grads, None)
    s.grad_dq[...] = dot_bt(s.phi[...], s.qd[...])
    s.fourier[pl.ds(0, FOUR, stride=2), :] = s.grad_dq[:, :LANES]
    s.fourier[pl.ds(1, FOUR, stride=2), :] = s.grad_dq[:, LANES:]
    s.grad_do[...] = dot_bt(s.u2[...], s.u3[...])
    table_sum.late(s.table_third)
    s.grad_p1[...] = dot_bt(s.o[...], s.kv[...])
    s.grad_p2[...] = dot_bt(s.e1[...], s.u1[...])
    zeros = jnp.zeros((share, LANES), f32)

    def rows_of(chunk, count=1):
        size = share * count
        return pl.ds(pl.multiple_of(chunk * size, size), size)

    def chunk_c(chunk):
        where = rows_of(chunk)
        return jnp.concatenate(
            [
                s.grad_do[where, :],
                s.grad_p1[where, :width],
                s.grad_p1[where, width:],
                s.grad_p2[rows_of(chunk, 2), :],
                jnp.concatenate([s.fourier[where, :], zeros], axis=1),
            ],
            axis=0,
        )

    sum_c = GradSum(at, s, "c", 0)
    sum_c.start(chunk_c)
    lax.fori_loop(0, tiles, outputs, None)
    end_out(s.layer_output, s.output_slots, 0)
    table_sum.last(s.table_third)
    aside_a.load()
    aside_b.load()
    sum_c.second()
    table_sum.finish(s.table_third)

    def phase_d(tile, _):
        where = columns(tile)
        mask = s.mask[0:1, where]
        keys, values = s.kvd[:width, where], s.kvd[width:, where]
        tables = [summary(s.table_third, tile, block) for block in range(tile_blocks)]
        grad_keys = per_block(tile, lambda b: dot_at(tables[b], values[:, lanes_of(b)])) * mask
        grad_values = per_block(tile, lambda b: dot(tables[b], keys[:, lanes_of(b)]))
        grad_pair = low(jnp.concatenate([grad_keys, grad_values], axis=0))
        s.kvd[:, where] = grad_pair
        grad_outer = dot(s.w_kv[...], grad_pair)
        scaled = s.xh3[:, where].astype(f32)
        add_sum(4, grad_outer * scaled)
        add_sum(5, grad_outer)
        grad_encoded = column_norm_back(
            grad_outer, scaled, s.root_three[0:1, where], column(4)
        )
        add_sum(6, grad_encoded)
        grad_encoded_low = low(grad_encoded)
        s.xh3[:, where] = grad_encoded_low
        grad_hidden = dot(s.w_w2[...], grad_encoded_low) * s.slope[:, where].astype(f32)
        add_sum(8, grad_hidden)
        grad_hidden = low(grad_hidden)
        s.slope[:, where] = grad_hidden
        grad_middle = dot(s.w_w1[...], grad_hidden)
        scaled = s.xh2[:, where].astype(f32)
        add_sum(2, grad_middle * scaled)
        add_sum(3, grad_middle)
        grad_first = grad_encoded + column_norm_back(
            grad_middle, scaled, s.root_two[0:1, where], column(2)
        )
        grad_first = low(grad_first)
        s.xh2[:, where] = grad_first
        grad_attended = low(dot(s.w_o[...], grad_first) * mask)
        s.qd[:, where] = grad_attended
        put_products(tile, grad_attended, s.q[:, where])

    lax.fori_loop(0, tiles // 2, phase_d, None)
    sum_c.third()
    lax.fori_loop(tiles // 2, tiles, phase_d, None)
    table_sum.start()
    s.grads_c[...] = sum_c.finish()
    table_sum.middle()
    aside_a.loaded()
    aside_b.loaded()

    def query_grads(tile, _):
        where = columns(tile)
        upstream = s.qd[:, where]
        grad = per_block(
            tile, lambda b: dot_at(summary(s.table_self, tile, b), upstream[:, lanes_of(b)])
        )
        s.q[:, where] = low(turn(grad, s.cosine[:, where], s.sine[:, where], -1.0))

    lax.fori_loop(0, tiles, query_grads, None)
    s.grad_o[...] = dot_bt(s.o[...], s.xh2[...])
    s.grad_qkv[:, :width] = dot_bt(s.u1[...], s.q[...])
    table_sum.late(s.table_other)
    s.grad_kv[...] = dot_bt(s.u3[...], s.kvd[...])
    s.grad_w2[...] = dot_bt(s.e1[...], s.xh3[...])
    s.grad_w1[...] = dot_bt(s.u2[...], s.slope[...])

    def chunk_d(chunk):
        where = rows_of(chunk)
        return jnp.concatenate(
            [
                s.grad_kv[where, :width],
                s.grad_kv[where, width:],
                s.grad_o[where, :],
                s.grad_w1[where, :width],
                s.grad_w1[where, width:],
                s.grad_w2[rows_of(chunk, 2), :],
                s.grad_qkv[where, :width],
            ],
            axis=0,
        )

    sum_d = GradSum(at, s, "d", 0)
    sum_d.start(chunk_d)
    table_sum.last(s.table_other)
    table_sum.finish(s.table_other)
    sum_d.second()

    def phase_e(tile, _):
        where = columns(tile)
        mask = s.mask[0:1, where]
        keys, values = s.kv[:width, where], s.kv[width:, where]
        tables = [summary(s.table_other, tile, block) for block in range(tile_blocks)]
        grad_keys = per_block(tile, lambda b: dot_at(tables[b], values[:, lanes_of(b)])) * mask
        grad_values = low(per_block(tile, lambda b: dot(tables[b], keys[:, lanes_of(b)])))
        s.kv[:width, where] = low(turn(grad_keys, s.cosine[:, where], s.sine[:, where], -1.0))
        s.kv[width:, where] = grad_values

    lax.fori_loop(0, tiles, phase_e, None)
    s.grad_qkv[:, width:] = dot_bt(s.u1[...], s.kv[...])
    sum_e = ChipSum(at, s, "e")

    @pl.loop(0, devices)
    def _(chunk):
        where = rows_of(chunk)
        s.chip_full_e[lax.rem(chunk, 2), lax.div(chunk, 2)] = low(
            jnp.concatenate(
                [s.grad_qkv[where, width : 2 * width], s.grad_qkv[where, 2 * width :]], axis=0
            )
        )

    sum_e.start()

    def phase_f(tile, _):
        where = columns(tile)
        grad_normed = dot(
            s.w_qkv[...], jnp.concatenate([s.q[:, where], s.kv[:, where]], axis=0)
        )
        turned = s.turned[:, where].astype(f32)
        root = s.root_one[0:1, where]
        scaled = (turned - jnp.sum(turned, axis=0, keepdims=True) * (1.0 / width)) * root
        add_sum(0, grad_normed * scaled)
        add_sum(1, grad_normed)
        grad_input = s.xh2[:, where].astype(f32) + column_norm_back(
            grad_normed, scaled, root, column(0)
        )
        put_out(tile, s.input_grad, s.input_slots, 1, grad_input)

    sum_d.third()
    sum_e.middle()
    lax.fori_loop(0, tiles, phase_f, None)
    end_out(s.input_grad, s.input_slots, 1)
    s.grads_d[...] = sum_d.finish()
    s.grads_e[...] = sum_e.total()
    squares = sum(
        jnp.sum(grads[...] * grads[...], axis=0, keepdims=True)
        for grads in (s.grads_c, s.grads_d, s.grads_e)
    )

    lane_wide = lax.broadcasted_iota(jnp.int32, (width, LANES), 1)
    sums = jnp.zeros((width, LANES), f32)
    for index in range(12):
        sums = jnp.where(
            lane_wide == index, jnp.sum(s.vector_sum[index], axis=1, keepdims=True), sums
        )
    s.vector_cols[...] = sums
    turned_sums = s.vector_cols[...].T
    high = low(squares).astype(f32)
    s.final_near[at.core] = low(
        jnp.concatenate(
            [turned_sums[:12], high, squares - high, jnp.zeros((2, width), f32)], axis=0
        )
    )

    def final_core(start):
        source = at.core if start else 1 - at.core
        return remote(
            s.final_near.at[at.core], s.final_near.at[source], s.sem_fs.at[0, 0],
            s.sem_fr.at[0, 0], at.chip * 2 + 1 - at.core,
        )

    def final_chips(step, start):
        source = at.chip if start else at.chip_at(step)
        return remote(
            s.final_far.at[at.chip], s.final_far.at[source], s.sem_fs.at[1, step],
            s.sem_fr.at[1, source], at.chip_at(step) * 2 + at.core,
        )

    final_core(True).start()
    final_core(False).wait()
    total = s.final_near[0].astype(f32) + s.final_near[1].astype(f32)
    square_sum = total[12:13] + total[13:14]
    high = low(square_sum).astype(f32)
    s.final_far[at.chip] = low(
        jnp.concatenate([total[:12], high, square_sum - high, total[14:]], axis=0)
    )
    for step in range(1, at.chips):
        final_chips(step, True).start()
    for step in range(1, at.chips):
        final_chips(step, False).wait()
    total = s.final_far[0].astype(f32)
    for index in range(1, at.chips):
        total = total + s.final_far[index].astype(f32)
    s.vector_all[...] = total


def update_kernel(share, *refs):
    sources, refs = refs[:2], refs[2:]
    grads_c, grads_d, grads_e, vector_all = refs[:4]
    weights_far = refs[4:22]
    targets = refs[22:24]
    norm_out = refs[24]
    results = refs[25:43]
    flat_square, flat_expand, flat_contract, *held, sems, weight_sems = refs[43:]
    held, weights = held[:2], held[2:]
    weight_loads = [
        pltpu.make_async_copy(far, near, weight_sems.at[index])
        for index, (far, near) in enumerate(zip(weights_far, weights))
    ]
    loads, stores = [], []
    for index, (source, target) in enumerate(zip(sources, targets)):
        size = source.shape[0] // PIECES
        for piece in range(PIECES):
            where = slice(piece * size, (piece + 1) * size)
            own = held[index].at[where]
            loads.append(pltpu.make_async_copy(source.at[where], own, sems.at[0, index, piece]))
            stores.append(pltpu.make_async_copy(own, target.at[where], sems.at[1, index, piece]))
    for load in weight_loads + loads:
        load.start()
    width = grads_c.shape[1]
    places = [(grads_d, 7), (grads_e, 0), (grads_e, 1), (grads_d, 2), (grads_d, 0), (grads_d, 1), (grads_c, 0)]
    for matrix, (source, piece) in enumerate(places):
        for row in range(share):
            start = piece * share + row
            flat_square[matrix : matrix + 1, row * width : (row + 1) * width] = source[
                start : start + 1, :
            ]
    for matrix, (source, piece) in enumerate(((grads_d, 3), (grads_c, 1))):
        for half in range(2):
            for row in range(share):
                start = (piece + half) * share + row
                target = row * F + half * width
                flat_expand[matrix : matrix + 1, target : target + width] = source[
                    start : start + 1, :
                ]
    for matrix, (source, piece) in enumerate(((grads_d, 5), (grads_c, 3))):
        for row in range(2 * share):
            start = piece * share + row
            flat_contract[matrix : matrix + 1, row * width : (row + 1) * width] = source[
                start : start + 1, :
            ]
    fourier = grads_c[5 * share : 6 * share, :LANES]
    turned = vector_all[...]
    rows = jnp.sum(turned[:12] * turned[:12], axis=0, keepdims=True) + turned[12:13] + turned[13:14]
    norm = jnp.sqrt(jnp.sum(rows, axis=1, keepdims=True))
    norm_out[...] = norm
    factor = jnp.minimum(1.0, CLIP_NORM / (norm + 1e-06))
    hidden = jnp.concatenate(
        [
            jnp.concatenate([turned[8:9], turned[9:10]], axis=1),
            jnp.concatenate([turned[10:11], turned[11:12]], axis=1),
        ],
        axis=0,
    )
    for load in weight_loads:
        load.wait()
    grads = (flat_square[...], flat_expand[...], flat_contract[...], fourier, turned[:8], hidden)
    rates = (RATE_MATRIX,) * 4 + (RATE_VECTOR,) * 2
    for index, (grad, rate) in enumerate(zip(grads, rates)):
        weight, first, second = (weights[3 * index + part][...] for part in range(3))
        values = adam_update(weight, first, second, grad, factor, rate)
        for part in range(3):
            results[3 * index + part][...] = values[part]
    for load, store in zip(loads, stores):
        load.wait()
        store.start()
    for store in stores:
        store.wait()


def fused(devices, features, coords, fourier_basis, block_items, point_mask, cotangent, *weights):
    points, width = features.shape
    blocks = points // BLOCK
    outers = devices // GROUP
    share = width // devices
    items = points * devices // ITEM_PTS
    bf16, f32 = jnp.bfloat16, jnp.float32
    square, expand, contract, fourier, vector, hidden = (weights[3 * i] for i in range(6))
    vmem = lambda shape, dtype: pltpu.VMEM(shape, dtype)
    inputs = {
        "items": block_items,
        "features_far": features,
        "coords": coords,
        "fourier_basis": fourier_basis,
        "point_mask": point_mask.reshape(blocks, BLOCK),
        "cotangent_far": cotangent,
        "square_weight": square,
        "expand_weight": expand,
        "contract_weight": contract,
        "fourier_weight": fourier.reshape(share, LANES),
        "vector_weight": vector,
        "hidden_weight": hidden,
    }
    rows_c, rows_d, rows_e = 6 * share, 8 * share, 2 * share
    chips = devices // 2
    outputs = {
        "layer_output": ((points, width), bf16),
        "input_grad": ((points, width), f32),
        "grads_c": ((rows_c, width), f32),
        "grads_d": ((rows_d, width), f32),
        "grads_e": ((rows_e, width), f32),
        "vector_all": ((16, width), f32),
        "aside": ((8 * width, points), bf16),
    }
    tall = lambda rows: vmem((rows, points), bf16)
    scratch = {
        "pack": vmem((16 * share, width), f32),
        "gather_one": vmem((2, 4, outers, 4 * share, width), bf16),
        "gather_two": vmem((2, 4, outers, 12 * share, width), bf16),
        "eye": vmem((width, width), bf16),
        "heads": vmem((width, width), bf16),
        "small": vmem((LANES, width), f32),
        "cols": vmem((width, LANES), f32),
        "spread": vmem((items * E, blocks * E), bf16),
        "vector_sum": vmem((12, width, LANES), f32),
        "vector_cols": vmem((width, LANES), f32),
        "grad_qkv": vmem((width, 3 * width), f32),
        "grad_o": vmem((width, width), f32),
        "grad_kv": vmem((width, 2 * width), f32),
        "grad_do": vmem((width, width), f32),
        "grad_w1": vmem((width, F), f32),
        "grad_p1": vmem((width, F), f32),
        "grad_w2": vmem((F, width), f32),
        "grad_p2": vmem((F, width), f32),
        "grad_dq": vmem((FOUR, width), f32),
        "fourier": vmem((2 * FOUR, LANES), f32),
        "w_qkv": vmem((width, 3 * width), bf16),
        "t_qkv": vmem((3 * width, width), bf16),
        "w_o": vmem((width, width), bf16),
        "t_o": vmem((width, width), bf16),
        "w_kv": vmem((width, 2 * width), bf16),
        "t_kv": vmem((2 * width, width), bf16),
        "w_do": vmem((width, width), bf16),
        "t_do": vmem((width, width), bf16),
        "w_w1": vmem((width, F), bf16),
        "t_w1": vmem((F, width), bf16),
        "w_p1": vmem((width, F), bf16),
        "t_p1": vmem((F, width), bf16),
        "w_w2": vmem((F, width), bf16),
        "t_w2": vmem((width, F), bf16),
        "w_p2": vmem((F, width), bf16),
        "t_p2": vmem((width, F), bf16),
        "t_dq": vmem((width, FOUR), bf16),
        "mask": vmem((1, points), f32),
        "root_one": vmem((1, points), f32),
        "root_two": vmem((1, points), f32),
        "root_three": vmem((1, points), f32),
        "cosine": vmem((E // 2, points), f32),
        "sine": vmem((E // 2, points), f32),
        "phi": tall(FOUR),
        "u1": tall(width),
        "q": tall(width),
        "kv": tall(2 * width),
        "qd": tall(width),
        "o": tall(width),
        "xh2": tall(width),
        "u2": tall(width),
        "e1": tall(F),
        "slope": tall(F),
        "xh3": tall(width),
        "u3": tall(width),
        "kvd": tall(2 * width),
        "per_block": vmem((blocks * E, width), bf16),
        "inverse": vmem((8, width), f32),
        "table_self": vmem((2, chips, 16, width), bf16),
        "table_other": vmem((2, chips, 16, width), bf16),
        "final_near": vmem((2, 16, width), bf16),
        "final_far": vmem((chips, 16, width), bf16),
        "turned": tall(width),
        "sem_in": pltpu.SemaphoreType.DMA((4,)),
        "sem_aside": pltpu.SemaphoreType.DMA((8 * width // LANES,)),
        "table_third": vmem((2, chips, 16, width), bf16),
        "load_slots": vmem((2, TILE, width), bf16),
        "output_slots": vmem((2, PUT, width), bf16),
        "input_slots": vmem((2, PUT, width), f32),
        "sem_out": pltpu.SemaphoreType.DMA((2, 2)),
    }
    for key in ("t", "e"):
        scratch["chip_full_" + key] = vmem((2, chips, 16, width), bf16)
        for part in ("chip_half_", "chip_others_"):
            scratch[part + key] = vmem((chips, 16, width), bf16)
    for key, rows in (("c", rows_c), ("d", rows_d)):
        for part in ("half_", "quarter_"):
            scratch[part + key] = vmem((4, outers, rows, width), bf16)
        scratch["last_" + key] = vmem((outers, rows, width), bf16)
    many = chips
    for key in ("ts", "tr", "g1s", "g1r", "g2s", "g2r", "cs", "cr", "ds", "dr", "es", "er"):
        scratch["sem_" + key] = pltpu.SemaphoreType.DMA((4, many))
    for key in ("fs", "fr"):
        scratch["sem_" + key] = pltpu.SemaphoreType.DMA((2, many))
    names = list(inputs) + list(outputs) + list(scratch)
    spaces = {"items": pltpu.SMEM, "features_far": pl.ANY, "cotangent_far": pl.ANY}
    in_specs = [pl.BlockSpec(memory_space=spaces.get(name, pltpu.VMEM)) for name in inputs]
    whole = pl.BlockSpec(memory_space=pltpu.VMEM)
    made = pl.pallas_call(
        functools.partial(layer_kernel, names, devices),
        out_shape=[jax.ShapeDtypeStruct(*shape) for shape in outputs.values()],
        in_specs=in_specs,
        out_specs=[pl.BlockSpec(memory_space=pl.ANY)] * 2
        + [whole] * 4
        + [pl.BlockSpec(memory_space=pl.ANY)],
        scratch_shapes=list(scratch.values()),
        compiler_params=pltpu.CompilerParams(
            collective_id=0, has_side_effects=True, vmem_limit_bytes=VMEM_BYTES
        ),
    )(*inputs.values())
    flat = list(weights)
    for part in range(9, 12):
        flat[part] = flat[part].reshape(share, LANES)
    shapes = [jax.ShapeDtypeStruct((1, 1), f32)] + [
        jax.ShapeDtypeStruct(flat[index].shape, f32) for index in range(18)
    ]
    order = []
    for index in range(6):
        order += [shapes[1 + 3 * index]] * 3
    updated = pl.pallas_call(
        functools.partial(update_kernel, share),
        out_shape=[jax.ShapeDtypeStruct(*shape) for shape in list(outputs.values())[:2]]
        + [shapes[0]]
        + order,
        in_specs=[pl.BlockSpec(memory_space=pl.ANY)] * 2
        + [whole] * 4
        + [pl.BlockSpec(memory_space=pl.ANY)] * 18,
        out_specs=[pl.BlockSpec(memory_space=pl.ANY)] * 2 + [whole] * 19,
        scratch_shapes=[
            vmem(square.shape, f32),
            vmem(expand.shape, f32),
            vmem(contract.shape, f32),
            vmem((points, width), bf16),
            vmem((points, width), f32),
            *(vmem(weight.shape, f32) for weight in flat),
            pltpu.SemaphoreType.DMA((2, 2, PIECES)),
            pltpu.SemaphoreType.DMA((18,)),
        ],
        compiler_params=pltpu.CompilerParams(vmem_limit_bytes=VMEM_BYTES),
    )(*made[:6], *flat)
    layer_output, input_grad, norm, *rest = updated
    for part in range(9, 12):
        rest[part] = rest[part].reshape(fourier.shape)
    return (layer_output, input_grad, norm.reshape(()), *rest)


def shards(features, *others):
    devices = lax.axis_size("pts")
    width = features.shape[1]
    if devices % GROUP == 0 and width == 8 * devices:
        return fused(devices, features, *others)
    return plain(features, *others)


def solution(mesh):
    in_specs = (
        P("pts", None),
        P(None, "pts"),
        P(),
        P("pts"),
        P("pts"),
        P("pts", None),
        P(None, "pts"),
        P(None, "pts"),
        P(None, "pts"),
        P(None, "pts"),
        P(None, "pts"),
        P(None, "pts"),
        P(None, "pts"),
        P(None, "pts"),
        P(None, "pts"),
        P("pts"),
        P("pts"),
        P("pts"),
        P(),
        P(),
        P(),
        P(),
        P(),
        P(),
    )
    out_specs = (
        P("pts", None),
        P("pts", None),
        P(),
        P(None, "pts"),
        P(None, "pts"),
        P(None, "pts"),
        P(None, "pts"),
        P(None, "pts"),
        P(None, "pts"),
        P(None, "pts"),
        P(None, "pts"),
        P(None, "pts"),
        P("pts"),
        P("pts"),
        P("pts"),
        P(),
        P(),
        P(),
        P(),
        P(),
        P(),
    )
    return jax.shard_map(shards, mesh=mesh, in_specs=in_specs, out_specs=out_specs, check_vma=False)
```

```python
import functools
import math
import types

import jax
import jax.numpy as jnp
from jax import lax
from jax.experimental import pallas as pl
from jax.experimental.pallas import tpu as pltpu
from jax.sharding import PartitionSpec as P

H = 8
E = 32
F = 512
FOUR = 128
BLOCK = 128
ITEM_PTS = 8192
STEP = 10


NORM_EPS = 1e-05
GELU_C = math.sqrt(2.0 / math.pi)
GELU_A = 0.044715
BETA_ONE = 0.9
BETA_TWO = 0.95
ADAM_EPS = 1e-08
WEIGHT_DECAY = 0.1
RATE_MATRIX = 0.05
RATE_VECTOR = 0.25
CLIP_NORM = 1.0
HIGHEST_PRECISION = lax.Precision.HIGHEST


def matmul(left, right):
    return jnp.dot(left, right, preferred_element_type=jnp.float32)


def matmul_left(left, right):
    return lax.dot_general(
        left, right, (((0,), (0,)), ((), ())), preferred_element_type=jnp.float32
    )


def matmul_right(left, right):
    return lax.dot_general(
        left, right, (((1,), (1,)), ((), ())), preferred_element_type=jnp.float32
    )


def gelu(values):
    return 0.5 * values * (1.0 + jnp.tanh(GELU_C * (values + GELU_A * values * values * values)))


def gelu_slope(values):
    tangent = jnp.tanh(GELU_C * (values + GELU_A * values * values * values))
    return 0.5 * (1.0 + tangent) + 0.5 * values * (1.0 - tangent * tangent) * GELU_C * (
        1.0 + 3.0 * GELU_A * values * values
    )


def norm_parts(values, norm_gain, norm_bias):
    centred = values - jnp.mean(values, axis=-1, keepdims=True)
    variance = jnp.mean(centred * centred, axis=-1, keepdims=True)
    root_inv = lax.rsqrt(variance + NORM_EPS)
    scaled = centred * root_inv
    return (scaled * norm_gain + norm_bias, scaled, root_inv)


def norm_back(upstream, scaled, root_inv, norm_gain):
    through = upstream * norm_gain
    centre = jnp.mean(through, axis=-1, keepdims=True)
    along = jnp.mean(through * scaled, axis=-1, keepdims=True)
    return root_inv * (through - centre - scaled * along)


def rotary_tables(coords):
    quarter = E // 4
    frequency = math.pi * (jnp.arange(quarter, dtype=jnp.float32) + 1.0) / quarter
    first_angle = coords[0][:, None] * frequency[None, :]
    second_angle = coords[1][:, None] * frequency[None, :]
    angles = jnp.concatenate([first_angle, first_angle, second_angle, second_angle], axis=1)
    return (jnp.cos(angles), jnp.sin(angles))


def rotate(values, cosine, sine):
    quarter = E // 4
    swapped = jnp.concatenate(
        [
            -values[..., quarter : 2 * quarter],
            values[..., :quarter],
            -values[..., 3 * quarter :],
            values[..., 2 * quarter : 3 * quarter],
        ],
        axis=-1,
    )
    return values * cosine[:, None, :] + swapped * sine[:, None, :]


def rotate_back(grads, cosine, sine):
    quarter = E // 4
    scaled = grads * sine[:, None, :]
    swapped = jnp.concatenate(
        [
            scaled[..., quarter : 2 * quarter],
            -scaled[..., :quarter],
            scaled[..., 3 * quarter :],
            -scaled[..., 2 * quarter : 3 * quarter],
        ],
        axis=-1,
    )
    return grads * cosine[:, None, :] + swapped


def fourier_features(coords, fourier_basis):
    phases = (
        2.0
        * math.pi
        * (
            coords[0][:, None] * fourier_basis[0][None, :]
            + coords[1][:, None] * fourier_basis[1][None, :]
        )
    )
    return jnp.concatenate([jnp.cos(phases), jnp.sin(phases)], axis=1)


def block_table(left, right, onehot):
    blocks = onehot.shape[0]
    per_block = jnp.einsum(
        "bphe,bphf->bhef",
        left.reshape(blocks, BLOCK, H, E),
        right.reshape(blocks, BLOCK, H, E),
        preferred_element_type=jnp.float32,
    )
    return jnp.einsum("ba,bhef->ahef", onehot, per_block, precision=HIGHEST_PRECISION)


def scale_round(table, inverse_count):
    return (table * inverse_count[:, None, None, None]).astype(jnp.bfloat16)


def spread(summary, onehot):
    selected = jnp.einsum(
        "ba,ahef->bhef", onehot.astype(jnp.bfloat16), summary, preferred_element_type=jnp.float32
    )
    return selected.astype(jnp.bfloat16)


def apply_summary(rows_low, block_summary, transposed):
    blocks = block_summary.shape[0]
    pattern = "bphf,bhef->bphe" if transposed else "bphe,bhef->bphf"
    mixed = jnp.einsum(
        pattern,
        rows_low.reshape(blocks, BLOCK, H, E),
        block_summary,
        preferred_element_type=jnp.float32,
    )
    return mixed.reshape(-1, H * E)


def galerkin_backward(
    grad_low, queries_low, keys_masked, values_low, block_summary, onehot, mask_float, reducer
):
    grad_masked = grad_low * mask_float.astype(jnp.bfloat16)
    grad_queries = apply_summary(grad_masked, block_summary, True)
    summary_grad = reducer(block_table(queries_low, grad_masked, onehot))
    block_grad = spread(summary_grad, onehot)
    grad_keys = apply_summary(values_low, block_grad, True) * mask_float
    grad_values = apply_summary(keys_masked, block_grad, False)
    return (grad_queries, grad_keys, grad_values)


def adam_update(weight, first, second, grad, factor, rate):
    clipped = grad * factor
    new_first = BETA_ONE * first + (1.0 - BETA_ONE) * clipped
    new_second = BETA_TWO * second + (1.0 - BETA_TWO) * clipped * clipped
    first_hat = new_first / (1.0 - BETA_ONE**STEP)
    second_hat = new_second / (1.0 - BETA_TWO**STEP)
    new_weight = weight - rate * (
        first_hat / (jnp.sqrt(second_hat) + ADAM_EPS) + WEIGHT_DECAY * weight
    )
    return (new_first, new_second, new_weight)


def own_share(full, width, along, start_index):
    return lax.dynamic_slice_in_dim(full, start_index * width, width, along)


def plain(
    features,
    coords,
    fourier_basis,
    block_items,
    point_mask,
    cotangent,
    square_weight,
    square_first,
    square_second,
    expand_weight,
    expand_first,
    expand_second,
    contract_weight,
    contract_first,
    contract_second,
    fourier_weight,
    fourier_first,
    fourier_second,
    vector_weight,
    vector_first,
    vector_second,
    hidden_weight,
    hidden_first,
    hidden_second,
):
    rows = features.shape[0]
    width = features.shape[1]
    blocks = rows // BLOCK
    devices = lax.axis_size("pts")
    items_total = rows * devices // ITEM_PTS
    gathered = (
        lax.all_gather(square_weight.astype(jnp.bfloat16), "pts", axis=1, tiled=True),
        lax.all_gather(expand_weight.astype(jnp.bfloat16), "pts", axis=1, tiled=True),
        lax.all_gather(contract_weight.astype(jnp.bfloat16), "pts", axis=1, tiled=True),
        lax.all_gather(fourier_weight.astype(jnp.bfloat16), "pts", axis=0, tiled=True),
    )
    square_full = gathered[0].reshape(7, width, width)
    expand_full = gathered[1].reshape(2, width, F)
    contract_full = gathered[2].reshape(2, F, width)
    fourier_full = gathered[3].reshape(FOUR, width)
    onehot = (block_items[:, None] == jnp.arange(items_total, dtype=jnp.int32)[None, :]).astype(
        jnp.float32
    )
    mask_float = point_mask.astype(jnp.float32)[:, None]
    mask_low = mask_float.astype(jnp.bfloat16)
    block_count = jnp.sum(mask_float.reshape(blocks, BLOCK), axis=1)
    local_count = jnp.dot(block_count, onehot, precision=HIGHEST_PRECISION)
    cosine, sine = rotary_tables(coords)
    phase_low = fourier_features(coords, fourier_basis).astype(jnp.bfloat16)
    inputs = features.astype(jnp.float32)
    normed, scaled_one, root_one = norm_parts(inputs, vector_weight[0], vector_weight[1])
    normed_low = normed.astype(jnp.bfloat16)
    joint_weight = jnp.concatenate([square_full[0], square_full[1], square_full[2]], axis=1)
    projected = matmul(normed_low, joint_weight)
    queries_low = (
        rotate(projected[:, :width].reshape(rows, H, E), cosine, sine)
        .reshape(rows, width)
        .astype(jnp.bfloat16)
    )
    keys_low = (
        rotate(projected[:, width : 2 * width].reshape(rows, H, E), cosine, sine)
        .reshape(rows, width)
        .astype(jnp.bfloat16)
    )
    keys_masked = keys_low * mask_low
    values_low = projected[:, 2 * width :].astype(jnp.bfloat16)
    self_local = block_table(keys_masked, values_low, onehot)
    self_table, item_count = lax.psum((self_local, local_count), "pts")
    inverse_count = 1.0 / item_count
    self_items = scale_round(self_table, inverse_count)
    self_summary = spread(self_items, onehot)
    attended_low = (apply_summary(queries_low, self_summary, False) * mask_float).astype(
        jnp.bfloat16
    )
    first_sum = inputs + matmul(attended_low, square_full[3])
    normed_mid, scaled_two, root_two = norm_parts(first_sum, vector_weight[2], vector_weight[3])
    middle_low = normed_mid.astype(jnp.bfloat16)
    hidden_pre = matmul(middle_low, expand_full[0]) + hidden_weight[0]
    hidden_low = gelu(hidden_pre).astype(jnp.bfloat16)
    encoded = first_sum + matmul(hidden_low, contract_full[0]) + vector_weight[6]
    normed_out, scaled_three, root_three = norm_parts(encoded, vector_weight[4], vector_weight[5])
    outer_low = normed_out.astype(jnp.bfloat16)
    pair_weight = jnp.concatenate([square_full[4], square_full[5]], axis=1)
    cross_projected = matmul(outer_low, pair_weight)
    cross_keys = cross_projected[:, :width].astype(jnp.bfloat16) * mask_low
    cross_values = cross_projected[:, width:].astype(jnp.bfloat16)
    cross_queries = matmul(phase_low, fourier_full).astype(jnp.bfloat16)
    cross_local = block_table(cross_keys, cross_values, onehot)
    cross_items = scale_round(lax.psum(cross_local, "pts"), inverse_count)
    cross_summary = spread(cross_items, onehot)
    decoded_low = (apply_summary(cross_queries, cross_summary, False) * mask_float).astype(
        jnp.bfloat16
    )
    latent = matmul(decoded_low, square_full[6])
    latent_low = latent.astype(jnp.bfloat16)
    spread_pre = matmul(latent_low, expand_full[1]) + hidden_weight[1]
    spread_low = gelu(spread_pre).astype(jnp.bfloat16)
    output = latent + matmul(spread_low, contract_full[1]) + vector_weight[7]
    cross_reducer = lambda table_part: scale_round(lax.psum(table_part, "pts"), inverse_count)
    self_reducer = lambda table_part: scale_round(lax.psum(table_part, "pts"), inverse_count)
    grad_output = cotangent.astype(jnp.float32)
    grad_bias_end = jnp.sum(grad_output, axis=0)
    grad_contract_spread = matmul_left(spread_low, cotangent)
    grad_spread = matmul_right(cotangent, contract_full[1]) * gelu_slope(spread_pre)
    grad_hidden_spread = jnp.sum(grad_spread, axis=0)
    grad_spread_low = grad_spread.astype(jnp.bfloat16)
    grad_expand_spread = matmul_left(latent_low, grad_spread_low)
    grad_latent = (grad_output + matmul_right(grad_spread_low, expand_full[1])).astype(jnp.bfloat16)
    grad_out_cross = matmul_left(decoded_low, grad_latent)
    grad_decoded = matmul_right(grad_latent, square_full[6]).astype(jnp.bfloat16)
    cross_back = galerkin_backward(
        grad_decoded,
        cross_queries,
        cross_keys,
        cross_values,
        cross_summary,
        onehot,
        mask_float,
        cross_reducer,
    )
    grad_fourier_full = matmul_left(phase_low, cross_back[0].astype(jnp.bfloat16))
    grad_pair_low = jnp.concatenate([cross_back[1], cross_back[2]], axis=1).astype(jnp.bfloat16)
    grad_pair_full = matmul_left(outer_low, grad_pair_low)
    grad_normed_out = matmul_right(grad_pair_low, pair_weight)
    grad_gain_three = jnp.sum(grad_normed_out * scaled_three, axis=0)
    grad_bias_three = jnp.sum(grad_normed_out, axis=0)
    grad_encoded = norm_back(grad_normed_out, scaled_three, root_three, vector_weight[4])
    grad_bias_middle = jnp.sum(grad_encoded, axis=0)
    grad_encoded_low = grad_encoded.astype(jnp.bfloat16)
    grad_contract_enc = matmul_left(hidden_low, grad_encoded_low)
    grad_hidden = matmul_right(grad_encoded_low, contract_full[0]) * gelu_slope(hidden_pre)
    grad_hidden_enc = jnp.sum(grad_hidden, axis=0)
    grad_hidden_low = grad_hidden.astype(jnp.bfloat16)
    grad_expand_enc = matmul_left(middle_low, grad_hidden_low)
    grad_middle = matmul_right(grad_hidden_low, expand_full[0])
    grad_gain_two = jnp.sum(grad_middle * scaled_two, axis=0)
    grad_bias_two = jnp.sum(grad_middle, axis=0)
    grad_first = grad_encoded + norm_back(grad_middle, scaled_two, root_two, vector_weight[2])
    grad_first_low = grad_first.astype(jnp.bfloat16)
    grad_out_self = matmul_left(attended_low, grad_first_low)
    grad_attended = matmul_right(grad_first_low, square_full[3]).astype(jnp.bfloat16)
    self_back = galerkin_backward(
        grad_attended,
        queries_low,
        keys_masked,
        values_low,
        self_summary,
        onehot,
        mask_float,
        self_reducer,
    )
    grad_queries = rotate_back(self_back[0].reshape(rows, H, E), cosine, sine).reshape(rows, width)
    grad_keys = rotate_back(self_back[1].reshape(rows, H, E), cosine, sine).reshape(rows, width)
    grad_joint_low = jnp.concatenate([grad_queries, grad_keys, self_back[2]], axis=1).astype(
        jnp.bfloat16
    )
    grad_joint_full = matmul_left(normed_low, grad_joint_low)
    grad_normed = matmul_right(grad_joint_low, joint_weight)
    grad_gain_one = jnp.sum(grad_normed * scaled_one, axis=0)
    grad_bias_one = jnp.sum(grad_normed, axis=0)
    grad_inputs = grad_first + norm_back(grad_normed, scaled_one, root_one, vector_weight[0])
    grad_square = jnp.stack(
        [
            grad_joint_full[:, :width],
            grad_joint_full[:, width : 2 * width],
            grad_joint_full[:, 2 * width :],
            grad_out_self,
            grad_pair_full[:, :width],
            grad_pair_full[:, width:],
            grad_out_cross,
        ]
    ).reshape(7, width * width)
    grad_expand = jnp.stack([grad_expand_enc, grad_expand_spread]).reshape(2, width * F)
    grad_contract = jnp.stack([grad_contract_enc, grad_contract_spread]).reshape(2, F * width)
    grad_fourier = grad_fourier_full.reshape(FOUR * width)
    grad_vector = jnp.stack(
        [
            grad_gain_one,
            grad_bias_one,
            grad_gain_two,
            grad_bias_two,
            grad_gain_three,
            grad_bias_three,
            grad_bias_middle,
            grad_bias_end,
        ]
    )
    grad_hidden_rows = jnp.stack([grad_hidden_enc, grad_hidden_spread])
    totals = lax.psum(
        (grad_square, grad_expand, grad_contract, grad_fourier, grad_vector, grad_hidden_rows),
        "pts",
    )
    squares = sum((jnp.sum(total_part * total_part) for total_part in totals))
    start_index = lax.axis_index("pts")
    share_square = own_share(totals[0], square_weight.shape[1], 1, start_index)
    share_expand = own_share(totals[1], expand_weight.shape[1], 1, start_index)
    share_contract = own_share(totals[2], contract_weight.shape[1], 1, start_index)
    share_fourier = own_share(totals[3], fourier_weight.shape[0], 0, start_index)
    vector_total = totals[4]
    hidden_total = totals[5]
    grad_norm = jnp.sqrt(squares)
    factor = jnp.minimum(1.0, CLIP_NORM / (grad_norm + 1e-06))
    new_square = adam_update(
        square_weight, square_first, square_second, share_square, factor, RATE_MATRIX
    )
    new_expand = adam_update(
        expand_weight, expand_first, expand_second, share_expand, factor, RATE_MATRIX
    )
    new_contract = adam_update(
        contract_weight, contract_first, contract_second, share_contract, factor, RATE_MATRIX
    )
    new_fourier = adam_update(
        fourier_weight, fourier_first, fourier_second, share_fourier, factor, RATE_MATRIX
    )
    new_vector = adam_update(
        vector_weight, vector_first, vector_second, vector_total, factor, RATE_VECTOR
    )
    new_hidden = adam_update(
        hidden_weight, hidden_first, hidden_second, hidden_total, factor, RATE_VECTOR
    )
    return (
        output.astype(jnp.bfloat16),
        grad_inputs,
        grad_norm,
        new_square[0],
        new_square[1],
        new_square[2],
        new_expand[0],
        new_expand[1],
        new_expand[2],
        new_contract[0],
        new_contract[1],
        new_contract[2],
        new_fourier[0],
        new_fourier[1],
        new_fourier[2],
        new_vector[0],
        new_vector[1],
        new_vector[2],
        new_hidden[0],
        new_hidden[1],
        new_hidden[2],
    )


GROUP = 8
TILE = 1024
PUT = 512
LANES = 128
E_BITS = E.bit_length() - 1
PIECES = 4
VMEM_BYTES = 64 * 1024 * 1024


def dot(left, right):
    return jnp.dot(left, right, preferred_element_type=jnp.float32)


def dot_bt(left, right):
    return lax.dot_general(
        left, right, (((1,), (1,)), ((), ())), preferred_element_type=jnp.float32
    )


def dot_at(left, right):
    return lax.dot_general(
        left, right, (((0,), (0,)), ((), ())), preferred_element_type=jnp.float32
    )


def low(values):
    return values.astype(jnp.bfloat16)


def column_norm(values):
    inverse = 1.0 / values.shape[0]
    centred = values - jnp.sum(values, axis=0, keepdims=True) * inverse
    variance = jnp.sum(centred * centred, axis=0, keepdims=True) * inverse
    root_inv = lax.rsqrt(variance + NORM_EPS)
    return (centred * root_inv, root_inv)


def column_norm_back(upstream, scaled, root_inv, gain):
    inverse = 1.0 / upstream.shape[0]
    through = upstream * gain
    centre = jnp.sum(through, axis=0, keepdims=True) * inverse
    along = jnp.sum(through * scaled, axis=0, keepdims=True) * inverse
    return root_inv * (through - centre - scaled * along)


def gelu_both(values):
    square = values * values
    half = 0.5 + 0.5 * jnp.tanh(values * (GELU_C + (GELU_C * GELU_A) * square))
    slope = half + values * (half * (1.0 - half)) * (
        2.0 * GELU_C + (6.0 * GELU_C * GELU_A) * square
    )
    return (values * half, slope)


def turn(values, cosine, sine, sign):
    quarter = E // 4
    first_cos, second_cos = cosine[:quarter], cosine[quarter:]
    first_sin, second_sin = sine[:quarter] * sign, sine[quarter:] * sign
    parts = []
    for base in range(0, values.shape[0], E):
        one, two, three, four = (
            values[base + quarter * step : base + quarter * (step + 1)] for step in range(4)
        )
        parts += [
            one * first_cos - two * first_sin,
            two * first_cos + one * first_sin,
            three * second_cos - four * second_sin,
            four * second_cos + three * second_sin,
        ]
    return jnp.concatenate(parts, axis=0)


def head_of(index):
    return lax.shift_right_logical(index, E_BITS)


def compress(full):
    width = full.shape[1]
    head = head_of(lax.broadcasted_iota(jnp.int32, (E, width), 1))
    result = full[:E]
    for index in range(1, H):
        result = jnp.where(head == index, full[E * index : E * (index + 1)], result)
    return result


def lane_sum(values):
    result = values[:, :LANES]
    for start in range(LANES, values.shape[1], LANES):
        result = result + values[:, start : start + LANES]
    return result


def remote(source, target, send_sem, recv_sem, device):
    return pltpu.make_async_remote_copy(
        src_ref=source,
        dst_ref=target,
        send_sem=send_sem,
        recv_sem=recv_sem,
        device_id=(device,),
        device_id_type=pl.DeviceIdType.MESH,
    )


class Place:
    def __init__(self, devices):
        self.devices = devices
        self.outers = devices // GROUP
        self.me = lax.axis_index("pts")
        self.inner = lax.rem(self.me, GROUP)
        self.outer = lax.div(self.me, GROUP)
        self.core = lax.rem(self.me, 2)
        self.pair = lax.div(self.inner, 2)
        self.chips = devices // 2
        self.chip = lax.div(self.me, 2)

    def chip_at(self, step):
        return lax.rem(self.chip + step, self.chips)

    def inner_at(self, step):
        return lax.rem(self.inner + step, GROUP)

    def outer_at(self, step):
        return lax.rem(self.outer + step, self.outers)

    def pair_at(self, step):
        return lax.rem(self.pair + step, 4)

    def device(self, outer, inner):
        return outer * GROUP + inner


class Gather:
    def __init__(self, place, buffer, scratch, slots):
        self.place, self.buffer = place, buffer
        self.send, self.recv = scratch.sem_send, scratch.sem_recv
        self.slots = slots

    def first(self, step, start):
        at = self.place
        slot = self.buffer.at[at.core, at.pair, at.outer if start else at.outer_at(step)]
        mine = self.buffer.at[at.core, at.pair, at.outer]
        source = at.outer if start else at.outer_at(step)
        return remote(
            mine, slot, self.send.at[self.slots[0], self.slots[1] + step],
            self.recv.at[self.slots[0], self.slots[1] + source],
            at.device(at.outer_at(step), at.inner),
        )

    def second(self, step, start):
        at = self.place
        source = at.pair if start else at.pair_at(step)
        return remote(
            self.buffer.at[at.core, at.pair], self.buffer.at[at.core, source],
            self.send.at[2, self.slots[2] + step], self.recv.at[2, self.slots[2] + source],
            at.device(at.outer, at.pair_at(step) * 2 + at.core),
        )

    def third(self, start):
        at = self.place
        source = at.core if start else 1 - at.core
        return remote(
            self.buffer.at[at.core], self.buffer.at[source], self.send.at[2, self.slots[3]],
            self.recv.at[2, self.slots[3]], at.device(at.outer, at.pair * 2 + 1 - at.core),
        )

    def start_first(self):
        for step in range(1, self.place.outers):
            self.first(step, True).start()

    def start_second(self):
        for step in range(1, self.place.outers):
            self.first(step, False).wait()
        for step in range(1, 4):
            self.second(step, True).start()

    def start_third(self):
        for step in range(1, 4):
            self.second(step, False).wait()
        self.third(True).start()

    def finish(self):
        self.third(False).wait()


class ChipSum:
    def __init__(self, place, scratch, key):
        self.place = place
        self.full, self.half, self.others = (
            getattr(scratch, name + key) for name in ("chip_full_", "chip_half_", "chip_others_")
        )
        self.send, self.recv = scratch.sem_send, scratch.sem_recv

    def swap(self):
        at = self.place
        return remote(
            self.full.at[1 - at.core], self.half, self.send.at[2, 0], self.recv.at[2, 0],
            at.chip * 2 + 1 - at.core,
        )

    def cross(self, step, start):
        at = self.place
        source = at.chip if start else at.chip_at(step)
        return remote(
            self.half.at[at.chip_at(step)], self.others.at[source], self.send.at[0, step],
            self.recv.at[0, source], at.chip_at(step) * 2 + at.core,
        )

    def start(self):
        self.swap().start()

    def middle(self):
        at = self.place
        self.swap().wait()
        self.half[...] = low(
            self.full[at.core].astype(jnp.float32) + self.half[...].astype(jnp.float32)
        )
        for step in range(1, at.chips):
            self.cross(step, True).start()

    def total(self):
        at = self.place
        total = self.half[at.chip].astype(jnp.float32)
        for step in range(1, at.chips):
            self.cross(step, False).wait()
            total = total + self.others[at.chip_at(step)].astype(jnp.float32)
        return total


class TableSum(ChipSum):
    def __init__(self, place, scratch):
        super().__init__(place, scratch, "t")
        self.s = scratch

    def share(self, step, start, result):
        at = self.place
        source = at.chip if start else at.chip_at(step)
        return remote(
            result.at[at.core, at.chip], result.at[at.core, source], self.send.at[1, step],
            self.recv.at[1, source], at.chip_at(step) * 2 + at.core,
        )

    def swap_back(self, start, result):
        at = self.place
        source = at.core if start else 1 - at.core
        return remote(
            result.at[at.core], result.at[source], self.send.at[2, 1], self.recv.at[2, 1],
            at.chip * 2 + 1 - at.core,
        )

    def start(self):
        s = self.s
        table = low(dot(s.spread[...], s.per_block[...]))
        for chunk in range(self.place.devices):
            self.full[chunk % 2, chunk // 2] = table[chunk * 16 : (chunk + 1) * 16]
        super().start()

    def late(self, result):
        at, s = self.place, self.s
        result[at.core, at.chip] = low(self.total() * s.inverse[0:1, :])
        for step in range(1, at.chips):
            self.share(step, True, result).start()

    def last(self, result):
        for step in range(1, self.place.chips):
            self.share(step, False, result).wait()
        self.swap_back(True, result).start()

    def finish(self, result):
        self.swap_back(False, result).wait()


class GradSum:
    def __init__(self, place, scratch, key, first):
        self.place = place
        self.half, self.quarter, self.last = (
            getattr(scratch, name + key) for name in ("half_", "quarter_", "last_")
        )
        self.full = scratch.gather_two.at[:, :, :, first : first + self.last.shape[1]]
        self.send, self.recv = scratch.sem_send, scratch.sem_recv

    def swap(self):
        at = self.place
        return remote(
            self.full.at[1 - at.core], self.half, self.send.at[2, 7], self.recv.at[2, 7],
            at.device(at.outer, at.pair * 2 + 1 - at.core),
        )

    def across(self, step, start):
        at = self.place
        source = at.pair if start else at.pair_at(step)
        return remote(
            self.half.at[at.pair_at(step)], self.quarter.at[source], self.send.at[2, 8 + step],
            self.recv.at[2, 8 + source], at.device(at.outer, at.pair_at(step) * 2 + at.core),
        )

    def along(self, step, start):
        at = self.place
        source = at.outer if start else at.outer_at(step)
        return remote(
            self.quarter.at[at.pair, at.outer_at(step)], self.last.at[source], self.send.at[2, 12 + step],
            self.recv.at[2, 12 + source], at.device(at.outer_at(step), at.inner),
        )

    def start(self, chunk_of):
        at = self.place

        @pl.loop(0, at.devices)
        def _(chunk):
            inner = lax.rem(chunk, GROUP)
            self.full[lax.rem(inner, 2), lax.div(inner, 2), lax.div(chunk, GROUP)] = low(
                chunk_of(chunk)
            )

        self.swap().start()

    def second(self):
        at = self.place
        self.swap().wait()

        @pl.loop(0, 4)
        def _(pair):
            self.half[pair] = low(
                self.full[at.core, pair].astype(jnp.float32) + self.half[pair].astype(jnp.float32)
            )

        for step in range(1, 4):
            self.across(step, True).start()

    def third(self):
        at = self.place
        total = self.half[at.pair].astype(jnp.float32)
        for step in range(1, 4):
            self.across(step, False).wait()
            total = total + self.quarter[at.pair_at(step)].astype(jnp.float32)
        self.quarter[at.pair] = low(total)
        for step in range(1, at.outers):
            self.along(step, True).start()

    def finish(self):
        at = self.place
        total = self.quarter[at.pair, at.outer].astype(jnp.float32)
        for step in range(1, at.outers):
            self.along(step, False).wait()
            total = total + self.last[at.outer_at(step)].astype(jnp.float32)
        return total


def layer_kernel(names, devices, *refs):
    s = types.SimpleNamespace(**dict(zip(names, refs)))
    at = Place(devices)
    points, width = s.features_far.shape
    tiles = points // TILE
    blocks = points // BLOCK
    share = width // devices
    tile_blocks = TILE // BLOCK
    f32 = jnp.float32

    barrier = pltpu.get_barrier_semaphore()
    pl.semaphore_signal(
        barrier, inc=1, device_id=(at.chip * 2 + 1 - at.core,),
        device_id_type=pl.DeviceIdType.MESH,
    )
    for step in range(1, at.chips):
        pl.semaphore_signal(
            barrier, inc=1, device_id=(at.chip_at(step) * 2 + at.core,),
            device_id_type=pl.DeviceIdType.MESH,
        )

    def tile_load(source, tile):
        slot = lax.rem(tile, 2)
        where = pl.ds(pl.multiple_of(tile * TILE, TILE), TILE)
        return pltpu.make_async_copy(
            source.at[where, :], s.load_slots.at[slot], s.sem_in.at[slot]
        )

    for tile in range(2):
        tile_load(s.features_far, tile).start()

    class Aside:
        def __init__(self, first, *buffers):
            self.pairs = []
            row = first
            for buffer in buffers:
                for start in range(0, buffer.shape[0], width):
                    near = buffer.at[start : start + width]
                    far = s.aside.at[row : row + width]
                    self.pairs.append((near, far, s.sem_aside.at[row // width]))
                    row += width

        def store(self):
            for near, far, sem in self.pairs:
                pltpu.make_async_copy(near, far, sem).start()

        def stored(self):
            for near, far, sem in self.pairs:
                pltpu.make_async_copy(near, far, sem).wait()

        def load(self):
            for near, far, sem in self.pairs:
                pltpu.make_async_copy(far, near, sem).start()

        def loaded(self):
            for near, far, sem in self.pairs:
                pltpu.make_async_copy(far, near, sem).wait()

    aside_a = Aside(0, s.u1, s.kv)
    aside_b = Aside(3 * width, s.e1, s.o, s.u2, s.u3)

    def columns(tile):
        return pl.ds(pl.multiple_of(tile * TILE, TILE), TILE)

    def block_columns(block):
        return pl.ds(pl.multiple_of(block * BLOCK, BLOCK), BLOCK)

    def column(index):
        return s.cols[:, index : index + 1]

    def hidden_column(index):
        return jnp.concatenate([column(8 + 2 * index), column(9 + 2 * index)], axis=0)

    def out_copy(tile, source, target):
        where = pl.ds(pl.multiple_of(tile * TILE, TILE), TILE)
        return pltpu.make_async_copy(
            source.at[:, where], target.at[:, where], s.sem_out.at[tile]
        )

    def end_out(source, target):
        for tile in range(tiles):
            out_copy(tile, source, target).wait()

    def pack_square(matrix):
        for row in range(share):
            s.pack[matrix * share + row : matrix * share + row + 1, :] = s.square_weight[
                matrix : matrix + 1, row * width : (row + 1) * width
            ]

    split = s.gather_one.shape[3]
    for matrix in range(4):
        pack_square(matrix)
    s.gather_one[at.core, at.pair, at.outer] = low(s.pack[:split, :])
    pl.semaphore_wait(barrier, at.chips)
    one = Gather(at, s.gather_one, s, (1, 0, 2, 6))
    two = Gather(at, s.gather_two, s, (2, 12, 8, 7))
    one.start_first()

    for matrix in range(4, 7):
        pack_square(matrix)
    for matrix in range(2):
        for half in range(2):
            for row in range(share):
                place = (7 + 2 * matrix + half) * share + row
                start = row * F + half * width
                s.pack[place : place + 1, :] = s.expand_weight[
                    matrix : matrix + 1, start : start + width
                ]
        for row in range(2 * share):
            place = (11 + 2 * matrix) * share + row
            s.pack[place : place + 1, :] = s.contract_weight[
                matrix : matrix + 1, row * width : (row + 1) * width
            ]
    s.pack[15 * share : 16 * share, :LANES] = s.fourier_weight[...]
    s.pack[15 * share : 16 * share, LANES:] = jnp.zeros((share, LANES), f32)
    live = s.point_mask[...].astype(f32)
    counts = dot_bt(jnp.ones((8, LANES), jnp.bfloat16), low(live))
    s.pack[15 * share : 15 * share + 1, LANES : LANES + blocks] = counts[:1]
    lane = lax.broadcasted_iota(jnp.int32, (1, LANES), 1)
    wide_block = head_of(lax.broadcasted_iota(jnp.int32, (1, E * blocks), 1))
    item_row = jnp.zeros((1, LANES), f32)
    item_wide = jnp.zeros((1, E * blocks), jnp.int32)
    for block in range(blocks):
        item_row = jnp.where(lane == block, s.items[block].astype(f32), item_row)
        item_wide = jnp.where(wide_block == block, s.items[block], item_wide)
    s.pack[15 * share + 1 : 15 * share + 2, LANES:] = item_row
    s.gather_two[at.core, at.pair, at.outer] = low(s.pack[split:, :])

    row_at = lax.broadcasted_iota(jnp.int32, (width, width), 0)
    lane_at = lax.broadcasted_iota(jnp.int32, (width, width), 1)
    s.eye[...] = jnp.where(row_at == lane_at, 1.0, 0.0).astype(jnp.bfloat16)
    s.heads[...] = jnp.where(head_of(row_at) == head_of(lane_at), 1.0, 0.0).astype(jnp.bfloat16)
    s.small[...] = jnp.zeros(s.small.shape, f32)
    s.small[0:8, :] = s.vector_weight[...]
    for row in range(2):
        for half in range(2):
            s.small[8 + 2 * row + half : 9 + 2 * row + half, :] = s.hidden_weight[
                row : row + 1, half * width : (half + 1) * width
            ]
    s.small[12:14, : FOUR // 2] = s.fourier_basis[...]
    s.cols[...] = s.small[...].T
    rows_wide = lax.broadcasted_iota(jnp.int32, s.spread.shape, 0)
    lanes_wide = lax.broadcasted_iota(jnp.int32, s.spread.shape, 1)
    s.spread[...] = jnp.where(
        (item_wide == head_of(rows_wide)) & (((rows_wide ^ lanes_wide) & (E - 1)) == 0), 1.0, 0.0
    ).astype(jnp.bfloat16)
    s.vector_sum[...] = jnp.zeros(s.vector_sum.shape, f32)
    speed = (lax.broadcasted_iota(jnp.int32, (E // 4, 1), 0).astype(f32) + 1.0) * (
        math.pi / (E // 4)
    )

    def add_sum(index, values):
        for part in range(values.shape[0] // width):
            s.vector_sum[index + part] += lane_sum(values[part * width : (part + 1) * width])

    def turned_load(source, tile):
        tile_load(source, tile).wait()
        turned = dot_bt(s.eye[...], s.load_slots[lax.rem(tile, 2)])

        @pl.when(tile + 2 < tiles)
        def _():
            tile_load(source, tile + 2).start()

        return turned

    def norm_one(tile, _):
        where = columns(tile)
        turned = turned_load(s.features_far, tile)
        s.turned[:, where] = low(turned)
        scaled, root = column_norm(turned)
        s.root_one[0:1, where] = root
        s.u1[:, where] = low(scaled * column(0) + column(1))

    def fourier_part(tile, _):
        where = pl.ds(pl.multiple_of(tile * PUT, PUT), PUT)
        x_row, y_row = s.coords[0:1, where], s.coords[1:2, where]
        basis = s.cols[: FOUR // 2, :]
        phases = 2.0 * math.pi * (basis[:, 12:13] * x_row + basis[:, 13:14] * y_row)
        s.phi[:, where] = low(jnp.concatenate([jnp.cos(phases), jnp.sin(phases)], axis=0))

    def angle_part(tile, _):
        where = pl.ds(pl.multiple_of(tile * PUT, PUT), PUT)
        angles = jnp.concatenate(
            [speed * s.coords[0:1, where], speed * s.coords[1:2, where]], axis=0
        )
        s.cosine[:, where] = jnp.cos(angles)
        s.sine[:, where] = jnp.sin(angles)
        for block in range(PUT // BLOCK):
            s.mask[0:1, pl.ds(pl.multiple_of(tile * PUT + block * BLOCK, BLOCK), BLOCK)] = (
                s.point_mask[pl.ds(tile * (PUT // BLOCK) + block, 1), :].astype(f32)
            )

    parts = points // PUT
    lax.fori_loop(0, tiles, norm_one, None)
    one.start_second()
    two.start_first()
    lax.fori_loop(0, 3 * parts // 4, fourier_part, None)
    one.start_third()
    two.start_second()
    lax.fori_loop(0, parts, angle_part, None)
    one.finish()

    group = 16 // share

    def chunk_pair(buffer, index):
        parts = []
        for step in range(group):
            chunk = index * group + step
            inner = lax.rem(chunk, GROUP)
            parts.append(
                buffer[lax.rem(inner, 2), lax.div(inner, 2), lax.div(chunk, GROUP)].astype(f32)
            )
        return parts

    def join(parts, piece):
        return low(
            jnp.concatenate([part[piece * share : (piece + 1) * share] for part in parts], axis=0)
        )

    @pl.loop(0, devices // group)
    def _(index):
        parts = chunk_pair(s.gather_one, index)
        where = pl.ds(pl.multiple_of(index * 16, 16), 16)
        for piece in range(3):
            s.w_qkv[where, piece * width : (piece + 1) * width] = join(parts, piece)
        s.w_o[where, :] = join(parts, 3)

    def flip(matrix):
        return low(dot_bt(s.eye[...], matrix))

    for piece in range(3):
        s.t_qkv[piece * width : (piece + 1) * width, :] = flip(
            s.w_qkv[:, piece * width : (piece + 1) * width]
        )
    s.t_o[...] = flip(s.w_o[...])

    def block_product(left, right):
        return compress(dot_bt(left, right))

    def put_products(tile, left, right):
        for block in range(tile_blocks):
            lanes = slice(block * BLOCK, (block + 1) * BLOCK)
            where = pl.ds(pl.multiple_of((tile * tile_blocks + block) * E, E), E)
            s.per_block[where, :] = low(block_product(left[:, lanes], right[:, lanes]))

    def summary(table, tile, block):
        item = s.items[tile * tile_blocks + block]
        rows = jnp.concatenate([table[0, item], table[1, item]], axis=0)
        return jnp.concatenate([rows] * H, axis=0) * s.heads[...]

    def per_block(tile, function):
        return jnp.concatenate([function(block) for block in range(tile_blocks)], axis=1)

    def lanes_of(block):
        return slice(block * BLOCK, (block + 1) * BLOCK)

    def phase_a(tile, _):
        where = columns(tile)
        projected = dot(s.t_qkv[...], s.u1[:, where])
        cosine, sine = s.cosine[:, where], s.sine[:, where]
        s.q[:, where] = low(turn(projected[:width], cosine, sine, 1.0))
        keys = low(turn(projected[width : 2 * width], cosine, sine, 1.0) * s.mask[0:1, where])
        values = low(projected[2 * width :])
        s.kv[:width, where] = keys
        s.kv[width:, where] = values
        put_products(tile, values, keys)

    lax.fori_loop(0, tiles, phase_a, None)
    table_sum = TableSum(at, s)
    table_sum.start()
    aside_a.store()
    table_sum.middle()
    lax.fori_loop(3 * parts // 4, parts, fourier_part, None)
    two.start_third()

    def take_two(index, carried):
        parts = chunk_pair(s.gather_two, index)
        where = pl.ds(pl.multiple_of(index * 16, 16), 16)
        for piece in range(2):
            s.w_kv[where, piece * width : (piece + 1) * width] = join(parts, piece)
            s.w_w1[where, piece * width : (piece + 1) * width] = join(parts, 3 + piece)
            s.w_p1[where, piece * width : (piece + 1) * width] = join(parts, 5 + piece)
        s.w_do[where, :] = join(parts, 2)
        both = pl.ds(pl.multiple_of(index * 32, 32), 32)
        for piece, target in ((7, s.w_w2), (9, s.w_p2)):
            target[both, :] = low(
                jnp.concatenate([part[piece * share : (piece + 2) * share] for part in parts], axis=0)
            )
        for part in parts:
            count_row = part[11 * share : 11 * share + 1, LANES:]
            item_at = part[11 * share + 1 : 11 * share + 2, LANES:]
            carried = carried + jnp.where(item_at == own_item, count_row, 0.0)
        s.fourier[where, :] = jnp.concatenate(
            [part[11 * share : 12 * share, :LANES] for part in parts], axis=0
        )
        return carried

    two.finish()
    own_item = at.chip.astype(f32)
    found = lax.fori_loop(0, devices // group, take_two, jnp.zeros((1, LANES), f32))
    s.inverse[0:1, :] = jnp.broadcast_to(1.0 / jnp.sum(found, axis=1, keepdims=True), (1, width))
    w_dq = jnp.concatenate(
        [s.fourier[pl.ds(0, FOUR, stride=2), :], s.fourier[pl.ds(1, FOUR, stride=2), :]], axis=1
    )
    s.t_dq[...] = low(w_dq.T)
    table_sum.late(s.table_self)
    for piece in range(2):
        cols = slice(piece * width, (piece + 1) * width)
        s.t_kv[cols, :] = flip(s.w_kv[:, cols])
        s.t_w1[cols, :] = flip(s.w_w1[:, cols])
        s.t_p1[cols, :] = flip(s.w_p1[:, cols])
        s.t_w2[:, cols] = flip(s.w_w2[cols, :])
        s.t_p2[:, cols] = flip(s.w_p2[cols, :])
    s.t_do[...] = flip(s.w_do[...])
    table_sum.last(s.table_self)
    table_sum.finish(s.table_self)

    def phase_b(tile, _):
        where = columns(tile)
        mask = s.mask[0:1, where]
        queries = s.q[:, where]
        mixed = per_block(
            tile, lambda b: dot(summary(s.table_self, tile, b), queries[:, lanes_of(b)])
        )
        attended = low(mixed * mask)
        s.o[:, where] = attended
        first_sum = s.turned[:, where].astype(f32) + dot(s.t_o[...], attended)
        scaled_two, root_two = column_norm(first_sum)
        s.root_two[0:1, where] = root_two
        s.xh2[:, where] = low(scaled_two)
        middle = low(scaled_two * column(2) + column(3))
        s.u2[:, where] = middle
        hidden_pre = dot(s.t_w1[...], middle) + hidden_column(0)
        hidden = low(gelu(hidden_pre))
        s.e1[:, where] = hidden
        s.slope[:, where] = low(hidden_pre)
        encoded = first_sum + dot(s.t_w2[...], hidden) + column(6)
        scaled_three, root_three = column_norm(encoded)
        s.root_three[0:1, where] = root_three
        s.xh3[:, where] = low(scaled_three)
        outer = low(scaled_three * column(4) + column(5))
        s.u3[:, where] = outer
        pair = dot(s.t_kv[...], outer)
        keys = low(pair[:width] * mask)
        values = low(pair[width:])
        s.kvd[:width, where] = keys
        s.kvd[width:, where] = values
        put_products(tile, values, keys)

    lax.fori_loop(0, tiles, phase_b, None)
    table_sum.start()
    aside_b.store()
    table_sum.middle()

    for tile in range(2):
        tile_load(s.cotangent_far, tile).start()
    aside_a.stored()

    def cross_inputs(tile, _):
        where = columns(tile)
        s.qd[:, where] = low(dot(s.t_dq[...], s.phi[:, where]))
        turned = turned_load(s.cotangent_far, tile)
        add_sum(7, turned)
        turned = low(turned)
        s.u1[:, where] = turned
        s.kv[:, where] = low(dot(s.w_p2[...], turned))

    def slopes(tile, _):
        where = columns(tile)
        s.slope[:, where] = low(gelu_slope(s.slope[:, where].astype(f32)))

    lax.fori_loop(0, tiles, cross_inputs, None)
    table_sum.late(s.table_other)
    lax.fori_loop(0, tiles, slopes, None)
    aside_b.stored()
    table_sum.last(s.table_other)
    table_sum.finish(s.table_other)

    def phase_c(tile, _):
        where = columns(tile)
        mask = s.mask[0:1, where]
        queries = s.qd[:, where]
        tables = [summary(s.table_other, tile, block) for block in range(tile_blocks)]
        decoded = low(
            per_block(tile, lambda b: dot(tables[b], queries[:, lanes_of(b)])) * mask
        )
        s.u2[:, where] = decoded
        latent_low = low(dot(s.t_do[...], decoded))
        s.o[:, where] = latent_low
        hidden, slope = gelu_both(dot(s.t_p1[...], latent_low) + hidden_column(1))
        s.e1[:, where] = low(hidden)
        grad_spread = s.kv[:, where].astype(f32) * slope
        add_sum(10, grad_spread)
        grad_spread = low(grad_spread)
        s.kv[:, where] = grad_spread
        grad_latent = low(s.u1[:, where].astype(f32) + dot(s.w_p1[...], grad_spread))
        s.u3[:, where] = grad_latent
        grad_decoded = low(dot(s.w_do[...], grad_latent) * mask)
        put_products(tile, grad_decoded, queries)
        s.qd[:, where] = grad_decoded

    lax.fori_loop(0, tiles, phase_c, None)
    table_sum.start()
    table_sum.middle()

    def cross_query_grads(tile, _):
        where = columns(tile)
        upstream = s.qd[:, where]
        grad = per_block(
            tile, lambda b: dot_at(summary(s.table_other, tile, b), upstream[:, lanes_of(b)])
        )
        s.qd[:, where] = low(grad)

    def outputs(tile, _):
        where = columns(tile)
        output = dot(s.t_do[...], s.u2[:, where]) + dot(s.t_p2[...], s.e1[:, where]) + column(7)
        s.qd[:, where] = low(output)
        out_copy(tile, s.qd, s.layer_output).start()

    lax.fori_loop(0, tiles, cross_query_grads, None)
    s.grad_dq[...] = dot_bt(s.phi[...], s.qd[...])
    s.fourier[pl.ds(0, FOUR, stride=2), :] = s.grad_dq[:, :LANES]
    s.fourier[pl.ds(1, FOUR, stride=2), :] = s.grad_dq[:, LANES:]
    s.grad_do[...] = dot_bt(s.u2[...], s.u3[...])
    table_sum.late(s.table_third)
    s.grad_p1[...] = dot_bt(s.o[...], s.kv[...])
    s.grad_p2[...] = dot_bt(s.e1[...], s.u1[...])
    zeros = jnp.zeros((share, LANES), f32)

    def rows_of(chunk, count=1):
        size = share * count
        return pl.ds(pl.multiple_of(chunk * size, size), size)

    def chunk_c(chunk):
        where = rows_of(chunk)
        return jnp.concatenate(
            [
                s.grad_do[where, :],
                s.grad_p1[where, :width],
                s.grad_p1[where, width:],
                s.grad_p2[rows_of(chunk, 2), :],
                jnp.concatenate([s.fourier[where, :], zeros], axis=1),
            ],
            axis=0,
        )

    sum_c = GradSum(at, s, "c", 0)
    sum_c.start(chunk_c)
    lax.fori_loop(0, tiles, outputs, None)
    table_sum.last(s.table_third)
    end_out(s.qd, s.layer_output)
    aside_a.load()
    aside_b.load()
    sum_c.second()
    table_sum.finish(s.table_third)

    def phase_d(tile, _):
        where = columns(tile)
        mask = s.mask[0:1, where]
        keys, values = s.kvd[:width, where], s.kvd[width:, where]
        tables = [summary(s.table_third, tile, block) for block in range(tile_blocks)]
        grad_keys = per_block(tile, lambda b: dot_at(tables[b], values[:, lanes_of(b)])) * mask
        grad_values = per_block(tile, lambda b: dot(tables[b], keys[:, lanes_of(b)]))
        grad_pair = low(jnp.concatenate([grad_keys, grad_values], axis=0))
        s.kvd[:, where] = grad_pair
        grad_outer = dot(s.w_kv[...], grad_pair)
        scaled = s.xh3[:, where].astype(f32)
        add_sum(4, grad_outer * scaled)
        add_sum(5, grad_outer)
        grad_encoded = column_norm_back(
            grad_outer, scaled, s.root_three[0:1, where], column(4)
        )
        add_sum(6, grad_encoded)
        grad_encoded_low = low(grad_encoded)
        s.xh3[:, where] = grad_encoded_low
        grad_hidden = dot(s.w_w2[...], grad_encoded_low) * s.slope[:, where].astype(f32)
        add_sum(8, grad_hidden)
        grad_hidden = low(grad_hidden)
        s.slope[:, where] = grad_hidden
        grad_middle = dot(s.w_w1[...], grad_hidden)
        scaled = s.xh2[:, where].astype(f32)
        add_sum(2, grad_middle * scaled)
        add_sum(3, grad_middle)
        grad_first = grad_encoded + column_norm_back(
            grad_middle, scaled, s.root_two[0:1, where], column(2)
        )
        grad_first = low(grad_first)
        s.xh2[:, where] = grad_first
        grad_attended = low(dot(s.w_o[...], grad_first) * mask)
        s.qd[:, where] = grad_attended
        put_products(tile, grad_attended, s.q[:, where])

    lax.fori_loop(0, tiles // 2, phase_d, None)
    sum_c.third()
    lax.fori_loop(tiles // 2, tiles, phase_d, None)
    table_sum.start()
    s.grads_c[...] = sum_c.finish()
    table_sum.middle()
    aside_a.loaded()
    aside_b.loaded()

    def query_grads(tile, _):
        where = columns(tile)
        upstream = s.qd[:, where]
        grad = per_block(
            tile, lambda b: dot_at(summary(s.table_self, tile, b), upstream[:, lanes_of(b)])
        )
        s.q[:, where] = low(turn(grad, s.cosine[:, where], s.sine[:, where], -1.0))

    lax.fori_loop(0, tiles, query_grads, None)
    s.grad_o[...] = dot_bt(s.o[...], s.xh2[...])
    s.grad_qkv[:, :width] = dot_bt(s.u1[...], s.q[...])
    table_sum.late(s.table_other)
    s.grad_kv[...] = dot_bt(s.u3[...], s.kvd[...])
    s.grad_w2[...] = dot_bt(s.e1[...], s.xh3[...])
    s.grad_w1[...] = dot_bt(s.u2[...], s.slope[...])

    def chunk_d(chunk):
        where = rows_of(chunk)
        return jnp.concatenate(
            [
                s.grad_kv[where, :width],
                s.grad_kv[where, width:],
                s.grad_o[where, :],
                s.grad_w1[where, :width],
                s.grad_w1[where, width:],
                s.grad_w2[rows_of(chunk, 2), :],
                s.grad_qkv[where, :width],
            ],
            axis=0,
        )

    sum_d = GradSum(at, s, "d", 0)
    sum_d.start(chunk_d)
    table_sum.last(s.table_other)
    table_sum.finish(s.table_other)
    sum_d.second()

    def phase_e(tile, _):
        where = columns(tile)
        mask = s.mask[0:1, where]
        keys, values = s.kv[:width, where], s.kv[width:, where]
        tables = [summary(s.table_other, tile, block) for block in range(tile_blocks)]
        grad_keys = per_block(tile, lambda b: dot_at(tables[b], values[:, lanes_of(b)])) * mask
        grad_values = low(per_block(tile, lambda b: dot(tables[b], keys[:, lanes_of(b)])))
        s.kv[:width, where] = low(turn(grad_keys, s.cosine[:, where], s.sine[:, where], -1.0))
        s.kv[width:, where] = grad_values

    lax.fori_loop(0, tiles, phase_e, None)
    s.grad_qkv[:, width:] = dot_bt(s.u1[...], s.kv[...])
    sum_e = ChipSum(at, s, "e")

    @pl.loop(0, devices)
    def _(chunk):
        where = rows_of(chunk)
        s.chip_full_e[lax.rem(chunk, 2), lax.div(chunk, 2)] = low(
            jnp.concatenate(
                [s.grad_qkv[where, width : 2 * width], s.grad_qkv[where, 2 * width :]], axis=0
            )
        )

    sum_e.start()

    def phase_f(tile, _):
        where = columns(tile)
        grad_normed = dot(
            s.w_qkv[...], jnp.concatenate([s.q[:, where], s.kv[:, where]], axis=0)
        )
        turned = s.turned[:, where].astype(f32)
        root = s.root_one[0:1, where]
        scaled = (turned - jnp.sum(turned, axis=0, keepdims=True) * (1.0 / width)) * root
        add_sum(0, grad_normed * scaled)
        add_sum(1, grad_normed)
        grad_input = s.xh2[:, where].astype(f32) + column_norm_back(
            grad_normed, scaled, root, column(0)
        )
        s.xh2[:, where] = low(grad_input)
        out_copy(tile, s.xh2, s.input_grad).start()

    sum_d.third()
    sum_e.middle()
    lax.fori_loop(0, tiles, phase_f, None)
    end_out(s.xh2, s.input_grad)
    s.grads_d[...] = sum_d.finish()
    s.grads_e[...] = sum_e.total()
    squares = sum(
        jnp.sum(grads[...] * grads[...], axis=0, keepdims=True)
        for grads in (s.grads_c, s.grads_d, s.grads_e)
    )

    lane_wide = lax.broadcasted_iota(jnp.int32, (width, LANES), 1)
    sums = jnp.zeros((width, LANES), f32)
    for index in range(12):
        sums = jnp.where(
            lane_wide == index, jnp.sum(s.vector_sum[index], axis=1, keepdims=True), sums
        )
    s.vector_cols[...] = sums
    turned_sums = s.vector_cols[...].T
    high = low(squares).astype(f32)
    s.final_near[at.core] = low(
        jnp.concatenate(
            [turned_sums[:12], high, squares - high, jnp.zeros((2, width), f32)], axis=0
        )
    )

    def final_core(start):
        source = at.core if start else 1 - at.core
        return remote(
            s.final_near.at[at.core], s.final_near.at[source], s.sem_send.at[2, 1],
            s.sem_recv.at[2, 1], at.chip * 2 + 1 - at.core,
        )

    def final_chips(step, start):
        source = at.chip if start else at.chip_at(step)
        return remote(
            s.final_far.at[at.chip], s.final_far.at[source], s.sem_send.at[1, step],
            s.sem_recv.at[1, source], at.chip_at(step) * 2 + at.core,
        )

    final_core(True).start()
    final_core(False).wait()
    total = s.final_near[0].astype(f32) + s.final_near[1].astype(f32)
    square_sum = total[12:13] + total[13:14]
    high = low(square_sum).astype(f32)
    s.final_far[at.chip] = low(
        jnp.concatenate([total[:12], high, square_sum - high, total[14:]], axis=0)
    )
    for step in range(1, at.chips):
        final_chips(step, True).start()
    for step in range(1, at.chips):
        final_chips(step, False).wait()
    total = s.final_far[0].astype(f32)
    for index in range(1, at.chips):
        total = total + s.final_far[index].astype(f32)
    s.vector_all[...] = total


def update_kernel(share, *refs):
    sources, refs = refs[:2], refs[2:]
    grads_c, grads_d, grads_e, vector_all = refs[:4]
    weights_far = refs[4:22]
    targets = refs[22:24]
    norm_out = refs[24]
    results = refs[25:43]
    flat_square, flat_expand, flat_contract, *held, sems, weight_sems = refs[43:]
    held, turned_out, weights = held[:2], held[2:4], held[4:]
    weight_loads = [
        pltpu.make_async_copy(far, near, weight_sems.at[index])
        for index, (far, near) in enumerate(zip(weights_far, weights))
    ]
    loads, stores = [], []
    size = targets[0].shape[0] // PIECES
    for piece in range(PIECES):
        where = slice(piece * size, (piece + 1) * size)
        for index in range(2):
            near = held[index].at[:, where]
            own = turned_out[index].at[where]
            loads.append(
                pltpu.make_async_copy(
                    sources[index].at[:, where], near, sems.at[0, index, piece]
                )
            )
            stores.append(
                pltpu.make_async_copy(own, targets[index].at[where], sems.at[1, index, piece])
            )
    for load in loads + weight_loads:
        load.start()
    for piece in range(PIECES):
        where = slice(piece * size, (piece + 1) * size)
        for index in range(2):
            loads[2 * piece + index].wait()
            part = held[index][:, where].astype(turned_out[index].dtype)
            turned_out[index][where] = part.T
            stores[2 * piece + index].start()
    width = grads_c.shape[1]
    places = [(grads_d, 7), (grads_e, 0), (grads_e, 1), (grads_d, 2), (grads_d, 0), (grads_d, 1), (grads_c, 0)]
    for matrix, (source, piece) in enumerate(places):
        for row in range(share):
            start = piece * share + row
            flat_square[matrix : matrix + 1, row * width : (row + 1) * width] = source[
                start : start + 1, :
            ]
    for matrix, (source, piece) in enumerate(((grads_d, 3), (grads_c, 1))):
        for half in range(2):
            for row in range(share):
                start = (piece + half) * share + row
                target = row * F + half * width
                flat_expand[matrix : matrix + 1, target : target + width] = source[
                    start : start + 1, :
                ]
    for matrix, (source, piece) in enumerate(((grads_d, 5), (grads_c, 3))):
        for row in range(2 * share):
            start = piece * share + row
            flat_contract[matrix : matrix + 1, row * width : (row + 1) * width] = source[
                start : start + 1, :
            ]
    fourier = grads_c[5 * share : 6 * share, :LANES]
    turned = vector_all[...]
    rows = jnp.sum(turned[:12] * turned[:12], axis=0, keepdims=True) + turned[12:13] + turned[13:14]
    norm = jnp.sqrt(jnp.sum(rows, axis=1, keepdims=True))
    norm_out[...] = norm
    factor = jnp.minimum(1.0, CLIP_NORM / (norm + 1e-06))
    hidden = jnp.concatenate(
        [
            jnp.concatenate([turned[8:9], turned[9:10]], axis=1),
            jnp.concatenate([turned[10:11], turned[11:12]], axis=1),
        ],
        axis=0,
    )
    for load in weight_loads:
        load.wait()
    grads = (flat_square[...], flat_expand[...], flat_contract[...], fourier, turned[:8], hidden)
    rates = (RATE_MATRIX,) * 4 + (RATE_VECTOR,) * 2
    for index, (grad, rate) in enumerate(zip(grads, rates)):
        weight, first, second = (weights[3 * index + part][...] for part in range(3))
        values = adam_update(weight, first, second, grad, factor, rate)
        for part in range(3):
            results[3 * index + part][...] = values[part]
    for store in stores:
        store.wait()


def fused(devices, features, coords, fourier_basis, block_items, point_mask, cotangent, *weights):
    points, width = features.shape
    blocks = points // BLOCK
    outers = devices // GROUP
    share = width // devices
    items = points * devices // ITEM_PTS
    bf16, f32 = jnp.bfloat16, jnp.float32
    square, expand, contract, fourier, vector, hidden = (weights[3 * i] for i in range(6))
    vmem = lambda shape, dtype: pltpu.VMEM(shape, dtype)
    inputs = {
        "items": block_items,
        "features_far": features,
        "coords": coords,
        "fourier_basis": fourier_basis,
        "point_mask": point_mask.reshape(blocks, BLOCK),
        "cotangent_far": cotangent,
        "square_weight": square,
        "expand_weight": expand,
        "contract_weight": contract,
        "fourier_weight": fourier.reshape(share, LANES),
        "vector_weight": vector,
        "hidden_weight": hidden,
    }
    rows_c, rows_d, rows_e = 6 * share, 8 * share, 2 * share
    chips = devices // 2
    outputs = {
        "layer_output": ((width, points), bf16),
        "input_grad": ((width, points), bf16),
        "grads_c": ((rows_c, width), f32),
        "grads_d": ((rows_d, width), f32),
        "grads_e": ((rows_e, width), f32),
        "vector_all": ((16, width), f32),
        "aside": ((8 * width, points), bf16),
    }
    tall = lambda rows: vmem((rows, points), bf16)
    scratch = {
        "pack": vmem((16 * share, width), f32),
        "gather_one": vmem((2, 4, outers, 4 * share, width), bf16),
        "gather_two": vmem((2, 4, outers, 12 * share, width), bf16),
        "eye": vmem((width, width), bf16),
        "heads": vmem((width, width), bf16),
        "small": vmem((LANES, width), f32),
        "cols": vmem((width, LANES), f32),
        "spread": vmem((items * E, blocks * E), bf16),
        "vector_sum": vmem((12, width, LANES), f32),
        "vector_cols": vmem((width, LANES), f32),
        "grad_qkv": vmem((width, 3 * width), f32),
        "grad_o": vmem((width, width), f32),
        "grad_kv": vmem((width, 2 * width), f32),
        "grad_do": vmem((width, width), f32),
        "grad_w1": vmem((width, F), f32),
        "grad_p1": vmem((width, F), f32),
        "grad_w2": vmem((F, width), f32),
        "grad_p2": vmem((F, width), f32),
        "grad_dq": vmem((FOUR, width), f32),
        "fourier": vmem((2 * FOUR, LANES), f32),
        "w_qkv": vmem((width, 3 * width), bf16),
        "t_qkv": vmem((3 * width, width), bf16),
        "w_o": vmem((width, width), bf16),
        "t_o": vmem((width, width), bf16),
        "w_kv": vmem((width, 2 * width), bf16),
        "t_kv": vmem((2 * width, width), bf16),
        "w_do": vmem((width, width), bf16),
        "t_do": vmem((width, width), bf16),
        "w_w1": vmem((width, F), bf16),
        "t_w1": vmem((F, width), bf16),
        "w_p1": vmem((width, F), bf16),
        "t_p1": vmem((F, width), bf16),
        "w_w2": vmem((F, width), bf16),
        "t_w2": vmem((width, F), bf16),
        "w_p2": vmem((F, width), bf16),
        "t_p2": vmem((width, F), bf16),
        "t_dq": vmem((width, FOUR), bf16),
        "mask": vmem((1, points), f32),
        "root_one": vmem((1, points), f32),
        "root_two": vmem((1, points), f32),
        "root_three": vmem((1, points), f32),
        "cosine": vmem((E // 2, points), f32),
        "sine": vmem((E // 2, points), f32),
        "phi": tall(FOUR),
        "u1": tall(width),
        "q": tall(width),
        "kv": tall(2 * width),
        "qd": tall(width),
        "o": tall(width),
        "xh2": tall(width),
        "u2": tall(width),
        "e1": tall(F),
        "slope": tall(F),
        "xh3": tall(width),
        "u3": tall(width),
        "kvd": tall(2 * width),
        "per_block": vmem((blocks * E, width), bf16),
        "inverse": vmem((8, width), f32),
        "table_self": vmem((2, chips, 16, width), bf16),
        "table_other": vmem((2, chips, 16, width), bf16),
        "final_near": vmem((2, 16, width), bf16),
        "final_far": vmem((chips, 16, width), bf16),
        "turned": tall(width),
        "sem_in": pltpu.SemaphoreType.DMA((2,)),
        "sem_aside": pltpu.SemaphoreType.DMA((8,)),
        "table_third": vmem((2, chips, 16, width), bf16),
        "load_slots": vmem((2, TILE, width), bf16),
        "sem_out": pltpu.SemaphoreType.DMA((points // TILE,)),
    }
    for key in ("t", "e"):
        scratch["chip_full_" + key] = vmem((2, chips, 16, width), bf16)
        for part in ("chip_half_", "chip_others_"):
            scratch[part + key] = vmem((chips, 16, width), bf16)
    for key, rows in (("c", rows_c), ("d", rows_d)):
        for part in ("half_", "quarter_"):
            scratch[part + key] = vmem((4, outers, rows, width), bf16)
        scratch["last_" + key] = vmem((outers, rows, width), bf16)
    for key in ("sem_send", "sem_recv"):
        scratch[key] = pltpu.SemaphoreType.DMA((3, chips))
    names = list(inputs) + list(outputs) + list(scratch)
    spaces = {"items": pltpu.SMEM, "features_far": pl.ANY, "cotangent_far": pl.ANY}
    in_specs = [pl.BlockSpec(memory_space=spaces.get(name, pltpu.VMEM)) for name in inputs]
    whole = pl.BlockSpec(memory_space=pltpu.VMEM)
    made = pl.pallas_call(
        functools.partial(layer_kernel, names, devices),
        out_shape=[jax.ShapeDtypeStruct(*shape) for shape in outputs.values()],
        in_specs=in_specs,
        out_specs=[pl.BlockSpec(memory_space=pl.ANY)] * 2
        + [whole] * 4
        + [pl.BlockSpec(memory_space=pl.ANY)],
        scratch_shapes=list(scratch.values()),
        compiler_params=pltpu.CompilerParams(
            collective_id=0, has_side_effects=True, vmem_limit_bytes=VMEM_BYTES
        ),
    )(*inputs.values())
    flat = list(weights)
    for part in range(9, 12):
        flat[part] = flat[part].reshape(share, LANES)
    shapes = [jax.ShapeDtypeStruct((1, 1), f32)] + [
        jax.ShapeDtypeStruct(flat[index].shape, f32) for index in range(18)
    ]
    order = []
    for index in range(6):
        order += [shapes[1 + 3 * index]] * 3
    updated = pl.pallas_call(
        functools.partial(update_kernel, share),
        out_shape=[jax.ShapeDtypeStruct((points, width), dtype) for dtype in (bf16, f32)]
        + [shapes[0]]
        + order,
        in_specs=[pl.BlockSpec(memory_space=pl.ANY)] * 2
        + [whole] * 4
        + [pl.BlockSpec(memory_space=pl.ANY)] * 18,
        out_specs=[pl.BlockSpec(memory_space=pl.ANY)] * 2 + [whole] * 19,
        scratch_shapes=[
            vmem(square.shape, f32),
            vmem(expand.shape, f32),
            vmem(contract.shape, f32),
            vmem((width, points), bf16),
            vmem((width, points), bf16),
            vmem((points, width), bf16),
            vmem((points, width), f32),
            *(vmem(weight.shape, f32) for weight in flat),
            pltpu.SemaphoreType.DMA((2, 2, PIECES)),
            pltpu.SemaphoreType.DMA((18,)),
        ],
        compiler_params=pltpu.CompilerParams(vmem_limit_bytes=VMEM_BYTES),
    )(*made[:6], *flat)
    layer_output, input_grad, norm, *rest = updated
    for part in range(9, 12):
        rest[part] = rest[part].reshape(fourier.shape)
    return (layer_output, input_grad, norm.reshape(()), *rest)


def shards(features, *others):
    devices = lax.axis_size("pts")
    width = features.shape[1]
    if devices % GROUP == 0 and width == 8 * devices:
        return fused(devices, features, *others)
    return plain(features, *others)


def solution(mesh):
    in_specs = (
        P("pts", None),
        P(None, "pts"),
        P(),
        P("pts"),
        P("pts"),
        P("pts", None),
        P(None, "pts"),
        P(None, "pts"),
        P(None, "pts"),
        P(None, "pts"),
        P(None, "pts"),
        P(None, "pts"),
        P(None, "pts"),
        P(None, "pts"),
        P(None, "pts"),
        P("pts"),
        P("pts"),
        P("pts"),
        P(),
        P(),
        P(),
        P(),
        P(),
        P(),
    )
    out_specs = (
        P("pts", None),
        P("pts", None),
        P(),
        P(None, "pts"),
        P(None, "pts"),
        P(None, "pts"),
        P(None, "pts"),
        P(None, "pts"),
        P(None, "pts"),
        P(None, "pts"),
        P(None, "pts"),
        P(None, "pts"),
        P("pts"),
        P("pts"),
        P("pts"),
        P(),
        P(),
        P(),
        P(),
        P(),
        P(),
    )
    return jax.shard_map(shards, mesh=mesh, in_specs=in_specs, out_specs=out_specs, check_vma=False)
```

```python
import functools
import math
import types

import jax
import jax.numpy as jnp
from jax import lax
from jax.experimental import pallas as pl
from jax.experimental.pallas import tpu as pltpu
from jax.sharding import PartitionSpec as P

H = 8
E = 32
F = 512
FOUR = 128
BLOCK = 128
ITEM_PTS = 8192
STEP = 10


NORM_EPS = 1e-05
GELU_C = math.sqrt(2.0 / math.pi)
GELU_A = 0.044715
BETA_ONE = 0.9
BETA_TWO = 0.95
ADAM_EPS = 1e-08
WEIGHT_DECAY = 0.1
RATE_MATRIX = 0.05
RATE_VECTOR = 0.25
CLIP_NORM = 1.0
HIGHEST_PRECISION = lax.Precision.HIGHEST


def matmul(left, right):
    return jnp.dot(left, right, preferred_element_type=jnp.float32)


def matmul_left(left, right):
    return lax.dot_general(
        left, right, (((0,), (0,)), ((), ())), preferred_element_type=jnp.float32
    )


def matmul_right(left, right):
    return lax.dot_general(
        left, right, (((1,), (1,)), ((), ())), preferred_element_type=jnp.float32
    )


def gelu(values):
    return 0.5 * values * (1.0 + jnp.tanh(GELU_C * (values + GELU_A * values * values * values)))


def gelu_slope(values):
    tangent = jnp.tanh(GELU_C * (values + GELU_A * values * values * values))
    return 0.5 * (1.0 + tangent) + 0.5 * values * (1.0 - tangent * tangent) * GELU_C * (
        1.0 + 3.0 * GELU_A * values * values
    )


def norm_parts(values, norm_gain, norm_bias):
    centred = values - jnp.mean(values, axis=-1, keepdims=True)
    variance = jnp.mean(centred * centred, axis=-1, keepdims=True)
    root_inv = lax.rsqrt(variance + NORM_EPS)
    scaled = centred * root_inv
    return (scaled * norm_gain + norm_bias, scaled, root_inv)


def norm_back(upstream, scaled, root_inv, norm_gain):
    through = upstream * norm_gain
    centre = jnp.mean(through, axis=-1, keepdims=True)
    along = jnp.mean(through * scaled, axis=-1, keepdims=True)
    return root_inv * (through - centre - scaled * along)


def rotary_tables(coords):
    quarter = E // 4
    frequency = math.pi * (jnp.arange(quarter, dtype=jnp.float32) + 1.0) / quarter
    first_angle = coords[0][:, None] * frequency[None, :]
    second_angle = coords[1][:, None] * frequency[None, :]
    angles = jnp.concatenate([first_angle, first_angle, second_angle, second_angle], axis=1)
    return (jnp.cos(angles), jnp.sin(angles))


def rotate(values, cosine, sine):
    quarter = E // 4
    swapped = jnp.concatenate(
        [
            -values[..., quarter : 2 * quarter],
            values[..., :quarter],
            -values[..., 3 * quarter :],
            values[..., 2 * quarter : 3 * quarter],
        ],
        axis=-1,
    )
    return values * cosine[:, None, :] + swapped * sine[:, None, :]


def rotate_back(grads, cosine, sine):
    quarter = E // 4
    scaled = grads * sine[:, None, :]
    swapped = jnp.concatenate(
        [
            scaled[..., quarter : 2 * quarter],
            -scaled[..., :quarter],
            scaled[..., 3 * quarter :],
            -scaled[..., 2 * quarter : 3 * quarter],
        ],
        axis=-1,
    )
    return grads * cosine[:, None, :] + swapped


def fourier_features(coords, fourier_basis):
    phases = (
        2.0
        * math.pi
        * (
            coords[0][:, None] * fourier_basis[0][None, :]
            + coords[1][:, None] * fourier_basis[1][None, :]
        )
    )
    return jnp.concatenate([jnp.cos(phases), jnp.sin(phases)], axis=1)


def block_table(left, right, onehot):
    blocks = onehot.shape[0]
    per_block = jnp.einsum(
        "bphe,bphf->bhef",
        left.reshape(blocks, BLOCK, H, E),
        right.reshape(blocks, BLOCK, H, E),
        preferred_element_type=jnp.float32,
    )
    return jnp.einsum("ba,bhef->ahef", onehot, per_block, precision=HIGHEST_PRECISION)


def scale_round(table, inverse_count):
    return (table * inverse_count[:, None, None, None]).astype(jnp.bfloat16)


def spread(summary, onehot):
    selected = jnp.einsum(
        "ba,ahef->bhef", onehot.astype(jnp.bfloat16), summary, preferred_element_type=jnp.float32
    )
    return selected.astype(jnp.bfloat16)


def apply_summary(rows_low, block_summary, transposed):
    blocks = block_summary.shape[0]
    pattern = "bphf,bhef->bphe" if transposed else "bphe,bhef->bphf"
    mixed = jnp.einsum(
        pattern,
        rows_low.reshape(blocks, BLOCK, H, E),
        block_summary,
        preferred_element_type=jnp.float32,
    )
    return mixed.reshape(-1, H * E)


def galerkin_backward(
    grad_low, queries_low, keys_masked, values_low, block_summary, onehot, mask_float, reducer
):
    grad_masked = grad_low * mask_float.astype(jnp.bfloat16)
    grad_queries = apply_summary(grad_masked, block_summary, True)
    summary_grad = reducer(block_table(queries_low, grad_masked, onehot))
    block_grad = spread(summary_grad, onehot)
    grad_keys = apply_summary(values_low, block_grad, True) * mask_float
    grad_values = apply_summary(keys_masked, block_grad, False)
    return (grad_queries, grad_keys, grad_values)


def adam_update(weight, first, second, grad, factor, rate):
    clipped = grad * factor
    new_first = BETA_ONE * first + (1.0 - BETA_ONE) * clipped
    new_second = BETA_TWO * second + (1.0 - BETA_TWO) * clipped * clipped
    first_hat = new_first / (1.0 - BETA_ONE**STEP)
    second_hat = new_second / (1.0 - BETA_TWO**STEP)
    new_weight = weight - rate * (
        first_hat / (jnp.sqrt(second_hat) + ADAM_EPS) + WEIGHT_DECAY * weight
    )
    return (new_first, new_second, new_weight)


def own_share(full, width, along, start_index):
    return lax.dynamic_slice_in_dim(full, start_index * width, width, along)


def plain(
    features,
    coords,
    fourier_basis,
    block_items,
    point_mask,
    cotangent,
    square_weight,
    square_first,
    square_second,
    expand_weight,
    expand_first,
    expand_second,
    contract_weight,
    contract_first,
    contract_second,
    fourier_weight,
    fourier_first,
    fourier_second,
    vector_weight,
    vector_first,
    vector_second,
    hidden_weight,
    hidden_first,
    hidden_second,
):
    rows = features.shape[0]
    width = features.shape[1]
    blocks = rows // BLOCK
    devices = lax.axis_size("pts")
    items_total = rows * devices // ITEM_PTS
    gathered = (
        lax.all_gather(square_weight.astype(jnp.bfloat16), "pts", axis=1, tiled=True),
        lax.all_gather(expand_weight.astype(jnp.bfloat16), "pts", axis=1, tiled=True),
        lax.all_gather(contract_weight.astype(jnp.bfloat16), "pts", axis=1, tiled=True),
        lax.all_gather(fourier_weight.astype(jnp.bfloat16), "pts", axis=0, tiled=True),
    )
    square_full = gathered[0].reshape(7, width, width)
    expand_full = gathered[1].reshape(2, width, F)
    contract_full = gathered[2].reshape(2, F, width)
    fourier_full = gathered[3].reshape(FOUR, width)
    onehot = (block_items[:, None] == jnp.arange(items_total, dtype=jnp.int32)[None, :]).astype(
        jnp.float32
    )
    mask_float = point_mask.astype(jnp.float32)[:, None]
    mask_low = mask_float.astype(jnp.bfloat16)
    block_count = jnp.sum(mask_float.reshape(blocks, BLOCK), axis=1)
    local_count = jnp.dot(block_count, onehot, precision=HIGHEST_PRECISION)
    cosine, sine = rotary_tables(coords)
    phase_low = fourier_features(coords, fourier_basis).astype(jnp.bfloat16)
    inputs = features.astype(jnp.float32)
    normed, scaled_one, root_one = norm_parts(inputs, vector_weight[0], vector_weight[1])
    normed_low = normed.astype(jnp.bfloat16)
    joint_weight = jnp.concatenate([square_full[0], square_full[1], square_full[2]], axis=1)
    projected = matmul(normed_low, joint_weight)
    queries_low = (
        rotate(projected[:, :width].reshape(rows, H, E), cosine, sine)
        .reshape(rows, width)
        .astype(jnp.bfloat16)
    )
    keys_low = (
        rotate(projected[:, width : 2 * width].reshape(rows, H, E), cosine, sine)
        .reshape(rows, width)
        .astype(jnp.bfloat16)
    )
    keys_masked = keys_low * mask_low
    values_low = projected[:, 2 * width :].astype(jnp.bfloat16)
    self_local = block_table(keys_masked, values_low, onehot)
    self_table, item_count = lax.psum((self_local, local_count), "pts")
    inverse_count = 1.0 / item_count
    self_items = scale_round(self_table, inverse_count)
    self_summary = spread(self_items, onehot)
    attended_low = (apply_summary(queries_low, self_summary, False) * mask_float).astype(
        jnp.bfloat16
    )
    first_sum = inputs + matmul(attended_low, square_full[3])
    normed_mid, scaled_two, root_two = norm_parts(first_sum, vector_weight[2], vector_weight[3])
    middle_low = normed_mid.astype(jnp.bfloat16)
    hidden_pre = matmul(middle_low, expand_full[0]) + hidden_weight[0]
    hidden_low = gelu(hidden_pre).astype(jnp.bfloat16)
    encoded = first_sum + matmul(hidden_low, contract_full[0]) + vector_weight[6]
    normed_out, scaled_three, root_three = norm_parts(encoded, vector_weight[4], vector_weight[5])
    outer_low = normed_out.astype(jnp.bfloat16)
    pair_weight = jnp.concatenate([square_full[4], square_full[5]], axis=1)
    cross_projected = matmul(outer_low, pair_weight)
    cross_keys = cross_projected[:, :width].astype(jnp.bfloat16) * mask_low
    cross_values = cross_projected[:, width:].astype(jnp.bfloat16)
    cross_queries = matmul(phase_low, fourier_full).astype(jnp.bfloat16)
    cross_local = block_table(cross_keys, cross_values, onehot)
    cross_items = scale_round(lax.psum(cross_local, "pts"), inverse_count)
    cross_summary = spread(cross_items, onehot)
    decoded_low = (apply_summary(cross_queries, cross_summary, False) * mask_float).astype(
        jnp.bfloat16
    )
    latent = matmul(decoded_low, square_full[6])
    latent_low = latent.astype(jnp.bfloat16)
    spread_pre = matmul(latent_low, expand_full[1]) + hidden_weight[1]
    spread_low = gelu(spread_pre).astype(jnp.bfloat16)
    output = latent + matmul(spread_low, contract_full[1]) + vector_weight[7]
    cross_reducer = lambda table_part: scale_round(lax.psum(table_part, "pts"), inverse_count)
    self_reducer = lambda table_part: scale_round(lax.psum(table_part, "pts"), inverse_count)
    grad_output = cotangent.astype(jnp.float32)
    grad_bias_end = jnp.sum(grad_output, axis=0)
    grad_contract_spread = matmul_left(spread_low, cotangent)
    grad_spread = matmul_right(cotangent, contract_full[1]) * gelu_slope(spread_pre)
    grad_hidden_spread = jnp.sum(grad_spread, axis=0)
    grad_spread_low = grad_spread.astype(jnp.bfloat16)
    grad_expand_spread = matmul_left(latent_low, grad_spread_low)
    grad_latent = (grad_output + matmul_right(grad_spread_low, expand_full[1])).astype(jnp.bfloat16)
    grad_out_cross = matmul_left(decoded_low, grad_latent)
    grad_decoded = matmul_right(grad_latent, square_full[6]).astype(jnp.bfloat16)
    cross_back = galerkin_backward(
        grad_decoded,
        cross_queries,
        cross_keys,
        cross_values,
        cross_summary,
        onehot,
        mask_float,
        cross_reducer,
    )
    grad_fourier_full = matmul_left(phase_low, cross_back[0].astype(jnp.bfloat16))
    grad_pair_low = jnp.concatenate([cross_back[1], cross_back[2]], axis=1).astype(jnp.bfloat16)
    grad_pair_full = matmul_left(outer_low, grad_pair_low)
    grad_normed_out = matmul_right(grad_pair_low, pair_weight)
    grad_gain_three = jnp.sum(grad_normed_out * scaled_three, axis=0)
    grad_bias_three = jnp.sum(grad_normed_out, axis=0)
    grad_encoded = norm_back(grad_normed_out, scaled_three, root_three, vector_weight[4])
    grad_bias_middle = jnp.sum(grad_encoded, axis=0)
    grad_encoded_low = grad_encoded.astype(jnp.bfloat16)
    grad_contract_enc = matmul_left(hidden_low, grad_encoded_low)
    grad_hidden = matmul_right(grad_encoded_low, contract_full[0]) * gelu_slope(hidden_pre)
    grad_hidden_enc = jnp.sum(grad_hidden, axis=0)
    grad_hidden_low = grad_hidden.astype(jnp.bfloat16)
    grad_expand_enc = matmul_left(middle_low, grad_hidden_low)
    grad_middle = matmul_right(grad_hidden_low, expand_full[0])
    grad_gain_two = jnp.sum(grad_middle * scaled_two, axis=0)
    grad_bias_two = jnp.sum(grad_middle, axis=0)
    grad_first = grad_encoded + norm_back(grad_middle, scaled_two, root_two, vector_weight[2])
    grad_first_low = grad_first.astype(jnp.bfloat16)
    grad_out_self = matmul_left(attended_low, grad_first_low)
    grad_attended = matmul_right(grad_first_low, square_full[3]).astype(jnp.bfloat16)
    self_back = galerkin_backward(
        grad_attended,
        queries_low,
        keys_masked,
        values_low,
        self_summary,
        onehot,
        mask_float,
        self_reducer,
    )
    grad_queries = rotate_back(self_back[0].reshape(rows, H, E), cosine, sine).reshape(rows, width)
    grad_keys = rotate_back(self_back[1].reshape(rows, H, E), cosine, sine).reshape(rows, width)
    grad_joint_low = jnp.concatenate([grad_queries, grad_keys, self_back[2]], axis=1).astype(
        jnp.bfloat16
    )
    grad_joint_full = matmul_left(normed_low, grad_joint_low)
    grad_normed = matmul_right(grad_joint_low, joint_weight)
    grad_gain_one = jnp.sum(grad_normed * scaled_one, axis=0)
    grad_bias_one = jnp.sum(grad_normed, axis=0)
    grad_inputs = grad_first + norm_back(grad_normed, scaled_one, root_one, vector_weight[0])
    grad_square = jnp.stack(
        [
            grad_joint_full[:, :width],
            grad_joint_full[:, width : 2 * width],
            grad_joint_full[:, 2 * width :],
            grad_out_self,
            grad_pair_full[:, :width],
            grad_pair_full[:, width:],
            grad_out_cross,
        ]
    ).reshape(7, width * width)
    grad_expand = jnp.stack([grad_expand_enc, grad_expand_spread]).reshape(2, width * F)
    grad_contract = jnp.stack([grad_contract_enc, grad_contract_spread]).reshape(2, F * width)
    grad_fourier = grad_fourier_full.reshape(FOUR * width)
    grad_vector = jnp.stack(
        [
            grad_gain_one,
            grad_bias_one,
            grad_gain_two,
            grad_bias_two,
            grad_gain_three,
            grad_bias_three,
            grad_bias_middle,
            grad_bias_end,
        ]
    )
    grad_hidden_rows = jnp.stack([grad_hidden_enc, grad_hidden_spread])
    totals = lax.psum(
        (grad_square, grad_expand, grad_contract, grad_fourier, grad_vector, grad_hidden_rows),
        "pts",
    )
    squares = sum((jnp.sum(total_part * total_part) for total_part in totals))
    start_index = lax.axis_index("pts")
    share_square = own_share(totals[0], square_weight.shape[1], 1, start_index)
    share_expand = own_share(totals[1], expand_weight.shape[1], 1, start_index)
    share_contract = own_share(totals[2], contract_weight.shape[1], 1, start_index)
    share_fourier = own_share(totals[3], fourier_weight.shape[0], 0, start_index)
    vector_total = totals[4]
    hidden_total = totals[5]
    grad_norm = jnp.sqrt(squares)
    factor = jnp.minimum(1.0, CLIP_NORM / (grad_norm + 1e-06))
    new_square = adam_update(
        square_weight, square_first, square_second, share_square, factor, RATE_MATRIX
    )
    new_expand = adam_update(
        expand_weight, expand_first, expand_second, share_expand, factor, RATE_MATRIX
    )
    new_contract = adam_update(
        contract_weight, contract_first, contract_second, share_contract, factor, RATE_MATRIX
    )
    new_fourier = adam_update(
        fourier_weight, fourier_first, fourier_second, share_fourier, factor, RATE_MATRIX
    )
    new_vector = adam_update(
        vector_weight, vector_first, vector_second, vector_total, factor, RATE_VECTOR
    )
    new_hidden = adam_update(
        hidden_weight, hidden_first, hidden_second, hidden_total, factor, RATE_VECTOR
    )
    return (
        output.astype(jnp.bfloat16),
        grad_inputs,
        grad_norm,
        new_square[0],
        new_square[1],
        new_square[2],
        new_expand[0],
        new_expand[1],
        new_expand[2],
        new_contract[0],
        new_contract[1],
        new_contract[2],
        new_fourier[0],
        new_fourier[1],
        new_fourier[2],
        new_vector[0],
        new_vector[1],
        new_vector[2],
        new_hidden[0],
        new_hidden[1],
        new_hidden[2],
    )


GROUP = 8
TILE = 1024
PUT = 512
LANES = 128
E_BITS = E.bit_length() - 1
PIECES = 4
VMEM_BYTES = 64 * 1024 * 1024


def dot(left, right):
    return jnp.dot(left, right, preferred_element_type=jnp.float32)


def dot_bt(left, right):
    return lax.dot_general(
        left, right, (((1,), (1,)), ((), ())), preferred_element_type=jnp.float32
    )


def dot_at(left, right):
    return lax.dot_general(
        left, right, (((0,), (0,)), ((), ())), preferred_element_type=jnp.float32
    )


def low(values):
    return values.astype(jnp.bfloat16)


def column_norm(values):
    inverse = 1.0 / values.shape[0]
    centred = values - jnp.sum(values, axis=0, keepdims=True) * inverse
    variance = jnp.sum(centred * centred, axis=0, keepdims=True) * inverse
    root_inv = lax.rsqrt(variance + NORM_EPS)
    return (centred * root_inv, root_inv)


def column_norm_back(upstream, scaled, root_inv, gain):
    inverse = 1.0 / upstream.shape[0]
    through = upstream * gain
    centre = jnp.sum(through, axis=0, keepdims=True) * inverse
    along = jnp.sum(through * scaled, axis=0, keepdims=True) * inverse
    return root_inv * (through - centre - scaled * along)


def gelu_alone(values):
    half = 0.5 * values
    return half + half * jnp.tanh(values * (GELU_C + (GELU_C * GELU_A) * (values * values)))


def gelu_both(values):
    square = values * values
    half = 0.5 + 0.5 * jnp.tanh(values * (GELU_C + (GELU_C * GELU_A) * square))
    slope = half + values * (half * (1.0 - half)) * (
        2.0 * GELU_C + (6.0 * GELU_C * GELU_A) * square
    )
    return (values * half, slope)


def turn(values, cosine, sine, sign):
    quarter = E // 4
    first_cos, second_cos = cosine[:quarter], cosine[quarter:]
    first_sin, second_sin = sine[:quarter] * sign, sine[quarter:] * sign
    parts = []
    for base in range(0, values.shape[0], E):
        one, two, three, four = (
            values[base + quarter * step : base + quarter * (step + 1)] for step in range(4)
        )
        parts += [
            one * first_cos - two * first_sin,
            two * first_cos + one * first_sin,
            three * second_cos - four * second_sin,
            four * second_cos + three * second_sin,
        ]
    return jnp.concatenate(parts, axis=0)


def head_of(index):
    return lax.shift_right_logical(index, E_BITS)


def compress(full):
    width = full.shape[1]
    head = head_of(lax.broadcasted_iota(jnp.int32, (E, width), 1))
    result = full[:E]
    for index in range(1, H):
        result = jnp.where(head == index, full[E * index : E * (index + 1)], result)
    return result


def lane_sum(values):
    result = values[:, :LANES]
    for start in range(LANES, values.shape[1], LANES):
        result = result + values[:, start : start + LANES]
    return result


def remote(source, target, send_sem, recv_sem, device):
    return pltpu.make_async_remote_copy(
        src_ref=source,
        dst_ref=target,
        send_sem=send_sem,
        recv_sem=recv_sem,
        device_id=(device,),
        device_id_type=pl.DeviceIdType.MESH,
    )


class Place:
    def __init__(self, devices):
        self.devices = devices
        self.outers = devices // GROUP
        self.me = lax.axis_index("pts")
        self.inner = lax.rem(self.me, GROUP)
        self.outer = lax.div(self.me, GROUP)
        self.core = lax.rem(self.me, 2)
        self.pair = lax.div(self.inner, 2)
        self.chips = devices // 2
        self.chip = lax.div(self.me, 2)

    def chip_at(self, step):
        return lax.rem(self.chip + step, self.chips)

    def inner_at(self, step):
        return lax.rem(self.inner + step, GROUP)

    def outer_at(self, step):
        return lax.rem(self.outer + step, self.outers)

    def pair_at(self, step):
        return lax.rem(self.pair + step, 4)

    def device(self, outer, inner):
        return outer * GROUP + inner


class Gather:
    def __init__(self, place, buffer, scratch, slots):
        self.place, self.buffer = place, buffer
        self.send, self.recv = scratch.sem_send, scratch.sem_recv
        self.slots = slots

    def first(self, step, start):
        at = self.place
        slot = self.buffer.at[at.core, at.pair, at.outer if start else at.outer_at(step)]
        mine = self.buffer.at[at.core, at.pair, at.outer]
        source = at.outer if start else at.outer_at(step)
        return remote(
            mine, slot, self.send.at[self.slots[0], self.slots[1] + step],
            self.recv.at[self.slots[0], self.slots[1] + source],
            at.device(at.outer_at(step), at.inner),
        )

    def second(self, step, start):
        at = self.place
        source = at.pair if start else at.pair_at(step)
        return remote(
            self.buffer.at[at.core, at.pair], self.buffer.at[at.core, source],
            self.send.at[2, self.slots[2] + step], self.recv.at[2, self.slots[2] + source],
            at.device(at.outer, at.pair_at(step) * 2 + at.core),
        )

    def third(self, start):
        at = self.place
        source = at.core if start else 1 - at.core
        return remote(
            self.buffer.at[at.core], self.buffer.at[source], self.send.at[2, self.slots[3]],
            self.recv.at[2, self.slots[3]], at.device(at.outer, at.pair * 2 + 1 - at.core),
        )

    def start_first(self):
        for step in range(1, self.place.outers):
            self.first(step, True).start()

    def start_second(self):
        for step in range(1, self.place.outers):
            self.first(step, False).wait()
        for step in range(1, 4):
            self.second(step, True).start()

    def start_third(self):
        for step in range(1, 4):
            self.second(step, False).wait()
        self.third(True).start()

    def finish(self):
        self.third(False).wait()


class ChipSum:
    def __init__(self, place, scratch, key):
        self.place = place
        self.full, self.half, self.others = (
            getattr(scratch, name + key) for name in ("chip_full_", "chip_half_", "chip_others_")
        )
        self.send, self.recv = scratch.sem_send, scratch.sem_recv

    def swap(self):
        at = self.place
        return remote(
            self.full.at[1 - at.core], self.half, self.send.at[2, 0], self.recv.at[2, 0],
            at.chip * 2 + 1 - at.core,
        )

    def cross(self, step, start):
        at = self.place
        source = at.chip if start else at.chip_at(step)
        return remote(
            self.half.at[at.chip_at(step)], self.others.at[source], self.send.at[0, step],
            self.recv.at[0, source], at.chip_at(step) * 2 + at.core,
        )

    def start(self):
        self.swap().start()

    def middle(self):
        at = self.place
        self.swap().wait()
        self.half[...] = low(
            self.full[at.core].astype(jnp.float32) + self.half[...].astype(jnp.float32)
        )
        for step in range(1, at.chips):
            self.cross(step, True).start()

    def total(self):
        at = self.place
        total = self.half[at.chip].astype(jnp.float32)
        for step in range(1, at.chips):
            self.cross(step, False).wait()
            total = total + self.others[at.chip_at(step)].astype(jnp.float32)
        return total


class TableSum(ChipSum):
    def __init__(self, place, scratch):
        super().__init__(place, scratch, "t")
        self.s = scratch

    def share(self, step, start, result):
        at = self.place
        source = at.chip if start else at.chip_at(step)
        return remote(
            result.at[at.core, at.chip], result.at[at.core, source], self.send.at[1, step],
            self.recv.at[1, source], at.chip_at(step) * 2 + at.core,
        )

    def swap_back(self, start, result):
        at = self.place
        source = at.core if start else 1 - at.core
        return remote(
            result.at[at.core], result.at[source], self.send.at[2, 1], self.recv.at[2, 1],
            at.chip * 2 + 1 - at.core,
        )

    def start(self):
        s = self.s
        table = low(dot(s.spread[...], s.per_block[...]))
        for chunk in range(self.place.devices):
            self.full[chunk % 2, chunk // 2] = table[chunk * 16 : (chunk + 1) * 16]
        super().start()

    def late(self, result):
        at, s = self.place, self.s
        result[at.core, at.chip] = low(self.total() * s.inverse[0:1, :])
        for step in range(1, at.chips):
            self.share(step, True, result).start()

    def last(self, result):
        for step in range(1, self.place.chips):
            self.share(step, False, result).wait()
        self.swap_back(True, result).start()

    def finish(self, result):
        self.swap_back(False, result).wait()


class GradSum:
    def __init__(self, place, scratch, key, first):
        self.place = place
        self.half, self.quarter, self.last = (
            getattr(scratch, name + key) for name in ("half_", "quarter_", "last_")
        )
        self.full = scratch.gather_two.at[:, :, :, first : first + self.last.shape[1]]
        self.send, self.recv = scratch.sem_send, scratch.sem_recv

    def swap(self):
        at = self.place
        return remote(
            self.full.at[1 - at.core], self.half, self.send.at[2, 7], self.recv.at[2, 7],
            at.device(at.outer, at.pair * 2 + 1 - at.core),
        )

    def across(self, step, start):
        at = self.place
        source = at.pair if start else at.pair_at(step)
        return remote(
            self.half.at[at.pair_at(step)], self.quarter.at[source], self.send.at[2, 8 + step],
            self.recv.at[2, 8 + source], at.device(at.outer, at.pair_at(step) * 2 + at.core),
        )

    def along(self, step, start):
        at = self.place
        source = at.outer if start else at.outer_at(step)
        return remote(
            self.quarter.at[at.pair, at.outer_at(step)], self.last.at[source], self.send.at[2, 12 + step],
            self.recv.at[2, 12 + source], at.device(at.outer_at(step), at.inner),
        )

    def start(self, chunk_of):
        at = self.place

        @pl.loop(0, at.devices)
        def _(chunk):
            inner = lax.rem(chunk, GROUP)
            self.full[lax.rem(inner, 2), lax.div(inner, 2), lax.div(chunk, GROUP)] = low(
                chunk_of(chunk)
            )

        self.swap().start()

    def second(self):
        at = self.place
        self.swap().wait()

        @pl.loop(0, 4)
        def _(pair):
            self.half[pair] = low(
                self.full[at.core, pair].astype(jnp.float32) + self.half[pair].astype(jnp.float32)
            )

        for step in range(1, 4):
            self.across(step, True).start()

    def third(self):
        at = self.place
        total = self.half[at.pair].astype(jnp.float32)
        for step in range(1, 4):
            self.across(step, False).wait()
            total = total + self.quarter[at.pair_at(step)].astype(jnp.float32)
        self.quarter[at.pair] = low(total)
        for step in range(1, at.outers):
            self.along(step, True).start()

    def finish(self):
        at = self.place
        total = self.quarter[at.pair, at.outer].astype(jnp.float32)
        for step in range(1, at.outers):
            self.along(step, False).wait()
            total = total + self.last[at.outer_at(step)].astype(jnp.float32)
        return total


def layer_kernel(names, devices, *refs):
    s = types.SimpleNamespace(**dict(zip(names, refs)))
    at = Place(devices)
    points, width = s.features_far.shape
    tiles = points // TILE
    blocks = points // BLOCK
    share = width // devices
    tile_blocks = TILE // BLOCK
    f32 = jnp.float32

    barrier = pltpu.get_barrier_semaphore()
    pl.semaphore_signal(
        barrier, inc=1, device_id=(at.chip * 2 + 1 - at.core,),
        device_id_type=pl.DeviceIdType.MESH,
    )
    for step in range(1, 4):
        pl.semaphore_signal(
            barrier, inc=1, device_id=(at.device(at.outer, at.pair_at(step) * 2 + at.core),),
            device_id_type=pl.DeviceIdType.MESH,
        )
    for step in range(1, at.outers):
        pl.semaphore_signal(
            barrier, inc=1, device_id=(at.device(at.outer_at(step), at.inner),),
            device_id_type=pl.DeviceIdType.MESH,
        )

    def tile_load(source, tile):
        slot = lax.rem(tile, 2)
        where = pl.ds(pl.multiple_of(tile * TILE, TILE), TILE)
        return pltpu.make_async_copy(
            source.at[where, :], s.load_slots.at[slot], s.sem_in.at[slot]
        )

    for tile in range(2):
        tile_load(s.features_far, tile).start()

    class Aside:
        def __init__(self, first, *buffers):
            self.pairs = []
            row = first
            for buffer in buffers:
                for start in range(0, buffer.shape[0], width):
                    near = buffer.at[start : start + width]
                    far = s.aside.at[row : row + width]
                    self.pairs.append((near, far, s.sem_aside.at[row // width]))
                    row += width

        def store(self):
            for near, far, sem in self.pairs:
                pltpu.make_async_copy(near, far, sem).start()

        def stored(self):
            for near, far, sem in self.pairs:
                pltpu.make_async_copy(near, far, sem).wait()

        def load(self):
            for near, far, sem in self.pairs:
                pltpu.make_async_copy(far, near, sem).start()

        def loaded(self):
            for near, far, sem in self.pairs:
                pltpu.make_async_copy(far, near, sem).wait()

    aside_a = Aside(0, s.u1, s.kv)
    aside_b = Aside(3 * width, s.e1, s.o, s.u2, s.u3)

    def columns(tile):
        return pl.ds(pl.multiple_of(tile * TILE, TILE), TILE)

    def block_columns(block):
        return pl.ds(pl.multiple_of(block * BLOCK, BLOCK), BLOCK)

    def column(index):
        return s.cols[:, index : index + 1]

    def hidden_column(index):
        return jnp.concatenate([column(8 + 2 * index), column(9 + 2 * index)], axis=0)

    def out_copy(tile, source, target):
        where = pl.ds(pl.multiple_of(tile * TILE, TILE), TILE)
        return pltpu.make_async_copy(
            source.at[:, where], target.at[:, where], s.sem_out.at[tile]
        )

    def end_out(source, target):
        for tile in range(tiles):
            out_copy(tile, source, target).wait()

    def pack_square(matrix):
        for row in range(share):
            s.pack[matrix * share + row : matrix * share + row + 1, :] = s.square_weight[
                matrix : matrix + 1, row * width : (row + 1) * width
            ]

    split = s.gather_one.shape[3]
    for matrix in range(4):
        pack_square(matrix)
    s.gather_one[at.core, at.pair, at.outer] = low(s.pack[:split, :])
    pl.semaphore_wait(barrier, 4 + at.outers - 1)
    one = Gather(at, s.gather_one, s, (1, 0, 2, 6))
    two = Gather(at, s.gather_two, s, (2, 12, 8, 7))
    one.start_first()

    for matrix in range(4, 7):
        pack_square(matrix)
    for matrix in range(2):
        for half in range(2):
            for row in range(share):
                place = (7 + 2 * matrix + half) * share + row
                start = row * F + half * width
                s.pack[place : place + 1, :] = s.expand_weight[
                    matrix : matrix + 1, start : start + width
                ]
        for row in range(2 * share):
            place = (11 + 2 * matrix) * share + row
            s.pack[place : place + 1, :] = s.contract_weight[
                matrix : matrix + 1, row * width : (row + 1) * width
            ]
    s.pack[15 * share : 16 * share, :LANES] = s.fourier_weight[...]
    s.pack[15 * share : 16 * share, LANES:] = jnp.zeros((share, LANES), f32)
    live = s.point_mask[...].astype(f32)
    counts = dot_bt(jnp.ones((8, LANES), jnp.bfloat16), low(live))
    s.pack[15 * share : 15 * share + 1, LANES : LANES + blocks] = counts[:1]
    lane = lax.broadcasted_iota(jnp.int32, (1, LANES), 1)
    wide_block = head_of(lax.broadcasted_iota(jnp.int32, (1, E * blocks), 1))
    item_row = jnp.zeros((1, LANES), f32)
    item_wide = jnp.zeros((1, E * blocks), jnp.int32)
    for block in range(blocks):
        item_row = jnp.where(lane == block, s.items[block].astype(f32), item_row)
        item_wide = jnp.where(wide_block == block, s.items[block], item_wide)
    s.pack[15 * share + 1 : 15 * share + 2, LANES:] = item_row
    s.gather_two[at.core, at.pair, at.outer] = low(s.pack[split:, :])

    row_at = lax.broadcasted_iota(jnp.int32, (width, width), 0)
    lane_at = lax.broadcasted_iota(jnp.int32, (width, width), 1)
    s.eye[...] = jnp.where(row_at == lane_at, 1.0, 0.0).astype(jnp.bfloat16)
    s.heads[...] = jnp.where(head_of(row_at) == head_of(lane_at), 1.0, 0.0).astype(jnp.bfloat16)
    s.small[...] = jnp.zeros(s.small.shape, f32)
    s.small[0:8, :] = s.vector_weight[...]
    for row in range(2):
        for half in range(2):
            s.small[8 + 2 * row + half : 9 + 2 * row + half, :] = s.hidden_weight[
                row : row + 1, half * width : (half + 1) * width
            ]
    s.small[12:14, : FOUR // 2] = s.fourier_basis[...]
    s.cols[...] = s.small[...].T
    rows_wide = lax.broadcasted_iota(jnp.int32, s.spread.shape, 0)
    lanes_wide = lax.broadcasted_iota(jnp.int32, s.spread.shape, 1)
    s.spread[...] = jnp.where(
        (item_wide == head_of(rows_wide)) & (((rows_wide ^ lanes_wide) & (E - 1)) == 0), 1.0, 0.0
    ).astype(jnp.bfloat16)
    s.vector_sum[...] = jnp.zeros(s.vector_sum.shape, f32)
    speed = (lax.broadcasted_iota(jnp.int32, (E // 4, 1), 0).astype(f32) + 1.0) * (
        math.pi / (E // 4)
    )

    def add_sum(index, values):
        for part in range(values.shape[0] // width):
            s.vector_sum[index + part] += lane_sum(values[part * width : (part + 1) * width])

    def turned_load(source, tile):
        tile_load(source, tile).wait()
        turned = dot_bt(s.eye[...], s.load_slots[lax.rem(tile, 2)])

        @pl.when(tile + 2 < tiles)
        def _():
            tile_load(source, tile + 2).start()

        return turned

    def norm_one(tile, _):
        where = columns(tile)
        turned = turned_load(s.features_far, tile)
        s.turned[:, where] = low(turned)
        scaled, root = column_norm(turned)
        s.root_one[0:1, where] = root
        s.u1[:, where] = low(scaled * column(0) + column(1))

    def fourier_part(tile, _):
        where = pl.ds(pl.multiple_of(tile * PUT, PUT), PUT)
        x_row, y_row = s.coords[0:1, where], s.coords[1:2, where]
        basis = s.cols[: FOUR // 2, :]
        phases = 2.0 * math.pi * (basis[:, 12:13] * x_row + basis[:, 13:14] * y_row)
        s.phi[:, where] = low(jnp.concatenate([jnp.cos(phases), jnp.sin(phases)], axis=0))

    def angle_part(tile, _):
        where = pl.ds(pl.multiple_of(tile * PUT, PUT), PUT)
        angles = jnp.concatenate(
            [speed * s.coords[0:1, where], speed * s.coords[1:2, where]], axis=0
        )
        s.cosine[:, where] = jnp.cos(angles)
        s.sine[:, where] = jnp.sin(angles)
        for block in range(PUT // BLOCK):
            s.mask[0:1, pl.ds(pl.multiple_of(tile * PUT + block * BLOCK, BLOCK), BLOCK)] = (
                s.point_mask[pl.ds(tile * (PUT // BLOCK) + block, 1), :].astype(f32)
            )

    parts = points // PUT
    lax.fori_loop(0, tiles, norm_one, None)
    one.start_second()
    two.start_first()
    lax.fori_loop(0, 3 * parts // 4, fourier_part, None)
    one.start_third()
    two.start_second()
    lax.fori_loop(0, parts, angle_part, None)
    one.finish()

    group = 16 // share

    def chunk_pair(buffer, index):
        parts = []
        for step in range(group):
            chunk = index * group + step
            inner = lax.rem(chunk, GROUP)
            parts.append(
                buffer[lax.rem(inner, 2), lax.div(inner, 2), lax.div(chunk, GROUP)].astype(f32)
            )
        return parts

    def join(parts, piece):
        return low(
            jnp.concatenate([part[piece * share : (piece + 1) * share] for part in parts], axis=0)
        )

    @pl.loop(0, devices // group)
    def _(index):
        parts = chunk_pair(s.gather_one, index)
        where = pl.ds(pl.multiple_of(index * 16, 16), 16)
        for piece in range(3):
            s.w_qkv[where, piece * width : (piece + 1) * width] = join(parts, piece)
        s.w_o[where, :] = join(parts, 3)

    def flip(matrix):
        return low(dot_bt(s.eye[...], matrix))

    for piece in range(3):
        s.t_qkv[piece * width : (piece + 1) * width, :] = flip(
            s.w_qkv[:, piece * width : (piece + 1) * width]
        )
    s.t_o[...] = flip(s.w_o[...])

    def block_product(left, right):
        return compress(dot_bt(left, right))

    def put_products(tile, left, right):
        for block in range(tile_blocks):
            lanes = slice(block * BLOCK, (block + 1) * BLOCK)
            where = pl.ds(pl.multiple_of((tile * tile_blocks + block) * E, E), E)
            s.per_block[where, :] = low(block_product(left[:, lanes], right[:, lanes]))

    def summary(table, tile, block):
        item = s.items[tile * tile_blocks + block]
        rows = jnp.concatenate([table[0, item], table[1, item]], axis=0)
        return jnp.concatenate([rows] * H, axis=0) * s.heads[...]

    def per_block(tile, function):
        return jnp.concatenate([function(block) for block in range(tile_blocks)], axis=1)

    def lanes_of(block):
        return slice(block * BLOCK, (block + 1) * BLOCK)

    def phase_a(tile, _):
        where = columns(tile)
        projected = dot(s.t_qkv[...], s.u1[:, where])
        cosine, sine = s.cosine[:, where], s.sine[:, where]
        s.q[:, where] = low(turn(projected[:width], cosine, sine, 1.0))
        keys = low(turn(projected[width : 2 * width], cosine, sine, 1.0) * s.mask[0:1, where])
        values = low(projected[2 * width :])
        s.kv[:width, where] = keys
        s.kv[width:, where] = values
        put_products(tile, values, keys)

    lax.fori_loop(0, tiles, phase_a, None)
    table_sum = TableSum(at, s)
    table_sum.start()
    aside_a.store()
    table_sum.middle()
    lax.fori_loop(3 * parts // 4, parts, fourier_part, None)
    two.start_third()

    def take_two(index, carried):
        parts = chunk_pair(s.gather_two, index)
        where = pl.ds(pl.multiple_of(index * 16, 16), 16)
        for piece in range(2):
            s.w_kv[where, piece * width : (piece + 1) * width] = join(parts, piece)
            s.w_w1[where, piece * width : (piece + 1) * width] = join(parts, 3 + piece)
            s.w_p1[where, piece * width : (piece + 1) * width] = join(parts, 5 + piece)
        s.w_do[where, :] = join(parts, 2)
        both = pl.ds(pl.multiple_of(index * 32, 32), 32)
        for piece, target in ((7, s.w_w2), (9, s.w_p2)):
            target[both, :] = low(
                jnp.concatenate([part[piece * share : (piece + 2) * share] for part in parts], axis=0)
            )
        for part in parts:
            count_row = part[11 * share : 11 * share + 1, LANES:]
            item_at = part[11 * share + 1 : 11 * share + 2, LANES:]
            carried = carried + jnp.where(item_at == own_item, count_row, 0.0)
        s.fourier[where, :] = jnp.concatenate(
            [part[11 * share : 12 * share, :LANES] for part in parts], axis=0
        )
        return carried

    two.finish()
    own_item = at.chip.astype(f32)
    found = lax.fori_loop(0, devices // group, take_two, jnp.zeros((1, LANES), f32))
    s.inverse[0:1, :] = jnp.broadcast_to(1.0 / jnp.sum(found, axis=1, keepdims=True), (1, width))
    w_dq = jnp.concatenate(
        [s.fourier[pl.ds(0, FOUR, stride=2), :], s.fourier[pl.ds(1, FOUR, stride=2), :]], axis=1
    )
    s.t_dq[...] = low(w_dq.T)
    table_sum.late(s.table_self)
    for piece in range(2):
        cols = slice(piece * width, (piece + 1) * width)
        s.t_kv[cols, :] = flip(s.w_kv[:, cols])
        s.t_w1[cols, :] = flip(s.w_w1[:, cols])
        s.t_p1[cols, :] = flip(s.w_p1[:, cols])
        s.t_w2[:, cols] = flip(s.w_w2[cols, :])
        s.t_p2[:, cols] = flip(s.w_p2[cols, :])
    s.t_do[...] = flip(s.w_do[...])
    table_sum.last(s.table_self)
    table_sum.finish(s.table_self)

    def phase_b(tile, _):
        where = columns(tile)
        mask = s.mask[0:1, where]
        queries = s.q[:, where]
        mixed = per_block(
            tile, lambda b: dot(summary(s.table_self, tile, b), queries[:, lanes_of(b)])
        )
        attended = low(mixed * mask)
        s.o[:, where] = attended
        first_sum = s.turned[:, where].astype(f32) + dot(s.t_o[...], attended)
        scaled_two, root_two = column_norm(first_sum)
        s.root_two[0:1, where] = root_two
        s.xh2[:, where] = low(scaled_two)
        middle = low(scaled_two * column(2) + column(3))
        s.u2[:, where] = middle
        hidden_pre = dot(s.t_w1[...], middle) + hidden_column(0)
        hidden = low(gelu_alone(hidden_pre))
        s.e1[:, where] = hidden
        s.slope[:, where] = low(hidden_pre)
        encoded = first_sum + dot(s.t_w2[...], hidden) + column(6)
        scaled_three, root_three = column_norm(encoded)
        s.root_three[0:1, where] = root_three
        s.xh3[:, where] = low(scaled_three)
        outer = low(scaled_three * column(4) + column(5))
        s.u3[:, where] = outer
        pair = dot(s.t_kv[...], outer)
        keys = low(pair[:width] * mask)
        values = low(pair[width:])
        s.kvd[:width, where] = keys
        s.kvd[width:, where] = values
        put_products(tile, values, keys)

    lax.fori_loop(0, tiles, phase_b, None)
    table_sum.start()
    aside_b.store()
    table_sum.middle()

    for tile in range(2):
        tile_load(s.cotangent_far, tile).start()
    aside_a.stored()

    def cross_inputs(tile, _):
        where = columns(tile)
        s.qd[:, where] = low(dot(s.t_dq[...], s.phi[:, where]))
        turned = turned_load(s.cotangent_far, tile)
        add_sum(7, turned)
        turned = low(turned)
        s.u1[:, where] = turned
        s.kv[:, where] = low(dot(s.w_p2[...], turned))

    def slopes(tile, _):
        where = columns(tile)
        s.slope[:, where] = low(gelu_slope(s.slope[:, where].astype(f32)))

    lax.fori_loop(0, tiles, cross_inputs, None)
    table_sum.late(s.table_other)
    lax.fori_loop(0, tiles, slopes, None)
    aside_b.stored()
    table_sum.last(s.table_other)
    table_sum.finish(s.table_other)

    def phase_c(tile, _):
        where = columns(tile)
        mask = s.mask[0:1, where]
        queries = s.qd[:, where]
        tables = [summary(s.table_other, tile, block) for block in range(tile_blocks)]
        decoded = low(
            per_block(tile, lambda b: dot(tables[b], queries[:, lanes_of(b)])) * mask
        )
        s.u2[:, where] = decoded
        latent_low = low(dot(s.t_do[...], decoded))
        s.o[:, where] = latent_low
        hidden, slope = gelu_both(dot(s.t_p1[...], latent_low) + hidden_column(1))
        s.e1[:, where] = low(hidden)
        grad_spread = s.kv[:, where].astype(f32) * slope
        add_sum(10, grad_spread)
        grad_spread = low(grad_spread)
        s.kv[:, where] = grad_spread
        grad_latent = low(s.u1[:, where].astype(f32) + dot(s.w_p1[...], grad_spread))
        s.u3[:, where] = grad_latent
        grad_decoded = low(dot(s.w_do[...], grad_latent) * mask)
        put_products(tile, grad_decoded, queries)
        s.qd[:, where] = grad_decoded

    lax.fori_loop(0, tiles, phase_c, None)
    table_sum.start()
    table_sum.middle()

    def cross_query_grads(tile, _):
        where = columns(tile)
        upstream = s.qd[:, where]
        grad = per_block(
            tile, lambda b: dot_at(summary(s.table_other, tile, b), upstream[:, lanes_of(b)])
        )
        s.qd[:, where] = low(grad)

    def outputs(tile, _):
        where = columns(tile)
        output = dot(s.t_do[...], s.u2[:, where]) + dot(s.t_p2[...], s.e1[:, where]) + column(7)
        s.qd[:, where] = low(output)
        out_copy(tile, s.qd, s.layer_output).start()

    lax.fori_loop(0, tiles, cross_query_grads, None)
    s.grad_dq[...] = dot_bt(s.phi[...], s.qd[...])
    s.fourier[pl.ds(0, FOUR, stride=2), :] = s.grad_dq[:, :LANES]
    s.fourier[pl.ds(1, FOUR, stride=2), :] = s.grad_dq[:, LANES:]
    s.grad_o[...] = dot_bt(s.u2[...], s.u3[...])
    table_sum.late(s.table_third)
    s.grad_w1[...] = dot_bt(s.o[...], s.kv[...])
    s.grad_w2[...] = dot_bt(s.e1[...], s.u1[...])
    zeros = jnp.zeros((share, LANES), f32)

    def rows_of(chunk, count=1):
        size = share * count
        return pl.ds(pl.multiple_of(chunk * size, size), size)

    def chunk_c(chunk):
        where = rows_of(chunk)
        return jnp.concatenate(
            [
                s.grad_o[where, :],
                s.grad_w1[where, :width],
                s.grad_w1[where, width:],
                s.grad_w2[rows_of(chunk, 2), :],
                jnp.concatenate([s.fourier[where, :], zeros], axis=1),
            ],
            axis=0,
        )

    sum_c = GradSum(at, s, "c", 0)
    sum_c.start(chunk_c)
    lax.fori_loop(0, tiles, outputs, None)
    table_sum.last(s.table_third)
    end_out(s.qd, s.layer_output)
    aside_a.load()
    aside_b.load()
    sum_c.second()
    table_sum.finish(s.table_third)

    def phase_d(tile, _):
        where = columns(tile)
        mask = s.mask[0:1, where]
        keys, values = s.kvd[:width, where], s.kvd[width:, where]
        tables = [summary(s.table_third, tile, block) for block in range(tile_blocks)]
        grad_keys = per_block(tile, lambda b: dot_at(tables[b], values[:, lanes_of(b)])) * mask
        grad_values = per_block(tile, lambda b: dot(tables[b], keys[:, lanes_of(b)]))
        grad_pair = low(jnp.concatenate([grad_keys, grad_values], axis=0))
        s.kvd[:, where] = grad_pair
        grad_outer = dot(s.w_kv[...], grad_pair)
        scaled = s.xh3[:, where].astype(f32)
        add_sum(4, grad_outer * scaled)
        add_sum(5, grad_outer)
        grad_encoded = column_norm_back(
            grad_outer, scaled, s.root_three[0:1, where], column(4)
        )
        add_sum(6, grad_encoded)
        grad_encoded_low = low(grad_encoded)
        s.xh3[:, where] = grad_encoded_low
        grad_hidden = dot(s.w_w2[...], grad_encoded_low) * s.slope[:, where].astype(f32)
        add_sum(8, grad_hidden)
        grad_hidden = low(grad_hidden)
        s.slope[:, where] = grad_hidden
        grad_middle = dot(s.w_w1[...], grad_hidden)
        scaled = s.xh2[:, where].astype(f32)
        add_sum(2, grad_middle * scaled)
        add_sum(3, grad_middle)
        grad_first = grad_encoded + column_norm_back(
            grad_middle, scaled, s.root_two[0:1, where], column(2)
        )
        grad_first = low(grad_first)
        s.xh2[:, where] = grad_first
        grad_attended = low(dot(s.w_o[...], grad_first) * mask)
        s.qd[:, where] = grad_attended
        put_products(tile, grad_attended, s.q[:, where])

    lax.fori_loop(0, tiles // 2, phase_d, None)
    sum_c.third()
    lax.fori_loop(tiles // 2, tiles, phase_d, None)
    table_sum.start()
    s.grads_c[...] = sum_c.finish()
    table_sum.middle()
    aside_a.loaded()
    aside_b.loaded()

    def query_grads(tile, _):
        where = columns(tile)
        upstream = s.qd[:, where]
        grad = per_block(
            tile, lambda b: dot_at(summary(s.table_self, tile, b), upstream[:, lanes_of(b)])
        )
        s.q[:, where] = low(turn(grad, s.cosine[:, where], s.sine[:, where], -1.0))

    lax.fori_loop(0, tiles, query_grads, None)
    s.grad_o[...] = dot_bt(s.o[...], s.xh2[...])
    s.grad_qkv[:, :width] = dot_bt(s.u1[...], s.q[...])
    table_sum.late(s.table_other)
    s.grad_kv[...] = dot_bt(s.u3[...], s.kvd[...])
    s.grad_w2[...] = dot_bt(s.e1[...], s.xh3[...])
    s.grad_w1[...] = dot_bt(s.u2[...], s.slope[...])

    def chunk_d(chunk):
        where = rows_of(chunk)
        return jnp.concatenate(
            [
                s.grad_kv[where, :width],
                s.grad_kv[where, width:],
                s.grad_o[where, :],
                s.grad_w1[where, :width],
                s.grad_w1[where, width:],
                s.grad_w2[rows_of(chunk, 2), :],
                s.grad_qkv[where, :width],
            ],
            axis=0,
        )

    sum_d = GradSum(at, s, "d", 0)
    sum_d.start(chunk_d)
    table_sum.last(s.table_other)
    table_sum.finish(s.table_other)
    sum_d.second()

    def phase_e(tile, _):
        where = columns(tile)
        mask = s.mask[0:1, where]
        keys, values = s.kv[:width, where], s.kv[width:, where]
        tables = [summary(s.table_other, tile, block) for block in range(tile_blocks)]
        grad_keys = per_block(tile, lambda b: dot_at(tables[b], values[:, lanes_of(b)])) * mask
        grad_values = low(per_block(tile, lambda b: dot(tables[b], keys[:, lanes_of(b)])))
        s.kv[:width, where] = low(turn(grad_keys, s.cosine[:, where], s.sine[:, where], -1.0))
        s.kv[width:, where] = grad_values

    lax.fori_loop(0, tiles, phase_e, None)
    s.grad_qkv[:, width:] = dot_bt(s.u1[...], s.kv[...])
    sum_e = ChipSum(at, s, "t")

    @pl.loop(0, devices)
    def _(chunk):
        where = rows_of(chunk)
        s.chip_full_t[lax.rem(chunk, 2), lax.div(chunk, 2)] = low(
            jnp.concatenate(
                [s.grad_qkv[where, width : 2 * width], s.grad_qkv[where, 2 * width :]], axis=0
            )
        )

    sum_e.start()

    def phase_f(tile, _):
        where = columns(tile)
        grad_normed = dot(
            s.w_qkv[...], jnp.concatenate([s.q[:, where], s.kv[:, where]], axis=0)
        )
        turned = s.turned[:, where].astype(f32)
        root = s.root_one[0:1, where]
        scaled = (turned - jnp.sum(turned, axis=0, keepdims=True) * (1.0 / width)) * root
        add_sum(0, grad_normed * scaled)
        add_sum(1, grad_normed)
        grad_input = s.xh2[:, where].astype(f32) + column_norm_back(
            grad_normed, scaled, root, column(0)
        )
        s.xh2[:, where] = low(grad_input)
        out_copy(tile, s.xh2, s.input_grad).start()

    sum_e.middle()
    lax.fori_loop(0, tiles // 2, phase_f, None)
    sum_d.third()
    lax.fori_loop(tiles // 2, tiles, phase_f, None)
    end_out(s.xh2, s.input_grad)
    s.grads_d[...] = sum_d.finish()
    s.grads_e[...] = sum_e.total()
    squares = sum(
        jnp.sum(grads[...] * grads[...], axis=0, keepdims=True)
        for grads in (s.grads_c, s.grads_d, s.grads_e)
    )

    lane_wide = lax.broadcasted_iota(jnp.int32, (width, LANES), 1)
    sums = jnp.zeros((width, LANES), f32)
    for index in range(12):
        sums = jnp.where(
            lane_wide == index, jnp.sum(s.vector_sum[index], axis=1, keepdims=True), sums
        )
    s.vector_cols[...] = sums
    turned_sums = s.vector_cols[...].T
    high = low(squares).astype(f32)
    s.final_near[at.core] = low(
        jnp.concatenate(
            [turned_sums[:12], high, squares - high, jnp.zeros((2, width), f32)], axis=0
        )
    )

    def final_core(start):
        source = at.core if start else 1 - at.core
        return remote(
            s.final_near.at[at.core], s.final_near.at[source], s.sem_send.at[2, 1],
            s.sem_recv.at[2, 1], at.chip * 2 + 1 - at.core,
        )

    def final_chips(step, start):
        source = at.chip if start else at.chip_at(step)
        return remote(
            s.final_far.at[at.chip], s.final_far.at[source], s.sem_send.at[1, step],
            s.sem_recv.at[1, source], at.chip_at(step) * 2 + at.core,
        )

    final_core(True).start()
    final_core(False).wait()
    total = s.final_near[0].astype(f32) + s.final_near[1].astype(f32)
    square_sum = total[12:13] + total[13:14]
    high = low(square_sum).astype(f32)
    s.final_far[at.chip] = low(
        jnp.concatenate([total[:12], high, square_sum - high, total[14:]], axis=0)
    )
    for step in range(1, at.chips):
        final_chips(step, True).start()
    for step in range(1, at.chips):
        final_chips(step, False).wait()
    total = s.final_far[0].astype(f32)
    for index in range(1, at.chips):
        total = total + s.final_far[index].astype(f32)
    s.vector_all[...] = total


def update_kernel(share, *refs):
    sources, refs = refs[:2], refs[2:]
    grads_c, grads_d, grads_e, vector_all = refs[:4]
    weights_far = refs[4:22]
    targets = refs[22:24]
    norm_out = refs[24]
    results = refs[25:43]
    flat_square, flat_expand, flat_contract, *held, sems, weight_sems = refs[43:]
    held, turned_out, weights = held[:2], held[2:4], held[4:]
    weight_loads = [
        pltpu.make_async_copy(far, near, weight_sems.at[index])
        for index, (far, near) in enumerate(zip(weights_far, weights))
    ]
    loads, stores = [], []
    size = targets[0].shape[0] // PIECES
    for piece in range(PIECES):
        where = slice(piece * size, (piece + 1) * size)
        for index in range(2):
            near = held[index].at[:, where]
            own = turned_out[index].at[where]
            loads.append(
                pltpu.make_async_copy(
                    sources[index].at[:, where], near, sems.at[0, index, piece]
                )
            )
            stores.append(
                pltpu.make_async_copy(own, targets[index].at[where], sems.at[1, index, piece])
            )
    for load in loads + weight_loads:
        load.start()
    for piece in range(PIECES):
        where = slice(piece * size, (piece + 1) * size)
        for index in range(2):
            loads[2 * piece + index].wait()
            part = held[index][:, where].astype(turned_out[index].dtype)
            turned_out[index][where] = part.T
            stores[2 * piece + index].start()
    width = grads_c.shape[1]
    places = [(grads_d, 7), (grads_e, 0), (grads_e, 1), (grads_d, 2), (grads_d, 0), (grads_d, 1), (grads_c, 0)]
    for matrix, (source, piece) in enumerate(places):
        for row in range(share):
            start = piece * share + row
            flat_square[matrix : matrix + 1, row * width : (row + 1) * width] = source[
                start : start + 1, :
            ]
    for matrix, (source, piece) in enumerate(((grads_d, 3), (grads_c, 1))):
        for half in range(2):
            for row in range(share):
                start = (piece + half) * share + row
                target = row * F + half * width
                flat_expand[matrix : matrix + 1, target : target + width] = source[
                    start : start + 1, :
                ]
    for matrix, (source, piece) in enumerate(((grads_d, 5), (grads_c, 3))):
        for row in range(2 * share):
            start = piece * share + row
            flat_contract[matrix : matrix + 1, row * width : (row + 1) * width] = source[
                start : start + 1, :
            ]
    fourier = grads_c[5 * share : 6 * share, :LANES]
    turned = vector_all[...]
    rows = jnp.sum(turned[:12] * turned[:12], axis=0, keepdims=True) + turned[12:13] + turned[13:14]
    norm = jnp.sqrt(jnp.sum(rows, axis=1, keepdims=True))
    norm_out[...] = norm
    factor = jnp.minimum(1.0, CLIP_NORM / (norm + 1e-06))
    hidden = jnp.concatenate(
        [
            jnp.concatenate([turned[8:9], turned[9:10]], axis=1),
            jnp.concatenate([turned[10:11], turned[11:12]], axis=1),
        ],
        axis=0,
    )
    for load in weight_loads:
        load.wait()
    grads = (flat_square[...], flat_expand[...], flat_contract[...], fourier, turned[:8], hidden)
    rates = (RATE_MATRIX,) * 4 + (RATE_VECTOR,) * 2
    for index, (grad, rate) in enumerate(zip(grads, rates)):
        weight, first, second = (weights[3 * index + part][...] for part in range(3))
        values = adam_update(weight, first, second, grad, factor, rate)
        for part in range(3):
            results[3 * index + part][...] = values[part]
    for store in stores:
        store.wait()


def fused(devices, features, coords, fourier_basis, block_items, point_mask, cotangent, *weights):
    points, width = features.shape
    blocks = points // BLOCK
    outers = devices // GROUP
    share = width // devices
    items = points * devices // ITEM_PTS
    bf16, f32 = jnp.bfloat16, jnp.float32
    square, expand, contract, fourier, vector, hidden = (weights[3 * i] for i in range(6))
    vmem = lambda shape, dtype: pltpu.VMEM(shape, dtype)
    inputs = {
        "items": block_items,
        "features_far": features,
        "coords": coords,
        "fourier_basis": fourier_basis,
        "point_mask": point_mask.reshape(blocks, BLOCK),
        "cotangent_far": cotangent,
        "square_weight": square,
        "expand_weight": expand,
        "contract_weight": contract,
        "fourier_weight": fourier.reshape(share, LANES),
        "vector_weight": vector,
        "hidden_weight": hidden,
    }
    rows_c, rows_d, rows_e = 6 * share, 8 * share, 2 * share
    chips = devices // 2
    outputs = {
        "layer_output": ((width, points), bf16),
        "input_grad": ((width, points), bf16),
        "grads_c": ((rows_c, width), f32),
        "grads_d": ((rows_d, width), f32),
        "grads_e": ((rows_e, width), f32),
        "vector_all": ((16, width), f32),
        "aside": ((8 * width, points), bf16),
    }
    tall = lambda rows: vmem((rows, points), bf16)
    scratch = {
        "pack": vmem((16 * share, width), f32),
        "gather_one": vmem((2, 4, outers, 4 * share, width), bf16),
        "gather_two": vmem((2, 4, outers, 12 * share, width), bf16),
        "eye": vmem((width, width), bf16),
        "heads": vmem((width, width), bf16),
        "small": vmem((LANES, width), f32),
        "cols": vmem((width, LANES), f32),
        "spread": vmem((items * E, blocks * E), bf16),
        "vector_sum": vmem((12, width, LANES), f32),
        "vector_cols": vmem((width, LANES), f32),
        "grad_qkv": vmem((width, 3 * width), f32),
        "grad_o": vmem((width, width), f32),
        "grad_kv": vmem((width, 2 * width), f32),
        "grad_w1": vmem((width, F), f32),
        "grad_w2": vmem((F, width), f32),
        "grad_dq": vmem((FOUR, width), f32),
        "fourier": vmem((2 * FOUR, LANES), f32),
        "w_qkv": vmem((width, 3 * width), bf16),
        "t_qkv": vmem((3 * width, width), bf16),
        "w_o": vmem((width, width), bf16),
        "t_o": vmem((width, width), bf16),
        "w_kv": vmem((width, 2 * width), bf16),
        "t_kv": vmem((2 * width, width), bf16),
        "w_do": vmem((width, width), bf16),
        "t_do": vmem((width, width), bf16),
        "w_w1": vmem((width, F), bf16),
        "t_w1": vmem((F, width), bf16),
        "w_p1": vmem((width, F), bf16),
        "t_p1": vmem((F, width), bf16),
        "w_w2": vmem((F, width), bf16),
        "t_w2": vmem((width, F), bf16),
        "w_p2": vmem((F, width), bf16),
        "t_p2": vmem((width, F), bf16),
        "t_dq": vmem((width, FOUR), bf16),
        "mask": vmem((1, points), f32),
        "root_one": vmem((1, points), f32),
        "root_two": vmem((1, points), f32),
        "root_three": vmem((1, points), f32),
        "cosine": vmem((E // 2, points), f32),
        "sine": vmem((E // 2, points), f32),
        "phi": tall(FOUR),
        "u1": tall(width),
        "q": tall(width),
        "kv": tall(2 * width),
        "qd": tall(width),
        "o": tall(width),
        "xh2": tall(width),
        "u2": tall(width),
        "e1": tall(F),
        "slope": tall(F),
        "xh3": tall(width),
        "u3": tall(width),
        "kvd": tall(2 * width),
        "per_block": vmem((blocks * E, width), bf16),
        "inverse": vmem((8, width), f32),
        "table_self": vmem((2, chips, 16, width), bf16),
        "table_other": vmem((2, chips, 16, width), bf16),
        "final_near": vmem((2, 16, width), bf16),
        "final_far": vmem((chips, 16, width), bf16),
        "turned": tall(width),
        "sem_in": pltpu.SemaphoreType.DMA((2,)),
        "sem_aside": pltpu.SemaphoreType.DMA((8,)),
        "table_third": vmem((2, chips, 16, width), bf16),
        "load_slots": vmem((2, TILE, width), bf16),
        "sem_out": pltpu.SemaphoreType.DMA((points // TILE,)),
    }
    for key in ("t",):
        scratch["chip_full_" + key] = vmem((2, chips, 16, width), bf16)
        for part in ("chip_half_", "chip_others_"):
            scratch[part + key] = vmem((chips, 16, width), bf16)
    for key, rows in (("c", rows_c), ("d", rows_d)):
        for part in ("half_", "quarter_"):
            scratch[part + key] = vmem((4, outers, rows, width), bf16)
        scratch["last_" + key] = vmem((outers, rows, width), bf16)
    for key in ("sem_send", "sem_recv"):
        scratch[key] = pltpu.SemaphoreType.DMA((3, chips))
    names = list(inputs) + list(outputs) + list(scratch)
    spaces = {"items": pltpu.SMEM, "features_far": pl.ANY, "cotangent_far": pl.ANY}
    in_specs = [pl.BlockSpec(memory_space=spaces.get(name, pltpu.VMEM)) for name in inputs]
    whole = pl.BlockSpec(memory_space=pltpu.VMEM)
    made = pl.pallas_call(
        functools.partial(layer_kernel, names, devices),
        out_shape=[jax.ShapeDtypeStruct(*shape) for shape in outputs.values()],
        in_specs=in_specs,
        out_specs=[pl.BlockSpec(memory_space=pl.ANY)] * 2
        + [whole] * 4
        + [pl.BlockSpec(memory_space=pl.ANY)],
        scratch_shapes=list(scratch.values()),
        compiler_params=pltpu.CompilerParams(
            collective_id=0, has_side_effects=True, vmem_limit_bytes=VMEM_BYTES
        ),
    )(*inputs.values())
    flat = list(weights)
    for part in range(9, 12):
        flat[part] = flat[part].reshape(share, LANES)
    shapes = [jax.ShapeDtypeStruct((1, 1), f32)] + [
        jax.ShapeDtypeStruct(flat[index].shape, f32) for index in range(18)
    ]
    order = []
    for index in range(6):
        order += [shapes[1 + 3 * index]] * 3
    updated = pl.pallas_call(
        functools.partial(update_kernel, share),
        out_shape=[jax.ShapeDtypeStruct((points, width), dtype) for dtype in (bf16, f32)]
        + [shapes[0]]
        + order,
        in_specs=[pl.BlockSpec(memory_space=pl.ANY)] * 2
        + [whole] * 4
        + [pl.BlockSpec(memory_space=pl.ANY)] * 18,
        out_specs=[pl.BlockSpec(memory_space=pl.ANY)] * 2 + [whole] * 19,
        scratch_shapes=[
            vmem(square.shape, f32),
            vmem(expand.shape, f32),
            vmem(contract.shape, f32),
            vmem((width, points), bf16),
            vmem((width, points), bf16),
            vmem((points, width), bf16),
            vmem((points, width), f32),
            *(vmem(weight.shape, f32) for weight in flat),
            pltpu.SemaphoreType.DMA((2, 2, PIECES)),
            pltpu.SemaphoreType.DMA((18,)),
        ],
        compiler_params=pltpu.CompilerParams(vmem_limit_bytes=VMEM_BYTES),
    )(*made[:6], *flat)
    layer_output, input_grad, norm, *rest = updated
    for part in range(9, 12):
        rest[part] = rest[part].reshape(fourier.shape)
    return (layer_output, input_grad, norm.reshape(()), *rest)


def shards(features, *others):
    devices = lax.axis_size("pts")
    width = features.shape[1]
    if devices % GROUP == 0 and width == 8 * devices:
        return fused(devices, features, *others)
    return plain(features, *others)


def solution(mesh):
    in_specs = (
        P("pts", None),
        P(None, "pts"),
        P(),
        P("pts"),
        P("pts"),
        P("pts", None),
        P(None, "pts"),
        P(None, "pts"),
        P(None, "pts"),
        P(None, "pts"),
        P(None, "pts"),
        P(None, "pts"),
        P(None, "pts"),
        P(None, "pts"),
        P(None, "pts"),
        P("pts"),
        P("pts"),
        P("pts"),
        P(),
        P(),
        P(),
        P(),
        P(),
        P(),
    )
    out_specs = (
        P("pts", None),
        P("pts", None),
        P(),
        P(None, "pts"),
        P(None, "pts"),
        P(None, "pts"),
        P(None, "pts"),
        P(None, "pts"),
        P(None, "pts"),
        P(None, "pts"),
        P(None, "pts"),
        P(None, "pts"),
        P("pts"),
        P("pts"),
        P("pts"),
        P(),
        P(),
        P(),
        P(),
        P(),
        P(),
    )
    return jax.shard_map(shards, mesh=mesh, in_specs=in_specs, out_specs=out_specs, check_vma=False)
```

```python
import functools
import math
import types

import jax
import jax.numpy as jnp
from jax import lax
from jax.experimental import pallas as pl
from jax.experimental.pallas import tpu as pltpu
from jax.sharding import PartitionSpec as P

H = 8
E = 32
F = 512
FOUR = 128
BLOCK = 128
ITEM_PTS = 8192
STEP = 10


NORM_EPS = 1e-05
GELU_C = math.sqrt(2.0 / math.pi)
GELU_A = 0.044715
BETA_ONE = 0.9
BETA_TWO = 0.95
ADAM_EPS = 1e-08
WEIGHT_DECAY = 0.1
RATE_MATRIX = 0.05
RATE_VECTOR = 0.25
CLIP_NORM = 1.0
HIGHEST_PRECISION = lax.Precision.HIGHEST


def matmul(left, right):
    return jnp.dot(left, right, preferred_element_type=jnp.float32)


def matmul_left(left, right):
    return lax.dot_general(
        left, right, (((0,), (0,)), ((), ())), preferred_element_type=jnp.float32
    )


def matmul_right(left, right):
    return lax.dot_general(
        left, right, (((1,), (1,)), ((), ())), preferred_element_type=jnp.float32
    )


def gelu(values):
    return 0.5 * values * (1.0 + jnp.tanh(GELU_C * (values + GELU_A * values * values * values)))


def gelu_slope(values):
    tangent = jnp.tanh(GELU_C * (values + GELU_A * values * values * values))
    return 0.5 * (1.0 + tangent) + 0.5 * values * (1.0 - tangent * tangent) * GELU_C * (
        1.0 + 3.0 * GELU_A * values * values
    )


def norm_parts(values, norm_gain, norm_bias):
    centred = values - jnp.mean(values, axis=-1, keepdims=True)
    variance = jnp.mean(centred * centred, axis=-1, keepdims=True)
    root_inv = lax.rsqrt(variance + NORM_EPS)
    scaled = centred * root_inv
    return (scaled * norm_gain + norm_bias, scaled, root_inv)


def norm_back(upstream, scaled, root_inv, norm_gain):
    through = upstream * norm_gain
    centre = jnp.mean(through, axis=-1, keepdims=True)
    along = jnp.mean(through * scaled, axis=-1, keepdims=True)
    return root_inv * (through - centre - scaled * along)


def rotary_tables(coords):
    quarter = E // 4
    frequency = math.pi * (jnp.arange(quarter, dtype=jnp.float32) + 1.0) / quarter
    first_angle = coords[0][:, None] * frequency[None, :]
    second_angle = coords[1][:, None] * frequency[None, :]
    angles = jnp.concatenate([first_angle, first_angle, second_angle, second_angle], axis=1)
    return (jnp.cos(angles), jnp.sin(angles))


def rotate(values, cosine, sine):
    quarter = E // 4
    swapped = jnp.concatenate(
        [
            -values[..., quarter : 2 * quarter],
            values[..., :quarter],
            -values[..., 3 * quarter :],
            values[..., 2 * quarter : 3 * quarter],
        ],
        axis=-1,
    )
    return values * cosine[:, None, :] + swapped * sine[:, None, :]


def rotate_back(grads, cosine, sine):
    quarter = E // 4
    scaled = grads * sine[:, None, :]
    swapped = jnp.concatenate(
        [
            scaled[..., quarter : 2 * quarter],
            -scaled[..., :quarter],
            scaled[..., 3 * quarter :],
            -scaled[..., 2 * quarter : 3 * quarter],
        ],
        axis=-1,
    )
    return grads * cosine[:, None, :] + swapped


def fourier_features(coords, fourier_basis):
    phases = (
        2.0
        * math.pi
        * (
            coords[0][:, None] * fourier_basis[0][None, :]
            + coords[1][:, None] * fourier_basis[1][None, :]
        )
    )
    return jnp.concatenate([jnp.cos(phases), jnp.sin(phases)], axis=1)


def block_table(left, right, onehot):
    blocks = onehot.shape[0]
    per_block = jnp.einsum(
        "bphe,bphf->bhef",
        left.reshape(blocks, BLOCK, H, E),
        right.reshape(blocks, BLOCK, H, E),
        preferred_element_type=jnp.float32,
    )
    return jnp.einsum("ba,bhef->ahef", onehot, per_block, precision=HIGHEST_PRECISION)


def scale_round(table, inverse_count):
    return (table * inverse_count[:, None, None, None]).astype(jnp.bfloat16)


def spread(summary, onehot):
    selected = jnp.einsum(
        "ba,ahef->bhef", onehot.astype(jnp.bfloat16), summary, preferred_element_type=jnp.float32
    )
    return selected.astype(jnp.bfloat16)


def apply_summary(rows_low, block_summary, transposed):
    blocks = block_summary.shape[0]
    pattern = "bphf,bhef->bphe" if transposed else "bphe,bhef->bphf"
    mixed = jnp.einsum(
        pattern,
        rows_low.reshape(blocks, BLOCK, H, E),
        block_summary,
        preferred_element_type=jnp.float32,
    )
    return mixed.reshape(-1, H * E)


def galerkin_backward(
    grad_low, queries_low, keys_masked, values_low, block_summary, onehot, mask_float, reducer
):
    grad_masked = grad_low * mask_float.astype(jnp.bfloat16)
    grad_queries = apply_summary(grad_masked, block_summary, True)
    summary_grad = reducer(block_table(queries_low, grad_masked, onehot))
    block_grad = spread(summary_grad, onehot)
    grad_keys = apply_summary(values_low, block_grad, True) * mask_float
    grad_values = apply_summary(keys_masked, block_grad, False)
    return (grad_queries, grad_keys, grad_values)


def adam_update(weight, first, second, grad, factor, rate):
    clipped = grad * factor
    new_first = BETA_ONE * first + (1.0 - BETA_ONE) * clipped
    new_second = BETA_TWO * second + (1.0 - BETA_TWO) * clipped * clipped
    first_hat = new_first / (1.0 - BETA_ONE**STEP)
    second_hat = new_second / (1.0 - BETA_TWO**STEP)
    new_weight = weight - rate * (
        first_hat / (jnp.sqrt(second_hat) + ADAM_EPS) + WEIGHT_DECAY * weight
    )
    return (new_first, new_second, new_weight)


def own_share(full, width, along, start_index):
    return lax.dynamic_slice_in_dim(full, start_index * width, width, along)


def plain(
    features,
    coords,
    fourier_basis,
    block_items,
    point_mask,
    cotangent,
    square_weight,
    square_first,
    square_second,
    expand_weight,
    expand_first,
    expand_second,
    contract_weight,
    contract_first,
    contract_second,
    fourier_weight,
    fourier_first,
    fourier_second,
    vector_weight,
    vector_first,
    vector_second,
    hidden_weight,
    hidden_first,
    hidden_second,
):
    rows = features.shape[0]
    width = features.shape[1]
    blocks = rows // BLOCK
    devices = lax.axis_size("pts")
    items_total = rows * devices // ITEM_PTS
    gathered = (
        lax.all_gather(square_weight.astype(jnp.bfloat16), "pts", axis=1, tiled=True),
        lax.all_gather(expand_weight.astype(jnp.bfloat16), "pts", axis=1, tiled=True),
        lax.all_gather(contract_weight.astype(jnp.bfloat16), "pts", axis=1, tiled=True),
        lax.all_gather(fourier_weight.astype(jnp.bfloat16), "pts", axis=0, tiled=True),
    )
    square_full = gathered[0].reshape(7, width, width)
    expand_full = gathered[1].reshape(2, width, F)
    contract_full = gathered[2].reshape(2, F, width)
    fourier_full = gathered[3].reshape(FOUR, width)
    onehot = (block_items[:, None] == jnp.arange(items_total, dtype=jnp.int32)[None, :]).astype(
        jnp.float32
    )
    mask_float = point_mask.astype(jnp.float32)[:, None]
    mask_low = mask_float.astype(jnp.bfloat16)
    block_count = jnp.sum(mask_float.reshape(blocks, BLOCK), axis=1)
    local_count = jnp.dot(block_count, onehot, precision=HIGHEST_PRECISION)
    cosine, sine = rotary_tables(coords)
    phase_low = fourier_features(coords, fourier_basis).astype(jnp.bfloat16)
    inputs = features.astype(jnp.float32)
    normed, scaled_one, root_one = norm_parts(inputs, vector_weight[0], vector_weight[1])
    normed_low = normed.astype(jnp.bfloat16)
    joint_weight = jnp.concatenate([square_full[0], square_full[1], square_full[2]], axis=1)
    projected = matmul(normed_low, joint_weight)
    queries_low = (
        rotate(projected[:, :width].reshape(rows, H, E), cosine, sine)
        .reshape(rows, width)
        .astype(jnp.bfloat16)
    )
    keys_low = (
        rotate(projected[:, width : 2 * width].reshape(rows, H, E), cosine, sine)
        .reshape(rows, width)
        .astype(jnp.bfloat16)
    )
    keys_masked = keys_low * mask_low
    values_low = projected[:, 2 * width :].astype(jnp.bfloat16)
    self_local = block_table(keys_masked, values_low, onehot)
    self_table, item_count = lax.psum((self_local, local_count), "pts")
    inverse_count = 1.0 / item_count
    self_items = scale_round(self_table, inverse_count)
    self_summary = spread(self_items, onehot)
    attended_low = (apply_summary(queries_low, self_summary, False) * mask_float).astype(
        jnp.bfloat16
    )
    first_sum = inputs + matmul(attended_low, square_full[3])
    normed_mid, scaled_two, root_two = norm_parts(first_sum, vector_weight[2], vector_weight[3])
    middle_low = normed_mid.astype(jnp.bfloat16)
    hidden_pre = matmul(middle_low, expand_full[0]) + hidden_weight[0]
    hidden_low = gelu(hidden_pre).astype(jnp.bfloat16)
    encoded = first_sum + matmul(hidden_low, contract_full[0]) + vector_weight[6]
    normed_out, scaled_three, root_three = norm_parts(encoded, vector_weight[4], vector_weight[5])
    outer_low = normed_out.astype(jnp.bfloat16)
    pair_weight = jnp.concatenate([square_full[4], square_full[5]], axis=1)
    cross_projected = matmul(outer_low, pair_weight)
    cross_keys = cross_projected[:, :width].astype(jnp.bfloat16) * mask_low
    cross_values = cross_projected[:, width:].astype(jnp.bfloat16)
    cross_queries = matmul(phase_low, fourier_full).astype(jnp.bfloat16)
    cross_local = block_table(cross_keys, cross_values, onehot)
    cross_items = scale_round(lax.psum(cross_local, "pts"), inverse_count)
    cross_summary = spread(cross_items, onehot)
    decoded_low = (apply_summary(cross_queries, cross_summary, False) * mask_float).astype(
        jnp.bfloat16
    )
    latent = matmul(decoded_low, square_full[6])
    latent_low = latent.astype(jnp.bfloat16)
    spread_pre = matmul(latent_low, expand_full[1]) + hidden_weight[1]
    spread_low = gelu(spread_pre).astype(jnp.bfloat16)
    output = latent + matmul(spread_low, contract_full[1]) + vector_weight[7]
    cross_reducer = lambda table_part: scale_round(lax.psum(table_part, "pts"), inverse_count)
    self_reducer = lambda table_part: scale_round(lax.psum(table_part, "pts"), inverse_count)
    grad_output = cotangent.astype(jnp.float32)
    grad_bias_end = jnp.sum(grad_output, axis=0)
    grad_contract_spread = matmul_left(spread_low, cotangent)
    grad_spread = matmul_right(cotangent, contract_full[1]) * gelu_slope(spread_pre)
    grad_hidden_spread = jnp.sum(grad_spread, axis=0)
    grad_spread_low = grad_spread.astype(jnp.bfloat16)
    grad_expand_spread = matmul_left(latent_low, grad_spread_low)
    grad_latent = (grad_output + matmul_right(grad_spread_low, expand_full[1])).astype(jnp.bfloat16)
    grad_out_cross = matmul_left(decoded_low, grad_latent)
    grad_decoded = matmul_right(grad_latent, square_full[6]).astype(jnp.bfloat16)
    cross_back = galerkin_backward(
        grad_decoded,
        cross_queries,
        cross_keys,
        cross_values,
        cross_summary,
        onehot,
        mask_float,
        cross_reducer,
    )
    grad_fourier_full = matmul_left(phase_low, cross_back[0].astype(jnp.bfloat16))
    grad_pair_low = jnp.concatenate([cross_back[1], cross_back[2]], axis=1).astype(jnp.bfloat16)
    grad_pair_full = matmul_left(outer_low, grad_pair_low)
    grad_normed_out = matmul_right(grad_pair_low, pair_weight)
    grad_gain_three = jnp.sum(grad_normed_out * scaled_three, axis=0)
    grad_bias_three = jnp.sum(grad_normed_out, axis=0)
    grad_encoded = norm_back(grad_normed_out, scaled_three, root_three, vector_weight[4])
    grad_bias_middle = jnp.sum(grad_encoded, axis=0)
    grad_encoded_low = grad_encoded.astype(jnp.bfloat16)
    grad_contract_enc = matmul_left(hidden_low, grad_encoded_low)
    grad_hidden = matmul_right(grad_encoded_low, contract_full[0]) * gelu_slope(hidden_pre)
    grad_hidden_enc = jnp.sum(grad_hidden, axis=0)
    grad_hidden_low = grad_hidden.astype(jnp.bfloat16)
    grad_expand_enc = matmul_left(middle_low, grad_hidden_low)
    grad_middle = matmul_right(grad_hidden_low, expand_full[0])
    grad_gain_two = jnp.sum(grad_middle * scaled_two, axis=0)
    grad_bias_two = jnp.sum(grad_middle, axis=0)
    grad_first = grad_encoded + norm_back(grad_middle, scaled_two, root_two, vector_weight[2])
    grad_first_low = grad_first.astype(jnp.bfloat16)
    grad_out_self = matmul_left(attended_low, grad_first_low)
    grad_attended = matmul_right(grad_first_low, square_full[3]).astype(jnp.bfloat16)
    self_back = galerkin_backward(
        grad_attended,
        queries_low,
        keys_masked,
        values_low,
        self_summary,
        onehot,
        mask_float,
        self_reducer,
    )
    grad_queries = rotate_back(self_back[0].reshape(rows, H, E), cosine, sine).reshape(rows, width)
    grad_keys = rotate_back(self_back[1].reshape(rows, H, E), cosine, sine).reshape(rows, width)
    grad_joint_low = jnp.concatenate([grad_queries, grad_keys, self_back[2]], axis=1).astype(
        jnp.bfloat16
    )
    grad_joint_full = matmul_left(normed_low, grad_joint_low)
    grad_normed = matmul_right(grad_joint_low, joint_weight)
    grad_gain_one = jnp.sum(grad_normed * scaled_one, axis=0)
    grad_bias_one = jnp.sum(grad_normed, axis=0)
    grad_inputs = grad_first + norm_back(grad_normed, scaled_one, root_one, vector_weight[0])
    grad_square = jnp.stack(
        [
            grad_joint_full[:, :width],
            grad_joint_full[:, width : 2 * width],
            grad_joint_full[:, 2 * width :],
            grad_out_self,
            grad_pair_full[:, :width],
            grad_pair_full[:, width:],
            grad_out_cross,
        ]
    ).reshape(7, width * width)
    grad_expand = jnp.stack([grad_expand_enc, grad_expand_spread]).reshape(2, width * F)
    grad_contract = jnp.stack([grad_contract_enc, grad_contract_spread]).reshape(2, F * width)
    grad_fourier = grad_fourier_full.reshape(FOUR * width)
    grad_vector = jnp.stack(
        [
            grad_gain_one,
            grad_bias_one,
            grad_gain_two,
            grad_bias_two,
            grad_gain_three,
            grad_bias_three,
            grad_bias_middle,
            grad_bias_end,
        ]
    )
    grad_hidden_rows = jnp.stack([grad_hidden_enc, grad_hidden_spread])
    totals = lax.psum(
        (grad_square, grad_expand, grad_contract, grad_fourier, grad_vector, grad_hidden_rows),
        "pts",
    )
    squares = sum((jnp.sum(total_part * total_part) for total_part in totals))
    start_index = lax.axis_index("pts")
    share_square = own_share(totals[0], square_weight.shape[1], 1, start_index)
    share_expand = own_share(totals[1], expand_weight.shape[1], 1, start_index)
    share_contract = own_share(totals[2], contract_weight.shape[1], 1, start_index)
    share_fourier = own_share(totals[3], fourier_weight.shape[0], 0, start_index)
    vector_total = totals[4]
    hidden_total = totals[5]
    grad_norm = jnp.sqrt(squares)
    factor = jnp.minimum(1.0, CLIP_NORM / (grad_norm + 1e-06))
    new_square = adam_update(
        square_weight, square_first, square_second, share_square, factor, RATE_MATRIX
    )
    new_expand = adam_update(
        expand_weight, expand_first, expand_second, share_expand, factor, RATE_MATRIX
    )
    new_contract = adam_update(
        contract_weight, contract_first, contract_second, share_contract, factor, RATE_MATRIX
    )
    new_fourier = adam_update(
        fourier_weight, fourier_first, fourier_second, share_fourier, factor, RATE_MATRIX
    )
    new_vector = adam_update(
        vector_weight, vector_first, vector_second, vector_total, factor, RATE_VECTOR
    )
    new_hidden = adam_update(
        hidden_weight, hidden_first, hidden_second, hidden_total, factor, RATE_VECTOR
    )
    return (
        output.astype(jnp.bfloat16),
        grad_inputs,
        grad_norm,
        new_square[0],
        new_square[1],
        new_square[2],
        new_expand[0],
        new_expand[1],
        new_expand[2],
        new_contract[0],
        new_contract[1],
        new_contract[2],
        new_fourier[0],
        new_fourier[1],
        new_fourier[2],
        new_vector[0],
        new_vector[1],
        new_vector[2],
        new_hidden[0],
        new_hidden[1],
        new_hidden[2],
    )


GROUP = 8
TILE = 1024
PUT = 512
LANES = 128
E_BITS = E.bit_length() - 1
PIECES = 4
VMEM_BYTES = 64 * 1024 * 1024


def dot(left, right):
    return jnp.dot(left, right, preferred_element_type=jnp.float32)


def dot_bt(left, right):
    return lax.dot_general(
        left, right, (((1,), (1,)), ((), ())), preferred_element_type=jnp.float32
    )


def dot_at(left, right):
    return lax.dot_general(
        left, right, (((0,), (0,)), ((), ())), preferred_element_type=jnp.float32
    )


def low(values):
    return values.astype(jnp.bfloat16)


def column_norm(values):
    inverse = 1.0 / values.shape[0]
    centred = values - jnp.sum(values, axis=0, keepdims=True) * inverse
    variance = jnp.sum(centred * centred, axis=0, keepdims=True) * inverse
    root_inv = lax.rsqrt(variance + NORM_EPS)
    return (centred * root_inv, root_inv)


def column_norm_back(upstream, scaled, root_inv, gain):
    inverse = 1.0 / upstream.shape[0]
    through = upstream * gain
    centre = jnp.sum(through, axis=0, keepdims=True) * inverse
    along = jnp.sum(through * scaled, axis=0, keepdims=True) * inverse
    return root_inv * (through - centre - scaled * along)


def gelu_alone(values):
    half = 0.5 * values
    return half + half * jnp.tanh(values * (GELU_C + (GELU_C * GELU_A) * (values * values)))


def gelu_both(values):
    square = values * values
    half = 0.5 + 0.5 * jnp.tanh(values * (GELU_C + (GELU_C * GELU_A) * square))
    slope = half + values * (half * (1.0 - half)) * (
        2.0 * GELU_C + (6.0 * GELU_C * GELU_A) * square
    )
    return (values * half, slope)


def turn(values, cosine, sine, sign):
    quarter = E // 4
    first_cos, second_cos = cosine[:quarter], cosine[quarter:]
    first_sin, second_sin = sine[:quarter] * sign, sine[quarter:] * sign
    parts = []
    for base in range(0, values.shape[0], E):
        one, two, three, four = (
            values[base + quarter * step : base + quarter * (step + 1)] for step in range(4)
        )
        parts += [
            one * first_cos - two * first_sin,
            two * first_cos + one * first_sin,
            three * second_cos - four * second_sin,
            four * second_cos + three * second_sin,
        ]
    return jnp.concatenate(parts, axis=0)


def head_of(index):
    return lax.shift_right_logical(index, E_BITS)


def compress(full):
    width = full.shape[1]
    head = head_of(lax.broadcasted_iota(jnp.int32, (E, width), 1))
    result = full[:E]
    for index in range(1, H):
        result = jnp.where(head == index, full[E * index : E * (index + 1)], result)
    return result


def lane_sum(values):
    result = values[:, :LANES]
    for start in range(LANES, values.shape[1], LANES):
        result = result + values[:, start : start + LANES]
    return result


def remote(source, target, send_sem, recv_sem, device):
    return pltpu.make_async_remote_copy(
        src_ref=source,
        dst_ref=target,
        send_sem=send_sem,
        recv_sem=recv_sem,
        device_id=(device,),
        device_id_type=pl.DeviceIdType.MESH,
    )


class Place:
    def __init__(self, devices):
        self.devices = devices
        self.outers = devices // GROUP
        self.me = lax.axis_index("pts")
        self.inner = lax.rem(self.me, GROUP)
        self.outer = lax.div(self.me, GROUP)
        self.core = lax.rem(self.me, 2)
        self.pair = lax.div(self.inner, 2)
        self.chips = devices // 2
        self.chip = lax.div(self.me, 2)

    def chip_at(self, step):
        return lax.rem(self.chip + step, self.chips)

    def inner_at(self, step):
        return lax.rem(self.inner + step, GROUP)

    def outer_at(self, step):
        return lax.rem(self.outer + step, self.outers)

    def pair_at(self, step):
        return lax.rem(self.pair + step, 4)

    def device(self, outer, inner):
        return outer * GROUP + inner


class Gather:
    def __init__(self, place, buffer, scratch, slots):
        self.place, self.buffer = place, buffer
        self.send, self.recv = scratch.sem_send, scratch.sem_recv
        self.slots = slots

    def first(self, step, start):
        at = self.place
        slot = self.buffer.at[at.core, at.pair, at.outer if start else at.outer_at(step)]
        mine = self.buffer.at[at.core, at.pair, at.outer]
        source = at.outer if start else at.outer_at(step)
        return remote(
            mine, slot, self.send.at[self.slots[0], self.slots[1] + step],
            self.recv.at[self.slots[0], self.slots[1] + source],
            at.device(at.outer_at(step), at.inner),
        )

    def second(self, step, start):
        at = self.place
        source = at.pair if start else at.pair_at(step)
        return remote(
            self.buffer.at[at.core, at.pair], self.buffer.at[at.core, source],
            self.send.at[2, self.slots[2] + step], self.recv.at[2, self.slots[2] + source],
            at.device(at.outer, at.pair_at(step) * 2 + at.core),
        )

    def third(self, start):
        at = self.place
        source = at.core if start else 1 - at.core
        return remote(
            self.buffer.at[at.core], self.buffer.at[source], self.send.at[2, self.slots[3]],
            self.recv.at[2, self.slots[3]], at.device(at.outer, at.pair * 2 + 1 - at.core),
        )

    def start_first(self):
        for step in range(1, self.place.outers):
            self.first(step, True).start()

    def start_second(self):
        for step in range(1, self.place.outers):
            self.first(step, False).wait()
        for step in range(1, 4):
            self.second(step, True).start()

    def start_third(self):
        for step in range(1, 4):
            self.second(step, False).wait()
        self.third(True).start()

    def finish(self):
        self.third(False).wait()


class ChipSum:
    def __init__(self, place, scratch, key):
        self.place = place
        self.full, self.half, self.others = (
            getattr(scratch, name + key) for name in ("chip_full_", "chip_half_", "chip_others_")
        )
        self.send, self.recv = scratch.sem_send, scratch.sem_recv

    def swap(self):
        at = self.place
        return remote(
            self.full.at[1 - at.core], self.half, self.send.at[2, 0], self.recv.at[2, 0],
            at.chip * 2 + 1 - at.core,
        )

    def cross(self, step, start):
        at = self.place
        source = at.chip if start else at.chip_at(step)
        return remote(
            self.half.at[at.chip_at(step)], self.others.at[source], self.send.at[0, step],
            self.recv.at[0, source], at.chip_at(step) * 2 + at.core,
        )

    def start(self):
        self.swap().start()

    def middle(self):
        at = self.place
        self.swap().wait()
        self.half[...] = low(
            self.full[at.core].astype(jnp.float32) + self.half[...].astype(jnp.float32)
        )
        for step in range(1, at.chips):
            self.cross(step, True).start()

    def total(self):
        at = self.place
        total = self.half[at.chip].astype(jnp.float32)
        for step in range(1, at.chips):
            self.cross(step, False).wait()
            total = total + self.others[at.chip_at(step)].astype(jnp.float32)
        return total


class TableSum(ChipSum):
    def __init__(self, place, scratch):
        super().__init__(place, scratch, "t")
        self.s = scratch

    def share(self, step, start, result):
        at = self.place
        source = at.chip if start else at.chip_at(step)
        return remote(
            result.at[at.core, at.chip], result.at[at.core, source], self.send.at[1, step],
            self.recv.at[1, source], at.chip_at(step) * 2 + at.core,
        )

    def swap_back(self, start, result):
        at = self.place
        source = at.core if start else 1 - at.core
        return remote(
            result.at[at.core], result.at[source], self.send.at[2, 1], self.recv.at[2, 1],
            at.chip * 2 + 1 - at.core,
        )

    def start(self):
        s = self.s
        table = low(dot(s.spread[...], s.per_block[...]))
        for chunk in range(self.place.devices):
            self.full[chunk % 2, chunk // 2] = table[chunk * 16 : (chunk + 1) * 16]
        super().start()

    def late(self, result):
        at, s = self.place, self.s
        result[at.core, at.chip] = low(self.total() * s.inverse[0:1, :])
        for step in range(1, at.chips):
            self.share(step, True, result).start()

    def last(self, result):
        for step in range(1, self.place.chips):
            self.share(step, False, result).wait()
        self.swap_back(True, result).start()

    def finish(self, result):
        self.swap_back(False, result).wait()


class GradSum:
    def __init__(self, place, scratch, key, first):
        self.place = place
        self.half, self.quarter, self.last = (
            getattr(scratch, name + key) for name in ("half_", "quarter_", "last_")
        )
        self.full = scratch.gather_two.at[:, :, :, first : first + self.last.shape[1]]
        self.send, self.recv = scratch.sem_send, scratch.sem_recv

    def swap(self):
        at = self.place
        return remote(
            self.full.at[1 - at.core], self.half, self.send.at[2, 7], self.recv.at[2, 7],
            at.device(at.outer, at.pair * 2 + 1 - at.core),
        )

    def across(self, step, start):
        at = self.place
        source = at.pair if start else at.pair_at(step)
        return remote(
            self.half.at[at.pair_at(step)], self.quarter.at[source], self.send.at[2, 8 + step],
            self.recv.at[2, 8 + source], at.device(at.outer, at.pair_at(step) * 2 + at.core),
        )

    def along(self, step, start):
        at = self.place
        source = at.outer if start else at.outer_at(step)
        return remote(
            self.quarter.at[at.pair, at.outer_at(step)], self.last.at[source], self.send.at[2, 12 + step],
            self.recv.at[2, 12 + source], at.device(at.outer_at(step), at.inner),
        )

    def start(self, chunk_of):
        at = self.place

        @pl.loop(0, at.devices)
        def _(chunk):
            inner = lax.rem(chunk, GROUP)
            self.full[lax.rem(inner, 2), lax.div(inner, 2), lax.div(chunk, GROUP)] = low(
                chunk_of(chunk)
            )

        self.swap().start()

    def second(self):
        at = self.place
        self.swap().wait()

        @pl.loop(0, 4)
        def _(pair):
            self.half[pair] = low(
                self.full[at.core, pair].astype(jnp.float32) + self.half[pair].astype(jnp.float32)
            )

        for step in range(1, 4):
            self.across(step, True).start()

    def third(self):
        at = self.place
        total = self.half[at.pair].astype(jnp.float32)
        for step in range(1, 4):
            self.across(step, False).wait()
            total = total + self.quarter[at.pair_at(step)].astype(jnp.float32)
        self.quarter[at.pair] = low(total)
        for step in range(1, at.outers):
            self.along(step, True).start()

    def finish(self):
        at = self.place
        total = self.quarter[at.pair, at.outer].astype(jnp.float32)
        for step in range(1, at.outers):
            self.along(step, False).wait()
            total = total + self.last[at.outer_at(step)].astype(jnp.float32)
        return total


def layer_kernel(names, devices, *refs):
    s = types.SimpleNamespace(**dict(zip(names, refs)))
    at = Place(devices)
    points, width = s.features_far.shape
    tiles = points // TILE
    blocks = points // BLOCK
    share = width // devices
    tile_blocks = TILE // BLOCK
    f32 = jnp.float32

    barrier = pltpu.get_barrier_semaphore()
    pl.semaphore_signal(
        barrier, inc=1, device_id=(at.chip * 2 + 1 - at.core,),
        device_id_type=pl.DeviceIdType.MESH,
    )
    for step in range(1, 4):
        pl.semaphore_signal(
            barrier, inc=1, device_id=(at.device(at.outer, at.pair_at(step) * 2 + at.core),),
            device_id_type=pl.DeviceIdType.MESH,
        )
    for step in range(1, at.outers):
        pl.semaphore_signal(
            barrier, inc=1, device_id=(at.device(at.outer_at(step), at.inner),),
            device_id_type=pl.DeviceIdType.MESH,
        )

    def tile_load(source, tile):
        slot = lax.rem(tile, 2)
        where = pl.ds(pl.multiple_of(tile * TILE, TILE), TILE)
        return pltpu.make_async_copy(
            source.at[where, :], s.load_slots.at[slot], s.sem_in.at[slot]
        )

    for tile in range(2):
        tile_load(s.features_far, tile).start()

    class Aside:
        def __init__(self, first, *buffers):
            self.pairs = []
            row = first
            for buffer in buffers:
                for start in range(0, buffer.shape[0], width):
                    near = buffer.at[start : start + width]
                    far = s.aside.at[row : row + width]
                    self.pairs.append((near, far, s.sem_aside.at[row // width]))
                    row += width

        def store(self):
            for near, far, sem in self.pairs:
                pltpu.make_async_copy(near, far, sem).start()

        def stored(self):
            for near, far, sem in self.pairs:
                pltpu.make_async_copy(near, far, sem).wait()

        def load(self):
            for near, far, sem in self.pairs:
                pltpu.make_async_copy(far, near, sem).start()

        def loaded(self):
            for near, far, sem in self.pairs:
                pltpu.make_async_copy(far, near, sem).wait()

    aside_a = Aside(0, s.u1, s.kv)
    aside_b = Aside(3 * width, s.e1, s.o, s.u2, s.u3)

    def columns(tile):
        return pl.ds(pl.multiple_of(tile * TILE, TILE), TILE)

    def block_columns(block):
        return pl.ds(pl.multiple_of(block * BLOCK, BLOCK), BLOCK)

    def column(index):
        return s.cols[:, index : index + 1]

    def hidden_column(index):
        return jnp.concatenate([column(8 + 2 * index), column(9 + 2 * index)], axis=0)

    def out_copy(tile, source, target):
        where = pl.ds(pl.multiple_of(tile * TILE, TILE), TILE)
        return pltpu.make_async_copy(
            source.at[:, where], target.at[:, where], s.sem_out.at[tile]
        )

    def end_out(source, target):
        for tile in range(tiles):
            out_copy(tile, source, target).wait()

    def pack_square(matrix):
        for row in range(share):
            s.pack[matrix * share + row : matrix * share + row + 1, :] = s.square_weight[
                matrix : matrix + 1, row * width : (row + 1) * width
            ]

    split = s.gather_one.shape[3]
    for matrix in range(4):
        pack_square(matrix)
    s.gather_one[at.core, at.pair, at.outer] = low(s.pack[:split, :])
    pl.semaphore_wait(barrier, 4 + at.outers - 1)
    one = Gather(at, s.gather_one, s, (1, 0, 2, 6))
    two = Gather(at, s.gather_two, s, (2, 12, 8, 7))
    one.start_first()

    for matrix in range(4, 7):
        pack_square(matrix)
    for matrix in range(2):
        for half in range(2):
            for row in range(share):
                place = (7 + 2 * matrix + half) * share + row
                start = row * F + half * width
                s.pack[place : place + 1, :] = s.expand_weight[
                    matrix : matrix + 1, start : start + width
                ]
        for row in range(2 * share):
            place = (11 + 2 * matrix) * share + row
            s.pack[place : place + 1, :] = s.contract_weight[
                matrix : matrix + 1, row * width : (row + 1) * width
            ]
    s.pack[15 * share : 16 * share, :LANES] = s.fourier_weight[...]
    s.pack[15 * share : 16 * share, LANES:] = jnp.zeros((share, LANES), f32)
    live = s.point_mask[...].astype(f32)
    counts = dot_bt(jnp.ones((8, LANES), jnp.bfloat16), low(live))
    s.pack[15 * share : 15 * share + 1, LANES : LANES + blocks] = counts[:1]
    lane = lax.broadcasted_iota(jnp.int32, (1, LANES), 1)
    wide_block = head_of(lax.broadcasted_iota(jnp.int32, (1, E * blocks), 1))
    item_row = jnp.zeros((1, LANES), f32)
    item_wide = jnp.zeros((1, E * blocks), jnp.int32)
    for block in range(blocks):
        item_row = jnp.where(lane == block, s.items[block].astype(f32), item_row)
        item_wide = jnp.where(wide_block == block, s.items[block], item_wide)
    s.pack[15 * share + 1 : 15 * share + 2, LANES:] = item_row
    s.gather_two[at.core, at.pair, at.outer] = low(s.pack[split:, :])

    row_at = lax.broadcasted_iota(jnp.int32, (width, width), 0)
    lane_at = lax.broadcasted_iota(jnp.int32, (width, width), 1)
    s.eye[...] = jnp.where(row_at == lane_at, 1.0, 0.0).astype(jnp.bfloat16)
    s.heads[...] = jnp.where(head_of(row_at) == head_of(lane_at), 1.0, 0.0).astype(jnp.bfloat16)
    s.small[...] = jnp.zeros(s.small.shape, f32)
    s.small[0:8, :] = s.vector_weight[...]
    for row in range(2):
        for half in range(2):
            s.small[8 + 2 * row + half : 9 + 2 * row + half, :] = s.hidden_weight[
                row : row + 1, half * width : (half + 1) * width
            ]
    s.small[12:14, : FOUR // 2] = s.fourier_basis[...]
    s.cols[...] = s.small[...].T
    rows_wide = lax.broadcasted_iota(jnp.int32, s.spread.shape, 0)
    lanes_wide = lax.broadcasted_iota(jnp.int32, s.spread.shape, 1)
    s.spread[...] = jnp.where(
        (item_wide == head_of(rows_wide)) & (((rows_wide ^ lanes_wide) & (E - 1)) == 0), 1.0, 0.0
    ).astype(jnp.bfloat16)
    s.vector_sum[...] = jnp.zeros(s.vector_sum.shape, f32)
    speed = (lax.broadcasted_iota(jnp.int32, (E // 4, 1), 0).astype(f32) + 1.0) * (
        math.pi / (E // 4)
    )

    def add_sum(index, values):
        for part in range(values.shape[0] // width):
            s.vector_sum[index + part] += lane_sum(values[part * width : (part + 1) * width])

    def turned_load(source, tile):
        tile_load(source, tile).wait()
        turned = dot_bt(s.eye[...], s.load_slots[lax.rem(tile, 2)])

        @pl.when(tile + 2 < tiles)
        def _():
            tile_load(source, tile + 2).start()

        return turned

    def norm_one(tile, _):
        where = columns(tile)
        turned = turned_load(s.features_far, tile)
        s.turned[:, where] = low(turned)
        scaled, root = column_norm(turned)
        s.root_one[0:1, where] = root
        s.u1[:, where] = low(scaled * column(0) + column(1))

    def fourier_part(tile, _):
        where = pl.ds(pl.multiple_of(tile * PUT, PUT), PUT)
        x_row, y_row = s.coords[0:1, where], s.coords[1:2, where]
        basis = s.cols[: FOUR // 2, :]
        phases = 2.0 * math.pi * (basis[:, 12:13] * x_row + basis[:, 13:14] * y_row)
        s.phi[:, where] = low(jnp.concatenate([jnp.cos(phases), jnp.sin(phases)], axis=0))

    def angle_part(tile, _):
        where = pl.ds(pl.multiple_of(tile * PUT, PUT), PUT)
        angles = jnp.concatenate(
            [speed * s.coords[0:1, where], speed * s.coords[1:2, where]], axis=0
        )
        s.cosine[:, where] = jnp.cos(angles)
        s.sine[:, where] = jnp.sin(angles)
        for block in range(PUT // BLOCK):
            s.mask[0:1, pl.ds(pl.multiple_of(tile * PUT + block * BLOCK, BLOCK), BLOCK)] = (
                s.point_mask[pl.ds(tile * (PUT // BLOCK) + block, 1), :].astype(f32)
            )

    parts = points // PUT
    lax.fori_loop(0, tiles, norm_one, None)
    one.start_second()
    two.start_first()
    lax.fori_loop(0, 3 * parts // 4, fourier_part, None)
    one.start_third()
    two.start_second()
    lax.fori_loop(0, parts, angle_part, None)
    one.finish()

    group = 16 // share

    def chunk_pair(buffer, index):
        parts = []
        for step in range(group):
            chunk = index * group + step
            inner = lax.rem(chunk, GROUP)
            parts.append(
                buffer[lax.rem(inner, 2), lax.div(inner, 2), lax.div(chunk, GROUP)].astype(f32)
            )
        return parts

    def join(parts, piece):
        return low(
            jnp.concatenate([part[piece * share : (piece + 1) * share] for part in parts], axis=0)
        )

    @pl.loop(0, devices // group)
    def _(index):
        parts = chunk_pair(s.gather_one, index)
        where = pl.ds(pl.multiple_of(index * 16, 16), 16)
        for piece in range(3):
            s.w_qkv[where, piece * width : (piece + 1) * width] = join(parts, piece)
        s.w_o[where, :] = join(parts, 3)

    def flip(matrix):
        return low(dot_bt(s.eye[...], matrix))

    for piece in range(3):
        s.t_qkv[piece * width : (piece + 1) * width, :] = flip(
            s.w_qkv[:, piece * width : (piece + 1) * width]
        )
    s.t_o[...] = flip(s.w_o[...])

    def block_product(left, right):
        return compress(dot_bt(left, right))

    def put_products(tile, left, right):
        for block in range(tile_blocks):
            lanes = slice(block * BLOCK, (block + 1) * BLOCK)
            where = pl.ds(pl.multiple_of((tile * tile_blocks + block) * E, E), E)
            s.per_block[where, :] = low(block_product(left[:, lanes], right[:, lanes]))

    def summary(table, tile, block):
        item = s.items[tile * tile_blocks + block]
        rows = jnp.concatenate([table[0, item], table[1, item]], axis=0)
        return jnp.concatenate([rows] * H, axis=0) * s.heads[...]

    def per_block(tile, function):
        return jnp.concatenate([function(block) for block in range(tile_blocks)], axis=1)

    def lanes_of(block):
        return slice(block * BLOCK, (block + 1) * BLOCK)

    def phase_a(tile, _):
        where = columns(tile)
        projected = dot(s.t_qkv[...], s.u1[:, where])
        cosine, sine = s.cosine[:, where], s.sine[:, where]
        s.q[:, where] = low(turn(projected[:width], cosine, sine, 1.0))
        keys = low(turn(projected[width : 2 * width], cosine, sine, 1.0) * s.mask[0:1, where])
        values = low(projected[2 * width :])
        s.kv[:width, where] = keys
        s.kv[width:, where] = values
        put_products(tile, values, keys)

    lax.fori_loop(0, tiles, phase_a, None)
    table_sum = TableSum(at, s)
    table_sum.start()
    aside_a.store()
    table_sum.middle()
    lax.fori_loop(3 * parts // 4, parts, fourier_part, None)
    two.start_third()

    def take_two(index, carried):
        parts = chunk_pair(s.gather_two, index)
        where = pl.ds(pl.multiple_of(index * 16, 16), 16)
        for piece in range(2):
            s.w_kv[where, piece * width : (piece + 1) * width] = join(parts, piece)
            s.w_w1[where, piece * width : (piece + 1) * width] = join(parts, 3 + piece)
            s.w_p1[where, piece * width : (piece + 1) * width] = join(parts, 5 + piece)
        s.w_do[where, :] = join(parts, 2)
        both = pl.ds(pl.multiple_of(index * 32, 32), 32)
        for piece, target in ((7, s.w_w2), (9, s.w_p2)):
            target[both, :] = low(
                jnp.concatenate([part[piece * share : (piece + 2) * share] for part in parts], axis=0)
            )
        for part in parts:
            count_row = part[11 * share : 11 * share + 1, LANES:]
            item_at = part[11 * share + 1 : 11 * share + 2, LANES:]
            carried = carried + jnp.where(item_at == own_item, count_row, 0.0)
        s.fourier[where, :] = jnp.concatenate(
            [part[11 * share : 12 * share, :LANES] for part in parts], axis=0
        )
        return carried

    two.finish()
    own_item = at.chip.astype(f32)
    found = lax.fori_loop(0, devices // group, take_two, jnp.zeros((1, LANES), f32))
    s.inverse[0:1, :] = jnp.broadcast_to(1.0 / jnp.sum(found, axis=1, keepdims=True), (1, width))
    w_dq = jnp.concatenate(
        [s.fourier[pl.ds(0, FOUR, stride=2), :], s.fourier[pl.ds(1, FOUR, stride=2), :]], axis=1
    )
    s.t_dq[...] = low(w_dq.T)
    table_sum.late(s.table_self)
    for piece in range(2):
        cols = slice(piece * width, (piece + 1) * width)
        s.t_kv[cols, :] = flip(s.w_kv[:, cols])
        s.t_w1[cols, :] = flip(s.w_w1[:, cols])
        s.t_p1[cols, :] = flip(s.w_p1[:, cols])
        s.t_w2[:, cols] = flip(s.w_w2[cols, :])
        s.t_p2[:, cols] = flip(s.w_p2[cols, :])
    s.t_do[...] = flip(s.w_do[...])
    table_sum.last(s.table_self)
    table_sum.finish(s.table_self)

    def phase_b(tile, _):
        where = columns(tile)
        mask = s.mask[0:1, where]
        queries = s.q[:, where]
        mixed = per_block(
            tile, lambda b: dot(summary(s.table_self, tile, b), queries[:, lanes_of(b)])
        )
        attended = low(mixed * mask)
        s.o[:, where] = attended
        first_sum = s.turned[:, where].astype(f32) + dot(s.t_o[...], attended)
        scaled_two, root_two = column_norm(first_sum)
        s.root_two[0:1, where] = root_two
        s.xh2[:, where] = low(scaled_two)
        middle = low(scaled_two * column(2) + column(3))
        s.u2[:, where] = middle
        hidden_pre = dot(s.t_w1[...], middle) + hidden_column(0)
        hidden = low(gelu_alone(hidden_pre))
        s.e1[:, where] = hidden
        s.slope[:, where] = low(hidden_pre)
        encoded = first_sum + dot(s.t_w2[...], hidden) + column(6)
        scaled_three, root_three = column_norm(encoded)
        s.root_three[0:1, where] = root_three
        s.xh3[:, where] = low(scaled_three)
        outer = low(scaled_three * column(4) + column(5))
        s.u3[:, where] = outer
        pair = dot(s.t_kv[...], outer)
        keys = low(pair[:width] * mask)
        values = low(pair[width:])
        s.kvd[:width, where] = keys
        s.kvd[width:, where] = values
        put_products(tile, values, keys)

    lax.fori_loop(0, tiles, phase_b, None)
    table_sum.start()
    aside_b.store()
    table_sum.middle()

    for tile in range(2):
        tile_load(s.cotangent_far, tile).start()
    aside_a.stored()

    def cross_inputs(tile, _):
        where = columns(tile)
        s.qd[:, where] = low(dot(s.t_dq[...], s.phi[:, where]))
        turned = turned_load(s.cotangent_far, tile)
        add_sum(7, turned)
        turned = low(turned)
        s.u1[:, where] = turned
        s.kv[:, where] = low(dot(s.w_p2[...], turned))

    def slopes(tile, _):
        where = columns(tile)
        s.slope[:, where] = low(gelu_slope(s.slope[:, where].astype(f32)))

    lax.fori_loop(0, tiles, cross_inputs, None)
    table_sum.late(s.table_other)
    lax.fori_loop(0, tiles, slopes, None)
    aside_b.stored()
    table_sum.last(s.table_other)
    table_sum.finish(s.table_other)

    def phase_c(tile, _):
        where = columns(tile)
        mask = s.mask[0:1, where]
        queries = s.qd[:, where]
        tables = [summary(s.table_other, tile, block) for block in range(tile_blocks)]
        decoded = low(
            per_block(tile, lambda b: dot(tables[b], queries[:, lanes_of(b)])) * mask
        )
        s.u2[:, where] = decoded
        latent_low = low(dot(s.t_do[...], decoded))
        s.o[:, where] = latent_low
        hidden, slope = gelu_both(dot(s.t_p1[...], latent_low) + hidden_column(1))
        s.e1[:, where] = low(hidden)
        grad_spread = s.kv[:, where].astype(f32) * slope
        add_sum(10, grad_spread)
        grad_spread = low(grad_spread)
        s.kv[:, where] = grad_spread
        grad_latent = low(s.u1[:, where].astype(f32) + dot(s.w_p1[...], grad_spread))
        s.u3[:, where] = grad_latent
        grad_decoded = low(dot(s.w_do[...], grad_latent) * mask)
        put_products(tile, grad_decoded, queries)
        s.qd[:, where] = grad_decoded

    lax.fori_loop(0, tiles, phase_c, None)
    table_sum.start()
    table_sum.middle()

    def cross_query_grads(tile, _):
        where = columns(tile)
        upstream = s.qd[:, where]
        grad = per_block(
            tile, lambda b: dot_at(summary(s.table_other, tile, b), upstream[:, lanes_of(b)])
        )
        s.qd[:, where] = low(grad)

    def outputs(tile, _):
        where = columns(tile)
        output = dot(s.t_do[...], s.u2[:, where]) + dot(s.t_p2[...], s.e1[:, where]) + column(7)
        s.qd[:, where] = low(output)
        out_copy(tile, s.qd, s.layer_output).start()

    lax.fori_loop(0, tiles, cross_query_grads, None)
    s.grad_dq[...] = dot_bt(s.phi[...], s.qd[...])
    s.fourier[pl.ds(0, FOUR, stride=2), :] = s.grad_dq[:, :LANES]
    s.fourier[pl.ds(1, FOUR, stride=2), :] = s.grad_dq[:, LANES:]
    s.grad_o[...] = dot_bt(s.u2[...], s.u3[...])
    table_sum.late(s.table_third)
    s.grad_w1[...] = dot_bt(s.o[...], s.kv[...])
    s.grad_w2[...] = dot_bt(s.e1[...], s.u1[...])
    zeros = jnp.zeros((share, LANES), f32)

    def rows_of(chunk, count=1):
        size = share * count
        return pl.ds(pl.multiple_of(chunk * size, size), size)

    def chunk_c(chunk):
        where = rows_of(chunk)
        return jnp.concatenate(
            [
                s.grad_o[where, :],
                s.grad_w1[where, :width],
                s.grad_w1[where, width:],
                s.grad_w2[rows_of(chunk, 2), :],
                jnp.concatenate([s.fourier[where, :], zeros], axis=1),
            ],
            axis=0,
        )

    sum_c = GradSum(at, s, "c", 0)
    sum_c.start(chunk_c)
    lax.fori_loop(0, tiles, outputs, None)
    table_sum.last(s.table_third)
    end_out(s.qd, s.layer_output)
    aside_a.load()
    aside_b.load()
    sum_c.second()
    table_sum.finish(s.table_third)

    def phase_d(tile, _):
        where = columns(tile)
        mask = s.mask[0:1, where]
        keys, values = s.kvd[:width, where], s.kvd[width:, where]
        tables = [summary(s.table_third, tile, block) for block in range(tile_blocks)]
        grad_keys = per_block(tile, lambda b: dot_at(tables[b], values[:, lanes_of(b)])) * mask
        grad_values = per_block(tile, lambda b: dot(tables[b], keys[:, lanes_of(b)]))
        grad_pair = low(jnp.concatenate([grad_keys, grad_values], axis=0))
        s.kvd[:, where] = grad_pair
        grad_outer = dot(s.w_kv[...], grad_pair)
        scaled = s.xh3[:, where].astype(f32)
        add_sum(4, grad_outer * scaled)
        add_sum(5, grad_outer)
        grad_encoded = column_norm_back(
            grad_outer, scaled, s.root_three[0:1, where], column(4)
        )
        add_sum(6, grad_encoded)
        grad_encoded_low = low(grad_encoded)
        s.xh3[:, where] = grad_encoded_low
        grad_hidden = dot(s.w_w2[...], grad_encoded_low) * s.slope[:, where].astype(f32)
        add_sum(8, grad_hidden)
        grad_hidden = low(grad_hidden)
        s.slope[:, where] = grad_hidden
        grad_middle = dot(s.w_w1[...], grad_hidden)
        scaled = s.xh2[:, where].astype(f32)
        add_sum(2, grad_middle * scaled)
        add_sum(3, grad_middle)
        grad_first = grad_encoded + column_norm_back(
            grad_middle, scaled, s.root_two[0:1, where], column(2)
        )
        grad_first = low(grad_first)
        s.xh2[:, where] = grad_first
        grad_attended = low(dot(s.w_o[...], grad_first) * mask)
        s.qd[:, where] = grad_attended
        put_products(tile, grad_attended, s.q[:, where])

    lax.fori_loop(0, tiles // 2, phase_d, None)
    sum_c.third()
    lax.fori_loop(tiles // 2, tiles, phase_d, None)
    table_sum.start()
    s.grads_c[...] = sum_c.finish()
    table_sum.middle()
    aside_a.loaded()
    aside_b.loaded()

    def query_grads(tile, _):
        where = columns(tile)
        upstream = s.qd[:, where]
        grad = per_block(
            tile, lambda b: dot_at(summary(s.table_self, tile, b), upstream[:, lanes_of(b)])
        )
        s.q[:, where] = low(turn(grad, s.cosine[:, where], s.sine[:, where], -1.0))

    lax.fori_loop(0, tiles, query_grads, None)
    s.grad_o[...] = dot_bt(s.o[...], s.xh2[...])
    s.grad_qkv[:, :width] = dot_bt(s.u1[...], s.q[...])
    table_sum.late(s.table_other)
    s.grad_kv[...] = dot_bt(s.u3[...], s.kvd[...])
    s.grad_w2[...] = dot_bt(s.e1[...], s.xh3[...])
    s.grad_w1[...] = dot_bt(s.u2[...], s.slope[...])

    def chunk_d(chunk):
        where = rows_of(chunk)
        return jnp.concatenate(
            [
                s.grad_kv[where, :width],
                s.grad_kv[where, width:],
                s.grad_o[where, :],
                s.grad_w1[where, :width],
                s.grad_w1[where, width:],
                s.grad_w2[rows_of(chunk, 2), :],
                s.grad_qkv[where, :width],
            ],
            axis=0,
        )

    sum_d = GradSum(at, s, "d", 0)
    sum_d.start(chunk_d)
    table_sum.last(s.table_other)
    table_sum.finish(s.table_other)
    sum_d.second()

    def phase_e(tile, _):
        where = columns(tile)
        mask = s.mask[0:1, where]
        keys, values = s.kv[:width, where], s.kv[width:, where]
        tables = [summary(s.table_other, tile, block) for block in range(tile_blocks)]
        grad_keys = per_block(tile, lambda b: dot_at(tables[b], values[:, lanes_of(b)])) * mask
        grad_values = low(per_block(tile, lambda b: dot(tables[b], keys[:, lanes_of(b)])))
        s.kv[:width, where] = low(turn(grad_keys, s.cosine[:, where], s.sine[:, where], -1.0))
        s.kv[width:, where] = grad_values

    lax.fori_loop(0, tiles, phase_e, None)
    s.grad_qkv[:, width:] = dot_bt(s.u1[...], s.kv[...])
    sum_e = ChipSum(at, s, "t")

    @pl.loop(0, devices)
    def _(chunk):
        where = rows_of(chunk)
        s.chip_full_t[lax.rem(chunk, 2), lax.div(chunk, 2)] = low(
            jnp.concatenate(
                [s.grad_qkv[where, width : 2 * width], s.grad_qkv[where, 2 * width :]], axis=0
            )
        )

    sum_e.start()

    def phase_f(tile, _):
        where = columns(tile)
        grad_normed = dot(
            s.w_qkv[...], jnp.concatenate([s.q[:, where], s.kv[:, where]], axis=0)
        )
        turned = s.turned[:, where].astype(f32)
        root = s.root_one[0:1, where]
        scaled = (turned - jnp.sum(turned, axis=0, keepdims=True) * (1.0 / width)) * root
        add_sum(0, grad_normed * scaled)
        add_sum(1, grad_normed)
        grad_input = s.xh2[:, where].astype(f32) + column_norm_back(
            grad_normed, scaled, root, column(0)
        )
        s.xh2[:, where] = low(grad_input)
        out_copy(tile, s.xh2, s.input_grad).start()

    sum_e.middle()

    def gather_sums(indices):
        lane_wide = lax.broadcasted_iota(jnp.int32, (width, LANES), 1)
        sums = s.vector_cols[...]
        for index in indices:
            sums = jnp.where(
                lane_wide == index, jnp.sum(s.vector_sum[index], axis=1, keepdims=True), sums
            )
        s.vector_cols[...] = sums

    s.vector_cols[...] = jnp.zeros(s.vector_cols.shape, f32)
    gather_sums(range(2, 12))
    lax.fori_loop(0, tiles // 2, phase_f, None)
    sum_d.third()
    lax.fori_loop(tiles // 2, tiles, phase_f, None)
    end_out(s.xh2, s.input_grad)
    s.grads_d[...] = sum_d.finish()
    s.grads_e[...] = sum_e.total()
    squares = sum(
        jnp.sum(grads[...] * grads[...], axis=0, keepdims=True)
        for grads in (s.grads_c, s.grads_d, s.grads_e)
    )

    gather_sums(range(2))
    turned_sums = s.vector_cols[...].T
    high = low(squares).astype(f32)
    s.final_near[at.core] = low(
        jnp.concatenate(
            [turned_sums[:12], high, squares - high, jnp.zeros((2, width), f32)], axis=0
        )
    )

    def final_core(start):
        source = at.core if start else 1 - at.core
        return remote(
            s.final_near.at[at.core], s.final_near.at[source], s.sem_send.at[2, 1],
            s.sem_recv.at[2, 1], at.chip * 2 + 1 - at.core,
        )

    def final_chips(step, start):
        source = at.chip if start else at.chip_at(step)
        return remote(
            s.final_far.at[at.chip], s.final_far.at[source], s.sem_send.at[1, step],
            s.sem_recv.at[1, source], at.chip_at(step) * 2 + at.core,
        )

    final_core(True).start()
    final_core(False).wait()
    total = s.final_near[0].astype(f32) + s.final_near[1].astype(f32)
    square_sum = total[12:13] + total[13:14]
    high = low(square_sum).astype(f32)
    s.final_far[at.chip] = low(
        jnp.concatenate([total[:12], high, square_sum - high, total[14:]], axis=0)
    )
    for step in range(1, at.chips):
        final_chips(step, True).start()
    for step in range(1, at.chips):
        final_chips(step, False).wait()
    total = s.final_far[0].astype(f32)
    for index in range(1, at.chips):
        total = total + s.final_far[index].astype(f32)
    s.vector_all[...] = total


def update_kernel(share, *refs):
    sources, refs = refs[:2], refs[2:]
    grads_c, grads_d, grads_e, vector_all = refs[:4]
    weights_far = refs[4:22]
    targets = refs[22:24]
    norm_out = refs[24]
    results = refs[25:43]
    flat_square, flat_expand, flat_contract, *held, sems, weight_sems = refs[43:]
    held, turned_out, weights = held[:2], held[2:4], held[4:]
    weight_loads = [
        pltpu.make_async_copy(far, near, weight_sems.at[index])
        for index, (far, near) in enumerate(zip(weights_far, weights))
    ]
    loads, stores = [], []
    size = targets[0].shape[0] // PIECES
    for piece in range(PIECES):
        where = slice(piece * size, (piece + 1) * size)
        for index in range(2):
            near = held[index].at[:, where]
            own = turned_out[index].at[where]
            loads.append(
                pltpu.make_async_copy(
                    sources[index].at[:, where], near, sems.at[0, index, piece]
                )
            )
            stores.append(
                pltpu.make_async_copy(own, targets[index].at[where], sems.at[1, index, piece])
            )
    for load in loads + weight_loads:
        load.start()
    for piece in range(PIECES):
        where = slice(piece * size, (piece + 1) * size)
        for index in range(2):
            loads[2 * piece + index].wait()
            part = held[index][:, where].astype(turned_out[index].dtype)
            turned_out[index][where] = part.T
            stores[2 * piece + index].start()
    width = grads_c.shape[1]
    places = [(grads_d, 7), (grads_e, 0), (grads_e, 1), (grads_d, 2), (grads_d, 0), (grads_d, 1), (grads_c, 0)]
    for matrix, (source, piece) in enumerate(places):
        for row in range(share):
            start = piece * share + row
            flat_square[matrix : matrix + 1, row * width : (row + 1) * width] = source[
                start : start + 1, :
            ]
    for matrix, (source, piece) in enumerate(((grads_d, 3), (grads_c, 1))):
        for half in range(2):
            for row in range(share):
                start = (piece + half) * share + row
                target = row * F + half * width
                flat_expand[matrix : matrix + 1, target : target + width] = source[
                    start : start + 1, :
                ]
    for matrix, (source, piece) in enumerate(((grads_d, 5), (grads_c, 3))):
        for row in range(2 * share):
            start = piece * share + row
            flat_contract[matrix : matrix + 1, row * width : (row + 1) * width] = source[
                start : start + 1, :
            ]
    fourier = grads_c[5 * share : 6 * share, :LANES]
    turned = vector_all[...]
    rows = jnp.sum(turned[:12] * turned[:12], axis=0, keepdims=True) + turned[12:13] + turned[13:14]
    norm = jnp.sqrt(jnp.sum(rows, axis=1, keepdims=True))
    norm_out[...] = norm
    factor = jnp.minimum(1.0, CLIP_NORM / (norm + 1e-06))
    hidden = jnp.concatenate(
        [
            jnp.concatenate([turned[8:9], turned[9:10]], axis=1),
            jnp.concatenate([turned[10:11], turned[11:12]], axis=1),
        ],
        axis=0,
    )
    for load in weight_loads:
        load.wait()
    grads = (flat_square[...], flat_expand[...], flat_contract[...], fourier, turned[:8], hidden)
    rates = (RATE_MATRIX,) * 4 + (RATE_VECTOR,) * 2
    for index, (grad, rate) in enumerate(zip(grads, rates)):
        weight, first, second = (weights[3 * index + part][...] for part in range(3))
        values = adam_update(weight, first, second, grad, factor, rate)
        for part in range(3):
            results[3 * index + part][...] = values[part]
    for store in stores:
        store.wait()


def fused(devices, features, coords, fourier_basis, block_items, point_mask, cotangent, *weights):
    points, width = features.shape
    blocks = points // BLOCK
    outers = devices // GROUP
    share = width // devices
    items = points * devices // ITEM_PTS
    bf16, f32 = jnp.bfloat16, jnp.float32
    square, expand, contract, fourier, vector, hidden = (weights[3 * i] for i in range(6))
    vmem = lambda shape, dtype: pltpu.VMEM(shape, dtype)
    inputs = {
        "items": block_items,
        "features_far": features,
        "coords": coords,
        "fourier_basis": fourier_basis,
        "point_mask": point_mask.reshape(blocks, BLOCK),
        "cotangent_far": cotangent,
        "square_weight": square,
        "expand_weight": expand,
        "contract_weight": contract,
        "fourier_weight": fourier.reshape(share, LANES),
        "vector_weight": vector,
        "hidden_weight": hidden,
    }
    rows_c, rows_d, rows_e = 6 * share, 8 * share, 2 * share
    chips = devices // 2
    outputs = {
        "layer_output": ((width, points), bf16),
        "input_grad": ((width, points), bf16),
        "grads_c": ((rows_c, width), f32),
        "grads_d": ((rows_d, width), f32),
        "grads_e": ((rows_e, width), f32),
        "vector_all": ((16, width), f32),
        "aside": ((8 * width, points), bf16),
    }
    tall = lambda rows: vmem((rows, points), bf16)
    scratch = {
        "pack": vmem((16 * share, width), f32),
        "gather_one": vmem((2, 4, outers, 4 * share, width), bf16),
        "gather_two": vmem((2, 4, outers, 12 * share, width), bf16),
        "eye": vmem((width, width), bf16),
        "heads": vmem((width, width), bf16),
        "small": vmem((LANES, width), f32),
        "cols": vmem((width, LANES), f32),
        "spread": vmem((items * E, blocks * E), bf16),
        "vector_sum": vmem((12, width, LANES), f32),
        "vector_cols": vmem((width, LANES), f32),
        "grad_qkv": vmem((width, 3 * width), f32),
        "grad_o": vmem((width, width), f32),
        "grad_kv": vmem((width, 2 * width), f32),
        "grad_w1": vmem((width, F), f32),
        "grad_w2": vmem((F, width), f32),
        "grad_dq": vmem((FOUR, width), f32),
        "fourier": vmem((2 * FOUR + 8, LANES), f32),
        "w_qkv": vmem((width, 3 * width), bf16),
        "t_qkv": vmem((3 * width, width), bf16),
        "w_o": vmem((width, width), bf16),
        "t_o": vmem((width, width), bf16),
        "w_kv": vmem((width, 2 * width), bf16),
        "t_kv": vmem((2 * width, width), bf16),
        "w_do": vmem((width, width), bf16),
        "t_do": vmem((width, width), bf16),
        "w_w1": vmem((width, F), bf16),
        "t_w1": vmem((F, width), bf16),
        "w_p1": vmem((width, F), bf16),
        "t_p1": vmem((F, width), bf16),
        "w_w2": vmem((F, width), bf16),
        "t_w2": vmem((width, F), bf16),
        "w_p2": vmem((F, width), bf16),
        "t_p2": vmem((width, F), bf16),
        "t_dq": vmem((width, FOUR), bf16),
        "mask": vmem((1, points), f32),
        "root_one": vmem((1, points), f32),
        "root_two": vmem((1, points), f32),
        "root_three": vmem((1, points), f32),
        "cosine": vmem((E // 2, points), f32),
        "sine": vmem((E // 2, points), f32),
        "phi": tall(FOUR),
        "u1": tall(width),
        "q": tall(width),
        "kv": tall(2 * width),
        "qd": tall(width),
        "o": tall(width),
        "xh2": tall(width),
        "u2": tall(width),
        "e1": tall(F),
        "slope": tall(F),
        "xh3": tall(width),
        "u3": tall(width),
        "kvd": tall(2 * width),
        "per_block": vmem((blocks * E, width), bf16),
        "inverse": vmem((8, width), f32),
        "table_self": vmem((2, chips, 16, width), bf16),
        "table_other": vmem((2, chips, 16, width), bf16),
        "final_near": vmem((2, 16, width), bf16),
        "final_far": vmem((chips, 16, width), bf16),
        "turned": tall(width),
        "sem_in": pltpu.SemaphoreType.DMA((2,)),
        "sem_aside": pltpu.SemaphoreType.DMA((8,)),
        "table_third": vmem((2, chips, 16, width), bf16),
        "load_slots": vmem((2, TILE, width), bf16),
        "sem_out": pltpu.SemaphoreType.DMA((points // TILE,)),
    }
    for key in ("t",):
        scratch["chip_full_" + key] = vmem((2, chips, 16, width), bf16)
        for part in ("chip_half_", "chip_others_"):
            scratch[part + key] = vmem((chips, 16, width), bf16)
    for key, rows in (("c", rows_c), ("d", rows_d)):
        for part in ("half_", "quarter_"):
            scratch[part + key] = vmem((4, outers, rows, width), bf16)
        scratch["last_" + key] = vmem((outers, rows, width), bf16)
    for key in ("sem_send", "sem_recv"):
        scratch[key] = pltpu.SemaphoreType.DMA((3, chips))
    names = list(inputs) + list(outputs) + list(scratch)
    spaces = {"items": pltpu.SMEM, "features_far": pl.ANY, "cotangent_far": pl.ANY}
    in_specs = [pl.BlockSpec(memory_space=spaces.get(name, pltpu.VMEM)) for name in inputs]
    whole = pl.BlockSpec(memory_space=pltpu.VMEM)
    made = pl.pallas_call(
        functools.partial(layer_kernel, names, devices),
        out_shape=[jax.ShapeDtypeStruct(*shape) for shape in outputs.values()],
        in_specs=in_specs,
        out_specs=[pl.BlockSpec(memory_space=pl.ANY)] * 2
        + [whole] * 4
        + [pl.BlockSpec(memory_space=pl.ANY)],
        scratch_shapes=list(scratch.values()),
        compiler_params=pltpu.CompilerParams(
            collective_id=0, has_side_effects=True, vmem_limit_bytes=VMEM_BYTES
        ),
    )(*inputs.values())
    flat = list(weights)
    for part in range(9, 12):
        flat[part] = flat[part].reshape(share, LANES)
    shapes = [jax.ShapeDtypeStruct((1, 1), f32)] + [
        jax.ShapeDtypeStruct(flat[index].shape, f32) for index in range(18)
    ]
    order = []
    for index in range(6):
        order += [shapes[1 + 3 * index]] * 3
    updated = pl.pallas_call(
        functools.partial(update_kernel, share),
        out_shape=[jax.ShapeDtypeStruct((points, width), dtype) for dtype in (bf16, f32)]
        + [shapes[0]]
        + order,
        in_specs=[pl.BlockSpec(memory_space=pl.ANY)] * 2
        + [whole] * 4
        + [pl.BlockSpec(memory_space=pl.ANY)] * 18,
        out_specs=[pl.BlockSpec(memory_space=pl.ANY)] * 2 + [whole] * 19,
        scratch_shapes=[
            vmem(square.shape, f32),
            vmem(expand.shape, f32),
            vmem(contract.shape, f32),
            vmem((width, points), bf16),
            vmem((width, points), bf16),
            vmem((points, width), bf16),
            vmem((points, width), f32),
            *(vmem(weight.shape, f32) for weight in flat),
            pltpu.SemaphoreType.DMA((2, 2, PIECES)),
            pltpu.SemaphoreType.DMA((18,)),
        ],
        compiler_params=pltpu.CompilerParams(vmem_limit_bytes=VMEM_BYTES),
    )(*made[:6], *flat)
    layer_output, input_grad, norm, *rest = updated
    for part in range(9, 12):
        rest[part] = rest[part].reshape(fourier.shape)
    return (layer_output, input_grad, norm.reshape(()), *rest)


def shards(features, *others):
    devices = lax.axis_size("pts")
    width = features.shape[1]
    if devices % GROUP == 0 and width == 8 * devices:
        return fused(devices, features, *others)
    return plain(features, *others)


def solution(mesh):
    in_specs = (
        P("pts", None),
        P(None, "pts"),
        P(),
        P("pts"),
        P("pts"),
        P("pts", None),
        P(None, "pts"),
        P(None, "pts"),
        P(None, "pts"),
        P(None, "pts"),
        P(None, "pts"),
        P(None, "pts"),
        P(None, "pts"),
        P(None, "pts"),
        P(None, "pts"),
        P("pts"),
        P("pts"),
        P("pts"),
        P(),
        P(),
        P(),
        P(),
        P(),
        P(),
    )
    out_specs = (
        P("pts", None),
        P("pts", None),
        P(),
        P(None, "pts"),
        P(None, "pts"),
        P(None, "pts"),
        P(None, "pts"),
        P(None, "pts"),
        P(None, "pts"),
        P(None, "pts"),
        P(None, "pts"),
        P(None, "pts"),
        P("pts"),
        P("pts"),
        P("pts"),
        P(),
        P(),
        P(),
        P(),
        P(),
        P(),
    )
    return jax.shard_map(shards, mesh=mesh, in_specs=in_specs, out_specs=out_specs, check_vma=False)
```
